32 devices in a mesh: ctx: 8 (over z, x), wt: 4 (over y, core).
Axes of the slice: x: 2, y: 2, z: 4, core: 2. Of those that a mesh axis runs over, the one named last changes fastest.
Arguments:
- layer_input: bfloat16 [4, 2048, 2048], P('wt', 'ctx'), may hold values from -6 to 6
- cotangent: bfloat16 [4, 2048, 2048], P('wt', 'ctx'), may hold values from -6 to 6
- document_length: int32 [4, 8], replicated, may hold values from 1 to 1793, 2048 in all within a row
- adapter_choice_index: int32 [1], replicated, may hold values from 0 to 7
- query_weight: bfloat16 [2048, 2048], P(('ctx', 'wt')), may hold values from -0.125 to 0.125
- key_weight: bfloat16 [2048, 2048], P(('ctx', 'wt')), may hold values from -0.125 to 0.125
- value_weight: bfloat16 [2048, 2048], P(('ctx', 'wt')), may hold values from -0.125 to 0.125
- output_weight: bfloat16 [2048, 2048], P(('ctx', 'wt')), may hold values from -0.125 to 0.125
- gate_weight: bfloat16 [2048, 8192], P(('ctx', 'wt')), may hold values from -0.125 to 0.125
- up_weight: bfloat16 [2048, 8192], P(('ctx', 'wt')), may hold values from -0.125 to 0.125
- down_weight: bfloat16 [8192, 2048], P(('ctx', 'wt')), may hold values from -0.0625 to 0.0625
- query_norm_gain: float32 [2048], replicated, may hold values from 0.25 to 1.75
- key_norm_gain: float32 [2048], replicated, may hold values from 0.25 to 1.75
- attention_norm_gain: float32 [2048], replicated, may hold values from 0.25 to 1.75
- feedforward_norm_gain: float32 [2048], replicated, may hold values from 0.25 to 1.75
- adapter_model_input_maps: bfloat16 [8, 6, 16, 2048], replicated, may hold values from -0.125 to 0.125
- adapter_down_input_maps: bfloat16 [8, 16, 8192], replicated, may hold values from -0.0625 to 0.0625
- adapter_model_output_maps: bfloat16 [8, 5, 16, 2048], replicated, may hold values from -1.5 to 1.5
- adapter_hidden_output_maps: bfloat16 [8, 2, 16, 8192], replicated, may hold values from -1.5 to 1.5
Outputs:
- result: bfloat16 [4, 2048, 2048], P('wt', 'ctx')
- grad_input: float32 [4, 2048, 2048], P('wt', 'ctx')
- grad_a_model: float32 [8, 6, 16, 2048], P(None, None, None, ('ctx', 'wt'))
- grad_a_hidden: float32 [8, 16, 8192], P(None, None, ('ctx', 'wt'))
- grad_b_model: float32 [8, 5, 16, 2048], P(None, None, None, ('ctx', 'wt'))
- grad_b_hidden: float32 [8, 2, 16, 8192], P(None, None, None, ('ctx', 'wt'))
The draws below stay inside these ranges and needn't reach their ends.
Inputs may be any that keep to these rules, and one draw needn't show every extreme that they name: `document_length`: each sequence's lengths sum to 2048; the longest of each is 1793.
All inputs are finite; a program needn't handle non-finite values.
Results may differ from the reference program's by a relative error of at most 0.015.
Values may be sent and summed in bfloat16 or wider, within the bound.
A program may use at most 512 MiB of HBM per device.

```python
import math
import jax
import jax.numpy as jnp
import numpy as np
from jax import lax

MODEL_WIDTH = 2048
NH = 16
HD = 128
FEEDFWD_UNITS = 8192
ADAPTER_RANK = 16
ADAPTER_COUNT = 8
WINDOW = 1024
DOCS = 8
TOK_DEV = 256
SEQ_LEN = 2048
SEQS = 4


def block_levels(stream_key, shape, cuts, low, top_value):
    loudness, own = 1.0, jax.random.fold_in(stream_key, 6)
    for position, blocks in cuts:
        steps = jnp.exp(jax.random.uniform(jax.random.fold_in(own, position), (blocks,), jnp.float32, low / len(cuts), top_value / len(cuts)))
        loudness = loudness * jnp.repeat(steps, shape[position] // blocks).reshape([-1 if axis == position else 1 for axis in range(len(shape))])
    return loudness


def split_up(count, total, most, lean):
    portions = [(1 << 20) // math.isqrt(rank ** lean) + 1 for rank in range(2, count + 1)]
    spare, counts = total - most - (count - 1), [1] * (count - 1)
    while spare > 0:
        movable = [i for i in range(count - 1) if counts[i] < most]
        whole, remaining = sum([portions[i] for i in movable]), spare
        for i in movable:
            addition = min(most - counts[i], max(1, remaining * portions[i] // whole), spare)
            counts[i] = counts[i] + addition
            spare = spare - addition
    return np.array([most] + counts)


def ragged_sizes(rng, number_of, total, most, slope):
    if number_of == 2:
        one = jax.random.randint(rng, (), max(1, total - most), min(most, total - 1) + 1)
        return jnp.stack([one, total - one])
    tallies = jnp.asarray(split_up(number_of, total, most, slope), jnp.int32)
    twos = (number_of - 1) // 2
    giver, taker = tallies[1:1 + 2 * twos:2], tallies[2:2 + 2 * twos:2]
    margin = jnp.minimum(giver - 1, most - taker)
    shifted = jax.random.randint(jax.random.fold_in(rng, 1), (twos,), 0, 1 << 20) % (margin + 1)
    tallies = tallies.at[1:1 + 2 * twos:2].set(giver - shifted).at[2:2 + 2 * twos:2].set(taker + shifted)
    return tallies[jax.random.permutation(jax.random.fold_in(rng, 2), number_of)]


def scatter_about(stream_key, shape, deviation, bound, shards=(), kind=jnp.bfloat16):
    level = block_levels(stream_key, shape, shards, -0.22, 0.18) if shards else 1.0
    array = jax.random.normal(stream_key, shape, jnp.float32) * deviation * level
    return jnp.minimum(jnp.maximum(array, -bound), bound).astype(kind)


def setup_inputs(seed: int = 0) -> dict:
    key_list = jax.random.split(jax.random.key(seed), 20)
    layer_input = scatter_about(key_list[0], (SEQS, SEQ_LEN, MODEL_WIDTH), 1.0, 6.0, ((0, 4), (1, 8)))
    cotangent = scatter_about(key_list[1], (SEQS, SEQ_LEN, MODEL_WIDTH), 1.0, 6.0, ((0, 4), (1, 8)))
    document_length = jax.vmap(lambda own: ragged_sizes(own, DOCS, SEQ_LEN, SEQ_LEN - TOK_DEV + 1, 2))(jax.random.split(key_list[2], SEQS)).reshape((SEQS, DOCS)).astype(jnp.int32)
    adapter_choice_index = jax.random.randint(key_list[3], (1,), 0, ADAPTER_COUNT).astype(jnp.int32)
    query_weight = scatter_about(key_list[4], (MODEL_WIDTH, MODEL_WIDTH), MODEL_WIDTH ** -0.5, 0.125, ((0, 32),))
    key_weight = scatter_about(key_list[5], (MODEL_WIDTH, MODEL_WIDTH), MODEL_WIDTH ** -0.5, 0.125, ((0, 32),))
    value_weight = scatter_about(key_list[6], (MODEL_WIDTH, MODEL_WIDTH), MODEL_WIDTH ** -0.5, 0.125, ((0, 32),))
    output_weight = scatter_about(key_list[7], (MODEL_WIDTH, MODEL_WIDTH), MODEL_WIDTH ** -0.5, 0.125, ((0, 32),))
    gate_weight = scatter_about(key_list[8], (MODEL_WIDTH, FEEDFWD_UNITS), MODEL_WIDTH ** -0.5, 0.125, ((0, 32),))
    up_weight = scatter_about(key_list[9], (MODEL_WIDTH, FEEDFWD_UNITS), MODEL_WIDTH ** -0.5, 0.125, ((0, 32),))
    down_weight = scatter_about(key_list[10], (FEEDFWD_UNITS, MODEL_WIDTH), FEEDFWD_UNITS ** -0.5, 0.0625, ((0, 32),))
    query_norm_gain = jnp.clip(1.0 + 0.15 * jax.random.normal(key_list[11], (MODEL_WIDTH,), jnp.float32), 0.25, 1.75)
    key_norm_gain = jnp.clip(1.0 + 0.15 * jax.random.normal(key_list[12], (MODEL_WIDTH,), jnp.float32), 0.25, 1.75)
    attention_norm_gain = jnp.clip(1.0 + 0.15 * jax.random.normal(key_list[13], (MODEL_WIDTH,), jnp.float32), 0.25, 1.75)
    feedforward_norm_gain = jnp.clip(1.0 + 0.15 * jax.random.normal(key_list[14], (MODEL_WIDTH,), jnp.float32), 0.25, 1.75)
    adapter_model_input_maps = scatter_about(key_list[15], (ADAPTER_COUNT, 6, ADAPTER_RANK, MODEL_WIDTH), MODEL_WIDTH ** -0.5, 0.125)
    adapter_down_input_maps = scatter_about(key_list[16], (ADAPTER_COUNT, ADAPTER_RANK, FEEDFWD_UNITS), FEEDFWD_UNITS ** -0.5, 0.0625)
    adapter_model_output_maps = scatter_about(key_list[17], (ADAPTER_COUNT, 5, ADAPTER_RANK, MODEL_WIDTH), ADAPTER_RANK ** -0.5, 1.5)
    adapter_hidden_output_maps = scatter_about(key_list[18], (ADAPTER_COUNT, 2, ADAPTER_RANK, FEEDFWD_UNITS), ADAPTER_RANK ** -0.5, 1.5)
    return {"layer_input": layer_input, "cotangent": cotangent, "document_length": document_length, "adapter_choice_index": adapter_choice_index, "query_weight": query_weight, "key_weight": key_weight, "value_weight": value_weight, "output_weight": output_weight, "gate_weight": gate_weight, "up_weight": up_weight, "down_weight": down_weight, "query_norm_gain": query_norm_gain, "key_norm_gain": key_norm_gain, "attention_norm_gain": attention_norm_gain, "feedforward_norm_gain": feedforward_norm_gain, "adapter_model_input_maps": adapter_model_input_maps, "adapter_down_input_maps": adapter_down_input_maps, "adapter_model_output_maps": adapter_model_output_maps, "adapter_hidden_output_maps": adapter_hidden_output_maps}


SCALE_ADAPT = 0.5
ROPE_BASE = 500000.0
EPS = 1e-06
NEG_FILL = -1e+30
HIGHEST = lax.Precision.HIGHEST

@jax.custom_vjp
def low(v):
    return lax.optimization_barrier(v.astype(jnp.bfloat16)).astype(jnp.float32)

@jax.custom_vjp
def low_back(v):
    return v

def low_keep(v):
    return (low(v), None)

def low_pass(kept, grad):
    return (grad,)

def back_keep(v):
    return (v, None)

def back_low(kept, grad):
    return (low(grad),)
low.defvjp(low_keep, low_pass)
low_back.defvjp(back_keep, back_low)

def rms_scale(values, gain):
    return values * lax.rsqrt(lax.optimization_barrier(jnp.mean(values * values, axis=-1, keepdims=True)) + EPS) * gain

def rope_tables(positions):
    half_dim = HD // 2
    inv_freq = ROPE_BASE ** (-(jnp.arange(half_dim, dtype=jnp.float32) * 2.0 / HD))
    angles = positions.astype(jnp.float32)[:, None] * inv_freq[None, :]
    return (jnp.cos(angles), jnp.sin(angles))

def rotate(values, cosines, sines):
    row_count = values.shape[0]
    half_dim = HD // 2
    shaped = values.reshape(row_count, NH, HD)
    front_half = shaped[..., :half_dim]
    back_half = shaped[..., half_dim:]
    cos_b = cosines[:, None, :]
    sin_b = sines[:, None, :]
    turned = jnp.concatenate([front_half * cos_b - back_half * sin_b, back_half * cos_b + front_half * sin_b], axis=-1)
    return turned.reshape(row_count, NH * HD)

def project(inputs, weight, adapt_in, adapt_out):
    narrow = jnp.dot(inputs, adapt_in.T, precision=HIGHEST)
    return jnp.dot(inputs, weight, precision=HIGHEST) + SCALE_ADAPT * jnp.dot(narrow, adapt_out, precision=HIGHEST)

def doc_index(positions, lengths):
    bounds = jnp.cumsum(lengths)
    return lax.optimization_barrier(jnp.sum((positions[:, None] >= bounds[None, :]).astype(jnp.int32), axis=1))

def attend(queries, key_all, values, documents):
    seq_count = queries.shape[0]
    block_rows = min(512, seq_count)
    keys_pad = jnp.pad(key_all, ((WINDOW, 0), (0, 0)))
    values_pad = jnp.pad(values, ((WINDOW, 0), (0, 0)))
    docs_pad = jnp.pad(documents, (WINDOW, 0), constant_values=-1)
    score_scale = HD ** (-0.5)

    def one_block(block_id):
        block_start = block_id * block_rows
        query_rows = lax.dynamic_slice_in_dim(queries, block_start, block_rows, 0).reshape(block_rows, NH, HD)
        key_rows = lax.dynamic_slice_in_dim(keys_pad, block_start, block_rows + WINDOW, 0).reshape(block_rows + WINDOW, NH, HD)
        value_rows = lax.dynamic_slice_in_dim(values_pad, block_start, block_rows + WINDOW, 0).reshape(block_rows + WINDOW, NH, HD)
        query_docs = lax.dynamic_slice_in_dim(documents, block_start, block_rows, 0)
        key_docs = lax.dynamic_slice_in_dim(docs_pad, block_start, block_rows + WINDOW, 0)
        query_pos = block_start + jnp.arange(block_rows, dtype=jnp.int32)
        key_pos = block_start - WINDOW + jnp.arange(block_rows + WINDOW, dtype=jnp.int32)
        distance = query_pos[:, None] - key_pos[None, :]
        allowed = (query_docs[:, None] == key_docs[None, :]) & (distance >= 0) & (distance < WINDOW)
        scores = low_back(jnp.einsum('qhd,khd->hqk', query_rows, key_rows, precision=HIGHEST) * score_scale)
        masked = jnp.where(allowed[None], scores, NEG_FILL)
        row_max = lax.optimization_barrier(jnp.max(masked, axis=-1, keepdims=True))
        shifted_exp = jnp.exp(masked - row_max)
        attn_probs = low(shifted_exp / lax.optimization_barrier(jnp.sum(shifted_exp, axis=-1, keepdims=True)))
        blended = jnp.einsum('hqk,khd->qhd', attn_probs, value_rows, precision=HIGHEST)
        return blended.reshape(block_rows, NH * HD)
    pieces = lax.map(jax.checkpoint(one_block), jnp.arange(seq_count // block_rows, dtype=jnp.int32))
    return pieces.reshape(seq_count, NH * HD)

def layer(inputs, lengths, frozen, select_model_input_map, select_hidden_input_map, select_model_output_map, select_hidden_output_map):
    query_weight, key_weight, value_weight, output_weight, gate_weight, up_weight, down_weight, query_norm_gain, key_norm_gain, attention_norm_gain, feedforward_norm_gain = frozen
    seq_count = inputs.shape[0]
    positions = jnp.arange(seq_count, dtype=jnp.int32)
    documents = doc_index(positions, lengths)
    cosines, sines = rope_tables(positions)
    query_pre = low_back(project(inputs, query_weight, select_model_input_map[0], select_model_output_map[0]))
    key_pre = low_back(project(inputs, key_weight, select_model_input_map[1], select_model_output_map[1]))
    value_low = low(low_back(project(inputs, value_weight, select_model_input_map[2], select_model_output_map[2])))
    query_rot = low(rotate(rms_scale(query_pre, query_norm_gain), cosines, sines))
    key_rot = low(rotate(rms_scale(key_pre, key_norm_gain), cosines, sines))
    attended = low(low_back(attend(query_rot, key_rot, value_low, documents)))
    attn_out = low_back(project(attended, output_weight, select_model_input_map[3], select_model_output_map[3]))
    middle = inputs + rms_scale(attn_out, attention_norm_gain)
    middle_low = low(middle)
    gate_pre = low_back(project(middle_low, gate_weight, select_model_input_map[4], select_hidden_output_map[0]))
    up_pre = low_back(project(middle_low, up_weight, select_model_input_map[5], select_hidden_output_map[1]))
    gated = low(jax.nn.silu(gate_pre) * up_pre)
    feed_out = low_back(project(gated, down_weight, select_hidden_input_map, select_model_output_map[4]))
    return middle + rms_scale(feed_out, feedforward_norm_gain)

def reference(layer_input, cotangent, document_length, adapter_choice_index, query_weight, key_weight, value_weight, output_weight, gate_weight, up_weight, down_weight, query_norm_gain, key_norm_gain, attention_norm_gain, feedforward_norm_gain, adapter_model_input_maps, adapter_down_input_maps, adapter_model_output_maps, adapter_hidden_output_maps):
    frozen = tuple((matrix.astype(jnp.float32) for matrix in (query_weight, key_weight, value_weight, output_weight, gate_weight, up_weight, down_weight, query_norm_gain, key_norm_gain, attention_norm_gain, feedforward_norm_gain)))
    selected_adapter = adapter_choice_index[0]

    def forward_layer(inputs, a_model, a_hidden, b_model, b_hidden):
        select_model_input_map = lax.dynamic_index_in_dim(a_model, selected_adapter, 0, keepdims=False)
        select_hidden_input_map = lax.dynamic_index_in_dim(a_hidden, selected_adapter, 0, keepdims=False)
        select_model_output_map = lax.dynamic_index_in_dim(b_model, selected_adapter, 0, keepdims=False)
        select_hidden_output_map = lax.dynamic_index_in_dim(b_hidden, selected_adapter, 0, keepdims=False)

        def one_sequence(paired):
            return layer(paired[0], paired[1], frozen, select_model_input_map, select_hidden_input_map, select_model_output_map, select_hidden_output_map)
        return lax.map(jax.checkpoint(one_sequence), (inputs, document_length))
    layer_output, backward_layer = jax.vjp(forward_layer, layer_input.astype(jnp.float32), adapter_model_input_maps.astype(jnp.float32), adapter_down_input_maps.astype(jnp.float32), adapter_model_output_maps.astype(jnp.float32), adapter_hidden_output_maps.astype(jnp.float32))
    grads = backward_layer(cotangent.astype(jnp.float32))
    return (layer_output.astype(jnp.bfloat16), grads[0], grads[1], grads[2], grads[3], grads[4])
```

```python
import functools

import jax
import jax.numpy as jnp
from jax import lax
from jax.experimental import pallas as pl
from jax.experimental.pallas import tpu as pltpu
from jax.sharding import Mesh
from jax.sharding import PartitionSpec as P

HD = 128
WINDOW = 1024
SCALE_ADAPT = 0.5
ROPE_BASE = 500000.0
EPS = 1e-06
BF = jnp.bfloat16
F32 = jnp.float32
VMEM_BYTES = 48 * 1024 * 1024


def cost(us):
    return pl.CostEstimate(flops=int(us * 1.1e9), bytes_accessed=int(us * 1e6), transcendentals=0)


def dot(a, b, dims=((1,), (0,))):
    return lax.dot_general(a, b, (dims, ((), ())), preferred_element_type=F32)


def dot_nt(a, b):
    return dot(a, b, ((1,), (1,)))


def dot_tn(a, b):
    return dot(a, b, ((0,), (0,)))


SWAP = [(0, 1), (1, 0)]


class Place:
    def __init__(self):
        self.np = lax.axis_size("p")
        self.p, self.x, self.y, self.c = (lax.axis_index(a) for a in ("p", "x", "y", "c"))
        self.quarter = 2 * self.x + self.c
        self.spot = jnp.stack([self.x, self.c, self.y]).astype(jnp.int32)

    def swap_core(self, value):
        return lax.ppermute(value, "c", SWAP)

    def swap_x(self, value):
        return lax.ppermute(value, "x", SWAP)

    def swap_both(self, value):
        return lax.ppermute(value, ("x", "c"), [(0, 3), (1, 2), (2, 1), (3, 0)])

    def swap_y(self, value):
        return lax.ppermute(value, "y", SWAP)

    def shift_p(self, value, by):
        return lax.ppermute(value, "p", [(p, p + by) for p in range(self.np) if 0 <= p + by < self.np])

    def turn_p(self, value, by):
        return lax.ppermute(value, "p", [(p, (p + by) % self.np) for p in range(self.np)])

    def gather4(self, own, work=None):
        across = self.swap_x(own)
        near = jnp.concatenate([own, self.swap_core(own)], axis=0)
        done = None
        if work is not None:
            done = work(near)
            across = after(across, done[0])
        far = jnp.concatenate([across, self.swap_core(across)], axis=0)
        return near, far, done

    def scatter4(self, far, near):
        rows = far.shape[0] // 2
        met = (far[:rows].astype(F32) + self.swap_core(far[rows:]).astype(F32)).astype(BF)
        across = self.swap_x(met)
        near = near(met)
        return near, self.swap_core(near[rows:]), across

    def sum4(self, value):
        def reordered(v, turn):
            v = v.reshape(v.shape[0], 2, 2, -1)
            return jnp.flip(v, turn).reshape(value.shape)

        value = value + reordered(self.swap_core(value), 2)
        return value + reordered(self.swap_x(value), 1)


def pick(v, axis, index):
    return lax.dynamic_index_in_dim(v, index, axis, keepdims=False)


def after(value, *others):
    return lax.optimization_barrier((value,) + others)[0]


def pack_kernel(count, width, offsets, spot_ref, *refs):
    x, c = spot_ref[0], spot_ref[1]
    outs = refs[-4:]
    for dx in range(2):
        for dc in range(2):
            places = offsets((x + dx) % 2, (c + dc) % 2)
            for w, ref in enumerate(refs[:count]):
                for k, place in enumerate(places):
                    at = (w * len(places) + k) * width
                    outs[2 * dx + dc][:, at : at + width] = ref[:, pl.ds(pl.multiple_of(place * width, HD), width)]


def pack(spot, weights, width, offsets):
    rows = weights[0].shape[0]
    size = len(weights) * len(offsets(0, 0)) * width
    if width % HD:
        outs = []
        for d in range(4):
            places = offsets((spot[0] + d // 2) % 2, (spot[1] + d % 2) % 2)
            cuts = [lax.dynamic_slice_in_dim(w, place * width, width, 1) for w in weights for place in places]
            outs.append(jnp.concatenate(cuts, axis=1))
        return outs
    whole = pl.BlockSpec(memory_space=pltpu.VMEM)
    return pl.pallas_call(
        functools.partial(pack_kernel, len(weights), width, offsets),
        in_specs=[pl.BlockSpec(memory_space=pltpu.SMEM)] + [whole] * len(weights),
        out_specs=[whole] * 4,
        out_shape=[jax.ShapeDtypeStruct((rows, size), BF)] * 4,
        compiler_params=pltpu.CompilerParams(vmem_limit_bytes=VMEM_BYTES),
        name="pack_columns",
        cost_estimate=cost(3),
    )(spot, *weights)


def join_kernel(spot_ref, *refs):
    x, c = spot_ref[0], spot_ref[1]
    rows = refs[0].shape[0]
    for dx in range(2):
        for dc in range(2):
            slot = 2 * ((x + dx) % 2) + (c + dc) % 2
            refs[4][pl.ds(pl.multiple_of(slot * rows, rows), rows), :] = refs[2 * dx + dc][...]


def join(spot, parts):
    rows, size = parts[0].shape
    whole = pl.BlockSpec(memory_space=pltpu.VMEM)
    return pl.pallas_call(
        join_kernel,
        in_specs=[pl.BlockSpec(memory_space=pltpu.SMEM)] + [whole] * 4,
        out_specs=whole,
        out_shape=jax.ShapeDtypeStruct((4 * rows, size), BF),
        compiler_params=pltpu.CompilerParams(vmem_limit_bytes=VMEM_BYTES),
        name="join_rows",
        cost_estimate=cost(2),
    )(spot, *parts)


def gate_up_kernel(spot_ref, x_ref, g0_ref, g1_ref, u0_ref, u1_ref, narrow_ref, maps_ref, gate_ref, up_ref, gated_ref):
    half, rank = g0_ref.shape[0], maps_ref.shape[1]
    y = spot_ref[2]
    x0 = x_ref[:, pl.ds(pl.multiple_of(y * half, HD), half)]
    x1 = x_ref[:, pl.ds(pl.multiple_of((1 - y) * half, HD), half)]
    gate = dot(x0, g0_ref[...]) + dot(x1, g1_ref[...])
    gate = gate + SCALE_ADAPT * dot(narrow_ref[:, :rank], maps_ref[0])
    up = dot(x0, u0_ref[...]) + dot(x1, u1_ref[...])
    up = up + SCALE_ADAPT * dot(narrow_ref[:, rank:], maps_ref[1])
    gate_ref[...] = gate.astype(BF)
    up_ref[...] = up.astype(BF)
    gated_ref[...] = (gate * jax.nn.sigmoid(gate) * up).astype(BF)


def gate_up(spot, x, gate_parts, up_parts, narrow, maps):
    rows, width = x.shape
    half, hidden = gate_parts[0].shape
    tile = 256
    steps = hidden // tile
    column = lambda s, spot: (0, (s + spot[2] * (steps // 2)) % steps)
    weight = pl.BlockSpec((half, tile), column)
    out = pl.BlockSpec((rows, tile), lambda s, spot: (0, s))
    return pl.pallas_call(
        gate_up_kernel,
        grid_spec=pltpu.PrefetchScalarGridSpec(
            num_scalar_prefetch=1,
            grid=(steps,),
            in_specs=[pl.BlockSpec((rows, width), lambda s, spot: (0, 0))]
            + [weight] * 4
            + [
                pl.BlockSpec(narrow.shape, lambda s, spot: (0, 0)),
                pl.BlockSpec(maps.shape[:2] + (tile,), lambda s, spot: (0, 0, s)),
            ],
            out_specs=[out] * 3,
        ),
        out_shape=[jax.ShapeDtypeStruct((rows, hidden), BF)] * 3,
        compiler_params=pltpu.CompilerParams(vmem_limit_bytes=VMEM_BYTES),
        name="gate_up",
        cost_estimate=cost(26),
    )(spot, x, *gate_parts, *up_parts, narrow, maps)


def down_kernel(gated_ref, *refs):
    d_refs = refs[:-4]
    in_maps_ref, out_maps_ref, feed_ref, narrow_ref = refs[-4:]
    depth = d_refs[0].shape[0]

    @pl.when(pl.program_id(0) == 0)
    def _():
        narrow_ref[...] = dot_nt(gated_ref[...], in_maps_ref[...]).astype(BF)

    feed = sum(dot(gated_ref[:, k * depth : (k + 1) * depth], ref[...]) for k, ref in enumerate(d_refs))
    feed_ref[...] = (feed + SCALE_ADAPT * dot(narrow_ref[...], out_maps_ref[...])).astype(BF)


def down(gated, part, parts, in_maps, out_maps):
    rows, hidden = gated.shape[0] // 2, gated.shape[1]
    depth, width = parts[0].shape
    rank = in_maps.shape[0]
    tile = 256
    weight = pl.BlockSpec((depth, tile), lambda s: (0, s))
    return pl.pallas_call(
        down_kernel,
        grid=(width // tile,),
        in_specs=[
            pl.BlockSpec((rows, hidden), lambda s: (part, 0)),
            *([weight] * len(parts)),
            pl.BlockSpec(in_maps.shape, lambda s: (0, 0)),
            pl.BlockSpec((rank, tile), lambda s: (0, s)),
        ],
        out_specs=[pl.BlockSpec((rows, tile), lambda s: (0, s)), pl.BlockSpec((rows, rank), lambda s: (0, 0))],
        out_shape=[jax.ShapeDtypeStruct((rows, width), BF), jax.ShapeDtypeStruct((rows, rank), BF)],
        compiler_params=pltpu.CompilerParams(vmem_limit_bytes=VMEM_BYTES),
        name="down",
        cost_estimate=cost(10),
    )(gated, *parts, in_maps, out_maps)


def feed_back_kernel(
    spot_ref,
    grad_ref,
    d0_ref,
    d1_ref,
    d2_ref,
    d3_ref,
    g0_ref,
    g1_ref,
    u0_ref,
    u1_ref,
    gate_ref,
    up_ref,
    gated_ref,
    narrow_ref,
    d_out_ref,
    d_in_ref,
    gu_out_ref,
    gu_in_ref,
    out_ref,
    back_gu_ref,
    maps_ref,
    total,
    grad_gated,
    back_d,
    back_gu,
):
    step, steps = pl.program_id(0), pl.num_programs(0)
    half, rank = g0_ref.shape[0], d_in_ref.shape[0]

    @pl.when(step == 0)
    def _():
        total[...] = jnp.zeros_like(total)
        back_gu[...] = jnp.zeros_like(back_gu)
        back_d[...] = dot_nt(grad_ref[...], d_out_ref[...]).astype(BF)

    for k, ref in enumerate((d0_ref, d1_ref, d2_ref, d3_ref)):

        @pl.when((step >= k * steps // 4) & (step < (k + 1) * steps // 4))
        def _(ref=ref):
            grad_gated[...] = dot_nt(grad_ref[...], ref[...])

    dm = grad_gated[...] + SCALE_ADAPT * dot(back_d[...], d_in_ref[...])
    gate, up = gate_ref[...].astype(F32), up_ref[...].astype(F32)
    sig = jax.nn.sigmoid(gate)
    silu = gate * sig
    du = (dm * silu).astype(BF)
    dg = (dm * up * (sig + silu * (1.0 - sig))).astype(BF)
    y = spot_ref[2]
    total[:, pl.ds(pl.multiple_of(y * half, HD), half)] += dot_nt(dg, g0_ref[...]) + dot_nt(du, u0_ref[...])
    total[:, pl.ds(pl.multiple_of((1 - y) * half, HD), half)] += dot_nt(dg, g1_ref[...]) + dot_nt(du, u1_ref[...])
    back_gu[:, :rank] += dot_nt(dg, gu_out_ref[0])
    back_gu[:, rank:] += dot_nt(du, gu_out_ref[1])
    maps_ref[0] = SCALE_ADAPT * dot_tn(back_d[...], gated_ref[...])
    maps_ref[1] = SCALE_ADAPT * dot_tn(narrow_ref[:, :rank], dg)
    maps_ref[2] = SCALE_ADAPT * dot_tn(narrow_ref[:, rank:], du)

    @pl.when(step == steps - 1)
    def _():
        low = back_gu[...].astype(BF)
        back_gu_ref[...] = low
        out_ref[...] = (total[...] + SCALE_ADAPT * dot(low, gu_in_ref[...])).astype(BF)


def feed_back(spot, part, grad, d_parts, g_parts, u_parts, gate, up, gated, narrow, d_out, d_in, gu_out, gu_in):
    rows, width = grad.shape
    half, hidden = g_parts[0].shape
    rank = d_in.shape[0]
    tile = 256
    steps = hidden // tile
    mid = steps // 2
    column = pl.BlockSpec((half, tile), lambda s, spot: (0, (s + spot[2] * mid) % steps))
    local = pl.BlockSpec((rows, tile), lambda s, spot: (part, s))
    fixed = lambda v: pl.BlockSpec(v.shape, lambda s, spot: (0,) * v.ndim)
    return pl.pallas_call(
        feed_back_kernel,
        grid_spec=pltpu.PrefetchScalarGridSpec(
            num_scalar_prefetch=1,
            grid=(steps,),
            in_specs=[
                fixed(grad),
            ]
            + [
                pl.BlockSpec((tile, width), lambda s, spot, k=k: (jnp.clip(s - k * mid // 2, 0, mid // 2 - 1), 0))
                for k in range(4)
            ]
            + [column] * 4
            + [local] * 3
            + [
                pl.BlockSpec((rows, 2 * rank), lambda s, spot: (part, 0)),
                fixed(d_out),
                pl.BlockSpec((rank, tile), lambda s, spot: (0, s)),
                pl.BlockSpec((2, rank, tile), lambda s, spot: (0, 0, s)),
                fixed(gu_in),
            ],
            out_specs=[
                pl.BlockSpec((rows, width), lambda s, spot: (0, 0)),
                pl.BlockSpec((rows, 2 * rank), lambda s, spot: (0, 0)),
                pl.BlockSpec((3, rank, tile), lambda s, spot: (0, 0, s)),
            ],
            scratch_shapes=[
                pltpu.VMEM((rows, width), F32),
                pltpu.VMEM((rows, tile), F32),
                pltpu.VMEM((rows, rank), BF),
                pltpu.VMEM((rows, 2 * rank), F32),
            ],
        ),
        out_shape=[
            jax.ShapeDtypeStruct((rows, width), BF),
            jax.ShapeDtypeStruct((rows, 2 * rank), BF),
            jax.ShapeDtypeStruct((3, rank, hidden), F32),
        ],
        compiler_params=pltpu.CompilerParams(vmem_limit_bytes=VMEM_BYTES),
        name="feed_backward",
        cost_estimate=cost(24),
    )(spot, grad, *d_parts, *g_parts, *u_parts, gate, up, gated, narrow, d_out, d_in, gu_out, gu_in)


def post_kernel(heads, pre_ref, inv_ref, gain_ref, cos_ref, sin_ref, q_ref, k_ref):
    width = heads * HD
    cos, sin = cos_ref[...], sin_ref[...]
    for part, out_ref in enumerate((q_ref, k_ref)):
        inv = inv_ref[:, part : part + 1]
        for h in range(heads):
            cols = slice(part * width + h * HD, part * width + (h + 1) * HD)
            v = pre_ref[:, cols] * inv * gain_ref[:, cols]
            out_ref[:, h * HD : (h + 1) * HD] = (v * cos + pltpu.roll(v, HD // 2, 1) * sin).astype(BF)


def post(pre, inv, gain, cos, sin, heads):
    rows, width = pre.shape[0], heads * HD
    tile = 256
    row = lambda n: pl.BlockSpec((tile, n), lambda r: (r, 0))
    return pl.pallas_call(
        functools.partial(post_kernel, heads),
        grid=(rows // tile,),
        in_specs=[row(2 * width), row(2), pl.BlockSpec((1, 2 * width), lambda r: (0, 0)), row(HD), row(HD)],
        out_specs=[row(width), row(width)],
        out_shape=[jax.ShapeDtypeStruct((rows, width), BF)] * 2,
        name="rope_forward",
        cost_estimate=cost(5),
    )(pre, inv, gain, cos, sin)


def unpost_kernel(heads, dq_ref, dk_ref, pre_ref, gain_ref, cos_ref, sin_ref, turn_ref, inner_ref):
    width = heads * HD
    cos, sin = cos_ref[...], sin_ref[...]
    for part, d_ref in enumerate((dq_ref, dk_ref)):
        total = None
        for h in range(heads):
            cols = slice(part * width + h * HD, part * width + (h + 1) * HD)
            v = d_ref[:, h * HD : (h + 1) * HD]
            turned = (v * cos - pltpu.roll(v, HD // 2, 1) * sin) * gain_ref[:, cols]
            turn_ref[:, cols] = turned
            inner = jnp.sum(turned * pre_ref[:, cols], axis=1, keepdims=True)
            total = inner if total is None else total + inner
        inner_ref[:, part : part + 1] = total


def unpost(dq, dk, pre, gain, cos, sin, heads):
    rows, width = pre.shape[0], heads * HD
    tile = 256
    row = lambda n: pl.BlockSpec((tile, n), lambda r: (r, 0))
    return pl.pallas_call(
        functools.partial(unpost_kernel, heads),
        grid=(rows // tile,),
        in_specs=[row(width), row(width), row(2 * width), pl.BlockSpec((1, 2 * width), lambda r: (0, 0)), row(HD), row(HD)],
        out_specs=[row(2 * width), row(2)],
        out_shape=[jax.ShapeDtypeStruct((rows, 2 * width), F32), jax.ShapeDtypeStruct((rows, 2), F32)],
        name="rope_backward",
        cost_estimate=cost(8),
    )(dq, dk, pre, gain, cos, sin)


NEG_FILL = -1e30


def attend_kernel(count, scale, q_ref, *refs):
    ks, vs = refs[:count], refs[count : 2 * count]
    lo_ref, pos_ref, key_ref, o_ref, log_ref = refs[2 * count :]
    rows = q_ref.shape[0] * q_ref.shape[2]
    q = q_ref[...].reshape(rows, HD)
    lo, pos = lo_ref[0], pos_ref[...]
    scores = []
    for t in range(count):
        s = dot_nt(q, ks[t][...].reshape(rows, HD)) * scale
        key = key_ref[t : t + 1, :]
        scores.append(jnp.where((key >= lo) & (key <= pos), s, NEG_FILL))
    top = functools.reduce(jnp.maximum, [jnp.max(s, axis=1, keepdims=True) for s in scores])
    powers = [jnp.exp(s - top) for s in scores]
    total = sum(jnp.sum(e, axis=1, keepdims=True) for e in powers)
    share = 1.0 / total
    out = sum(dot((e * share).astype(BF), vs[t][...].reshape(rows, HD)) for t, e in enumerate(powers))
    o_ref[...] = out.astype(BF).reshape(o_ref.shape)
    log_ref[0] = top + jnp.log(total)


def attend_back_kernel(count, first, scale, q_ref, do_ref, o_ref, *refs):
    ks, vs = refs[:count], refs[count : 2 * count]
    lo_ref, pos_ref, key_ref, log_ref = refs[2 * count : 2 * count + 4]
    refs = refs[2 * count + 4 :]
    dq = None
    rows = q_ref.shape[0] * q_ref.shape[2]
    if not first:
        dq = refs[0][...].reshape(rows, HD)
        refs = refs[1:]
    dq_ref, dks, dvs = refs[0], refs[1 : 1 + count], refs[1 + count :]
    q = q_ref[...].reshape(rows, HD)
    do = do_ref[...].reshape(rows, HD)
    inner = jnp.sum(do.astype(F32) * o_ref[...].reshape(rows, HD).astype(F32), axis=1, keepdims=True)
    lo, pos, log_total = lo_ref[0], pos_ref[...], log_ref[0]
    for t in range(count):
        k, v = ks[t][...].reshape(rows, HD), vs[t][...].reshape(rows, HD)
        key = key_ref[t : t + 1, :]
        s = dot_nt(q, k) * scale
        probs = jnp.where((key >= lo) & (key <= pos), jnp.exp(s - log_total), 0.0)
        ds = (probs * (dot_nt(do, v) - inner)).astype(BF)
        dvs[t][...] = dot_tn(probs.astype(BF), do).astype(dvs[t].dtype).reshape(dvs[t].shape)
        dks[t][...] = (dot_tn(ds, q) * scale).astype(dks[t].dtype).reshape(dks[t].shape)
        part = dot(ds, k) * scale
        dq = part if dq is None else dq + part
    dq_ref[...] = dq.reshape(dq_ref.shape)


class Attention:
    def __init__(self, rows, heads, count, lo, pos, key):
        self.rows, self.heads, self.count = rows, heads, count
        self.tables = (lo, pos, key)
        full = 2 * rows
        self.block = pl.BlockSpec((2, 1, rows, HD), lambda s, h: (0, s, 0, h))
        self.table_specs = lambda n: [
            pl.BlockSpec((1, full, 1), lambda s, h: (s, 0, 0)),
            pl.BlockSpec((full, 1), lambda s, h: (0, 0)),
            pl.BlockSpec((n, full), lambda s, h: (0, 0)),
        ]
        self.log_spec = pl.BlockSpec((1, full, 1), lambda s, h: (s * heads + h, 0, 0))
        self.params = pltpu.CompilerParams(vmem_limit_bytes=VMEM_BYTES)

    def shape(self, dtype):
        return jax.ShapeDtypeStruct((2, 2, self.rows, self.heads * HD), dtype)

    def view(self, v):
        return v.reshape(2, 2, self.rows, v.shape[-1])

    def forward(self, q, ks, vs):
        count = self.count
        out, log = pl.pallas_call(
            functools.partial(attend_kernel, count, HD**-0.5),
            grid=(2, self.heads),
            in_specs=[self.block] * (1 + 2 * count) + self.table_specs(count),
            out_specs=[self.block, self.log_spec],
            out_shape=[self.shape(BF), jax.ShapeDtypeStruct((2 * self.heads, 2 * self.rows, 1), F32)],
            compiler_params=self.params,
            name="attend_forward",
            cost_estimate=cost(23),
        )(*[self.view(v) for v in [q] + ks + vs], *self.tables)
        return out.reshape(q.shape), log

    def backward(self, q, do, o, ks, vs, log, blocks, dtypes, dq=None):
        lo, pos, key = self.tables
        count = len(blocks)
        grads = [self.shape(d) for d in dtypes]
        key = jnp.concatenate([key[t : t + 1] for t in blocks], axis=0)
        more = [] if dq is None else [self.view(dq)]
        outs = pl.pallas_call(
            functools.partial(attend_back_kernel, count, dq is None, HD**-0.5),
            grid=(2, self.heads),
            in_specs=[self.block] * (3 + 2 * count) + self.table_specs(count) + [self.log_spec] + [self.block] * len(more),
            out_specs=[self.block] * (1 + 2 * count),
            out_shape=[self.shape(F32)] + grads + grads,
            compiler_params=self.params,
            name="attend_backward",
            cost_estimate=cost(4 + 8 * count),
        )(*[self.view(v) for v in [q, do, o] + ks + vs], lo, pos, key, log, *more)
        flat = [v.reshape(q.shape) for v in outs]
        return flat[0], flat[1 : 1 + count], flat[1 + count :]


def rms_inverse(v):
    return lax.rsqrt(jnp.mean(v * v, axis=-1, keepdims=True) + EPS)


def rms_backward(v, gain, grad):
    inv = rms_inverse(v)
    turn = grad * gain
    inner = jnp.mean(v * turn, axis=-1, keepdims=True)
    return inv * turn - v * (inv * inv * inv) * inner


def fold(v, unit, groups):
    lead = v.shape[:-1]
    v = v.reshape(lead + (2 * groups, 2, unit))
    return jnp.swapaxes(v, -3, -2).reshape(lead + (-1,))


def unfold(v, unit, groups):
    lead = v.shape[:-1]
    v = v.reshape(lead + (2, 2 * groups, unit))
    return jnp.swapaxes(v, -3, -2).reshape(lead + (-1,))


def fold_blocks(v):
    blocks = v.shape[1] // HD
    return jnp.concatenate([v[:, k * HD : (k + 1) * HD] for y in range(2) for k in range(y, blocks, 2)], axis=1)


def unfold_blocks(v):
    half = v.shape[1] // HD // 2
    order = [y * half + k for k in range(half) for y in range(2)]
    return jnp.concatenate([v[:, k * HD : (k + 1) * HD] for k in order], axis=1)


def sum3(refs):
    return refs[0][...].astype(F32) + refs[1][...].astype(F32) + refs[2][...].astype(F32)


def fold_kernel(v_ref, out_ref):
    out_ref[...] = fold_blocks(v_ref[...])


def after_attention_kernel(folding, *refs):
    inputs_ref, gain_ref, attn_ref, middle_ref, low_ref = refs[3:]
    attn = sum3(refs)
    attn_ref[...] = attn
    middle = inputs_ref[...].astype(F32) + attn * rms_inverse(attn) * gain_ref[...]
    middle_ref[...] = middle
    low = middle.astype(BF)
    low_ref[...] = fold_blocks(low) if folding else low


def after_feed_kernel(*refs):
    middle_ref, gain_ref, cot_ref, result_ref, grad_ref = refs[3:]
    feed = sum3(refs)
    gain = gain_ref[...]
    result_ref[...] = (middle_ref[...] + feed * rms_inverse(feed) * gain).astype(BF)
    grad_ref[...] = rms_backward(feed, gain, cot_ref[...].astype(F32)).astype(BF)


def middle_kernel(folding, *refs):
    cot_ref, attn_ref, gain_ref, mid_ref, grad_ref = refs[3:]
    total = sum3(refs)
    mid = cot_ref[...].astype(F32) + (unfold_blocks(total) if folding else total)
    mid_ref[...] = mid
    grad_ref[...] = rms_backward(attn_ref[...], gain_ref[...], mid).astype(BF)


def end_kernel(folding, *refs):
    mid_ref, out_ref = refs[3:]
    total = sum3(refs)
    out_ref[...] = mid_ref[...] + (unfold_blocks(total) if folding else total)


def by_rows(kernel, name, rows, width, args, dtypes, us):
    tile = 64 if rows % 64 == 0 else rows
    spec = lambda v: pl.BlockSpec((1, width), lambda r: (0, 0)) if v.shape[0] == 1 else pl.BlockSpec((tile, width), lambda r: (r, 0))
    row = pl.BlockSpec((tile, width), lambda r: (r, 0))
    return pl.pallas_call(
        kernel,
        grid=(rows // tile,),
        in_specs=[spec(v) for v in args],
        out_specs=[row] * len(dtypes),
        out_shape=[jax.ShapeDtypeStruct((rows, width), d) for d in dtypes],
        compiler_params=pltpu.CompilerParams(vmem_limit_bytes=VMEM_BYTES),
        name=name,
        cost_estimate=cost(us),
    )(*args)


def on_device(
    layer_input,
    cotangent,
    document_length,
    adapter_choice_index,
    query_weight,
    key_weight,
    value_weight,
    output_weight,
    gate_weight,
    up_weight,
    down_weight,
    query_norm_gain,
    key_norm_gain,
    attention_norm_gain,
    feedforward_norm_gain,
    adapter_model_input_maps,
    adapter_down_input_maps,
    adapter_model_output_maps,
    adapter_hidden_output_maps,
):
    at = Place()
    rows = layer_input.shape[1]
    width = layer_input.shape[2]
    heads = width // HD // 4
    local = heads * HD
    rank = adapter_model_input_maps.shape[2]
    depth = query_weight.shape[0]
    hidden_rows = down_weight.shape[0]
    hidden = hidden_rows * at.np * 2
    reach = WINDOW // (2 * rows)
    count = reach + 1

    def head_cols(v, quarter):
        return pick(v.reshape(v.shape[:-1] + (heads, 4, HD)), v.ndim, quarter).reshape(v.shape[:-1] + (local,))

    def hidden_cols(v):
        lead = v.shape[:-1]
        n = len(lead)
        v = v.reshape(lead + (at.np, 2, 2, 2, 2, hidden_rows // 2))
        v = pick(v, n + 3, at.c)
        v = pick(v, n + 1, at.x)
        v = jnp.moveaxis(v, n, n + 2)
        first, second = (jnp.where(at.y == 0, v[..., k, :, :, :], v[..., 1 - k, :, :, :]) for k in range(2))
        return jnp.concatenate([first.reshape(lead + (-1,)), second.reshape(lead + (-1,))], axis=-1)

    def regroup(weights, size, offsets, *earlier):
        own, core, across, both = pack(at.spot, weights, size, offsets)
        core = after(core, *earlier)
        return join(at.spot, [own, at.swap_core(core), at.swap_x(across), at.swap_both(both)])

    def gather_p(v):
        return lax.all_gather(v, "p", axis=0, tiled=True)

    def in_order(own, other):
        size = own.shape[0]
        buf = jnp.zeros((2 * size,) + own.shape[1:], own.dtype)
        buf = lax.dynamic_update_slice(buf, own, (at.y * size, 0))
        return lax.dynamic_update_slice(buf, other, ((1 - at.y) * size, 0))

    own_inputs = layer_input[0]
    unit = 2 * depth
    folding = unit % HD == 0
    if folding:
        (folded_inputs,) = by_rows(fold_kernel, "fold", rows, width, [own_inputs], [BF], 2)
    else:
        folded_inputs = fold(own_inputs, unit, at.np)
    half_rows = hidden_rows // 2
    head_offsets = lambda x, c: [4 * k + 2 * x + c for k in range(heads)]
    feed_offsets = lambda x, c: [
        (((2 * p + x) * 2 + y) * 2 + c) * 2 + half for y in range(2) for half in range(2) for p in range(at.np)
    ]
    qkv_piece = regroup([query_weight, key_weight, value_weight], HD, head_offsets)
    gate_piece = regroup([gate_weight], half_rows, feed_offsets, qkv_piece)
    up_piece = regroup([up_weight], half_rows, feed_offsets, gate_piece)
    inputs = jnp.concatenate(at.gather4(folded_inputs)[:2])

    qkv_own = gather_p(qkv_piece)
    qkv_other = at.swap_y(qkv_own)
    w_qkv = in_order(qkv_own, qkv_other)
    gate_own = gather_p(gate_piece)
    up_own = gather_p(up_piece)
    if 2 * depth == HD:
        o_own = gather_p(after(output_weight, qkv_own))
        sent = lambda target: lax.ppermute(o_own, ("y", "c"), target)
        same = at.y == at.c
        mine_half = jnp.where(same, o_own, sent([(0, 2), (3, 1)]))
        other_half = jnp.where(same, sent([(1, 0), (2, 3)]), sent([(1, 2), (2, 1)]))
        halves = [jnp.where(at.c == 0, mine_half, other_half), jnp.where(at.c == 0, other_half, mine_half)]
        w_o = jnp.stack([v.reshape(at.np, depth, width) for v in halves], axis=1).reshape(local, width)
    else:
        o_own = qkv_own
        o_full = lax.all_gather(output_weight, ("p", "x", "y", "c"), axis=0, tiled=True)
        w_o = pick(o_full.reshape(heads, 4, HD, width), 1, at.quarter).reshape(local, width)
    down_own = [gather_p(after(down_weight[:half_rows], gate_own)), gather_p(after(down_weight[half_rows:], up_own))]
    w_g = (gate_own, at.swap_y(after(gate_own, qkv_other)))
    w_u = (up_own, at.swap_y(after(up_own, w_g[1])))
    down_other = [at.swap_y(after(down_own[0], w_u[1]))]
    down_other.append(at.swap_y(after(down_own[1], down_other[0])))
    w_d = (*down_own, *down_other)

    selected = adapter_choice_index[0]
    a_model = pick(adapter_model_input_maps, 0, selected)
    a_hidden = pick(adapter_down_input_maps, 0, selected)
    b_model = pick(adapter_model_output_maps, 0, selected)
    b_hidden = pick(adapter_hidden_output_maps, 0, selected)
    a_qkv = fold(a_model[:3].reshape(3 * rank, width), unit, at.np)
    a_gu = fold(a_model[4:6].reshape(2 * rank, width), unit, at.np)
    a_o = head_cols(a_model[3], at.quarter)
    a_d = hidden_cols(a_hidden)
    b_qkv = head_cols(b_model[:3], at.quarter)
    b_o, b_d = b_model[3], b_model[4]
    b_gu = hidden_cols(b_hidden)

    def diagonal(maps):
        k, r, n = maps.shape
        zero = jnp.zeros((r, n), BF)
        return jnp.concatenate(
            [jnp.concatenate([maps[a] if a == b else zero for b in range(k)], axis=1) for a in range(k)], axis=0
        )

    b_qkv_diag = diagonal(b_qkv)
    gain = jnp.concatenate(
        [head_cols(query_norm_gain[None], at.quarter), head_cols(key_norm_gain[None], at.quarter)], axis=1
    )

    step_rows = jnp.arange(rows, dtype=jnp.int32)
    spot = lambda xx: at.p * 2 * rows + xx * rows + step_rows
    pos = jnp.concatenate([spot(at.x), spot(1 - at.x)])
    lengths = lax.dynamic_slice_in_dim(document_length, 2 * at.y, 2, 0)
    bounds = jnp.cumsum(lengths, axis=1)
    bounds = jnp.where(at.c == 0, bounds, bounds[::-1])
    begin = jnp.max(jnp.where(bounds[:, None, :] <= pos[None, :, None], bounds[:, None, :], 0), axis=2)
    lo = jnp.maximum(begin, pos[None] - (WINDOW - 1))
    key = jnp.stack([pos - 2 * rows * t for t in range(count)])
    attention = Attention(rows, heads, count, lo[:, :, None], pos[:, None], key)

    half_dim = HD // 2
    inv_freq = ROPE_BASE ** (-(jnp.arange(half_dim, dtype=F32) * 2.0 / HD))
    angles = jnp.concatenate([spot(at.x), spot(at.x), spot(1 - at.x), spot(1 - at.x)]).astype(F32)[:, None] * inv_freq
    cos, sin = jnp.cos(angles), jnp.sin(angles)
    cos = jnp.concatenate([cos, cos], axis=1)
    sin = jnp.concatenate([-sin, sin], axis=1)

    narrow_qkv = dot_nt(inputs, a_qkv).astype(BF)
    pre = dot(inputs, w_qkv) + SCALE_ADAPT * dot(narrow_qkv, b_qkv_diag)
    value = pre[:, 2 * local :].astype(BF)
    squares = jnp.stack(
        [jnp.sum(jnp.square(pre[:, k * local : (k + 1) * local]), axis=1) for k in range(2)], axis=0
    )
    inv = lax.rsqrt(at.sum4(squares) / width + EPS).T
    query, key_own = post(pre, inv, gain, cos, sin, heads)
    keys, values = [key_own], [value]
    for _ in range(reach):
        values.append(at.shift_p(values[-1], 1))
        keys.append(at.shift_p(keys[-1], 1))
    o, log = attention.forward(query, keys, values)
    narrow_o = dot_nt(o, a_o).astype(BF)
    def attn_part(part, mark=None):
        ins, narrow = o[part], narrow_o[part]
        if mark is not None:
            ins = after(ins, mark)
        return (dot(ins, w_o) + SCALE_ADAPT * dot(narrow, b_o)).astype(BF)

    near_rows, far_rows = slice(0, 2 * rows), slice(2 * rows, 4 * rows)
    attn_parts = at.scatter4(attn_part(far_rows), lambda mark: attn_part(near_rows, mark))
    attn_gain, feed_gain = attention_norm_gain[None], feedforward_norm_gain[None]
    attn_out, middle, low = by_rows(
        functools.partial(after_attention_kernel, folding),
        "after_attention",
        rows,
        width,
        [*attn_parts, own_inputs, attn_gain],
        [F32, F32, BF],
        4,
    )
    middle_low = jnp.concatenate(at.gather4(low if folding else fold(low, unit, at.np))[:2])
    narrow_gu = dot_nt(middle_low, a_gu).astype(BF)
    gate, up, gated = gate_up(at.spot, middle_low, w_g, w_u, narrow_gu, b_gu)
    feed_far, narrow_d_far = down(gated, 1, w_d, a_d, b_d)
    narrow_d = []

    def feed_near(mark):
        part, narrow = down(after(gated, mark), 0, w_d, a_d, b_d)
        narrow_d.append(narrow)
        return part

    feed_parts = at.scatter4(feed_far, feed_near)
    narrow_d = jnp.concatenate([narrow_d[0], narrow_d_far])
    cot = cotangent[0]
    result, grad_feed_own = by_rows(
        after_feed_kernel,
        "after_feed",
        rows,
        width,
        [*feed_parts, middle, feed_gain, cot],
        [BF, BF],
        4,
    )

    feed_args = (w_d, w_g, w_u, gate, up, gated, narrow_gu, b_d, a_d, b_gu, a_gu)
    grad_near, grad_far, (mid_near, back_gu_near, maps_near) = at.gather4(
        grad_feed_own, lambda near: feed_back(at.spot, 0, near, *feed_args)
    )
    mid_far, back_gu_far, maps_far = feed_back(at.spot, 1, grad_far, *feed_args)
    grad_feed = jnp.concatenate([grad_near, grad_far])
    back_gu = jnp.concatenate([back_gu_near, back_gu_far])
    mid_parts = at.scatter4(mid_far, lambda mark: mid_near)
    if not folding:
        mid_parts = [unfold(v, unit, at.np) for v in mid_parts]
    grad_mid, grad_attn_own = by_rows(
        functools.partial(middle_kernel, folding),
        "middle",
        rows,
        width,
        [*mid_parts, cot, attn_out, attn_gain],
        [F32, BF],
        4,
    )
    grad_attn = jnp.concatenate(at.gather4(grad_attn_own)[:2])
    back_o = dot_nt(grad_attn, b_o).astype(BF)
    grad_o = (dot_nt(grad_attn, w_o) + SCALE_ADAPT * dot(back_o, a_o)).astype(BF)
    dq, dks, dvs = attention.backward(query, grad_o, o, keys[reach:], values[reach:], log, [reach], [BF])
    moved_k, moved_v = at.shift_p(dks[0], -1), at.shift_p(dvs[0], -1)
    dq, dks, dvs = attention.backward(
        query, grad_o, o, keys[:reach], values[:reach], log, range(reach), [F32] + [BF] * (reach - 1), dq
    )
    for t in range(reach - 1, 0, -1):
        moved_k = at.shift_p((dks[t].astype(F32) + moved_k.astype(F32)).astype(BF), -1)
        moved_v = at.shift_p((dvs[t].astype(F32) + moved_v.astype(F32)).astype(BF), -1)
    dk = dks[0] + moved_k.astype(F32)
    dv = dvs[0] + moved_v.astype(F32)
    turn, inner = unpost(dq, dk, pre, gain, cos, sin, heads)
    inner = at.sum4(inner.T).T / width

    def unnorm(part):
        cols = slice(part * local, (part + 1) * local)
        scale = inv[:, part : part + 1]
        return (scale * turn[:, cols] - pre[:, cols] * (scale * scale * scale * inner[:, part : part + 1])).astype(BF)

    grad_qkv = jnp.concatenate([unnorm(0), unnorm(1), dv.astype(BF)], axis=1)
    back_qkv = dot_nt(grad_qkv, b_qkv_diag).astype(BF)
    def end_part(part, mark=None):
        ins, back = grad_qkv[part], back_qkv[part]
        if mark is not None:
            ins = after(ins, mark)
        return (dot_nt(ins, w_qkv) + SCALE_ADAPT * dot(back, a_qkv)).astype(BF)

    end_parts = at.scatter4(end_part(far_rows), lambda mark: end_part(near_rows, mark))
    if not folding:
        end_parts = [unfold(v, unit, at.np) for v in end_parts]
    (grad_input,) = by_rows(
        functools.partial(end_kernel, folding), "end", rows, width, [*end_parts, grad_mid], [F32], 3
    )

    ga_qkv = SCALE_ADAPT * dot_tn(back_qkv, inputs)
    ga_gu = SCALE_ADAPT * dot_tn(back_gu, middle_low)
    ga_o = SCALE_ADAPT * dot_tn(back_o, o)
    gb_qkv = [
        SCALE_ADAPT * dot_tn(narrow_qkv[:, k * rank : (k + 1) * rank], grad_qkv[:, k * local : (k + 1) * local])
        for k in range(3)
    ]
    gb_o = SCALE_ADAPT * dot_tn(narrow_o, grad_attn)
    gb_d = SCALE_ADAPT * dot_tn(narrow_d, grad_feed)
    mine = (jnp.arange(4) == at.quarter).astype(F32)

    def spread(v):
        return (v.reshape(-1, heads, 1, HD) * mine[:, None]).reshape(-1, width)

    def share_y(mine, other):
        return mine + at.swap_y(other)

    def share_p(v):
        total = pick(v, 1, at.p)
        for by in range(1, at.np):
            total = total + at.turn_p(pick(v, 1, (at.p + by) % at.np), by)
        return total

    def sum_model(folded, plain):
        folded = folded.reshape(-1, 2, at.np, 2, 2 * depth)
        plain = plain.reshape(-1, at.np, 2, 2, 2 * depth)

        def cut(x):
            plain_part = jnp.swapaxes(pick(plain, 2, x), 1, 2)
            return jnp.concatenate([pick(folded, 3, x), plain_part], axis=0)

        v = cut(at.x) + at.swap_x(cut(1 - at.x))
        v = share_p(share_y(pick(v, 1, at.y), pick(v, 1, 1 - at.y)))
        v = v.reshape(v.shape[0], 2, depth)
        return (pick(v, 1, at.c) + at.swap_core(pick(v, 1, 1 - at.c))).reshape(-1, rank, depth)

    def sum_hidden(v):
        v = v.reshape(-1, 2, 2, at.np, half_rows)
        v = share_y(v[:, 0], v[:, 1])
        return share_p(jnp.swapaxes(v, 1, 2)).reshape(-1, rank, hidden_rows)

    wide = sum_hidden(maps_near + maps_far)
    early = sum_model(ga_gu, jnp.concatenate([spread(ga_o), gb_o, gb_d]))
    late = sum_model(ga_qkv, spread(jnp.concatenate(gb_qkv)))
    choose = (jnp.arange(adapter_model_input_maps.shape[0], dtype=jnp.int32) == selected).astype(F32)
    sum_a_model = choose[:, None, None, None] * jnp.concatenate([late[:3], early[2:3], early[:2]])[None]
    sum_a_hidden = choose[:, None, None] * wide[0][None]
    sum_b_model = choose[:, None, None, None] * jnp.concatenate([late[3:], early[3:]])[None]
    sum_b_hidden = choose[:, None, None, None] * wide[1:][None]
    return (result[None], grad_input[None], sum_a_model, sum_a_hidden, sum_b_model, sum_b_hidden)


def solution(mesh):
    grid = mesh.devices.reshape(mesh.shape["ctx"] // 2, 2, mesh.shape["wt"] // 2, 2)
    split = Mesh(grid, ("p", "x", "y", "c"))
    everyone = ("p", "x", "y", "c")
    rows = P(everyone, None)
    tokens = P(("y", "c"), ("p", "x"), None)
    placed = (tokens, tokens, P(), P()) + (rows,) * 7 + (P(),) * 8
    return jax.shard_map(
        on_device,
        mesh=split,
        in_specs=placed,
        out_specs=(
            tokens,
            tokens,
            P(None, None, None, everyone),
            P(None, None, everyone),
            P(None, None, None, everyone),
            P(None, None, None, everyone),
        ),
        check_vma=False,
    )
```

```python
import functools

import jax
import jax.numpy as jnp
from jax import lax
from jax.experimental import pallas as pl
from jax.experimental.pallas import tpu as pltpu
from jax.sharding import Mesh
from jax.sharding import PartitionSpec as P

HD = 128
WINDOW = 1024
SCALE_ADAPT = 0.5
ROPE_BASE = 500000.0
EPS = 1e-06
BF = jnp.bfloat16
F32 = jnp.float32
VMEM_BYTES = 56 * 1024 * 1024


def cost(us):
    return pl.CostEstimate(flops=int(us * 1.1e9), bytes_accessed=int(us * 1e6), transcendentals=0)


def dot(a, b, dims=((1,), (0,))):
    return lax.dot_general(a, b, (dims, ((), ())), preferred_element_type=F32)


def dot_nt(a, b):
    return dot(a, b, ((1,), (1,)))


def dot_tn(a, b):
    return dot(a, b, ((0,), (0,)))


SWAP = [(0, 1), (1, 0)]


class Place:
    def __init__(self):
        self.np = lax.axis_size("p")
        self.p, self.x, self.y, self.c = (lax.axis_index(a) for a in ("p", "x", "y", "c"))
        self.quarter = 2 * self.x + self.c
        self.spot = jnp.stack([self.x, self.y, self.c]).astype(jnp.int32)

    def swap_core(self, value):
        return lax.ppermute(value, "c", SWAP)

    def swap_x(self, value):
        return lax.ppermute(value, "x", SWAP)

    def swap_both(self, value):
        return lax.ppermute(value, ("x", "c"), [(0, 3), (1, 2), (2, 1), (3, 0)])

    def swap_y(self, value):
        return lax.ppermute(value, "y", SWAP)

    def shift_p(self, value, by):
        return lax.ppermute(value, "p", [(p, p + by) for p in range(self.np) if 0 <= p + by < self.np])

    def turn_p(self, value, by):
        return lax.ppermute(value, "p", [(p, (p + by) % self.np) for p in range(self.np)])

    def gather4(self, own):
        across = self.swap_x(own)
        return self.paired(own), self.paired(across)

    def paired(self, block):
        return jnp.concatenate([block, self.swap_core(block)], axis=0)

    def gather8(self, own, work=None):
        half = own.shape[0] // 2
        across, over = self.swap_x(own), self.swap_y(own)
        first = self.paired(own)
        done = None
        if work is not None:
            done = work(first)
            across, over = after(across, done[0]), after(over, done[0])
        far = jnp.concatenate([self.swap_y(across[:half]), self.swap_x(over[half:])])
        return (first, self.paired(across), self.paired(over), self.paired(far)), done

    def met(self, pair):
        rows = pair.shape[0] // 2
        return (pair[:rows].astype(F32) + self.swap_core(pair[rows:]).astype(F32)).astype(BF)

    def scatter4(self, second, first):
        met = self.met(second)
        across = self.swap_x(met)
        first = first(met)
        return first, self.swap_core(first[first.shape[0] // 2 :]), across

    def scatter8(self, second, third, fourth, first):
        far = self.met(fourth)
        half = far.shape[0] // 2
        by_x, by_y = self.swap_x(far[:half]), self.swap_y(far[half:])
        second, third = self.met(second), self.met(third)
        add = lambda u, v: (u.astype(F32) + v.astype(F32)).astype(BF)
        across = [self.swap_x(second[:half]), self.swap_x(add(second[half:], by_y))]
        over = [self.swap_y(add(third[:half], by_x)), self.swap_y(third[half:])]
        first = first(far)
        core = self.swap_core(first[first.shape[0] // 2 :])
        return first, core, jnp.concatenate(across), jnp.concatenate(over)

    def sum4(self, value, parts):
        def reordered(v, x, c):
            v = v.reshape(v.shape[0], parts, 2, 2, -1)
            if x:
                v = jnp.concatenate([v[:, :, 1:], v[:, :, :1]], axis=2)
            if c:
                v = jnp.concatenate([v[:, :, :, 1:], v[:, :, :, :1]], axis=3)
            return v.reshape(value.shape)

        core, across, both = self.swap_core(value), self.swap_x(value), self.swap_both(value)
        return value + reordered(core, 0, 1) + reordered(across, 1, 0) + reordered(both, 1, 1)


def pick(v, axis, index):
    return lax.dynamic_index_in_dim(v, index, axis, keepdims=False)


def after(value, *others):
    return lax.optimization_barrier((value,) + others)[0]


def pack_kernel(count, width, offsets, turns, spot_ref, *refs):
    spot = [spot_ref[k] for k in range(3)]
    for out, turn in zip(refs[count:], turns):
        places = offsets(*[(s + t) % 2 for s, t in zip(spot, turn)])
        for w, ref in enumerate(refs[:count]):
            for k, place in enumerate(places):
                at = (w * len(places) + k) * width
                out[:, at : at + width] = ref[:, pl.ds(pl.multiple_of(place * width, HD), width)]


def pack(spot, weights, width, offsets, turns):
    rows = weights[0].shape[0]
    size = len(weights) * len(offsets(0, 0, 0)) * width
    if width % HD:
        outs = []
        for turn in turns:
            places = offsets(*[(spot[k] + turn[k]) % 2 for k in range(3)])
            cuts = [lax.dynamic_slice_in_dim(w, place * width, width, 1) for w in weights for place in places]
            outs.append(jnp.concatenate(cuts, axis=1))
        return outs
    whole = pl.BlockSpec(memory_space=pltpu.VMEM)
    return pl.pallas_call(
        functools.partial(pack_kernel, len(weights), width, offsets, turns),
        in_specs=[pl.BlockSpec(memory_space=pltpu.SMEM)] + [whole] * len(weights),
        out_specs=[whole] * len(turns),
        out_shape=[jax.ShapeDtypeStruct((rows, size), BF)] * len(turns),
        compiler_params=pltpu.CompilerParams(vmem_limit_bytes=VMEM_BYTES),
        name="pack_columns",
        cost_estimate=cost(3),
    )(spot, *weights)


TURNS8 = [(dx, dy, dc) for dy in range(2) for dx in range(2) for dc in range(2)]
TURNS4 = TURNS8[:4]


def start_kernel(groups, reach, *refs):
    qkv_pack, feed_packs, x_ref = refs[0:4], (refs[4:12], refs[12:20]), refs[20]
    w_ref, gate_ref, up_ref, all_ref, local_sem, send_sem, recv_sem = refs[21:]
    p, x, y, c = (lax.axis_index(a) for a in ("p", "x", "y", "c"))
    turned = lambda u, t: 1 - u if t else u
    group = [(p, turned(x, dx), turned(y, dy), turned(c, dc)) for dx, dy, dc in TURNS8]
    core, across, over = group[1], group[2], group[4]
    right, left = (lax.rem(p + 1, groups), x, y, c), (lax.rem(p + groups - 1, groups), x, y, c)
    rows, depth = x_ref.shape[0], qkv_pack[0].shape[0]
    used = [0]

    def remote(src, dst, device):
        k = used[0]
        used[0] += 1
        copy = pltpu.make_async_remote_copy(
            src_ref=src,
            dst_ref=dst,
            send_sem=send_sem.at[k],
            recv_sem=recv_sem.at[k],
            device_id=device,
            device_id_type=pl.DeviceIdType.MESH,
        )
        copy.start()
        return copy

    def local(k, src, dst):
        copy = pltpu.make_async_copy(src, dst, local_sem.at[k])
        copy.start()
        return copy

    barrier = pltpu.get_barrier_semaphore()
    for device in group[1:] + [right, left]:
        pl.semaphore_signal(barrier, inc=1, device_id=device, device_id_type=pl.DeviceIdType.MESH)
    pl.semaphore_wait(barrier, 9)

    def at(ref, start, size):
        return ref.at[pl.ds(pl.multiple_of(start, 16), size)]

    def tokens(t, block):
        return all_ref.at[pl.ds((4 * t + block) * rows, rows)]

    def owned(q):
        return w_ref.at[lax.rem(p + 2 * groups - q, groups), :, y]

    slot = (4 * x + 2 * y + c) * depth
    mine = [
        w_ref.at[p, x, y, pl.ds(pl.multiple_of(c * depth, 16), depth)],
        at(gate_ref, slot, depth),
        at(up_ref, slot, depth),
    ]
    firsts = (qkv_pack[0], feed_packs[0][0], feed_packs[1][0])
    kept = [local(k, firsts[k], mine[k]) for k in range(3)] + [local(3, x_ref, tokens(0, 0))]
    regrouped = [remote(qkv_pack[d], mine[0], group[d]) for d in (1, 2, 3)]
    moves = [remote(x_ref, tokens(1, 0), right)]
    sent = list(regrouped) + moves
    kept[0].wait()
    for copy in regrouped:
        copy.wait_recv()
    along = remote(owned(0), owned(0), right)
    later = [remote(owned(0), owned(0), over)]
    spread = [(remote(x_ref, tokens(0, 1), core), remote(x_ref, tokens(0, 2), across))]
    for k in (1, 2):
        later += [remote(feed_packs[k - 1][d], mine[k], group[d]) for d in range(1, 8)]
    sent.append(along)
    step = 1
    ready = 0

    def pass_on(t):
        spread[t][1].wait_recv()
        later.append(remote(tokens(t, 2), tokens(t, 3), core))

    while step < groups or ready <= reach:
        if ready < reach:
            moves[ready].wait_recv()
            if ready + 1 < reach:
                moves.append(remote(tokens(ready + 1, 0), tokens(ready + 2, 0), right))
                sent.append(moves[-1])
            spread.append(
                (
                    remote(tokens(ready + 1, 0), tokens(ready + 1, 1), core),
                    remote(tokens(ready + 1, 0), tokens(ready + 1, 2), across),
                )
            )
        if step < groups:
            along.wait_recv()
            if step < groups - 1:
                along = remote(owned(step), owned(step), right)
                sent.append(along)
            later.append(remote(owned(step), owned(step), over))
            step += 1
        if ready <= reach:
            pass_on(ready)
            ready += 1
    for near, far in spread:
        near.wait_recv()
        sent += [near, far]
    for copy in later:
        copy.wait_recv()
    for copy in sent + later:
        copy.wait_send()
    for copy in kept[1:]:
        copy.wait()


def start(groups, reach, qkv_pack, gate_pack, up_pack, own_inputs):
    depth, size = qkv_pack[0].shape
    rows, width = own_inputs.shape
    hidden = gate_pack[0].shape[1]
    copies = 3 + 1 + 1 + 1 + 14 + (groups - 2) + (groups - 1) + (reach - 1) + 2 * (reach + 1) + (reach + 1)
    anywhere = pl.BlockSpec(memory_space=pl.ANY)
    weight, gate, up, inputs = pl.pallas_call(
        functools.partial(start_kernel, groups, reach),
        in_specs=[anywhere] * 21,
        out_specs=[anywhere] * 4,
        out_shape=[
            jax.ShapeDtypeStruct((groups, 2, 2, 2 * depth, size), BF),
            jax.ShapeDtypeStruct((8 * depth, hidden), BF),
            jax.ShapeDtypeStruct((8 * depth, hidden), BF),
            jax.ShapeDtypeStruct((4 * (reach + 1) * rows, width), BF),
        ],
        scratch_shapes=[
            pltpu.SemaphoreType.DMA((4,)),
            pltpu.SemaphoreType.DMA((copies,)),
            pltpu.SemaphoreType.DMA((copies,)),
        ],
        compiler_params=pltpu.CompilerParams(collective_id=0, has_side_effects=True),
        name="start",
        cost_estimate=cost(120),
    )(*qkv_pack, *gate_pack, *up_pack, own_inputs)
    return weight.reshape(-1, size), gate, up, inputs


def gate_up_kernel(x_ref, gate_w_ref, up_w_ref, narrow_ref, maps_ref, gate_ref, up_ref, gated_ref):
    rank = maps_ref.shape[1]
    gate = dot(x_ref[...], gate_w_ref[...]) + SCALE_ADAPT * dot(narrow_ref[:, :rank], maps_ref[0])
    up = dot(x_ref[...], up_w_ref[...]) + SCALE_ADAPT * dot(narrow_ref[:, rank:], maps_ref[1])
    gate_ref[...] = gate.astype(BF)
    up_ref[...] = up.astype(BF)
    gated_ref[...] = (gate * jax.nn.sigmoid(gate) * up).astype(BF)


def gate_up(x, gate_w, up_w, narrow, maps):
    rows, width = x.shape
    hidden = gate_w.shape[1]
    tile = 256
    weight = pl.BlockSpec((width, tile), lambda s: (0, s))
    out = pl.BlockSpec((rows, tile), lambda s: (0, s))
    return pl.pallas_call(
        gate_up_kernel,
        grid=(hidden // tile,),
        in_specs=[
            pl.BlockSpec((rows, width), lambda s: (0, 0)),
            weight,
            weight,
            pl.BlockSpec(narrow.shape, lambda s: (0, 0)),
            pl.BlockSpec(maps.shape[:2] + (tile,), lambda s: (0, 0, s)),
        ],
        out_specs=[out] * 3,
        out_shape=[jax.ShapeDtypeStruct((rows, hidden), BF)] * 3,
        compiler_params=pltpu.CompilerParams(vmem_limit_bytes=VMEM_BYTES),
        name="gate_up",
        cost_estimate=cost(26),
    )(x, gate_w, up_w, narrow, maps)


def down_kernel(gated_ref, weight_ref, in_maps_ref, out_maps_ref, feed_ref, narrow_ref):
    @pl.when(pl.program_id(0) == 0)
    def _():
        narrow_ref[...] = dot_nt(gated_ref[...], in_maps_ref[...]).astype(BF)

    feed = dot(gated_ref[...], weight_ref[...]) + SCALE_ADAPT * dot(narrow_ref[...], out_maps_ref[...])
    feed_ref[...] = feed.astype(BF)


def down(gated, weight, in_maps, out_maps):
    rows, hidden = gated.shape
    width = weight.shape[1]
    rank = in_maps.shape[0]
    tile = 512
    return pl.pallas_call(
        down_kernel,
        grid=(width // tile,),
        in_specs=[
            pl.BlockSpec((rows, hidden), lambda s: (0, 0)),
            pl.BlockSpec((hidden, tile), lambda s: (0, s)),
            pl.BlockSpec(in_maps.shape, lambda s: (0, 0)),
            pl.BlockSpec((rank, tile), lambda s: (0, s)),
        ],
        out_specs=[pl.BlockSpec((rows, tile), lambda s: (0, s)), pl.BlockSpec((rows, rank), lambda s: (0, 0))],
        out_shape=[jax.ShapeDtypeStruct((rows, width), BF), jax.ShapeDtypeStruct((rows, rank), BF)],
        compiler_params=pltpu.CompilerParams(vmem_limit_bytes=VMEM_BYTES),
        name="down",
        cost_estimate=cost(15),
    )(gated, weight, in_maps, out_maps)


def feed_back_kernel(
    grad_ref,
    down_ref,
    gate_w_ref,
    up_w_ref,
    gate_ref,
    up_ref,
    gated_ref,
    narrow_ref,
    d_out_ref,
    d_in_ref,
    gu_out_ref,
    gu_in_ref,
    out_ref,
    back_gu_ref,
    maps_ref,
):
    rank = d_in_ref.shape[0]
    grad = grad_ref[...]
    back_d = dot_nt(grad, d_out_ref[...]).astype(BF)
    dm = dot_nt(grad, down_ref[...]) + SCALE_ADAPT * dot(back_d, d_in_ref[...])
    gate, up = gate_ref[...].astype(F32), up_ref[...].astype(F32)
    sig = jax.nn.sigmoid(gate)
    silu = gate * sig
    du = (dm * silu).astype(BF)
    dg = (dm * up * (sig + silu * (1.0 - sig))).astype(BF)
    back_g = dot_nt(dg, gu_out_ref[0]).astype(BF)
    back_u = dot_nt(du, gu_out_ref[1]).astype(BF)
    back_gu_ref[:, :rank] = back_g
    back_gu_ref[:, rank:] = back_u
    into = dot_nt(dg, gate_w_ref[...]) + dot_nt(du, up_w_ref[...])
    into = into + SCALE_ADAPT * (dot(back_g, gu_in_ref[:rank, :]) + dot(back_u, gu_in_ref[rank:, :]))
    out_ref[...] = into.astype(BF)

    @pl.when(pl.program_id(0) == 0)
    def _():
        maps_ref[...] = jnp.zeros_like(maps_ref)

    maps_ref[0] += SCALE_ADAPT * dot_tn(back_d, gated_ref[...])
    maps_ref[1] += SCALE_ADAPT * dot_tn(narrow_ref[:, :rank], dg)
    maps_ref[2] += SCALE_ADAPT * dot_tn(narrow_ref[:, rank:], du)


def feed_back(first, grad, down_w, gate_w, up_w, gate, up, gated, narrow, d_out, d_in, gu_out, gu_in):
    rows, width = grad.shape
    hidden = gate_w.shape[1]
    rank = d_in.shape[0]
    tile = 256
    row = lambda n: pl.BlockSpec((tile, n), lambda r: (r, 0))
    local = lambda n: pl.BlockSpec((tile, n), lambda r: (r + first, 0))
    fixed = lambda v: pl.BlockSpec(v.shape, lambda r: (0,) * v.ndim, pipeline_mode=pl.Buffered(1))
    return pl.pallas_call(
        feed_back_kernel,
        grid=(rows // tile,),
        in_specs=[
            row(width),
            fixed(down_w),
            fixed(gate_w),
            fixed(up_w),
            local(hidden),
            local(hidden),
            local(hidden),
            local(2 * rank),
            fixed(d_out),
            fixed(d_in),
            fixed(gu_out),
            fixed(gu_in),
        ],
        out_specs=[row(width), row(2 * rank), pl.BlockSpec((3, rank, hidden), lambda r: (0, 0, 0))],
        out_shape=[
            jax.ShapeDtypeStruct((rows, width), BF),
            jax.ShapeDtypeStruct((rows, 2 * rank), BF),
            jax.ShapeDtypeStruct((3, rank, hidden), F32),
        ],
        compiler_params=pltpu.CompilerParams(vmem_limit_bytes=VMEM_BYTES),
        name="feed_backward",
        cost_estimate=cost(2 + rows // 50),
    )(grad, down_w, gate_w, up_w, gate, up, gated, narrow, d_out, d_in, gu_out, gu_in)


def project_kernel(heads, own_tiles, x_ref, w_ref, in_maps_ref, out_maps_ref, *out_refs):
    pre_q_ref, pre_k_ref, value_ref, narrow_ref, square_q_ref, square_k_ref = out_refs
    width = heads * HD
    rank = out_maps_ref.shape[1]
    narrow_ref[...] = dot_nt(x_ref[...], in_maps_ref[...]).astype(BF)

    def part(k):
        cols = slice(k * width, (k + 1) * width)
        return dot(x_ref[...], w_ref[:, cols]) + SCALE_ADAPT * dot(narrow_ref[:, k * rank : (k + 1) * rank], out_maps_ref[k])

    ones = jnp.ones((8, width), BF)
    key = part(1)
    pre_k_ref[...] = key
    square_k_ref[...] = dot_nt(ones, (key * key).astype(BF))
    value_ref[...] = part(2).astype(BF)

    @pl.when(pl.program_id(0) < own_tiles)
    def _():
        query = part(0)
        pre_q_ref[...] = query
        square_q_ref[...] = dot_nt(ones, (query * query).astype(BF))


def project(x, own_rows, weight, in_maps, out_maps, heads):
    rows, width = x.shape
    local = heads * HD
    tile = 512
    own_tiles = own_rows // tile
    fixed = lambda v: pl.BlockSpec(v.shape, lambda t: (0,) * v.ndim)
    row = lambda n: pl.BlockSpec((tile, n), lambda t: (t, 0))
    return pl.pallas_call(
        functools.partial(project_kernel, heads, own_tiles),
        grid=(rows // tile,),
        in_specs=[row(width), fixed(weight), fixed(in_maps), fixed(out_maps)],
        out_specs=[
            pl.BlockSpec((tile, local), lambda t: (jnp.minimum(t, own_tiles - 1), 0)),
            row(local),
            row(local),
            row(in_maps.shape[0]),
            pl.BlockSpec((8, tile), lambda t: (0, jnp.minimum(t, own_tiles - 1))),
            pl.BlockSpec((8, tile), lambda t: (0, t)),
        ],
        out_shape=[
            jax.ShapeDtypeStruct((own_rows, local), F32),
            jax.ShapeDtypeStruct((rows, local), F32),
            jax.ShapeDtypeStruct((rows, local), BF),
            jax.ShapeDtypeStruct((rows, in_maps.shape[0]), BF),
            jax.ShapeDtypeStruct((8, own_rows), F32),
            jax.ShapeDtypeStruct((8, rows), F32),
        ],
        compiler_params=pltpu.CompilerParams(vmem_limit_bytes=VMEM_BYTES),
        name="project",
        cost_estimate=cost(30),
    )(x, weight, in_maps, out_maps)


def post_kernel(heads, own_tiles, q_ref, k_ref, inv_q_ref, inv_k_ref, gain_ref, cos_ref, sin_ref, q_out, k_out):
    width = heads * HD
    cos, sin = cos_ref[...], sin_ref[...]

    def turn(pre_ref, inv, part, out_ref):
        for h in range(heads):
            cols = slice(h * HD, (h + 1) * HD)
            v = pre_ref[:, cols] * inv * gain_ref[:, part * width + h * HD : part * width + (h + 1) * HD]
            out_ref[:, cols] = (v * cos + pltpu.roll(v, HD // 2, 1) * sin).astype(BF)

    turn(k_ref, inv_k_ref[...], 1, k_out)

    @pl.when(pl.program_id(0) < own_tiles)
    def _():
        turn(q_ref, inv_q_ref[...], 0, q_out)


def post(pre_q, pre_k, inv_q, inv_k, gain, cos, sin, heads):
    rows, width = pre_k.shape
    tile = 256
    own_tiles = pre_q.shape[0] // tile
    row = lambda n: pl.BlockSpec((tile, n), lambda r: (r, 0))
    own = lambda n: pl.BlockSpec((tile, n), lambda r: (jnp.minimum(r, own_tiles - 1), 0))
    return pl.pallas_call(
        functools.partial(post_kernel, heads, own_tiles),
        grid=(rows // tile,),
        in_specs=[
            own(width),
            row(width),
            own(1),
            row(1),
            pl.BlockSpec((1, 2 * width), lambda r: (0, 0)),
            row(HD),
            row(HD),
        ],
        out_specs=[own(width), row(width)],
        out_shape=[jax.ShapeDtypeStruct(pre_q.shape, BF), jax.ShapeDtypeStruct(pre_k.shape, BF)],
        name="rope_forward",
        cost_estimate=cost(10),
    )(pre_q, pre_k, inv_q, inv_k, gain, cos, sin)


def unpost_kernel(heads, dq_ref, dk_ref, pre_q_ref, pre_k_ref, gain_ref, cos_ref, sin_ref, turn_ref, inner_ref):
    width = heads * HD
    cos, sin = cos_ref[...], sin_ref[...]
    for part, (d_ref, pre_ref) in enumerate(((dq_ref, pre_q_ref), (dk_ref, pre_k_ref))):
        total = None
        for h in range(heads):
            cols = slice(part * width + h * HD, part * width + (h + 1) * HD)
            v = d_ref[:, h * HD : (h + 1) * HD]
            turned = (v * cos - pltpu.roll(v, HD // 2, 1) * sin) * gain_ref[:, cols]
            turn_ref[:, cols] = turned
            inner = jnp.sum(turned * pre_ref[:, h * HD : (h + 1) * HD], axis=1, keepdims=True)
            total = inner if total is None else total + inner
        inner_ref[:, part : part + 1] = total


def unpost(dq, dk, pre_q, pre_k, gain, cos, sin, heads):
    rows, width = dq.shape
    tile = 256
    row = lambda n: pl.BlockSpec((tile, n), lambda r: (r, 0))
    return pl.pallas_call(
        functools.partial(unpost_kernel, heads),
        grid=(rows // tile,),
        in_specs=[row(width)] * 4 + [pl.BlockSpec((1, 2 * width), lambda r: (0, 0)), row(HD), row(HD)],
        out_specs=[row(2 * width), row(2)],
        out_shape=[jax.ShapeDtypeStruct((rows, 2 * width), F32), jax.ShapeDtypeStruct((rows, 2), F32)],
        name="rope_backward",
        cost_estimate=cost(8),
    )(dq, dk, pre_q, pre_k, gain, cos, sin)


NEG_FILL = -1e30


def attend_kernel(count, scale, q_ref, *refs):
    ks, vs = refs[:count], refs[count : 2 * count]
    lo_ref, pos_ref, key_ref, o_ref, log_ref = refs[2 * count :]
    rows = q_ref.shape[0] * q_ref.shape[2]
    q = q_ref[...].reshape(rows, HD)
    lo, pos = lo_ref[0], pos_ref[...]
    scores = []
    for t in range(count):
        s = dot_nt(q, ks[t][...].reshape(rows, HD)) * scale
        key = key_ref[t : t + 1, :]
        scores.append(jnp.where((key >= lo) & (key <= pos), s, NEG_FILL))
    top = functools.reduce(jnp.maximum, [jnp.max(s, axis=1, keepdims=True) for s in scores])
    powers = [jnp.exp(s - top) for s in scores]
    total = sum(jnp.sum(e, axis=1, keepdims=True) for e in powers)
    share = 1.0 / total
    out = sum(dot((e * share).astype(BF), vs[t][...].reshape(rows, HD)) for t, e in enumerate(powers))
    o_ref[...] = out.astype(BF).reshape(o_ref.shape)
    log_ref[0] = top + jnp.log(total)


def attend_back_kernel(count, first, scale, q_ref, do_ref, o_ref, *refs):
    ks, vs = refs[:count], refs[count : 2 * count]
    lo_ref, pos_ref, key_ref, log_ref = refs[2 * count : 2 * count + 4]
    refs = refs[2 * count + 4 :]
    dq = None
    rows = q_ref.shape[0] * q_ref.shape[2]
    if not first:
        dq = refs[0][...].reshape(rows, HD)
        refs = refs[1:]
    dq_ref, dks, dvs = refs[0], refs[1 : 1 + count], refs[1 + count :]
    q = q_ref[...].reshape(rows, HD)
    do = do_ref[...].reshape(rows, HD)
    inner = jnp.sum(do.astype(F32) * o_ref[...].reshape(rows, HD).astype(F32), axis=1, keepdims=True)
    lo, pos, log_total = lo_ref[0], pos_ref[...], log_ref[0]
    for t in range(count):
        k, v = ks[t][...].reshape(rows, HD), vs[t][...].reshape(rows, HD)
        key = key_ref[t : t + 1, :]
        s = dot_nt(q, k) * scale
        probs = jnp.where((key >= lo) & (key <= pos), jnp.exp(s - log_total), 0.0)
        ds = (probs * (dot_nt(do, v) - inner)).astype(BF)
        dvs[t][...] = dot_tn(probs.astype(BF), do).astype(dvs[t].dtype).reshape(dvs[t].shape)
        dks[t][...] = (dot_tn(ds, q) * scale).astype(dks[t].dtype).reshape(dks[t].shape)
        part = dot(ds, k) * scale
        dq = part if dq is None else dq + part
    dq_ref[...] = dq.reshape(dq_ref.shape)


class Attention:
    def __init__(self, rows, heads, count, lo, pos, key):
        self.rows, self.heads, self.count = rows, heads, count
        self.tables = (lo, pos, key)
        full = 2 * rows
        self.block = pl.BlockSpec((2, 1, rows, HD), lambda s, h: (0, s, 0, h))
        self.part = lambda t: pl.BlockSpec((2, 1, rows, HD), lambda s, h: (t, s, 0, h))
        self.table_specs = lambda n: [
            pl.BlockSpec((1, full, 1), lambda s, h: (s, 0, 0)),
            pl.BlockSpec((full, 1), lambda s, h: (0, 0)),
            pl.BlockSpec((n, full), lambda s, h: (0, 0)),
        ]
        self.log_spec = pl.BlockSpec((1, full, 1), lambda s, h: (s * heads + h, 0, 0))
        self.params = pltpu.CompilerParams(vmem_limit_bytes=VMEM_BYTES)

    def shape(self, dtype):
        return jax.ShapeDtypeStruct((2, 2, self.rows, self.heads * HD), dtype)

    def view(self, v):
        return v.reshape(-1, 2, self.rows, v.shape[-1])

    def forward(self, q, key, value):
        count = self.count
        parts = [self.part(t) for t in range(count)]
        out, log = pl.pallas_call(
            functools.partial(attend_kernel, count, HD**-0.5),
            grid=(2, self.heads),
            in_specs=[self.block] + parts * 2 + self.table_specs(count),
            out_specs=[self.block, self.log_spec],
            out_shape=[self.shape(BF), jax.ShapeDtypeStruct((2 * self.heads, 2 * self.rows, 1), F32)],
            compiler_params=self.params,
            name="attend_forward",
            cost_estimate=cost(23),
        )(self.view(q), *[self.view(key)] * count, *[self.view(value)] * count, *self.tables)
        return out.reshape(q.shape), log

    def backward(self, q, do, o, key, value, log, blocks, dtypes, dq=None):
        lo, pos, key_pos = self.tables
        count = len(blocks)
        grads = [self.shape(d) for d in dtypes]
        key_pos = jnp.concatenate([key_pos[t : t + 1] for t in blocks], axis=0)
        more = [] if dq is None else [self.view(dq)]
        parts = [self.part(t) for t in blocks]
        outs = pl.pallas_call(
            functools.partial(attend_back_kernel, count, dq is None, HD**-0.5),
            grid=(2, self.heads),
            in_specs=[self.block] * 3 + parts * 2 + self.table_specs(count) + [self.log_spec] + [self.block] * len(more),
            out_specs=[self.block] * (1 + 2 * count),
            out_shape=[self.shape(F32)] + grads + grads,
            compiler_params=self.params,
            name="attend_backward",
            cost_estimate=cost(4 + 8 * count),
        )(
            *[self.view(v) for v in [q, do, o]],
            *[self.view(key)] * count,
            *[self.view(value)] * count,
            lo,
            pos,
            key_pos,
            log,
            *more,
        )
        flat = [v.reshape(q.shape) for v in outs]
        return flat[0], flat[1 : 1 + count], flat[1 + count :]


def rms_inverse(v):
    return lax.rsqrt(jnp.mean(v * v, axis=-1, keepdims=True) + EPS)


def rms_backward(v, gain, grad):
    inv = rms_inverse(v)
    turn = grad * gain
    inner = jnp.mean(v * turn, axis=-1, keepdims=True)
    return inv * turn - v * (inv * inv * inv) * inner


def total(refs):
    return sum(ref[...].astype(F32) for ref in refs)


def after_attention_kernel(*refs):
    inputs_ref, gain_ref, attn_ref, middle_ref, low_ref = refs[3:]
    attn = total(refs[:3])
    attn_ref[...] = attn
    middle = inputs_ref[...].astype(F32) + attn * rms_inverse(attn) * gain_ref[...]
    middle_ref[...] = middle
    low_ref[...] = middle.astype(BF)


def after_feed_kernel(*refs):
    middle_ref, gain_ref, cot_ref, result_ref, grad_ref = refs[4:]
    feed = total(refs[:4])
    gain = gain_ref[...]
    result_ref[...] = (middle_ref[...] + feed * rms_inverse(feed) * gain).astype(BF)
    grad_ref[...] = rms_backward(feed, gain, cot_ref[...].astype(F32)).astype(BF)


def middle_kernel(*refs):
    cot_ref, attn_ref, gain_ref, mid_ref, grad_ref = refs[4:]
    mid = cot_ref[...].astype(F32) + total(refs[:4])
    mid_ref[...] = mid
    grad_ref[...] = rms_backward(attn_ref[...], gain_ref[...], mid).astype(BF)


def end_kernel(*refs):
    mid_ref, out_ref = refs[3:]
    out_ref[...] = mid_ref[...] + total(refs[:3])


def by_rows(kernel, name, rows, width, args, dtypes, us):
    tile = 64 if rows % 64 == 0 else rows
    spec = lambda v: pl.BlockSpec((1, width), lambda r: (0, 0)) if v.shape[0] == 1 else pl.BlockSpec((tile, width), lambda r: (r, 0))
    row = pl.BlockSpec((tile, width), lambda r: (r, 0))
    return pl.pallas_call(
        kernel,
        grid=(rows // tile,),
        in_specs=[spec(v) for v in args],
        out_specs=[row] * len(dtypes),
        out_shape=[jax.ShapeDtypeStruct((rows, width), d) for d in dtypes],
        compiler_params=pltpu.CompilerParams(vmem_limit_bytes=VMEM_BYTES),
        name=name,
        cost_estimate=cost(us),
    )(*args)


def on_device(
    layer_input,
    cotangent,
    document_length,
    adapter_choice_index,
    query_weight,
    key_weight,
    value_weight,
    output_weight,
    gate_weight,
    up_weight,
    down_weight,
    query_norm_gain,
    key_norm_gain,
    attention_norm_gain,
    feedforward_norm_gain,
    adapter_model_input_maps,
    adapter_down_input_maps,
    adapter_model_output_maps,
    adapter_hidden_output_maps,
):
    at = Place()
    rows = layer_input.shape[1]
    width = layer_input.shape[2]
    heads = width // HD // 4
    local = heads * HD
    rank = adapter_model_input_maps.shape[2]
    depth = query_weight.shape[0]
    hidden_rows = down_weight.shape[0]
    hidden = hidden_rows * at.np
    reach = WINDOW // (2 * rows)
    count = reach + 1

    def head_cols(v, quarter):
        return pick(v.reshape(v.shape[:-1] + (heads, 4, HD)), v.ndim, quarter).reshape(v.shape[:-1] + (local,))

    def hidden_cols(v):
        lead = v.shape[:-1]
        n = len(lead)
        v = v.reshape(lead + (at.np, 2, 2, 2, hidden_rows))
        v = pick(v, n + 3, at.c)
        v = pick(v, n + 2, at.y)
        return pick(v, n + 1, at.x).reshape(lead + (-1,))

    def gather_p(v):
        return lax.all_gather(v, "p", axis=0, tiled=True)

    own_inputs = layer_input[0]
    head_offsets = lambda x, y, c: [4 * k + 2 * x + c for k in range(heads)]
    feed_offsets = lambda x, y, c: [((2 * p + x) * 2 + y) * 2 + c for p in range(at.np)]
    w_qkv, gate_piece, up_piece, inputs = start(
        at.np,
        reach,
        pack(at.spot, [query_weight, key_weight, value_weight], HD, head_offsets, TURNS4),
        pack(at.spot, [gate_weight], hidden_rows, feed_offsets, TURNS8),
        pack(at.spot, [up_weight], hidden_rows, feed_offsets, TURNS8),
        own_inputs,
    )
    w_g = gather_p(gate_piece)
    w_u = gather_p(up_piece)
    w_d = gather_p(after(down_weight, w_g))
    if 2 * depth == HD:
        o_own = gather_p(output_weight)
        o_sent = after(o_own, w_qkv)
        sent = lambda target: lax.ppermute(o_sent, ("y", "c"), target)
        same = at.y == at.c
        mine_half = jnp.where(same, o_own, sent([(0, 2), (3, 1)]))
        other_half = jnp.where(same, sent([(1, 0), (2, 3)]), sent([(1, 2), (2, 1)]))
        halves = [jnp.where(at.c == 0, mine_half, other_half), jnp.where(at.c == 0, other_half, mine_half)]
        w_o = jnp.stack([v.reshape(at.np, depth, width) for v in halves], axis=1).reshape(local, width)
    else:
        o_full = lax.all_gather(output_weight, ("p", "x", "y", "c"), axis=0, tiled=True)
        w_o = pick(o_full.reshape(heads, 4, HD, width), 1, at.quarter).reshape(local, width)
    selected = adapter_choice_index[0]
    a_model = pick(adapter_model_input_maps, 0, selected)
    a_hidden = pick(adapter_down_input_maps, 0, selected)
    b_model = pick(adapter_model_output_maps, 0, selected)
    b_hidden = pick(adapter_hidden_output_maps, 0, selected)
    a_qkv = a_model[:3].reshape(3 * rank, width)
    a_gu = a_model[4:6].reshape(2 * rank, width)
    a_o = head_cols(a_model[3], at.quarter)
    a_d = hidden_cols(a_hidden)
    b_qkv = head_cols(b_model[:3], at.quarter)
    b_o, b_d = b_model[3], b_model[4]
    b_gu = hidden_cols(b_hidden)

    def diagonal(maps):
        k, r, n = maps.shape
        zero = jnp.zeros((r, n), BF)
        return jnp.concatenate(
            [jnp.concatenate([maps[a] if a == b else zero for b in range(k)], axis=1) for a in range(k)], axis=0
        )

    b_qkv_diag = diagonal(b_qkv)
    gain = jnp.concatenate(
        [head_cols(query_norm_gain[None], at.quarter), head_cols(key_norm_gain[None], at.quarter)], axis=1
    )

    step_rows = jnp.arange(rows, dtype=jnp.int32)
    spot = lambda xx: at.p * 2 * rows + xx * rows + step_rows
    pos = jnp.concatenate([spot(at.x), spot(1 - at.x)])
    lengths = lax.dynamic_slice_in_dim(document_length, 2 * at.y, 2, 0)
    bounds = jnp.cumsum(lengths, axis=1)
    bounds = jnp.where(at.c == 0, bounds, bounds[::-1])
    begin = jnp.max(jnp.where(bounds[:, None, :] <= pos[None, :, None], bounds[:, None, :], 0), axis=2)
    lo = jnp.maximum(begin, pos[None] - (WINDOW - 1))
    key = jnp.stack([pos - 2 * rows * t for t in range(count)])
    attention = Attention(rows, heads, count, lo[:, :, None], pos[:, None], key)

    half_dim = HD // 2
    inv_freq = ROPE_BASE ** (-(jnp.arange(half_dim, dtype=F32) * 2.0 / HD))
    spots = jnp.concatenate([spot(at.x), spot(at.x), spot(1 - at.x), spot(1 - at.x)])
    angles = jnp.concatenate([spots - 2 * rows * t for t in range(count)]).astype(F32)[:, None] * inv_freq
    cos, sin = jnp.cos(angles), jnp.sin(angles)
    cos = jnp.concatenate([cos, cos], axis=1)
    sin = jnp.concatenate([-sin, sin], axis=1)

    own = 4 * rows
    pre_q, pre_k, value_all, narrow_qkv, square_q, square_k = project(
        inputs, own, w_qkv, a_qkv, b_qkv, heads
    )
    inputs = inputs[:own]
    narrow_qkv = narrow_qkv[:own]
    squares = jnp.concatenate([square_q[:1], square_k[:1]], axis=1)
    inv = lax.rsqrt(at.sum4(squares, 2 + reach) / width + EPS).reshape(-1, 1)
    inv_q, inv_k = inv[:own], inv[own:]
    query, key_all = post(pre_q, pre_k, inv_q, inv_k, gain, cos, sin, heads)
    cos, sin = cos[:own], sin[:own]
    inv_k = inv_k[:own]
    o, log = attention.forward(query, key_all, value_all)
    narrow_o = dot_nt(o, a_o).astype(BF)
    def attn_part(part, mark=None):
        ins, narrow = o[part], narrow_o[part]
        if mark is not None:
            ins = after(ins, mark)
        return (dot(ins, w_o) + SCALE_ADAPT * dot(narrow, b_o)).astype(BF)

    near_rows, far_rows = slice(0, 2 * rows), slice(2 * rows, 4 * rows)
    attn_parts = at.scatter4(attn_part(far_rows), lambda mark: attn_part(near_rows, mark))
    attn_gain, feed_gain = attention_norm_gain[None], feedforward_norm_gain[None]
    attn_out, middle, low = by_rows(
        after_attention_kernel,
        "after_attention",
        rows,
        width,
        [*attn_parts, own_inputs, attn_gain],
        [F32, F32, BF],
        4,
    )
    middle_low = jnp.concatenate(at.gather8(low)[0])
    narrow_gu = dot_nt(middle_low, a_gu).astype(BF)
    gate, up, gated = gate_up(middle_low, w_g, w_u, narrow_gu, b_gu)
    feed, narrow_d = down(gated, w_d, a_d, b_d)
    pairs = [feed[2 * rows * k : 2 * rows * (k + 1)] for k in range(4)]
    feed_parts = at.scatter8(*pairs[1:], lambda mark: pairs[0])
    cot = cotangent[0]
    result, grad_feed_own = by_rows(
        after_feed_kernel,
        "after_feed",
        rows,
        width,
        [*feed_parts, middle, feed_gain, cot],
        [BF, BF],
        4,
    )

    feed_args = (w_d, w_g, w_u, gate, up, gated, narrow_gu, b_d, a_d, b_gu, a_gu)
    grad_feed, first = at.gather8(grad_feed_own, lambda pair: feed_back(0, pair, *feed_args))
    tiles = 2 * rows // 256
    backs = [first, feed_back(tiles, grad_feed[1], *feed_args)]
    backs.append(feed_back(2 * tiles, jnp.concatenate(grad_feed[2:]), *feed_args))
    mids = [backs[1][0], backs[2][0][: 2 * rows], backs[2][0][2 * rows :]]
    back_gu = jnp.concatenate([back[1] for back in backs])
    mid_parts = at.scatter8(*mids, lambda mark: backs[0][0])
    grad_mid, grad_attn_own = by_rows(
        middle_kernel, "middle", rows, width, [*mid_parts, cot, attn_out, attn_gain], [F32, BF], 4
    )
    grad_attn = jnp.concatenate(at.gather4(grad_attn_own))
    back_o = dot_nt(grad_attn, b_o).astype(BF)
    grad_o = (dot_nt(grad_attn, w_o) + SCALE_ADAPT * dot(back_o, a_o)).astype(BF)
    dq, dks, dvs = attention.backward(query, grad_o, o, key_all, value_all, log, [reach], [BF])
    moved_k, moved_v = at.shift_p(dks[0], -1), at.shift_p(dvs[0], -1)
    dq, dks, dvs = attention.backward(
        query, grad_o, o, key_all, value_all, log, range(reach), [F32] + [BF] * (reach - 1), dq
    )
    for t in range(reach - 1, 0, -1):
        moved_k = at.shift_p((dks[t].astype(F32) + moved_k.astype(F32)).astype(BF), -1)
        moved_v = at.shift_p((dvs[t].astype(F32) + moved_v.astype(F32)).astype(BF), -1)
    dk = dks[0] + moved_k.astype(F32)
    dv = dvs[0] + moved_v.astype(F32)
    def share_y(mine, other):
        return mine + at.swap_y(other)

    def share_p(v):
        total = pick(v, 1, at.p)
        for by in range(1, at.np):
            total = total + at.turn_p(pick(v, 1, (at.p + by) % at.np), by)
        return total

    def sum_model(v):
        v = v.reshape(-1, at.np, 2, 2, 2 * depth)
        v = pick(v, 2, at.x) + at.swap_x(pick(v, 2, 1 - at.x))
        return share_y(pick(v, 2, at.y), pick(v, 2, 1 - at.y))

    mine = (jnp.arange(4) == at.quarter).astype(F32)

    def spread(v):
        return (v.reshape(-1, heads, 1, HD) * mine[:, None]).reshape(-1, width)

    ga_gu = SCALE_ADAPT * dot_tn(back_gu, middle_low)
    ga_o = SCALE_ADAPT * dot_tn(back_o, o)
    gb_o = SCALE_ADAPT * dot_tn(narrow_o, grad_attn)
    gb_d = SCALE_ADAPT * sum(
        dot_tn(narrow_d[2 * rows * k : 2 * rows * (k + 1)], grad_feed[k]) for k in range(4)
    )
    early = sum_model(after(jnp.concatenate([ga_gu, spread(ga_o), gb_o, gb_d]), dq))
    wide = sum(back[2] for back in backs).reshape(-1, at.np, hidden_rows)
    dk = after(dk, early)
    turn, inner = unpost(dq, dk, pre_q, pre_k, gain, cos, sin, heads)
    inner = at.sum4(inner.T, 1).T / width

    def unnorm(part, pre, scale):
        cols = slice(part * local, (part + 1) * local)
        return (scale * turn[:, cols] - pre * (scale * scale * scale * inner[:, part : part + 1])).astype(BF)

    grad_qkv = jnp.concatenate(
        [unnorm(0, pre_q, inv_q), unnorm(1, pre_k[:own], inv_k), dv.astype(BF)], axis=1
    )
    back_qkv = dot_nt(grad_qkv, b_qkv_diag).astype(BF)

    def late_adapters(mark):
        back = after(back_qkv, mark)
        ga_qkv = SCALE_ADAPT * dot_tn(back, inputs)
        gb_qkv = [
            SCALE_ADAPT * dot_tn(narrow_qkv[:, k * rank : (k + 1) * rank], grad_qkv[:, k * local : (k + 1) * local])
            for k in range(3)
        ]
        return sum_model(jnp.concatenate([ga_qkv, spread(jnp.concatenate(gb_qkv))]))

    def end_part(part, mark=None):
        ins, back = grad_qkv[part], back_qkv[part]
        if mark is not None:
            ins = after(ins, mark)
        return (dot_nt(ins, w_qkv) + SCALE_ADAPT * dot(back, a_qkv)).astype(BF)

    marks = []

    def end_near(mark):
        marks.append(mark)
        return end_part(near_rows, mark)

    end_parts = at.scatter4(end_part(far_rows), end_near)
    (grad_input,) = by_rows(end_kernel, "end", rows, width, [*end_parts, grad_mid], [F32], 3)
    late = late_adapters(marks[0])
    narrow_sums = share_p(jnp.concatenate([late, early], axis=0))
    narrow_sums = narrow_sums.reshape(narrow_sums.shape[0], 2, depth)
    sums = pick(narrow_sums, 1, at.c) + at.swap_core(pick(narrow_sums, 1, 1 - at.c))
    sums = sums.reshape(-1, rank, depth)
    late, early = sums[:6], sums[6:]
    wide = share_p(after(wide, marks[0])).reshape(-1, rank, hidden_rows)
    choose = (jnp.arange(adapter_model_input_maps.shape[0], dtype=jnp.int32) == selected).astype(F32)
    sum_a_model = choose[:, None, None, None] * jnp.concatenate([late[:3], early[2:3], early[:2]])[None]
    sum_a_hidden = choose[:, None, None] * wide[0][None]
    sum_b_model = choose[:, None, None, None] * jnp.concatenate([late[3:], early[3:]])[None]
    sum_b_hidden = choose[:, None, None, None] * wide[1:][None]
    return (result[None], grad_input[None], sum_a_model, sum_a_hidden, sum_b_model, sum_b_hidden)


def solution(mesh):
    grid = mesh.devices.reshape(mesh.shape["ctx"] // 2, 2, mesh.shape["wt"] // 2, 2)
    split = Mesh(grid, ("p", "x", "y", "c"))
    everyone = ("p", "x", "y", "c")
    rows = P(everyone, None)
    tokens = P(("y", "c"), ("p", "x"), None)
    placed = (tokens, tokens, P(), P()) + (rows,) * 7 + (P(),) * 8
    return jax.shard_map(
        on_device,
        mesh=split,
        in_specs=placed,
        out_specs=(
            tokens,
            tokens,
            P(None, None, None, everyone),
            P(None, None, everyone),
            P(None, None, None, everyone),
            P(None, None, None, everyone),
        ),
        check_vma=False,
    )
```

```python
import functools

import jax
import jax.numpy as jnp
from jax import lax
from jax.experimental import pallas as pl
from jax.experimental.pallas import tpu as pltpu
from jax.sharding import Mesh
from jax.sharding import PartitionSpec as P

HD = 128
WINDOW = 1024
SCALE_ADAPT = 0.5
ROPE_BASE = 500000.0
EPS = 1e-06
BF = jnp.bfloat16
F32 = jnp.float32
VMEM_BYTES = 56 * 1024 * 1024


def cost(us):
    return pl.CostEstimate(flops=int(us * 1.1e9), bytes_accessed=int(us * 1e6), transcendentals=0)


def dot(a, b, dims=((1,), (0,))):
    return lax.dot_general(a, b, (dims, ((), ())), preferred_element_type=F32)


def dot_nt(a, b):
    return dot(a, b, ((1,), (1,)))


def dot_tn(a, b):
    return dot(a, b, ((0,), (0,)))


SWAP = [(0, 1), (1, 0)]


class Place:
    def __init__(self):
        self.np = lax.axis_size("p")
        self.p, self.x, self.y, self.c = (lax.axis_index(a) for a in ("p", "x", "y", "c"))
        self.quarter = 2 * self.x + self.c
        self.spot = jnp.stack([self.x, self.y, self.c]).astype(jnp.int32)

    def swap_core(self, value):
        return lax.ppermute(value, "c", SWAP)

    def swap_x(self, value):
        return lax.ppermute(value, "x", SWAP)

    def swap_both(self, value):
        return lax.ppermute(value, ("x", "c"), [(0, 3), (1, 2), (2, 1), (3, 0)])

    def swap_y(self, value):
        return lax.ppermute(value, "y", SWAP)

    def shift_p(self, value, by):
        return lax.ppermute(value, "p", [(p, p + by) for p in range(self.np) if 0 <= p + by < self.np])

    def turn_p(self, value, by):
        return lax.ppermute(value, "p", [(p, (p + by) % self.np) for p in range(self.np)])

    def gather4(self, own):
        across = self.swap_x(own)
        return self.paired(own), self.paired(across)

    def paired(self, block):
        return jnp.concatenate([block, self.swap_core(block)], axis=0)

    def gather8(self, own, work=None):
        half = own.shape[0] // 2
        across, over = self.swap_x(own), self.swap_y(own)
        first = self.paired(own)
        done = None
        if work is not None:
            done = work(first)
            across, over = after(across, done[0]), after(over, done[0])
        far = jnp.concatenate([self.swap_y(across[:half]), self.swap_x(over[half:])])
        return (first, self.paired(across), self.paired(over), self.paired(far)), done

    def met(self, pair):
        rows = pair.shape[0] // 2
        return (pair[:rows].astype(F32) + self.swap_core(pair[rows:]).astype(F32)).astype(BF)

    def scatter4(self, second, first):
        met = self.met(second)
        across = self.swap_x(met)
        first = first(met)
        return first, self.swap_core(first[first.shape[0] // 2 :]), across

    def scatter8(self, second, third, fourth, first):
        far = self.met(fourth)
        half = far.shape[0] // 2
        by_x, by_y = self.swap_x(far[:half]), self.swap_y(far[half:])
        second, third = self.met(second), self.met(third)
        add = lambda u, v: (u.astype(F32) + v.astype(F32)).astype(BF)
        across = [self.swap_x(second[:half]), self.swap_x(add(second[half:], by_y))]
        over = [self.swap_y(add(third[:half], by_x)), self.swap_y(third[half:])]
        first = first(far)
        core = self.swap_core(first[first.shape[0] // 2 :])
        return first, core, jnp.concatenate(across), jnp.concatenate(over)

    def sum4(self, value, parts):
        def reordered(v, x, c):
            v = v.reshape(v.shape[0], parts, 2, 2, -1)
            if x:
                v = jnp.concatenate([v[:, :, 1:], v[:, :, :1]], axis=2)
            if c:
                v = jnp.concatenate([v[:, :, :, 1:], v[:, :, :, :1]], axis=3)
            return v.reshape(value.shape)

        core, across, both = self.swap_core(value), self.swap_x(value), self.swap_both(value)
        return value + reordered(core, 0, 1) + reordered(across, 1, 0) + reordered(both, 1, 1)


def pick(v, axis, index):
    return lax.dynamic_index_in_dim(v, index, axis, keepdims=False)


def after(value, *others):
    return lax.optimization_barrier((value,) + others)[0]


class Copies:
    def __init__(self, send_sem, recv_sem):
        self.sems, self.used, self.all = (send_sem, recv_sem), 0, []

    def remote(self, src, dst, device):
        k = self.used
        self.used += 1
        copy = pltpu.make_async_remote_copy(
            src_ref=src,
            dst_ref=dst,
            send_sem=self.sems[0].at[k],
            recv_sem=self.sems[1].at[k],
            device_id=device,
            device_id_type=pl.DeviceIdType.MESH,
        )
        copy.start()
        self.all.append(copy)
        return copy

    def finish(self):
        for copy in self.all:
            copy.wait_send()


def pack_kernel(count, width, offsets, turns, spot_ref, *refs):
    spot = [spot_ref[k] for k in range(3)]
    for out, turn in zip(refs[count:], turns):
        places = offsets(*[(s + t) % 2 for s, t in zip(spot, turn)])
        for w, ref in enumerate(refs[:count]):
            for k, place in enumerate(places):
                at = (w * len(places) + k) * width
                out[:, at : at + width] = ref[:, pl.ds(pl.multiple_of(place * width, HD), width)]


def pack(spot, weights, width, offsets, turns):
    rows = weights[0].shape[0]
    size = len(weights) * len(offsets(0, 0, 0)) * width
    if width % HD:
        outs = []
        for turn in turns:
            places = offsets(*[(spot[k] + turn[k]) % 2 for k in range(3)])
            cuts = [lax.dynamic_slice_in_dim(w, place * width, width, 1) for w in weights for place in places]
            outs.append(jnp.concatenate(cuts, axis=1))
        return outs
    whole = pl.BlockSpec(memory_space=pltpu.VMEM)
    return pl.pallas_call(
        functools.partial(pack_kernel, len(weights), width, offsets, turns),
        in_specs=[pl.BlockSpec(memory_space=pltpu.SMEM)] + [whole] * len(weights),
        out_specs=[whole] * len(turns),
        out_shape=[jax.ShapeDtypeStruct((rows, size), BF)] * len(turns),
        compiler_params=pltpu.CompilerParams(vmem_limit_bytes=VMEM_BYTES),
        name="pack_columns",
        cost_estimate=cost(3),
    )(spot, *weights)


TURNS8 = [(dx, dy, dc) for dy in range(2) for dx in range(2) for dc in range(2)]
TURNS4 = TURNS8[:4]


def start_kernel(groups, reach, *refs):
    qkv_pack, feed_packs, x_ref = refs[0:4], (refs[4:12], refs[12:20]), refs[20]
    w_ref, gate_ref, up_ref, all_ref, local_sem, send_sem, recv_sem = refs[21:]
    p, x, y, c = (lax.axis_index(a) for a in ("p", "x", "y", "c"))
    turned = lambda u, t: 1 - u if t else u
    group = [(p, turned(x, dx), turned(y, dy), turned(c, dc)) for dx, dy, dc in TURNS8]
    core, across, over = group[1], group[2], group[4]
    right, left = (lax.rem(p + 1, groups), x, y, c), (lax.rem(p + groups - 1, groups), x, y, c)
    rows, depth = x_ref.shape[0], qkv_pack[0].shape[0]
    used = [0]

    def remote(src, dst, device):
        k = used[0]
        used[0] += 1
        copy = pltpu.make_async_remote_copy(
            src_ref=src,
            dst_ref=dst,
            send_sem=send_sem.at[k],
            recv_sem=recv_sem.at[k],
            device_id=device,
            device_id_type=pl.DeviceIdType.MESH,
        )
        copy.start()
        return copy

    def local(k, src, dst):
        copy = pltpu.make_async_copy(src, dst, local_sem.at[k])
        copy.start()
        return copy

    barrier = pltpu.get_barrier_semaphore()
    for device in group[1:] + [right, left]:
        pl.semaphore_signal(barrier, inc=1, device_id=device, device_id_type=pl.DeviceIdType.MESH)
    pl.semaphore_wait(barrier, 9)

    def at(ref, start, size):
        return ref.at[pl.ds(pl.multiple_of(start, 16), size)]

    def tokens(t, block):
        return all_ref.at[pl.ds((4 * t + block) * rows, rows)]

    def owned(q):
        return w_ref.at[lax.rem(p + 2 * groups - q, groups), :, y]

    slot = (4 * x + 2 * y + c) * depth
    mine = [
        w_ref.at[p, x, y, pl.ds(pl.multiple_of(c * depth, 16), depth)],
        at(gate_ref, slot, depth),
        at(up_ref, slot, depth),
    ]
    firsts = (qkv_pack[0], feed_packs[0][0], feed_packs[1][0])
    kept = [local(k, firsts[k], mine[k]) for k in range(3)] + [local(3, x_ref, tokens(0, 0))]
    regrouped = [remote(qkv_pack[d], mine[0], group[d]) for d in (1, 2, 3)]
    moves = [remote(x_ref, tokens(1, 0), right)]
    sent = list(regrouped) + moves
    kept[0].wait()
    for copy in regrouped:
        copy.wait_recv()
    along = remote(owned(0), owned(0), right)
    later = [remote(owned(0), owned(0), over)]
    spread = [(remote(x_ref, tokens(0, 1), core), remote(x_ref, tokens(0, 2), across))]
    for k in (1, 2):
        later += [remote(feed_packs[k - 1][d], mine[k], group[d]) for d in range(1, 8)]
    sent.append(along)
    step = 1
    ready = 0

    def pass_on(t):
        spread[t][1].wait_recv()
        later.append(remote(tokens(t, 2), tokens(t, 3), core))

    while step < groups or ready <= reach:
        if ready < reach:
            moves[ready].wait_recv()
            if ready + 1 < reach:
                moves.append(remote(tokens(ready + 1, 0), tokens(ready + 2, 0), right))
                sent.append(moves[-1])
            spread.append(
                (
                    remote(tokens(ready + 1, 0), tokens(ready + 1, 1), core),
                    remote(tokens(ready + 1, 0), tokens(ready + 1, 2), across),
                )
            )
        if step < groups:
            along.wait_recv()
            if step < groups - 1:
                along = remote(owned(step), owned(step), right)
                sent.append(along)
            later.append(remote(owned(step), owned(step), over))
            step += 1
        if ready <= reach:
            pass_on(ready)
            ready += 1
    for near, far in spread:
        near.wait_recv()
        sent += [near, far]
    for copy in later:
        copy.wait_recv()
    for copy in sent + later:
        copy.wait_send()
    for copy in kept[1:]:
        copy.wait()


def start(groups, reach, qkv_pack, gate_pack, up_pack, own_inputs):
    depth, size = qkv_pack[0].shape
    rows, width = own_inputs.shape
    hidden = gate_pack[0].shape[1]
    copies = 3 + 1 + 1 + 1 + 14 + (groups - 2) + (groups - 1) + (reach - 1) + 2 * (reach + 1) + (reach + 1)
    anywhere = pl.BlockSpec(memory_space=pl.ANY)
    weight, gate, up, inputs = pl.pallas_call(
        functools.partial(start_kernel, groups, reach),
        in_specs=[anywhere] * 21,
        out_specs=[anywhere] * 4,
        out_shape=[
            jax.ShapeDtypeStruct((groups, 2, 2, 2 * depth, size), BF),
            jax.ShapeDtypeStruct((8 * depth, hidden), BF),
            jax.ShapeDtypeStruct((8 * depth, hidden), BF),
            jax.ShapeDtypeStruct((4 * (reach + 1) * rows, width), BF),
        ],
        scratch_shapes=[
            pltpu.SemaphoreType.DMA((4,)),
            pltpu.SemaphoreType.DMA((copies,)),
            pltpu.SemaphoreType.DMA((copies,)),
        ],
        compiler_params=pltpu.CompilerParams(collective_id=0, has_side_effects=True),
        name="start",
        cost_estimate=cost(120),
    )(*qkv_pack, *gate_pack, *up_pack, own_inputs)
    return weight.reshape(-1, size), gate, up, inputs


def gate_up_kernel(x_ref, gate_w_ref, up_w_ref, narrow_ref, maps_ref, gate_ref, up_ref, gated_ref):
    rank = maps_ref.shape[1]
    gate = dot(x_ref[...], gate_w_ref[...]) + SCALE_ADAPT * dot(narrow_ref[:, :rank], maps_ref[0])
    up = dot(x_ref[...], up_w_ref[...]) + SCALE_ADAPT * dot(narrow_ref[:, rank:], maps_ref[1])
    gate_ref[...] = gate.astype(BF)
    up_ref[...] = up.astype(BF)
    gated_ref[...] = (gate * jax.nn.sigmoid(gate) * up).astype(BF)


def gate_up(x, gate_w, up_w, narrow, maps):
    rows, width = x.shape
    hidden = gate_w.shape[1]
    tile = 256
    weight = pl.BlockSpec((width, tile), lambda s: (0, s))
    out = pl.BlockSpec((rows, tile), lambda s: (0, s))
    return pl.pallas_call(
        gate_up_kernel,
        grid=(hidden // tile,),
        in_specs=[
            pl.BlockSpec((rows, width), lambda s: (0, 0)),
            weight,
            weight,
            pl.BlockSpec(narrow.shape, lambda s: (0, 0)),
            pl.BlockSpec(maps.shape[:2] + (tile,), lambda s: (0, 0, s)),
        ],
        out_specs=[out] * 3,
        out_shape=[jax.ShapeDtypeStruct((rows, hidden), BF)] * 3,
        compiler_params=pltpu.CompilerParams(vmem_limit_bytes=VMEM_BYTES),
        name="gate_up",
        cost_estimate=cost(26),
    )(x, gate_w, up_w, narrow, maps)


def project_kernel(heads, own_tiles, x_ref, w_ref, in_maps_ref, out_maps_ref, *out_refs):
    pre_q_ref, pre_k_ref, value_ref, narrow_ref, square_q_ref, square_k_ref = out_refs
    width = heads * HD
    rank = out_maps_ref.shape[1]
    narrow_ref[...] = dot_nt(x_ref[...], in_maps_ref[...]).astype(BF)

    def part(k):
        cols = slice(k * width, (k + 1) * width)
        return dot(x_ref[...], w_ref[:, cols]) + SCALE_ADAPT * dot(narrow_ref[:, k * rank : (k + 1) * rank], out_maps_ref[k])

    ones = jnp.ones((8, width), BF)
    key = part(1)
    pre_k_ref[...] = key
    square_k_ref[...] = dot_nt(ones, (key * key).astype(BF))
    value_ref[...] = part(2).astype(BF)

    @pl.when(pl.program_id(0) < own_tiles)
    def _():
        query = part(0)
        pre_q_ref[...] = query
        square_q_ref[...] = dot_nt(ones, (query * query).astype(BF))


def project(x, own_rows, weight, in_maps, out_maps, heads):
    rows, width = x.shape
    local = heads * HD
    tile = 512
    own_tiles = own_rows // tile
    fixed = lambda v: pl.BlockSpec(v.shape, lambda t: (0,) * v.ndim)
    row = lambda n: pl.BlockSpec((tile, n), lambda t: (t, 0))
    return pl.pallas_call(
        functools.partial(project_kernel, heads, own_tiles),
        grid=(rows // tile,),
        in_specs=[row(width), fixed(weight), fixed(in_maps), fixed(out_maps)],
        out_specs=[
            pl.BlockSpec((tile, local), lambda t: (jnp.minimum(t, own_tiles - 1), 0)),
            row(local),
            row(local),
            row(in_maps.shape[0]),
            pl.BlockSpec((8, tile), lambda t: (0, jnp.minimum(t, own_tiles - 1))),
            pl.BlockSpec((8, tile), lambda t: (0, t)),
        ],
        out_shape=[
            jax.ShapeDtypeStruct((own_rows, local), F32),
            jax.ShapeDtypeStruct((rows, local), F32),
            jax.ShapeDtypeStruct((rows, local), BF),
            jax.ShapeDtypeStruct((rows, in_maps.shape[0]), BF),
            jax.ShapeDtypeStruct((8, own_rows), F32),
            jax.ShapeDtypeStruct((8, rows), F32),
        ],
        compiler_params=pltpu.CompilerParams(vmem_limit_bytes=VMEM_BYTES),
        name="project",
        cost_estimate=cost(30),
    )(x, weight, in_maps, out_maps)


def post_kernel(heads, own_tiles, q_ref, k_ref, inv_q_ref, inv_k_ref, gain_ref, cos_ref, sin_ref, q_out, k_out):
    width = heads * HD
    cos, sin = cos_ref[...], sin_ref[...]

    def turn(pre_ref, inv, part, out_ref):
        for h in range(heads):
            cols = slice(h * HD, (h + 1) * HD)
            v = pre_ref[:, cols] * inv * gain_ref[:, part * width + h * HD : part * width + (h + 1) * HD]
            out_ref[:, cols] = (v * cos + pltpu.roll(v, HD // 2, 1) * sin).astype(BF)

    turn(k_ref, inv_k_ref[...], 1, k_out)

    @pl.when(pl.program_id(0) < own_tiles)
    def _():
        turn(q_ref, inv_q_ref[...], 0, q_out)


def post(pre_q, pre_k, inv_q, inv_k, gain, cos, sin, heads):
    rows, width = pre_k.shape
    tile = 256
    own_tiles = pre_q.shape[0] // tile
    row = lambda n: pl.BlockSpec((tile, n), lambda r: (r, 0))
    own = lambda n: pl.BlockSpec((tile, n), lambda r: (jnp.minimum(r, own_tiles - 1), 0))
    return pl.pallas_call(
        functools.partial(post_kernel, heads, own_tiles),
        grid=(rows // tile,),
        in_specs=[
            own(width),
            row(width),
            own(1),
            row(1),
            pl.BlockSpec((1, 2 * width), lambda r: (0, 0)),
            row(HD),
            row(HD),
        ],
        out_specs=[own(width), row(width)],
        out_shape=[jax.ShapeDtypeStruct(pre_q.shape, BF), jax.ShapeDtypeStruct(pre_k.shape, BF)],
        name="rope_forward",
        cost_estimate=cost(10),
    )(pre_q, pre_k, inv_q, inv_k, gain, cos, sin)


def unpost_kernel(heads, dq_ref, dk_ref, pre_q_ref, pre_k_ref, gain_ref, cos_ref, sin_ref, turn_ref, inner_ref):
    width = heads * HD
    cos, sin = cos_ref[...], sin_ref[...]
    for part, (d_ref, pre_ref) in enumerate(((dq_ref, pre_q_ref), (dk_ref, pre_k_ref))):
        total = None
        for h in range(heads):
            cols = slice(part * width + h * HD, part * width + (h + 1) * HD)
            v = d_ref[:, h * HD : (h + 1) * HD]
            turned = (v * cos - pltpu.roll(v, HD // 2, 1) * sin) * gain_ref[:, cols]
            turn_ref[:, cols] = turned
            inner = jnp.sum(turned * pre_ref[:, h * HD : (h + 1) * HD], axis=1, keepdims=True)
            total = inner if total is None else total + inner
        inner_ref[:, part : part + 1] = total


def unpost(dq, dk, pre_q, pre_k, gain, cos, sin, heads):
    rows, width = dq.shape
    tile = 256
    row = lambda n: pl.BlockSpec((tile, n), lambda r: (r, 0))
    return pl.pallas_call(
        functools.partial(unpost_kernel, heads),
        grid=(rows // tile,),
        in_specs=[row(width)] * 4 + [pl.BlockSpec((1, 2 * width), lambda r: (0, 0)), row(HD), row(HD)],
        out_specs=[row(2 * width), row(2)],
        out_shape=[jax.ShapeDtypeStruct((rows, 2 * width), F32), jax.ShapeDtypeStruct((rows, 2), F32)],
        name="rope_backward",
        cost_estimate=cost(8),
    )(dq, dk, pre_q, pre_k, gain, cos, sin)


def finish_kernel(groups, heads, early_rows, *refs):
    (
        dq_ref,
        dk_ref,
        dv_ref,
        more_k_ref,
        more_v_ref,
        pre_q_ref,
        pre_k_ref,
        inv_q_ref,
        inv_k_ref,
        gain_ref,
        cos_ref,
        sin_ref,
        in_maps_ref,
        out_maps_ref,
        narrow_ref,
        early_ref,
        wide_ref,
        weight_any,
        inputs_any,
        mid_any,
    ) = refs[:20]
    out_ref, sums_ref, wide_out_ref = refs[20:23]
    (
        weight,
        inputs,
        mid,
        turn,
        grad,
        back,
        stat,
        stat_in,
        far,
        near,
        core_in,
        met,
        across_in,
        near_in,
        maps,
        maps_in,
        by_x,
        by_y,
        by_y_in,
        by_p_in,
        own_sum,
        own_sum_in,
        wide_in,
        local_sem,
        send_sem,
        recv_sem,
    ) = refs[23:]
    p, x, y, c = (lax.axis_index(a) for a in ("p", "x", "y", "c"))
    core, across, both, over = (p, x, y, 1 - c), (p, 1 - x, y, c), (p, 1 - x, y, 1 - c), (p, x, 1 - y, c)
    others = [lax.rem(p + s, groups) for s in range(1, groups)]
    width = heads * HD
    rows = out_ref.shape[0]
    model = out_ref.shape[1]
    rank = out_maps_ref.shape[1]
    copies = Copies(send_sem, recv_sem)
    loads = []
    for k, (src, dst) in enumerate(((weight_any, weight), (inputs_any, inputs), (mid_any, mid))):
        loads.append(pltpu.make_async_copy(src, dst, local_sem.at[k]))
        loads[-1].start()

    barrier = pltpu.get_barrier_semaphore()
    for device in [core, across, both, over] + [(q, x, y, c) for q in others]:
        pl.semaphore_signal(barrier, inc=1, device_id=device, device_id_type=pl.DeviceIdType.MESH)

    ones = jnp.ones((8, HD), BF)

    def unturn(b, carry):
        here = pl.ds(pl.multiple_of(b * rows, rows), rows)
        cos, sin = cos_ref[here, :], sin_ref[here, :]
        for part, pre_ref in enumerate((pre_q_ref, pre_k_ref)):
            product = None
            for h in range(heads):
                cols = slice(h * HD, (h + 1) * HD)
                wide_cols = slice(part * width + h * HD, part * width + (h + 1) * HD)
                v = dq_ref[here, cols] if part == 0 else dk_ref[here, cols] + more_k_ref[here, cols].astype(F32)
                turned = (v * cos - pltpu.roll(v, HD // 2, 1) * sin) * gain_ref[:, wide_cols]
                turn[here, wide_cols] = turned
                term = turned * pre_ref[here, cols]
                product = term if product is None else product + term
            high = product.astype(BF)
            low = (product - high.astype(F32)).astype(BF)
            summed = dot_nt(ones, high) + dot_nt(ones, low)
            stat[part : part + 1, here] = summed[:1, :]
        grad[here, 2 * width :] = (dv_ref[here, :] + more_v_ref[here, :].astype(F32)).astype(BF)
        return carry

    stat[...] = jnp.zeros_like(stat)
    lax.fori_loop(0, 4, unturn, 0)
    for b in range(2 * groups):
        maps[b, :early_rows, :] = early_ref[:, b * 256 : (b + 1) * 256]
    pl.semaphore_wait(barrier, 3 + groups)
    stats = [copies.remote(stat, stat_in.at[k], device) for k, device in enumerate((core, across, both))]
    early = pl.ds(0, early_rows)
    exchanged = [copies.remote(maps.at[2 * q + 1 - x, early], maps_in.at[q, early], across) for q in range(groups)]
    wides = [
        copies.remote(wide_ref.at[:, pl.ds(pl.multiple_of(q * 256, 256), 256)], wide_in.at[k], (q, x, y, c))
        for k, q in enumerate(others)
    ]
    for copy in stats:
        copy.wait_recv()

    for b in range(4):
        here = slice(b * rows, (b + 1) * rows)
        total_row = stat[:, here]
        for k in range(3):
            d = b ^ (k + 1)
            total_row = total_row + stat_in[k, :, d * rows : (d + 1) * rows]
        inner = total_row.T / model
        for part, (pre_ref, inv_ref) in enumerate(((pre_q_ref, inv_q_ref), (pre_k_ref, inv_k_ref))):
            cols = slice(part * width, (part + 1) * width)
            inv = inv_ref[here, :]
            scale = inv * inv * inv * inner[:, part : part + 1]
            grad[here, cols] = (inv * turn[here, cols] - pre_ref[here, :] * scale).astype(BF)

    loads[0].wait()

    def into(start, dst):
        here = slice(start, start + 2 * rows)
        for k in range(3):
            part = dot_nt(grad[here, k * width : (k + 1) * width], out_maps_ref[k])
            back[here, k * rank : (k + 1) * rank] = part.astype(BF)

        def columns(n, carry):
            cols = pl.ds(pl.multiple_of(n * 512, 512), 512)
            full = dot_nt(grad[here, :], weight[cols, :]) + SCALE_ADAPT * dot(back[here, :], in_maps_ref[:, cols])
            dst[:, cols] = full.astype(BF)
            return carry

        lax.fori_loop(0, model // 512, columns, 0)

    into(2 * rows, far)
    far_copy = copies.remote(far.at[pl.ds(rows, rows)], core_in, core)
    far_copy.wait_recv()
    met[...] = (far[:rows, :].astype(F32) + core_in[...].astype(F32)).astype(BF)
    across_copy = copies.remote(met, across_in, across)
    into(0, near)
    near_copy = copies.remote(near.at[pl.ds(rows, rows)], near_in, core)

    loads[1].wait()
    late = early_rows + 3 * rank
    for b in range(2 * groups):
        cols = slice(b * 256, (b + 1) * 256)
        maps[b, early_rows:late, :] = SCALE_ADAPT * dot_tn(back[...], inputs[:, cols])
    send_late = pl.ds(early_rows, 3 * rank)
    exchanged += [
        copies.remote(maps.at[2 * q + 1 - x, send_late], maps_in.at[q, send_late], across) for q in range(groups)
    ]
    for q in range(groups):
        by_x[q, late:, :] = jnp.zeros_like(by_x[q, late:, :])
    for k in range(3):
        own = SCALE_ADAPT * dot_tn(narrow_ref[:, k * rank : (k + 1) * rank], grad[:, k * width : (k + 1) * width])
        here = slice(late + k * rank, late + (k + 1) * rank)
        for q in range(groups):
            by_x[q, here, pl.ds(pl.multiple_of(c * HD, HD), HD)] = own[:, q * HD : (q + 1) * HD]
    for copy in exchanged:
        copy.wait_recv()
    for q in range(groups):
        by_x[q, :late, :] = maps[2 * q + x, :late, :] + maps_in[q]
    halves = lambda ref, q, side: ref.at[q, :, pl.ds(pl.multiple_of(side * HD, HD), HD)]
    exchanged = [copies.remote(halves(by_x, q, 1 - y), by_y_in.at[q], over) for q in range(groups)]
    for q, copy in enumerate(exchanged):
        copy.wait_recv()
        by_y[q] = by_x[q, :, pl.ds(pl.multiple_of(y * HD, HD), HD)] + by_y_in[q]
    exchanged = [copies.remote(by_y.at[q], by_p_in.at[k], (q, x, y, c)) for k, q in enumerate(others)]
    summed = by_y[p]
    wide_sum = wide_ref[:, pl.ds(pl.multiple_of(p * 256, 256), 256)]
    for k, copy in enumerate(exchanged):
        copy.wait_recv()
        summed = summed + by_p_in[k]
    own_sum[...] = summed
    last = copies.remote(own_sum, own_sum_in, core)
    for k, copy in enumerate(wides):
        copy.wait_recv()
        wide_sum = wide_sum + wide_in[k]
    wide_out_ref[...] = wide_sum
    last.wait_recv()
    summed = summed + own_sum_in[...]
    sums_ref[...] = jnp.where(c == 0, summed[:, : HD // 2], summed[:, HD // 2 :])

    loads[2].wait()
    near_copy.wait_recv()
    across_copy.wait_recv()
    out_ref[...] = (
        mid[...]
        + near[:rows, :].astype(F32)
        + near_in[...].astype(F32)
        + across_in[...].astype(F32)
    )
    copies.finish()


def finish(groups, heads, args, weight, inputs, mid):
    own, width = args[0].shape
    rows, model = mid.shape
    rank = args[13].shape[1]
    early_rows, wide_rows = args[15].shape[0], args[16].shape[0]
    total_rows = early_rows + 6 * rank
    late = early_rows + 3 * rank
    vm = pl.BlockSpec(memory_space=pltpu.VMEM)
    anywhere = pl.BlockSpec(memory_space=pl.ANY)
    count = 3 + groups + (groups - 1) + 3 + 2 * groups + (groups - 1) + 1
    block = lambda *shape: pltpu.VMEM(shape, BF)
    full = lambda *shape: pltpu.VMEM(shape, F32)
    return pl.pallas_call(
        functools.partial(finish_kernel, groups, heads, early_rows),
        in_specs=[vm] * 17 + [anywhere] * 3,
        out_specs=[vm] * 3,
        out_shape=[
            jax.ShapeDtypeStruct((rows, model), F32),
            jax.ShapeDtypeStruct((total_rows, HD // 2), F32),
            jax.ShapeDtypeStruct((wide_rows, 256), F32),
        ],
        scratch_shapes=[
            pltpu.VMEM(weight.shape, BF),
            pltpu.VMEM(inputs.shape, BF),
            pltpu.VMEM(mid.shape, F32),
            full(own, 2 * width),
            block(own, 3 * width),
            block(own, 3 * rank),
            full(8, own),
            full(3, 8, own),
            block(2 * rows, model),
            block(2 * rows, model),
            block(rows, model),
            block(rows, model),
            block(rows, model),
            block(rows, model),
            full(2 * groups, late, 256),
            full(groups, late, 256),
            full(groups, total_rows, 256),
            full(groups, total_rows, HD),
            full(groups, total_rows, HD),
            full(groups - 1, total_rows, HD),
            full(total_rows, HD),
            full(total_rows, HD),
            full(groups - 1, wide_rows, 256),
            pltpu.SemaphoreType.DMA((3,)),
            pltpu.SemaphoreType.DMA((count,)),
            pltpu.SemaphoreType.DMA((count,)),
        ],
        compiler_params=pltpu.CompilerParams(
            collective_id=1, has_side_effects=True, vmem_limit_bytes=VMEM_BYTES
        ),
        name="finish",
        cost_estimate=cost(60),
    )(*args, weight, inputs, mid)


NEG_FILL = -1e30


def attend_kernel(count, scale, q_ref, *refs):
    ks, vs = refs[:count], refs[count : 2 * count]
    lo_ref, pos_ref, key_ref, o_ref, log_ref = refs[2 * count :]
    rows = q_ref.shape[0] * q_ref.shape[2]
    q = q_ref[...].reshape(rows, HD)
    lo, pos = lo_ref[0], pos_ref[...]
    scores = []
    for t in range(count):
        s = dot_nt(q, ks[t][...].reshape(rows, HD)) * scale
        key = key_ref[t : t + 1, :]
        scores.append(jnp.where((key >= lo) & (key <= pos), s, NEG_FILL))
    top = functools.reduce(jnp.maximum, [jnp.max(s, axis=1, keepdims=True) for s in scores])
    powers = [jnp.exp(s - top) for s in scores]
    total = sum(jnp.sum(e, axis=1, keepdims=True) for e in powers)
    share = 1.0 / total
    out = sum(dot((e * share).astype(BF), vs[t][...].reshape(rows, HD)) for t, e in enumerate(powers))
    o_ref[...] = out.astype(BF).reshape(o_ref.shape)
    log_ref[0] = top + jnp.log(total)


def attend_back_kernel(count, first, scale, q_ref, do_ref, o_ref, *refs):
    ks, vs = refs[:count], refs[count : 2 * count]
    lo_ref, pos_ref, key_ref, log_ref = refs[2 * count : 2 * count + 4]
    refs = refs[2 * count + 4 :]
    dq = None
    rows = q_ref.shape[0] * q_ref.shape[2]
    if not first:
        dq = refs[0][...].reshape(rows, HD)
        refs = refs[1:]
    dq_ref, dks, dvs = refs[0], refs[1 : 1 + count], refs[1 + count :]
    q = q_ref[...].reshape(rows, HD)
    do = do_ref[...].reshape(rows, HD)
    inner = jnp.sum(do.astype(F32) * o_ref[...].reshape(rows, HD).astype(F32), axis=1, keepdims=True)
    lo, pos, log_total = lo_ref[0], pos_ref[...], log_ref[0]
    for t in range(count):
        k, v = ks[t][...].reshape(rows, HD), vs[t][...].reshape(rows, HD)
        key = key_ref[t : t + 1, :]
        s = dot_nt(q, k) * scale
        probs = jnp.where((key >= lo) & (key <= pos), jnp.exp(s - log_total), 0.0)
        ds = (probs * (dot_nt(do, v) - inner)).astype(BF)
        dvs[t][...] = dot_tn(probs.astype(BF), do).astype(dvs[t].dtype).reshape(dvs[t].shape)
        dks[t][...] = (dot_tn(ds, q) * scale).astype(dks[t].dtype).reshape(dks[t].shape)
        part = dot(ds, k) * scale
        dq = part if dq is None else dq + part
    dq_ref[...] = dq.reshape(dq_ref.shape)


class Attention:
    def __init__(self, rows, heads, count, lo, pos, key):
        self.rows, self.heads, self.count = rows, heads, count
        self.tables = (lo, pos, key)
        full = 2 * rows
        self.block = pl.BlockSpec((2, 1, rows, HD), lambda s, h: (0, s, 0, h))
        self.part = lambda t: pl.BlockSpec((2, 1, rows, HD), lambda s, h: (t, s, 0, h))
        self.table_specs = lambda n: [
            pl.BlockSpec((1, full, 1), lambda s, h: (s, 0, 0)),
            pl.BlockSpec((full, 1), lambda s, h: (0, 0)),
            pl.BlockSpec((n, full), lambda s, h: (0, 0)),
        ]
        self.log_spec = pl.BlockSpec((1, full, 1), lambda s, h: (s * heads + h, 0, 0))
        self.params = pltpu.CompilerParams(vmem_limit_bytes=VMEM_BYTES)

    def shape(self, dtype):
        return jax.ShapeDtypeStruct((2, 2, self.rows, self.heads * HD), dtype)

    def view(self, v):
        return v.reshape(-1, 2, self.rows, v.shape[-1])

    def forward(self, q, key, value):
        count = self.count
        parts = [self.part(t) for t in range(count)]
        out, log = pl.pallas_call(
            functools.partial(attend_kernel, count, HD**-0.5),
            grid=(2, self.heads),
            in_specs=[self.block] + parts * 2 + self.table_specs(count),
            out_specs=[self.block, self.log_spec],
            out_shape=[self.shape(BF), jax.ShapeDtypeStruct((2 * self.heads, 2 * self.rows, 1), F32)],
            compiler_params=self.params,
            name="attend_forward",
            cost_estimate=cost(23),
        )(self.view(q), *[self.view(key)] * count, *[self.view(value)] * count, *self.tables)
        return out.reshape(q.shape), log

    def backward(self, q, do, o, key, value, log, blocks, dtypes, dq=None):
        lo, pos, key_pos = self.tables
        count = len(blocks)
        grads = [self.shape(d) for d in dtypes]
        key_pos = jnp.concatenate([key_pos[t : t + 1] for t in blocks], axis=0)
        more = [] if dq is None else [self.view(dq)]
        parts = [self.part(t) for t in blocks]
        outs = pl.pallas_call(
            functools.partial(attend_back_kernel, count, dq is None, HD**-0.5),
            grid=(2, self.heads),
            in_specs=[self.block] * 3 + parts * 2 + self.table_specs(count) + [self.log_spec] + [self.block] * len(more),
            out_specs=[self.block] * (1 + 2 * count),
            out_shape=[self.shape(F32)] + grads + grads,
            compiler_params=self.params,
            name="attend_backward",
            cost_estimate=cost(4 + 8 * count),
        )(
            *[self.view(v) for v in [q, do, o]],
            *[self.view(key)] * count,
            *[self.view(value)] * count,
            lo,
            pos,
            key_pos,
            log,
            *more,
        )
        flat = [v.reshape(q.shape) for v in outs]
        return flat[0], flat[1 : 1 + count], flat[1 + count :]


def rms_inverse(v):
    return lax.rsqrt(jnp.mean(v * v, axis=-1, keepdims=True) + EPS)


def rms_backward(v, gain, grad):
    inv = rms_inverse(v)
    turn = grad * gain
    inner = jnp.mean(v * turn, axis=-1, keepdims=True)
    return inv * turn - v * (inv * inv * inv) * inner


def total(refs):
    return sum(ref[...].astype(F32) for ref in refs)


def after_attention_kernel(*refs):
    inputs_ref, gain_ref, attn_ref, middle_ref, low_ref = refs[3:]
    attn = total(refs[:3])
    attn_ref[...] = attn
    middle = inputs_ref[...].astype(F32) + attn * rms_inverse(attn) * gain_ref[...]
    middle_ref[...] = middle
    low_ref[...] = middle.astype(BF)


def end_kernel(*refs):
    mid_ref, out_ref = refs[3:]
    out_ref[...] = mid_ref[...] + total(refs[:3])


def feed_kernel(*refs):
    (
        d_in_ref,
        d_out_ref,
        gu_out_ref,
        gu_in_ref,
        feed_gain_ref,
        attn_gain_ref,
        narrow_gu_ref,
        gated_any,
        gate_any,
        up_any,
        down_any,
        gate_w_any,
        up_w_any,
        middle_any,
        cot_any,
        attn_any,
    ) = refs[:16]
    result_ref, mid_ref, grad_attn_ref, back_gu_ref, maps_ref, gb_d_ref = refs[16:22]
    (
        down_w,
        gate_w,
        up_w,
        acts,
        blocks,
        own_pair,
        core_in,
        by_x,
        by_y,
        across_in,
        over_in,
        tokens,
        cot,
        dgu,
        narrow_d,
        load_sem,
        act_sem,
        free_sem,
        send_sem,
        recv_sem,
    ) = refs[22:]
    p, x, y, c = (lax.axis_index(a) for a in ("p", "x", "y", "c"))
    core, across, over = (p, x, y, 1 - c), (p, 1 - x, y, c), (p, x, 1 - y, c)
    rows, model = result_ref.shape
    pair = 2 * rows
    half = rows // 2
    hidden = down_w.shape[0]
    rank = d_in_ref.shape[0]
    copies = Copies(send_sem, recv_sem)

    def load(k, src, dst):
        copy = pltpu.make_async_copy(src, dst, load_sem.at[k])
        copy.start()
        return copy

    def load_acts(turn, kind, k):
        src = (gated_any, gate_any, up_any)[kind].at[pl.ds(k * pair, pair)]
        copy = pltpu.make_async_copy(src, acts.at[turn % 2, kind], act_sem.at[turn % 2, kind])
        copy.start()
        return copy

    first_order, back_order = (3, 1, 2, 0), (0, 1, 3, 2)
    loaded = load(0, down_any, down_w)
    gated_loads = [load_acts(0, 0, first_order[0]), load_acts(1, 0, first_order[1])]
    middle_load, cot_load = load(1, middle_any, tokens), load(2, cot_any, cot)
    gate_load, up_load = load(3, gate_w_any, gate_w), load(4, up_w_any, up_w)
    barrier = pltpu.get_barrier_semaphore()
    for device in (core, across, over):
        pl.semaphore_signal(barrier, inc=1, device_id=device, device_id_type=pl.DeviceIdType.MESH)
    pl.semaphore_wait(barrier, 3)
    maps_ref[...] = jnp.zeros_like(maps_ref)
    gb_d_ref[...] = jnp.zeros_like(gb_d_ref)

    def part(k):
        return own_pair if k == 0 else blocks.at[pl.ds(2 * k, 2)]

    def store(k, cols, value):
        dst = part(k)
        dst[0, :, cols] = value[:rows].astype(BF)
        dst[1, :, cols] = value[rows:].astype(BF)

    def columns(n):
        return pl.ds(pl.multiple_of(n * 512, 512), 512)

    def forward(k, slot):
        here = slice(k * pair, (k + 1) * pair)
        narrow_d[here, :] = dot_nt(acts[slot, 0], d_in_ref[...]).astype(BF)

        def body(n, carry):
            cols = columns(n)
            value = dot(acts[slot, 0], down_w[:, cols])
            store(k, cols, value + SCALE_ADAPT * dot(narrow_d[here, :], d_out_ref[:, cols]))
            return carry

        lax.fori_loop(0, model // 512, body, 0)

    def backward(k, slot):
        here = slice(k * pair, (k + 1) * pair)
        grad = blocks[2 * k : 2 * k + 2].reshape(pair, model)
        back_d = dot_nt(grad, d_out_ref[...]).astype(BF)
        gb_d_ref[...] += SCALE_ADAPT * dot_tn(narrow_d[here, :], grad)

        def tile(t, carry):
            cols = pl.ds(pl.multiple_of(t * 256, 256), 256)
            grad = blocks[2 * k : 2 * k + 2].reshape(pair, model)
            dm = dot_nt(grad, down_w[cols, :]) + SCALE_ADAPT * dot(back_d, d_in_ref[:, cols])
            gate, up = acts[slot, 1, :, cols].astype(F32), acts[slot, 2, :, cols].astype(F32)
            sig = jax.nn.sigmoid(gate)
            silu = gate * sig
            du = (dm * silu).astype(BF)
            dg = (dm * up * (sig + silu * (1.0 - sig))).astype(BF)
            dgu[0, :, cols] = dg
            dgu[1, :, cols] = du
            narrow = narrow_gu_ref[here, :]
            maps_ref[0, :, cols] += SCALE_ADAPT * dot_tn(back_d, acts[slot, 0, :, cols])
            maps_ref[1, :, cols] += SCALE_ADAPT * dot_tn(narrow[:, :rank], dg)
            maps_ref[2, :, cols] += SCALE_ADAPT * dot_tn(narrow[:, rank:], du)
            return carry

        lax.fori_loop(0, hidden // 256, tile, 0)
        back_g = dot_nt(dgu[0], gu_out_ref[0]).astype(BF)
        back_u = dot_nt(dgu[1], gu_out_ref[1]).astype(BF)
        back_gu_ref[here, :rank] = back_g
        back_gu_ref[here, rank:] = back_u

        def body(n, carry):
            cols = columns(n)
            value = dot_nt(dgu[0], gate_w[cols, :]) + dot_nt(dgu[1], up_w[cols, :])
            value = value + SCALE_ADAPT * (dot(back_g, gu_in_ref[:rank, cols]) + dot(back_u, gu_in_ref[rank:, cols]))
            store(k, cols, value)
            return carry

        lax.fori_loop(0, model // 512, body, 0)

    def to_core(k):
        return copies.remote(part(k).at[1], core_in.at[k], core)

    def meet(k, copy):
        copy.wait_recv()
        blocks[2 * k] = (blocks[2 * k].astype(F32) + core_in[k].astype(F32)).astype(BF)

    top, low = pl.ds(0, half), pl.ds(half, half)

    def add(block, here, more):
        blocks[block, here, :] = (blocks[block, here, :].astype(F32) + more[...].astype(F32)).astype(BF)

    def far_halves():
        return (
            copies.remote(blocks.at[6, top], by_x, across),
            copies.remote(blocks.at[6, low], by_y, over),
        )

    def send_top_across():
        return copies.remote(blocks.at[2, top], across_in.at[top], across)

    def finish_sum(far, own, parts):
        far_x, far_y = far
        parts.append(copies.remote(blocks.at[4, low], over_in.at[low], over))
        far_y.wait_recv()
        add(2, low, by_y)
        parts.append(copies.remote(blocks.at[2, low], across_in.at[low], across))
        far_x.wait_recv()
        add(4, top, by_x)
        parts.append(copies.remote(blocks.at[4, top], over_in.at[top], over))
        own.wait_recv()
        for copy in parts:
            copy.wait_recv()
        return (
            own_pair[0].astype(F32) + core_in[0].astype(F32) + across_in[...].astype(F32) + over_in[...].astype(F32)
        )

    loaded.wait()
    gated_loads[0].wait()
    forward(3, 0)
    sent = to_core(3)
    gated_loads.append(load_acts(2, 0, first_order[2]))
    gated_loads[1].wait()
    forward(1, 1)
    sent1 = to_core(1)
    meet(3, sent)
    far = far_halves()
    gated_loads.append(load_acts(3, 0, first_order[3]))
    gated_loads[2].wait()
    forward(2, 0)
    sent2 = to_core(2)
    meet(1, sent1)
    parts = [send_top_across()]
    gated_loads[3].wait()
    forward(0, 1)
    own = to_core(0)
    meet(2, sent2)
    act_loads = [[load_acts(0, kind, 0) for kind in range(3)], [load_acts(1, kind, 1) for kind in range(3)]]
    feed = finish_sum(far, own, parts)
    copies.finish()
    for device in (core, across, over):
        pl.semaphore_signal(free_sem, inc=1, device_id=device, device_id_type=pl.DeviceIdType.MESH)
    gain = feed_gain_ref[...]
    middle_load.wait()
    cot_load.wait()
    result_ref[...] = (tokens[...] + feed * rms_inverse(feed) * gain).astype(BF)
    blocks[0] = rms_backward(feed, gain, cot[...].astype(F32)).astype(BF)

    pl.semaphore_wait(free_sem, 3)
    copies.all = []
    to_x = copies.remote(blocks.at[0], blocks.at[2], across)
    to_y = copies.remote(blocks.at[0], blocks.at[4], over)
    to_c = copies.remote(blocks.at[0], blocks.at[1], core)
    attn_load = load(5, attn_any, tokens)
    gate_load.wait()
    up_load.wait()
    to_c.wait_recv()
    for copy in act_loads[0]:
        copy.wait()
    backward(0, 0)
    own = to_core(0)
    act_loads.append([load_acts(2, kind, 3) for kind in range(3)])
    to_x.wait_recv()
    x_on = [copies.remote(blocks.at[2], blocks.at[3], core), copies.remote(blocks.at[2, top], blocks.at[6, top], over)]
    to_y.wait_recv()
    y_on = [copies.remote(blocks.at[4], blocks.at[5], core), copies.remote(blocks.at[4, low], blocks.at[6, low], across)]
    x_on[0].wait_recv()
    for copy in act_loads[1]:
        copy.wait()
    for copy in x_on:
        copy.wait_send()
    backward(1, 1)
    sent1 = to_core(1)
    act_loads.append([load_acts(3, kind, 2) for kind in range(3)])
    x_on[1].wait_recv()
    y_on[1].wait_recv()
    far_on = copies.remote(blocks.at[6], blocks.at[7], core)
    meet(1, sent1)
    parts = [send_top_across()]
    far_on.wait_recv()
    for copy in act_loads[2]:
        copy.wait()
    far_on.wait_send()
    backward(3, 0)
    sent = to_core(3)
    meet(3, sent)
    far = far_halves()
    y_on[0].wait_recv()
    for copy in act_loads[3]:
        copy.wait()
    for copy in y_on:
        copy.wait_send()
    backward(2, 1)
    sent2 = to_core(2)
    meet(2, sent2)
    total_grad = finish_sum(far, own, parts)
    mid = cot[...].astype(F32) + total_grad
    mid_ref[...] = mid
    attn_load.wait()
    grad_attn_ref[:rows, :] = rms_backward(tokens[...], attn_gain_ref[...], mid).astype(BF)

    def block(k):
        return grad_attn_ref.at[pl.ds(k * rows, rows)]

    to_x = copies.remote(block(0), block(2), across)
    to_c = copies.remote(block(0), block(1), core)
    to_x.wait_recv()
    on = copies.remote(block(2), block(3), core)
    to_c.wait_recv()
    on.wait_recv()
    done = (*x_on, far_on, *y_on)
    for copy in copies.all:
        if not any(copy is other for other in done):
            copy.wait_send()


def feed_layer(maps, narrow_gu, acts, weights, middle, cot, attn_out):
    rows, model = cot.shape
    hidden = weights[0].shape[0]
    rank = maps[0].shape[0]
    vm = pl.BlockSpec(memory_space=pltpu.VMEM)
    anywhere = pl.BlockSpec(memory_space=pl.ANY)
    block = lambda *shape: pltpu.VMEM(shape, BF)
    count = 48
    return pl.pallas_call(
        feed_kernel,
        in_specs=[vm] * 7 + [anywhere] * 9,
        out_specs=[vm] * 6,
        out_shape=[
            jax.ShapeDtypeStruct((rows, model), BF),
            jax.ShapeDtypeStruct((rows, model), F32),
            jax.ShapeDtypeStruct((4 * rows, model), BF),
            jax.ShapeDtypeStruct((8 * rows, 2 * rank), BF),
            jax.ShapeDtypeStruct((3, rank, hidden), F32),
            jax.ShapeDtypeStruct((rank, model), F32),
        ],
        scratch_shapes=[
            block(hidden, model),
            block(model, hidden),
            block(model, hidden),
            block(2, 3, 2 * rows, hidden),
            block(8, rows, model),
            block(2, rows, model),
            block(4, rows, model),
            block(rows // 2, model),
            block(rows // 2, model),
            block(rows, model),
            block(rows, model),
            pltpu.VMEM((rows, model), F32),
            block(rows, model),
            block(2, 2 * rows, hidden),
            block(8 * rows, rank),
            pltpu.SemaphoreType.DMA((6,)),
            pltpu.SemaphoreType.DMA((2, 3)),
            pltpu.SemaphoreType.REGULAR,
            pltpu.SemaphoreType.DMA((count,)),
            pltpu.SemaphoreType.DMA((count,)),
        ],
        compiler_params=pltpu.CompilerParams(
            collective_id=2, has_side_effects=True, vmem_limit_bytes=60 * 1024 * 1024
        ),
        name="feed_layer",
        cost_estimate=cost(170),
    )(*maps, narrow_gu, *acts, *weights, middle, cot, attn_out)


def by_rows(kernel, name, rows, width, args, dtypes, us):
    tile = 64 if rows % 64 == 0 else rows
    spec = lambda v: pl.BlockSpec((1, width), lambda r: (0, 0)) if v.shape[0] == 1 else pl.BlockSpec((tile, width), lambda r: (r, 0))
    row = pl.BlockSpec((tile, width), lambda r: (r, 0))
    return pl.pallas_call(
        kernel,
        grid=(rows // tile,),
        in_specs=[spec(v) for v in args],
        out_specs=[row] * len(dtypes),
        out_shape=[jax.ShapeDtypeStruct((rows, width), d) for d in dtypes],
        compiler_params=pltpu.CompilerParams(vmem_limit_bytes=VMEM_BYTES),
        name=name,
        cost_estimate=cost(us),
    )(*args)


def on_device(
    layer_input,
    cotangent,
    document_length,
    adapter_choice_index,
    query_weight,
    key_weight,
    value_weight,
    output_weight,
    gate_weight,
    up_weight,
    down_weight,
    query_norm_gain,
    key_norm_gain,
    attention_norm_gain,
    feedforward_norm_gain,
    adapter_model_input_maps,
    adapter_down_input_maps,
    adapter_model_output_maps,
    adapter_hidden_output_maps,
):
    at = Place()
    rows = layer_input.shape[1]
    width = layer_input.shape[2]
    heads = width // HD // 4
    local = heads * HD
    rank = adapter_model_input_maps.shape[2]
    depth = query_weight.shape[0]
    hidden_rows = down_weight.shape[0]
    hidden = hidden_rows * at.np
    reach = WINDOW // (2 * rows)
    count = reach + 1

    def head_cols(v, quarter):
        return pick(v.reshape(v.shape[:-1] + (heads, 4, HD)), v.ndim, quarter).reshape(v.shape[:-1] + (local,))

    def hidden_cols(v):
        lead = v.shape[:-1]
        n = len(lead)
        v = v.reshape(lead + (at.np, 2, 2, 2, hidden_rows))
        v = pick(v, n + 3, at.c)
        v = pick(v, n + 2, at.y)
        return pick(v, n + 1, at.x).reshape(lead + (-1,))

    def gather_p(v):
        return lax.all_gather(v, "p", axis=0, tiled=True)

    own_inputs = layer_input[0]
    head_offsets = lambda x, y, c: [4 * k + 2 * x + c for k in range(heads)]
    feed_offsets = lambda x, y, c: [((2 * p + x) * 2 + y) * 2 + c for p in range(at.np)]
    w_qkv, gate_piece, up_piece, inputs = start(
        at.np,
        reach,
        pack(at.spot, [query_weight, key_weight, value_weight], HD, head_offsets, TURNS4),
        pack(at.spot, [gate_weight], hidden_rows, feed_offsets, TURNS8),
        pack(at.spot, [up_weight], hidden_rows, feed_offsets, TURNS8),
        own_inputs,
    )
    w_g = gather_p(gate_piece)
    w_u = gather_p(up_piece)
    w_d = gather_p(after(down_weight, w_g))
    if 2 * depth == HD:
        o_own = gather_p(output_weight)
        o_sent = after(o_own, w_qkv)
        sent = lambda target: lax.ppermute(o_sent, ("y", "c"), target)
        same = at.y == at.c
        mine_half = jnp.where(same, o_own, sent([(0, 2), (3, 1)]))
        other_half = jnp.where(same, sent([(1, 0), (2, 3)]), sent([(1, 2), (2, 1)]))
        halves = [jnp.where(at.c == 0, mine_half, other_half), jnp.where(at.c == 0, other_half, mine_half)]
        w_o = jnp.stack([v.reshape(at.np, depth, width) for v in halves], axis=1).reshape(local, width)
    else:
        o_full = lax.all_gather(output_weight, ("p", "x", "y", "c"), axis=0, tiled=True)
        w_o = pick(o_full.reshape(heads, 4, HD, width), 1, at.quarter).reshape(local, width)
    selected = adapter_choice_index[0]
    a_model = pick(adapter_model_input_maps, 0, selected)
    a_hidden = pick(adapter_down_input_maps, 0, selected)
    b_model = pick(adapter_model_output_maps, 0, selected)
    b_hidden = pick(adapter_hidden_output_maps, 0, selected)
    a_qkv = a_model[:3].reshape(3 * rank, width)
    a_gu = a_model[4:6].reshape(2 * rank, width)
    a_o = head_cols(a_model[3], at.quarter)
    a_d = hidden_cols(a_hidden)
    b_qkv = head_cols(b_model[:3], at.quarter)
    b_o, b_d = b_model[3], b_model[4]
    b_gu = hidden_cols(b_hidden)

    def diagonal(maps):
        k, r, n = maps.shape
        zero = jnp.zeros((r, n), BF)
        return jnp.concatenate(
            [jnp.concatenate([maps[a] if a == b else zero for b in range(k)], axis=1) for a in range(k)], axis=0
        )

    b_qkv_diag = diagonal(b_qkv)
    gain = jnp.concatenate(
        [head_cols(query_norm_gain[None], at.quarter), head_cols(key_norm_gain[None], at.quarter)], axis=1
    )

    step_rows = jnp.arange(rows, dtype=jnp.int32)
    spot = lambda xx: at.p * 2 * rows + xx * rows + step_rows
    pos = jnp.concatenate([spot(at.x), spot(1 - at.x)])
    lengths = lax.dynamic_slice_in_dim(document_length, 2 * at.y, 2, 0)
    bounds = jnp.cumsum(lengths, axis=1)
    bounds = jnp.where(at.c == 0, bounds, bounds[::-1])
    begin = jnp.max(jnp.where(bounds[:, None, :] <= pos[None, :, None], bounds[:, None, :], 0), axis=2)
    lo = jnp.maximum(begin, pos[None] - (WINDOW - 1))
    key = jnp.stack([pos - 2 * rows * t for t in range(count)])
    attention = Attention(rows, heads, count, lo[:, :, None], pos[:, None], key)

    half_dim = HD // 2
    inv_freq = ROPE_BASE ** (-(jnp.arange(half_dim, dtype=F32) * 2.0 / HD))
    spots = jnp.concatenate([spot(at.x), spot(at.x), spot(1 - at.x), spot(1 - at.x)])
    angles = jnp.concatenate([spots - 2 * rows * t for t in range(count)]).astype(F32)[:, None] * inv_freq
    cos, sin = jnp.cos(angles), jnp.sin(angles)
    cos = jnp.concatenate([cos, cos], axis=1)
    sin = jnp.concatenate([-sin, sin], axis=1)

    own = 4 * rows
    pre_q, pre_k, value_all, narrow_qkv, square_q, square_k = project(
        inputs, own, w_qkv, a_qkv, b_qkv, heads
    )
    inputs = inputs[:own]
    narrow_qkv = narrow_qkv[:own]
    squares = jnp.concatenate([square_q[:1], square_k[:1]], axis=1)
    inv = lax.rsqrt(at.sum4(squares, 2 + reach) / width + EPS).reshape(-1, 1)
    inv_q, inv_k = inv[:own], inv[own:]
    query, key_all = post(pre_q, pre_k, inv_q, inv_k, gain, cos, sin, heads)
    cos, sin = cos[:own], sin[:own]
    inv_k = inv_k[:own]
    o, log = attention.forward(query, key_all, value_all)
    narrow_o = dot_nt(o, a_o).astype(BF)
    def attn_part(part, mark=None):
        ins, narrow = o[part], narrow_o[part]
        if mark is not None:
            ins = after(ins, mark)
        return (dot(ins, w_o) + SCALE_ADAPT * dot(narrow, b_o)).astype(BF)

    near_rows, far_rows = slice(0, 2 * rows), slice(2 * rows, 4 * rows)
    attn_parts = at.scatter4(attn_part(far_rows), lambda mark: attn_part(near_rows, mark))
    attn_gain, feed_gain = attention_norm_gain[None], feedforward_norm_gain[None]
    attn_out, middle, low = by_rows(
        after_attention_kernel,
        "after_attention",
        rows,
        width,
        [*attn_parts, own_inputs, attn_gain],
        [F32, F32, BF],
        4,
    )
    middle_low = jnp.concatenate(at.gather8(low)[0])
    narrow_gu = dot_nt(middle_low, a_gu).astype(BF)
    gate, up, gated = gate_up(middle_low, w_g, w_u, narrow_gu, b_gu)
    result, grad_mid, grad_attn, back_gu, wide, gb_d = feed_layer(
        (a_d, b_d, b_gu, a_gu, feed_gain, attn_gain),
        narrow_gu,
        (gated, gate, up),
        (w_d, w_g, w_u),
        middle,
        cotangent[0],
        attn_out,
    )
    back_o = dot_nt(grad_attn, b_o).astype(BF)
    grad_o = (dot_nt(grad_attn, w_o) + SCALE_ADAPT * dot(back_o, a_o)).astype(BF)
    dq, dks, dvs = attention.backward(query, grad_o, o, key_all, value_all, log, [reach], [BF])
    moved_k, moved_v = at.shift_p(dks[0], -1), at.shift_p(dvs[0], -1)
    dq, dks, dvs = attention.backward(
        query, grad_o, o, key_all, value_all, log, range(reach), [F32] + [BF] * (reach - 1), dq
    )
    for t in range(reach - 1, 0, -1):
        moved_k = at.shift_p((dks[t].astype(F32) + moved_k.astype(F32)).astype(BF), -1)
        moved_v = at.shift_p((dvs[t].astype(F32) + moved_v.astype(F32)).astype(BF), -1)
    def share_y(mine, other):
        return mine + at.swap_y(other)

    def share_p(v):
        total = pick(v, 1, at.p)
        for by in range(1, at.np):
            total = total + at.turn_p(pick(v, 1, (at.p + by) % at.np), by)
        return total

    def sum_model(v):
        v = v.reshape(-1, at.np, 2, 2, 2 * depth)
        v = pick(v, 2, at.x) + at.swap_x(pick(v, 2, 1 - at.x))
        return share_y(pick(v, 2, at.y), pick(v, 2, 1 - at.y))

    mine = (jnp.arange(4) == at.quarter).astype(F32)

    def spread(v):
        return (v.reshape(-1, heads, 1, HD) * mine[:, None]).reshape(-1, width)

    ga_gu = SCALE_ADAPT * dot_tn(back_gu, middle_low)
    ga_o = SCALE_ADAPT * dot_tn(back_o, o)
    gb_o = SCALE_ADAPT * dot_tn(narrow_o, grad_attn)
    early = jnp.concatenate([ga_gu, spread(ga_o), gb_o, gb_d])
    wide = wide.reshape(3 * rank, -1)
    if 2 * depth == HD and hidden_rows == 2 * HD:
        grad_input, sums, wide = finish(
            at.np,
            heads,
            [
                dq,
                dks[0],
                dvs[0],
                moved_k,
                moved_v,
                pre_q,
                pre_k[:own],
                inv_q,
                inv_k,
                gain,
                cos,
                sin,
                a_qkv,
                b_qkv,
                narrow_qkv,
                early,
                wide,
            ],
            w_qkv,
            inputs,
            grad_mid,
        )
        sums, wide = sums.reshape(-1, rank, depth), wide.reshape(-1, rank, hidden_rows)
        early, late = sums[:5], sums[5:]
    else:
        early = sum_model(after(early, dq))
        wide = wide.reshape(-1, at.np, hidden_rows)
        dk = after(dks[0] + moved_k.astype(F32), early)
        dv = dvs[0] + moved_v.astype(F32)
        turn, inner = unpost(dq, dk, pre_q, pre_k, gain, cos, sin, heads)
        inner = at.sum4(inner.T, 1).T / width

        def unnorm(part, pre, scale):
            cols = slice(part * local, (part + 1) * local)
            return (scale * turn[:, cols] - pre * (scale * scale * scale * inner[:, part : part + 1])).astype(BF)

        grad_qkv = jnp.concatenate(
            [unnorm(0, pre_q, inv_q), unnorm(1, pre_k[:own], inv_k), dv.astype(BF)], axis=1
        )
        back_qkv = dot_nt(grad_qkv, b_qkv_diag).astype(BF)

        def late_adapters(mark):
            back = after(back_qkv, mark)
            ga_qkv = SCALE_ADAPT * dot_tn(back, inputs)
            gb_qkv = [
                SCALE_ADAPT * dot_tn(narrow_qkv[:, k * rank : (k + 1) * rank], grad_qkv[:, k * local : (k + 1) * local])
                for k in range(3)
            ]
            return sum_model(jnp.concatenate([ga_qkv, spread(jnp.concatenate(gb_qkv))]))

        def end_part(part, mark=None):
            ins, back = grad_qkv[part], back_qkv[part]
            if mark is not None:
                ins = after(ins, mark)
            return (dot_nt(ins, w_qkv) + SCALE_ADAPT * dot(back, a_qkv)).astype(BF)

        marks = []

        def end_near(mark):
            marks.append(mark)
            return end_part(near_rows, mark)

        end_parts = at.scatter4(end_part(far_rows), end_near)
        (grad_input,) = by_rows(end_kernel, "end", rows, width, [*end_parts, grad_mid], [F32], 3)
        late = late_adapters(marks[0])
        narrow_sums = share_p(jnp.concatenate([late, early], axis=0))
        narrow_sums = narrow_sums.reshape(narrow_sums.shape[0], 2, depth)
        sums = pick(narrow_sums, 1, at.c) + at.swap_core(pick(narrow_sums, 1, 1 - at.c))
        sums = sums.reshape(-1, rank, depth)
        late, early = sums[:6], sums[6:]
        wide = share_p(after(wide, marks[0])).reshape(-1, rank, hidden_rows)
    choose = (jnp.arange(adapter_model_input_maps.shape[0], dtype=jnp.int32) == selected).astype(F32)
    sum_a_model = choose[:, None, None, None] * jnp.concatenate([late[:3], early[2:3], early[:2]])[None]
    sum_a_hidden = choose[:, None, None] * wide[0][None]
    sum_b_model = choose[:, None, None, None] * jnp.concatenate([late[3:], early[3:]])[None]
    sum_b_hidden = choose[:, None, None, None] * wide[1:][None]
    return (result[None], grad_input[None], sum_a_model, sum_a_hidden, sum_b_model, sum_b_hidden)


def solution(mesh):
    grid = mesh.devices.reshape(mesh.shape["ctx"] // 2, 2, mesh.shape["wt"] // 2, 2)
    split = Mesh(grid, ("p", "x", "y", "c"))
    everyone = ("p", "x", "y", "c")
    rows = P(everyone, None)
    tokens = P(("y", "c"), ("p", "x"), None)
    placed = (tokens, tokens, P(), P()) + (rows,) * 7 + (P(),) * 8
    return jax.shard_map(
        on_device,
        mesh=split,
        in_specs=placed,
        out_specs=(
            tokens,
            tokens,
            P(None, None, None, everyone),
            P(None, None, everyone),
            P(None, None, None, everyone),
            P(None, None, None, everyone),
        ),
        check_vma=False,
    )
```

```python
import functools

import jax
import jax.numpy as jnp
from jax import lax
from jax.experimental import pallas as pl
from jax.experimental.pallas import tpu as pltpu
from jax.sharding import Mesh
from jax.sharding import PartitionSpec as P

HD = 128
WINDOW = 1024
SCALE_ADAPT = 0.5
ROPE_BASE = 500000.0
EPS = 1e-06
BF = jnp.bfloat16
F32 = jnp.float32
VMEM_BYTES = 56 * 1024 * 1024


def cost(us):
    return pl.CostEstimate(flops=int(us * 1.1e9), bytes_accessed=int(us * 1e6), transcendentals=0)


def dot(a, b, dims=((1,), (0,))):
    return lax.dot_general(a, b, (dims, ((), ())), preferred_element_type=F32)


def dot_nt(a, b):
    return dot(a, b, ((1,), (1,)))


def dot_tn(a, b):
    return dot(a, b, ((0,), (0,)))


SWAP = [(0, 1), (1, 0)]


class Place:
    def __init__(self):
        self.np = lax.axis_size("p")
        self.p, self.x, self.y, self.c = (lax.axis_index(a) for a in ("p", "x", "y", "c"))
        self.quarter = 2 * self.x + self.c
        self.spot = jnp.stack([self.x, self.y, self.c]).astype(jnp.int32)

    def swap_core(self, value):
        return lax.ppermute(value, "c", SWAP)

    def swap_x(self, value):
        return lax.ppermute(value, "x", SWAP)

    def swap_both(self, value):
        return lax.ppermute(value, ("x", "c"), [(0, 3), (1, 2), (2, 1), (3, 0)])

    def swap_y(self, value):
        return lax.ppermute(value, "y", SWAP)

    def shift_p(self, value, by):
        return lax.ppermute(value, "p", [(p, p + by) for p in range(self.np) if 0 <= p + by < self.np])

    def turn_p(self, value, by):
        return lax.ppermute(value, "p", [(p, (p + by) % self.np) for p in range(self.np)])

    def gather4(self, own):
        across = self.swap_x(own)
        return self.paired(own), self.paired(across)

    def paired(self, block):
        return jnp.concatenate([block, self.swap_core(block)], axis=0)

    def gather8(self, own, work=None):
        half = own.shape[0] // 2
        across, over = self.swap_x(own), self.swap_y(own)
        first = self.paired(own)
        done = None
        if work is not None:
            done = work(first)
            across, over = after(across, done[0]), after(over, done[0])
        far = jnp.concatenate([self.swap_y(across[:half]), self.swap_x(over[half:])])
        return (first, self.paired(across), self.paired(over), self.paired(far)), done

    def met(self, pair):
        rows = pair.shape[0] // 2
        return (pair[:rows].astype(F32) + self.swap_core(pair[rows:]).astype(F32)).astype(BF)

    def scatter4(self, second, first):
        met = self.met(second)
        across = self.swap_x(met)
        first = first(met)
        return first, self.swap_core(first[first.shape[0] // 2 :]), across

    def scatter8(self, second, third, fourth, first):
        far = self.met(fourth)
        half = far.shape[0] // 2
        by_x, by_y = self.swap_x(far[:half]), self.swap_y(far[half:])
        second, third = self.met(second), self.met(third)
        add = lambda u, v: (u.astype(F32) + v.astype(F32)).astype(BF)
        across = [self.swap_x(second[:half]), self.swap_x(add(second[half:], by_y))]
        over = [self.swap_y(add(third[:half], by_x)), self.swap_y(third[half:])]
        first = first(far)
        core = self.swap_core(first[first.shape[0] // 2 :])
        return first, core, jnp.concatenate(across), jnp.concatenate(over)

    def sum4(self, value, parts):
        def reordered(v, x, c):
            v = v.reshape(v.shape[0], parts, 2, 2, -1)
            if x:
                v = jnp.concatenate([v[:, :, 1:], v[:, :, :1]], axis=2)
            if c:
                v = jnp.concatenate([v[:, :, :, 1:], v[:, :, :, :1]], axis=3)
            return v.reshape(value.shape)

        core, across, both = self.swap_core(value), self.swap_x(value), self.swap_both(value)
        return value + reordered(core, 0, 1) + reordered(across, 1, 0) + reordered(both, 1, 1)


def pick(v, axis, index):
    return lax.dynamic_index_in_dim(v, index, axis, keepdims=False)


def after(value, *others):
    return lax.optimization_barrier((value,) + others)[0]


class Copies:
    def __init__(self, send_sem, recv_sem):
        self.sems, self.used, self.all = (send_sem, recv_sem), 0, []

    def remote(self, src, dst, device):
        k = self.used
        self.used += 1
        copy = pltpu.make_async_remote_copy(
            src_ref=src,
            dst_ref=dst,
            send_sem=self.sems[0].at[k],
            recv_sem=self.sems[1].at[k],
            device_id=device,
            device_id_type=pl.DeviceIdType.MESH,
        )
        copy.start()
        self.all.append(copy)
        return copy

    def finish(self):
        for copy in self.all:
            copy.wait_send()


def pack_kernel(count, width, offsets, turns, spot_ref, *refs):
    spot = [spot_ref[k] for k in range(3)]
    for out, turn in zip(refs[count:], turns):
        places = offsets(*[(s + t) % 2 for s, t in zip(spot, turn)])
        for w, ref in enumerate(refs[:count]):
            for k, place in enumerate(places):
                at = (w * len(places) + k) * width
                out[:, at : at + width] = ref[:, pl.ds(pl.multiple_of(place * width, HD), width)]


def pack(spot, weights, width, offsets, turns):
    rows = weights[0].shape[0]
    size = len(weights) * len(offsets(0, 0, 0)) * width
    if width % HD:
        outs = []
        for turn in turns:
            places = offsets(*[(spot[k] + turn[k]) % 2 for k in range(3)])
            cuts = [lax.dynamic_slice_in_dim(w, place * width, width, 1) for w in weights for place in places]
            outs.append(jnp.concatenate(cuts, axis=1))
        return outs
    whole = pl.BlockSpec(memory_space=pltpu.VMEM)
    return pl.pallas_call(
        functools.partial(pack_kernel, len(weights), width, offsets, turns),
        in_specs=[pl.BlockSpec(memory_space=pltpu.SMEM)] + [whole] * len(weights),
        out_specs=[whole] * len(turns),
        out_shape=[jax.ShapeDtypeStruct((rows, size), BF)] * len(turns),
        compiler_params=pltpu.CompilerParams(vmem_limit_bytes=VMEM_BYTES),
        name="pack_columns",
        cost_estimate=cost(3),
    )(spot, *weights)


TURNS8 = [(dx, dy, dc) for dy in range(2) for dx in range(2) for dc in range(2)]
TURNS4 = TURNS8[:4]


def start_kernel(groups, reach, *refs):
    qkv_pack, feed_packs, x_ref, o_ref = refs[0:4], (refs[4:12], refs[12:20]), refs[20], refs[21]
    w_ref, feed_ref, all_ref, o_all_ref, local_sem, send_sem, recv_sem = refs[22:]
    p, x, y, c = (lax.axis_index(a) for a in ("p", "x", "y", "c"))
    turned = lambda u, t: 1 - u if t else u
    group = [(p, turned(x, dx), turned(y, dy), turned(c, dc)) for dx, dy, dc in TURNS8]
    core, across, over = group[1], group[2], group[4]
    right, left = (lax.rem(p + 1, groups), x, y, c), (lax.rem(p + groups - 1, groups), x, y, c)
    rows, depth, hidden = x_ref.shape[0], qkv_pack[0].shape[0], feed_packs[0][0].shape[1]
    used = [0]

    def remote(src, dst, device):
        k = used[0]
        used[0] += 1
        copy = pltpu.make_async_remote_copy(
            src_ref=src,
            dst_ref=dst,
            send_sem=send_sem.at[k],
            recv_sem=recv_sem.at[k],
            device_id=device,
            device_id_type=pl.DeviceIdType.MESH,
        )
        copy.start()
        return copy

    def local(k, src, dst):
        copy = pltpu.make_async_copy(src, dst, local_sem.at[k])
        copy.start()
        return copy

    barrier = pltpu.get_barrier_semaphore()
    for device in group[1:] + [right, left]:
        pl.semaphore_signal(barrier, inc=1, device_id=device, device_id_type=pl.DeviceIdType.MESH)
    pl.semaphore_wait(barrier, 9)

    def at(ref, start, size):
        return ref.at[pl.ds(pl.multiple_of(start, 16), size)]

    def tokens(t, block):
        return all_ref.at[pl.ds((4 * t + block) * rows, rows)]

    def owned(q):
        return w_ref.at[lax.rem(p + 2 * groups - q, groups), :, y]

    slot = (4 * x + 2 * y + c) * depth
    mine = [
        w_ref.at[p, x, y, pl.ds(pl.multiple_of(c * depth, 16), depth)],
        feed_ref.at[pl.ds(pl.multiple_of(slot, 16), depth), pl.ds(0, hidden)],
        feed_ref.at[pl.ds(pl.multiple_of(slot, 16), depth), pl.ds(hidden, hidden)],
    ]
    firsts = (qkv_pack[0], feed_packs[0][0], feed_packs[1][0])
    kept = [local(k, firsts[k], mine[k]) for k in range(3)] + [local(3, x_ref, tokens(0, 0))]
    kept.append(local(4, o_ref, o_all_ref.at[p]))
    o_of = lambda q: o_all_ref.at[lax.rem(p + 2 * groups - q, groups)]
    regrouped = [remote(qkv_pack[d], mine[0], group[d]) for d in (1, 2, 3)]
    moves = [remote(x_ref, tokens(1, 0), right)]
    sent = list(regrouped) + moves
    kept[0].wait()
    for copy in regrouped:
        copy.wait_recv()
    along = remote(owned(0), owned(0), right)
    o_along = remote(o_ref, o_of(0), right)
    sent.append(o_along)
    later = [remote(owned(0), owned(0), over)]
    spread = [(remote(x_ref, tokens(0, 1), core), remote(x_ref, tokens(0, 2), across))]
    for k in (1, 2):
        later += [remote(feed_packs[k - 1][d], mine[k], group[d]) for d in range(1, 8)]
    sent.append(along)
    step = 1
    ready = 0

    def pass_on(t):
        spread[t][1].wait_recv()
        later.append(remote(tokens(t, 2), tokens(t, 3), core))

    while step < groups or ready <= reach:
        if ready < reach:
            moves[ready].wait_recv()
            if ready + 1 < reach:
                moves.append(remote(tokens(ready + 1, 0), tokens(ready + 2, 0), right))
                sent.append(moves[-1])
            spread.append(
                (
                    remote(tokens(ready + 1, 0), tokens(ready + 1, 1), core),
                    remote(tokens(ready + 1, 0), tokens(ready + 1, 2), across),
                )
            )
        if step < groups:
            along.wait_recv()
            if step < groups - 1:
                along = remote(owned(step), owned(step), right)
                sent.append(along)
            later.append(remote(owned(step), owned(step), over))
            o_along.wait_recv()
            if step < groups - 1:
                o_along = remote(o_of(step), o_of(step), right)
                sent.append(o_along)
            step += 1
        if ready <= reach:
            pass_on(ready)
            ready += 1
    for near, far in spread:
        near.wait_recv()
        sent += [near, far]
    for copy in later:
        copy.wait_recv()
    for copy in sent + later:
        copy.wait_send()
    for copy in kept[1:]:
        copy.wait()


def start(groups, reach, qkv_pack, gate_pack, up_pack, own_inputs, own_o):
    depth, size = qkv_pack[0].shape
    rows, width = own_inputs.shape
    hidden = gate_pack[0].shape[1]
    copies = 3 + 1 + 1 + 1 + 14 + (groups - 1) + (groups - 2) + (groups - 1) + (reach - 1) + 2 * (reach + 1) + (reach + 1)
    anywhere = pl.BlockSpec(memory_space=pl.ANY)
    weight, feed, inputs, o_all = pl.pallas_call(
        functools.partial(start_kernel, groups, reach),
        in_specs=[anywhere] * 22,
        out_specs=[anywhere] * 4,
        out_shape=[
            jax.ShapeDtypeStruct((groups, 2, 2, 2 * depth, size), BF),
            jax.ShapeDtypeStruct((8 * depth, 2 * hidden), BF),
            jax.ShapeDtypeStruct((4 * (reach + 1) * rows, width), BF),
            jax.ShapeDtypeStruct((groups,) + own_o.shape, BF),
        ],
        scratch_shapes=[
            pltpu.SemaphoreType.DMA((5,)),
            pltpu.SemaphoreType.DMA((copies,)),
            pltpu.SemaphoreType.DMA((copies,)),
        ],
        compiler_params=pltpu.CompilerParams(collective_id=0, has_side_effects=True),
        name="start",
        cost_estimate=cost(120),
    )(*qkv_pack, *gate_pack, *up_pack, own_inputs, own_o)
    return weight.reshape(-1, size), feed, inputs, o_all.reshape(-1, width)


def gate_up_kernel(x_ref, gate_w_ref, up_w_ref, narrow_ref, maps_ref, gate_ref, up_ref, gated_ref):
    rank, tile = maps_ref.shape[1:]
    gate_w, up_w = gate_w_ref[...].reshape(-1, tile), up_w_ref[...].reshape(-1, tile)
    gate = dot(x_ref[...], gate_w) + SCALE_ADAPT * dot(narrow_ref[:, :rank], maps_ref[0])
    up = dot(x_ref[...], up_w) + SCALE_ADAPT * dot(narrow_ref[:, rank:], maps_ref[1])
    gate_ref[...] = gate.astype(BF)
    up_ref[...] = up.astype(BF)
    gated_ref[...] = (gate * jax.nn.sigmoid(gate) * up).astype(BF)


def gate_up(x, weight, narrow, maps):
    rows, width = x.shape
    groups = weight.shape[0]
    hidden = weight.shape[2] // 2
    tile = 256
    steps = hidden // tile
    out = pl.BlockSpec((rows, tile), lambda s: (0, s))
    return pl.pallas_call(
        gate_up_kernel,
        grid=(steps,),
        in_specs=[
            pl.BlockSpec((rows, width), lambda s: (0, 0)),
            pl.BlockSpec((groups, width // groups, tile), lambda s: (0, 0, s)),
            pl.BlockSpec((groups, width // groups, tile), lambda s: (0, 0, s + steps)),
            pl.BlockSpec(narrow.shape, lambda s: (0, 0)),
            pl.BlockSpec(maps.shape[:2] + (tile,), lambda s: (0, 0, s)),
        ],
        out_specs=[out] * 3,
        out_shape=[jax.ShapeDtypeStruct((rows, hidden), BF)] * 3,
        compiler_params=pltpu.CompilerParams(vmem_limit_bytes=VMEM_BYTES),
        name="gate_up",
        cost_estimate=cost(1),
    )(x, weight, weight, narrow, maps)


def project_kernel(heads, own_tiles, x_ref, w_ref, in_maps_ref, out_maps_ref, *out_refs):
    pre_q_ref, pre_k_ref, value_ref, narrow_ref, square_q_ref, square_k_ref = out_refs
    width = heads * HD
    rank = out_maps_ref.shape[1]
    narrow_ref[...] = dot_nt(x_ref[...], in_maps_ref[...]).astype(BF)

    def part(k):
        cols = slice(k * width, (k + 1) * width)
        return dot(x_ref[...], w_ref[:, cols]) + SCALE_ADAPT * dot(narrow_ref[:, k * rank : (k + 1) * rank], out_maps_ref[k])

    ones = jnp.ones((8, width), BF)
    key = part(1)
    pre_k_ref[...] = key
    square_k_ref[...] = dot_nt(ones, (key * key).astype(BF))
    value_ref[...] = part(2).astype(BF)

    @pl.when(pl.program_id(0) < own_tiles)
    def _():
        query = part(0)
        pre_q_ref[...] = query
        square_q_ref[...] = dot_nt(ones, (query * query).astype(BF))


def project(x, own_rows, weight, in_maps, out_maps, heads):
    rows, width = x.shape
    local = heads * HD
    tile = 512
    own_tiles = own_rows // tile
    fixed = lambda v: pl.BlockSpec(v.shape, lambda t: (0,) * v.ndim)
    row = lambda n: pl.BlockSpec((tile, n), lambda t: (t, 0))
    return pl.pallas_call(
        functools.partial(project_kernel, heads, own_tiles),
        grid=(rows // tile,),
        in_specs=[row(width), fixed(weight), fixed(in_maps), fixed(out_maps)],
        out_specs=[
            pl.BlockSpec((tile, local), lambda t: (jnp.minimum(t, own_tiles - 1), 0)),
            row(local),
            row(local),
            row(in_maps.shape[0]),
            pl.BlockSpec((8, tile), lambda t: (0, jnp.minimum(t, own_tiles - 1))),
            pl.BlockSpec((8, tile), lambda t: (0, t)),
        ],
        out_shape=[
            jax.ShapeDtypeStruct((own_rows, local), F32),
            jax.ShapeDtypeStruct((rows, local), F32),
            jax.ShapeDtypeStruct((rows, local), BF),
            jax.ShapeDtypeStruct((rows, in_maps.shape[0]), BF),
            jax.ShapeDtypeStruct((8, own_rows), F32),
            jax.ShapeDtypeStruct((8, rows), F32),
        ],
        compiler_params=pltpu.CompilerParams(vmem_limit_bytes=VMEM_BYTES),
        name="project",
        cost_estimate=cost(1),
    )(x, weight, in_maps, out_maps)


def post_kernel(heads, own_tiles, q_ref, k_ref, inv_q_ref, inv_k_ref, gain_ref, cos_ref, sin_ref, q_out, k_out):
    width = heads * HD
    cos, sin = cos_ref[...], sin_ref[...]

    def turn(pre_ref, inv, part, out_ref):
        for h in range(heads):
            cols = slice(h * HD, (h + 1) * HD)
            v = pre_ref[:, cols] * inv * gain_ref[:, part * width + h * HD : part * width + (h + 1) * HD]
            out_ref[:, cols] = (v * cos + pltpu.roll(v, HD // 2, 1) * sin).astype(BF)

    turn(k_ref, inv_k_ref[...], 1, k_out)

    @pl.when(pl.program_id(0) < own_tiles)
    def _():
        turn(q_ref, inv_q_ref[...], 0, q_out)


def post(pre_q, pre_k, inv_q, inv_k, gain, cos, sin, heads):
    rows, width = pre_k.shape
    tile = 256
    own_tiles = pre_q.shape[0] // tile
    row = lambda n: pl.BlockSpec((tile, n), lambda r: (r, 0))
    own = lambda n: pl.BlockSpec((tile, n), lambda r: (jnp.minimum(r, own_tiles - 1), 0))
    return pl.pallas_call(
        functools.partial(post_kernel, heads, own_tiles),
        grid=(rows // tile,),
        in_specs=[
            own(width),
            row(width),
            own(1),
            row(1),
            pl.BlockSpec((1, 2 * width), lambda r: (0, 0)),
            row(HD),
            row(HD),
        ],
        out_specs=[own(width), row(width)],
        out_shape=[jax.ShapeDtypeStruct(pre_q.shape, BF), jax.ShapeDtypeStruct(pre_k.shape, BF)],
        name="rope_forward",
        cost_estimate=cost(1),
    )(pre_q, pre_k, inv_q, inv_k, gain, cos, sin)


def unpost_kernel(heads, dq_ref, dk_ref, pre_q_ref, pre_k_ref, gain_ref, cos_ref, sin_ref, turn_ref, inner_ref):
    width = heads * HD
    cos, sin = cos_ref[...], sin_ref[...]
    for part, (d_ref, pre_ref) in enumerate(((dq_ref, pre_q_ref), (dk_ref, pre_k_ref))):
        total = None
        for h in range(heads):
            cols = slice(part * width + h * HD, part * width + (h + 1) * HD)
            v = d_ref[:, h * HD : (h + 1) * HD]
            turned = (v * cos - pltpu.roll(v, HD // 2, 1) * sin) * gain_ref[:, cols]
            turn_ref[:, cols] = turned
            inner = jnp.sum(turned * pre_ref[:, h * HD : (h + 1) * HD], axis=1, keepdims=True)
            total = inner if total is None else total + inner
        inner_ref[:, part : part + 1] = total


def unpost(dq, dk, pre_q, pre_k, gain, cos, sin, heads):
    rows, width = dq.shape
    tile = 256
    row = lambda n: pl.BlockSpec((tile, n), lambda r: (r, 0))
    return pl.pallas_call(
        functools.partial(unpost_kernel, heads),
        grid=(rows // tile,),
        in_specs=[row(width)] * 4 + [pl.BlockSpec((1, 2 * width), lambda r: (0, 0)), row(HD), row(HD)],
        out_specs=[row(2 * width), row(2)],
        out_shape=[jax.ShapeDtypeStruct((rows, 2 * width), F32), jax.ShapeDtypeStruct((rows, 2), F32)],
        name="rope_backward",
        cost_estimate=cost(8),
    )(dq, dk, pre_q, pre_k, gain, cos, sin)


def finish_kernel(groups, heads, early_rows, *refs):
    (
        dq_ref,
        dk_ref,
        dv_ref,
        pre_q_ref,
        pre_k_ref,
        inv_q_ref,
        inv_k_ref,
        gain_ref,
        cos_ref,
        sin_ref,
        in_maps_ref,
        out_maps_ref,
        narrow_ref,
        early_ref,
        wide_ref,
        weight_any,
        inputs_any,
        mid_any,
    ) = refs[:18]
    out_ref, sums_ref, wide_out_ref = refs[18:21]
    (
        weight,
        inputs,
        mid,
        turn,
        grad,
        back,
        stat,
        stat_in,
        far,
        near,
        core_in,
        met,
        across_in,
        near_in,
        maps,
        maps_in,
        by_x,
        by_y,
        by_y_in,
        by_p_in,
        own_sum,
        own_sum_in,
        wide_in,
        local_sem,
        send_sem,
        recv_sem,
    ) = refs[21:]
    p, x, y, c = (lax.axis_index(a) for a in ("p", "x", "y", "c"))
    core, across, both, over = (p, x, y, 1 - c), (p, 1 - x, y, c), (p, 1 - x, y, 1 - c), (p, x, 1 - y, c)
    others = [lax.rem(p + s, groups) for s in range(1, groups)]
    width = heads * HD
    rows = out_ref.shape[0]
    model = out_ref.shape[1]
    rank = out_maps_ref.shape[1]
    copies = Copies(send_sem, recv_sem)
    loads = []
    for k, (src, dst) in enumerate(((weight_any, weight), (inputs_any.at[pl.ds(0, 4 * mid.shape[0])], inputs), (mid_any, mid))):
        loads.append(pltpu.make_async_copy(src, dst, local_sem.at[k]))
        loads[-1].start()

    barrier = pltpu.get_barrier_semaphore()
    for device in [core, across, both, over] + [(q, x, y, c) for q in others]:
        pl.semaphore_signal(barrier, inc=1, device_id=device, device_id_type=pl.DeviceIdType.MESH)

    ones = jnp.ones((8, HD), BF)

    def unturn(b, carry):
        here = pl.ds(pl.multiple_of(b * rows, rows), rows)
        cos, sin = cos_ref[here, :], sin_ref[here, :]
        for part, pre_ref in enumerate((pre_q_ref, pre_k_ref)):
            product = None
            for h in range(heads):
                cols = slice(h * HD, (h + 1) * HD)
                wide_cols = slice(part * width + h * HD, part * width + (h + 1) * HD)
                v = dq_ref[here, cols] if part == 0 else dk_ref[here, cols]
                turned = (v * cos - pltpu.roll(v, HD // 2, 1) * sin) * gain_ref[:, wide_cols]
                turn[here, wide_cols] = turned
                term = turned * pre_ref[here, cols]
                product = term if product is None else product + term
            high = product.astype(BF)
            low = (product - high.astype(F32)).astype(BF)
            summed = dot_nt(ones, high) + dot_nt(ones, low)
            stat[part : part + 1, here] = summed[:1, :]
        grad[here, 2 * width :] = dv_ref[here, :].astype(BF)
        return carry

    stat[...] = jnp.zeros_like(stat)
    lax.fori_loop(0, 4, unturn, 0)
    for b in range(2 * groups):
        maps[b, :early_rows, :] = early_ref[:, b * 256 : (b + 1) * 256]
    pl.semaphore_wait(barrier, 3 + groups)
    stats = [copies.remote(stat, stat_in.at[k], device) for k, device in enumerate((core, across, both))]
    early = pl.ds(0, early_rows)
    exchanged = [copies.remote(maps.at[2 * q + 1 - x, early], maps_in.at[q, early], across) for q in range(groups)]
    wides = [
        copies.remote(wide_ref.at[:, pl.ds(pl.multiple_of(q * 256, 256), 256)], wide_in.at[k], (q, x, y, c))
        for k, q in enumerate(others)
    ]
    for copy in stats:
        copy.wait_recv()

    for b in range(4):
        here = slice(b * rows, (b + 1) * rows)
        total_row = stat[:, here]
        for k in range(3):
            d = b ^ (k + 1)
            total_row = total_row + stat_in[k, :, d * rows : (d + 1) * rows]
        inner = total_row.T / model
        for part, (pre_ref, inv_ref) in enumerate(((pre_q_ref, inv_q_ref), (pre_k_ref, inv_k_ref))):
            cols = slice(part * width, (part + 1) * width)
            inv = inv_ref[here, :]
            scale = inv * inv * inv * inner[:, part : part + 1]
            grad[here, cols] = (inv * turn[here, cols] - pre_ref[here, :] * scale).astype(BF)

    loads[0].wait()

    def into(start, dst):
        here = slice(start, start + 2 * rows)
        for k in range(3):
            part = dot_nt(grad[here, k * width : (k + 1) * width], out_maps_ref[k])
            back[here, k * rank : (k + 1) * rank] = part.astype(BF)

        def columns(n, carry):
            cols = pl.ds(pl.multiple_of(n * 512, 512), 512)
            full = dot_nt(grad[here, :], weight[cols, :]) + SCALE_ADAPT * dot(back[here, :], in_maps_ref[:, cols])
            dst[:, cols] = full.astype(BF)
            return carry

        lax.fori_loop(0, model // 512, columns, 0)

    into(2 * rows, far)
    far_copy = copies.remote(far.at[pl.ds(rows, rows)], core_in, core)
    far_copy.wait_recv()
    met[...] = (far[:rows, :].astype(F32) + core_in[...].astype(F32)).astype(BF)
    across_copy = copies.remote(met, across_in, across)
    into(0, near)
    near_copy = copies.remote(near.at[pl.ds(rows, rows)], near_in, core)

    loads[1].wait()
    late = early_rows + 3 * rank
    for b in range(2 * groups):
        cols = slice(b * 256, (b + 1) * 256)
        maps[b, early_rows:late, :] = SCALE_ADAPT * dot_tn(back[...], inputs[:, cols])
    send_late = pl.ds(early_rows, 3 * rank)
    exchanged += [
        copies.remote(maps.at[2 * q + 1 - x, send_late], maps_in.at[q, send_late], across) for q in range(groups)
    ]
    for q in range(groups):
        by_x[q, late:, :] = jnp.zeros_like(by_x[q, late:, :])
    for k in range(3):
        own = SCALE_ADAPT * dot_tn(narrow_ref[:, k * rank : (k + 1) * rank], grad[:, k * width : (k + 1) * width])
        here = slice(late + k * rank, late + (k + 1) * rank)
        for q in range(groups):
            by_x[q, here, pl.ds(pl.multiple_of(c * HD, HD), HD)] = own[:, q * HD : (q + 1) * HD]
    for copy in exchanged:
        copy.wait_recv()
    for q in range(groups):
        by_x[q, :late, :] = maps[2 * q + x, :late, :] + maps_in[q]
    halves = lambda ref, q, side: ref.at[q, :, pl.ds(pl.multiple_of(side * HD, HD), HD)]
    exchanged = [copies.remote(halves(by_x, q, 1 - y), by_y_in.at[q], over) for q in range(groups)]
    for q, copy in enumerate(exchanged):
        copy.wait_recv()
        by_y[q] = by_x[q, :, pl.ds(pl.multiple_of(y * HD, HD), HD)] + by_y_in[q]
    exchanged = [copies.remote(by_y.at[q], by_p_in.at[k], (q, x, y, c)) for k, q in enumerate(others)]
    summed = by_y[p]
    wide_sum = wide_ref[:, pl.ds(pl.multiple_of(p * 256, 256), 256)]
    for k, copy in enumerate(exchanged):
        copy.wait_recv()
        summed = summed + by_p_in[k]
    own_sum[...] = summed
    last = copies.remote(own_sum, own_sum_in, core)
    for k, copy in enumerate(wides):
        copy.wait_recv()
        wide_sum = wide_sum + wide_in[k]
    wide_out_ref[...] = wide_sum
    last.wait_recv()
    summed = summed + own_sum_in[...]
    sums_ref[...] = jnp.where(c == 0, summed[:, : HD // 2], summed[:, HD // 2 :])

    loads[2].wait()
    near_copy.wait_recv()
    across_copy.wait_recv()
    out_ref[...] = (
        mid[...]
        + near[:rows, :].astype(F32)
        + near_in[...].astype(F32)
        + across_in[...].astype(F32)
    )
    copies.finish()


def finish(groups, heads, args, weight, inputs, mid):
    own, width = args[0].shape
    rows, model = mid.shape
    rank = args[11].shape[1]
    early_rows, wide_rows = args[13].shape[0], args[14].shape[0]
    total_rows = early_rows + 6 * rank
    late = early_rows + 3 * rank
    vm = pl.BlockSpec(memory_space=pltpu.VMEM)
    anywhere = pl.BlockSpec(memory_space=pl.ANY)
    count = 3 + groups + (groups - 1) + 3 + 2 * groups + (groups - 1) + 1
    block = lambda *shape: pltpu.VMEM(shape, BF)
    full = lambda *shape: pltpu.VMEM(shape, F32)
    first_rows = lambda v: vm if v.shape[0] <= own else pl.BlockSpec(
        (own, v.shape[1]), lambda k: (0, 0), pipeline_mode=pl.Buffered(1)
    )
    return pl.pallas_call(
        functools.partial(finish_kernel, groups, heads, early_rows),
        grid=(1,),
        in_specs=[first_rows(v) for v in args] + [anywhere] * 3,
        out_specs=[vm] * 3,
        out_shape=[
            jax.ShapeDtypeStruct((rows, model), F32),
            jax.ShapeDtypeStruct((total_rows, HD // 2), F32),
            jax.ShapeDtypeStruct((wide_rows, 256), F32),
        ],
        scratch_shapes=[
            pltpu.VMEM(weight.shape, BF),
            pltpu.VMEM((own, model), BF),
            pltpu.VMEM(mid.shape, F32),
            full(own, 2 * width),
            block(own, 3 * width),
            block(own, 3 * rank),
            full(8, own),
            full(3, 8, own),
            block(2 * rows, model),
            block(2 * rows, model),
            block(rows, model),
            block(rows, model),
            block(rows, model),
            block(rows, model),
            full(2 * groups, late, 256),
            full(groups, late, 256),
            full(groups, total_rows, 256),
            full(groups, total_rows, HD),
            full(groups, total_rows, HD),
            full(groups - 1, total_rows, HD),
            full(total_rows, HD),
            full(total_rows, HD),
            full(groups - 1, wide_rows, 256),
            pltpu.SemaphoreType.DMA((3,)),
            pltpu.SemaphoreType.DMA((count,)),
            pltpu.SemaphoreType.DMA((count,)),
        ],
        compiler_params=pltpu.CompilerParams(
            collective_id=1, has_side_effects=True, vmem_limit_bytes=VMEM_BYTES
        ),
        name="finish",
        cost_estimate=cost(60),
    )(*args, weight, inputs, mid)


NEG_FILL = -1e30


def attend_kernel(count, scale, q_ref, *refs):
    ks, vs = refs[:count], refs[count : 2 * count]
    lo_ref, pos_ref, key_ref, o_ref, log_ref = refs[2 * count :]
    rows = q_ref.shape[0] * q_ref.shape[2]
    q = q_ref[...].reshape(rows, HD)
    lo, pos = lo_ref[0], pos_ref[...]
    scores = []
    for t in range(count):
        s = dot_nt(q, ks[t][...].reshape(rows, HD)) * scale
        key = key_ref[t : t + 1, :]
        scores.append(jnp.where((key >= lo) & (key <= pos), s, NEG_FILL))
    top = functools.reduce(jnp.maximum, [jnp.max(s, axis=1, keepdims=True) for s in scores])
    powers = [jnp.exp(s - top) for s in scores]
    total = sum(jnp.sum(e, axis=1, keepdims=True) for e in powers)
    share = 1.0 / total
    out = sum(dot((e * share).astype(BF), vs[t][...].reshape(rows, HD)) for t, e in enumerate(powers))
    o_ref[...] = out.astype(BF).reshape(o_ref.shape)
    log_ref[0] = top + jnp.log(total)


def attend_back_kernel(groups, reach, heads, scale, *refs):
    (
        grad_ref,
        weight_ref,
        in_maps_ref,
        out_maps_ref,
        lo_ref,
        pos_ref,
        key_ref,
        lo_rows_ref,
        query_rows_ref,
        log_ref,
        log_rows_ref,
        q_any,
        k_any,
        v_any,
        o_any,
    ) = refs[:15]
    later_any = refs[15]
    dq_ref, dk_ref, dv_ref, back_ref = refs[16:20]
    (
        q_buf,
        k_buf,
        v_buf,
        o_buf,
        later_buf,
        do_buf,
        do_in,
        inner,
        inner_in,
        load_sem,
        send_sem,
        recv_sem,
    ) = refs[20:]
    p, x, y, c = (lax.axis_index(a) for a in ("p", "x", "y", "c"))
    right, left = (lax.rem(p + 1, groups), x, y, c), (lax.rem(p + groups - 1, groups), x, y, c)
    rows = q_buf.shape[2]
    full = 2 * rows
    copies = Copies(send_sem, recv_sem)
    sources = [(q_any, q_buf), (k_any, k_buf), (v_any, v_buf), (o_any, o_buf)]
    sources.append((later_any, later_buf))
    loads = []
    for n, (src, dst) in enumerate(sources):
        loads.append(pltpu.make_async_copy(src, dst, load_sem.at[n]))
        loads[-1].start()
    barrier = pltpu.get_barrier_semaphore()
    for device in (left, right):
        pl.semaphore_signal(barrier, inc=1, device_id=device, device_id_type=pl.DeviceIdType.MESH)

    for b in range(2):
        here = slice(b * full, (b + 1) * full)
        low = dot_nt(grad_ref[here, :], out_maps_ref[...]).astype(BF)
        back_ref[here, :] = low
        value = dot_nt(grad_ref[here, :], weight_ref[...]) + SCALE_ADAPT * dot(low, in_maps_ref[...])
        do_buf[b] = value.astype(BF).reshape(2, rows, heads * HD)
    pl.semaphore_wait(barrier, 2)
    moves = [copies.remote(do_buf, do_in.at[0], left)]
    for load in loads:
        load.wait()

    def piece(ref, s, cols, first=0):
        return ref[first : first + 2, s, :, cols].reshape(full, HD)

    def put(ref, s, cols, value):
        ref[:, s, :, cols] = value.reshape(2, rows, HD)

    ones = jnp.ones((8, HD), BF)

    def sums(n, carry):
        s, cols = n // heads, pl.ds(pl.multiple_of(n % heads * HD, HD), HD)
        product = piece(do_buf, s, cols).astype(F32) * piece(o_buf, s, cols).astype(F32)
        high = product.astype(BF)
        low = (product - high.astype(F32)).astype(BF)
        inner[pl.ds(n, 1), :] = (dot_nt(ones, high) + dot_nt(ones, low))[:1, :]
        return carry

    lax.fori_loop(0, 2 * heads, sums, 0)
    inner_moves = [copies.remote(inner, inner_in.at[0], left)]

    def own(n, carry):
        s, cols = n // heads, pl.ds(pl.multiple_of(n % heads * HD, HD), HD)
        q, do = piece(q_buf, s, cols), piece(do_buf, s, cols)
        delta = jnp.sum(do.astype(F32) * piece(o_buf, s, cols).astype(F32), axis=1, keepdims=True)
        lo, pos, log_total = lo_ref[s], pos_ref[...], log_ref[n]
        dq = None
        for t in range(reach + 1):
            k, v = piece(k_buf, s, cols, 2 * t), piece(v_buf, s, cols, 2 * t)
            key = key_ref[t : t + 1, :]
            score = dot_nt(q, k) * scale
            probs = jnp.where((key >= lo) & (key <= pos), jnp.exp(score - log_total), 0.0)
            ds = (probs * (dot_nt(do, v) - delta)).astype(BF)
            part = dot(ds, k)
            dq = part if dq is None else dq + part
            if t == 0:
                put(dv_ref, s, cols, dot_tn(probs.astype(BF), do))
                put(dk_ref, s, cols, dot_tn(ds, q) * scale)
        put(dq_ref, s, cols, dq * scale)
        return carry

    lax.fori_loop(0, 2 * heads, own, 0)

    for t in range(1, reach + 1):
        moves[-1].wait_recv()
        inner_moves[-1].wait_recv()
        if t < reach:
            moves.append(copies.remote(do_in.at[t - 1], do_in.at[t], left))
            inner_moves.append(copies.remote(inner_in.at[t - 1], inner_in.at[t], left))

        def from_later(n, carry, t=t):
            s, cols = n // heads, pl.ds(pl.multiple_of(n % heads * HD, HD), HD)
            k, v = piece(k_buf, s, cols), piece(v_buf, s, cols)
            q, do = piece(later_buf.at[t - 1], s, cols), piece(do_in.at[t - 1], s, cols)
            score = dot_nt(k, q) * scale
            key = pos_ref[...]
            lo, pos = lo_rows_ref[t, pl.ds(s, 1), :], query_rows_ref[t : t + 1, :]
            probs = jnp.where((key >= lo) & (key <= pos), jnp.exp(score - log_rows_ref[t - 1, pl.ds(n, 1), :]), 0.0)
            ds = (probs * (dot_nt(v, do) - inner_in[t - 1, pl.ds(n, 1), :])).astype(BF)
            put(dv_ref, s, cols, piece(dv_ref, s, cols) + dot(probs.astype(BF), do))
            put(dk_ref, s, cols, piece(dk_ref, s, cols) + dot(ds, q) * scale)
            return carry

        lax.fori_loop(0, 2 * heads, from_later, 0)
    copies.finish()


def attend_back(groups, reach, heads, rows, args, later):
    own = 4 * rows
    local = heads * HD
    vm = pl.BlockSpec(memory_space=pltpu.VMEM)
    anywhere = pl.BlockSpec(memory_space=pl.ANY)
    block = lambda n: pltpu.VMEM((2 * n, 2, rows, local), BF)
    view = lambda v: v.reshape(-1, 2, rows, local)
    count = 2 * reach
    dq, dk, dv, back = pl.pallas_call(
        functools.partial(attend_back_kernel, groups, reach, heads, HD**-0.5),
        in_specs=[vm] * 11 + [anywhere] * 5,
        out_specs=[vm] * 4,
        out_shape=[jax.ShapeDtypeStruct((2, 2, rows, local), F32)] * 3
        + [jax.ShapeDtypeStruct((own, args[2].shape[0]), BF)],
        scratch_shapes=[
            block(1),
            block(reach + 1),
            block(reach + 1),
            block(1),
            pltpu.VMEM((reach, 2, 2, rows, local), BF),
            block(1),
            pltpu.VMEM((reach, 2, 2, rows, local), BF),
            pltpu.VMEM((2 * heads, 2 * rows), F32),
            pltpu.VMEM((reach, 2 * heads, 2 * rows), F32),
            pltpu.SemaphoreType.DMA((5,)),
            pltpu.SemaphoreType.DMA((count,)),
            pltpu.SemaphoreType.DMA((count,)),
        ],
        compiler_params=pltpu.CompilerParams(
            collective_id=3, has_side_effects=True, vmem_limit_bytes=VMEM_BYTES
        ),
        name="attend_backward",
        cost_estimate=cost(70),
    )(*args[:11], *[view(v) for v in args[11:]], later.reshape(reach, 2, 2, rows, local))
    return [v.reshape(own, local) for v in (dq, dk, dv)], back


class Attention:
    def __init__(self, rows, heads, count, lo, pos, key):
        self.rows, self.heads, self.count = rows, heads, count
        self.tables = (lo, pos, key)
        full = 2 * rows
        self.block = pl.BlockSpec((2, 1, rows, HD), lambda s, h: (0, s, 0, h))
        self.part = lambda t: pl.BlockSpec((2, 1, rows, HD), lambda s, h: (t, s, 0, h))
        self.table_specs = lambda n: [
            pl.BlockSpec((1, full, 1), lambda s, h: (s, 0, 0)),
            pl.BlockSpec((full, 1), lambda s, h: (0, 0)),
            pl.BlockSpec((n, full), lambda s, h: (0, 0)),
        ]
        self.log_spec = pl.BlockSpec((1, full, 1), lambda s, h: (s * heads + h, 0, 0))
        self.params = pltpu.CompilerParams(vmem_limit_bytes=VMEM_BYTES)

    def shape(self, dtype):
        return jax.ShapeDtypeStruct((2, 2, self.rows, self.heads * HD), dtype)

    def view(self, v):
        return v.reshape(-1, 2, self.rows, v.shape[-1])

    def forward(self, q, key, value):
        count = self.count
        parts = [self.part(t) for t in range(count)]
        out, log = pl.pallas_call(
            functools.partial(attend_kernel, count, HD**-0.5),
            grid=(2, self.heads),
            in_specs=[self.block] + parts * 2 + self.table_specs(count),
            out_specs=[self.block, self.log_spec],
            out_shape=[self.shape(BF), jax.ShapeDtypeStruct((2 * self.heads, 2 * self.rows, 1), F32)],
            compiler_params=self.params,
            name="attend_forward",
            cost_estimate=cost(1),
        )(self.view(q), *[self.view(key)] * count, *[self.view(value)] * count, *self.tables)
        return out.reshape(q.shape), log


def rms_inverse(v):
    return lax.rsqrt(jnp.mean(v * v, axis=-1, keepdims=True) + EPS)


def rms_backward(v, gain, grad):
    inv = rms_inverse(v)
    turn = grad * gain
    inner = jnp.mean(v * turn, axis=-1, keepdims=True)
    return inv * turn - v * (inv * inv * inv) * inner


def total(refs):
    return sum(ref[...].astype(F32) for ref in refs)


def after_attention_kernel(*refs):
    inputs_ref, gain_ref, attn_ref, middle_ref, low_ref = refs[3:]
    attn = total(refs[:3])
    attn_ref[...] = attn
    middle = inputs_ref[...].astype(F32) + attn * rms_inverse(attn) * gain_ref[...]
    middle_ref[...] = middle
    low_ref[...] = middle.astype(BF)


def end_kernel(*refs):
    mid_ref, out_ref = refs[3:]
    out_ref[...] = mid_ref[...] + total(refs[:3])


def feed_kernel(*refs):
    (
        d_in_ref,
        d_out_ref,
        gu_out_ref,
        gu_in_ref,
        feed_gain_ref,
        attn_gain_ref,
        narrow_gu_ref,
        gated_any,
        gate_any,
        up_any,
        feed_any,
        down_any,
        middle_any,
        cot_any,
        attn_any,
        query_any,
        log_any,
    ) = refs[:17]
    result_ref, mid_ref, grad_attn_ref, back_gu_ref, maps_ref, gb_d_ref, later_any, later_log_any = refs[17:25]
    (
        down_w,
        gate_w,
        up_w,
        acts,
        blocks,
        own_pair,
        core_in,
        by_x,
        by_y,
        across_in,
        over_in,
        tokens,
        cot,
        dgu,
        narrow_d,
        back_d,
        load_sem,
        act_sem,
        free_sem,
        send_sem,
        recv_sem,
    ) = refs[25:]
    p, x, y, c = (lax.axis_index(a) for a in ("p", "x", "y", "c"))
    core, across, over = (p, x, y, 1 - c), (p, 1 - x, y, c), (p, x, 1 - y, c)
    rows, model = result_ref.shape
    pair = 2 * rows
    half = rows // 2
    hidden = down_w.shape[0]
    rank = d_in_ref.shape[0]
    copies = Copies(send_sem, recv_sem)

    def load(k, src, dst):
        copy = pltpu.make_async_copy(src, dst, load_sem.at[k])
        copy.start()
        return copy

    def load_acts(turn, kind, k):
        src = (gated_any, gate_any, up_any)[kind].at[pl.ds(k * pair, pair)]
        copy = pltpu.make_async_copy(src, acts.at[turn % 2, kind], act_sem.at[turn % 2, kind])
        copy.start()
        return copy

    first_order, back_order = (3, 1, 2, 0), (0, 1, 3, 2)
    groups = feed_any.shape[0]
    depth = model // groups
    reach = later_any.shape[0]
    loaded = load(0, down_any, down_w)
    gated_loads = [load_acts(0, 0, first_order[0]), load_acts(1, 0, first_order[1])]
    middle_load, cot_load = load(1, middle_any, tokens), load(2, cot_any, cot)
    feed_loads = []
    for k in range(groups):
        for n, dst in enumerate((gate_w, up_w)):
            src = feed_any.at[k, :, pl.ds(n * hidden, hidden)]
            feed_loads.append(load(4 + 2 * k + n, src, dst.at[pl.ds(k * depth, depth)]))
    ring = lax.axis_size("p")
    right, left = (lax.rem(p + 1, ring), x, y, c), (lax.rem(p + ring - 1, ring), x, y, c)
    barrier = pltpu.get_barrier_semaphore()
    for device in (core, across, over, right, left):
        pl.semaphore_signal(barrier, inc=1, device_id=device, device_id_type=pl.DeviceIdType.MESH)
    pl.semaphore_wait(barrier, 5)

    def pull(t):
        src = (query_any, log_any) if t == 0 else (later_any.at[t - 1], later_log_any.at[t - 1])
        return [copies.remote(src[0], later_any.at[t], left), copies.remote(src[1], later_log_any.at[t], left)]

    pulls = pull(0)
    maps_ref[...] = jnp.zeros_like(maps_ref)
    gb_d_ref[...] = jnp.zeros_like(gb_d_ref)

    def part(k):
        return own_pair if k == 0 else blocks.at[pl.ds(2 * k, 2)]

    def store(k, cols, value):
        dst = part(k)
        dst[0, :, cols] = value[:rows].astype(BF)
        dst[1, :, cols] = value[rows:].astype(BF)

    def columns(n):
        return pl.ds(pl.multiple_of(n * 512, 512), 512)

    def forward(k, slot):
        here = slice(k * pair, (k + 1) * pair)
        narrow_d[here, :] = dot_nt(acts[slot, 0], d_in_ref[...]).astype(BF)

        def body(n, carry):
            cols = columns(n)
            value = dot(acts[slot, 0], down_w[:, cols])
            store(k, cols, value + SCALE_ADAPT * dot(narrow_d[here, :], d_out_ref[:, cols]))
            return carry

        lax.fori_loop(0, model // 512, body, 0)

    def backward(k, slot):
        here = slice(k * pair, (k + 1) * pair)
        grad = blocks[2 * k : 2 * k + 2].reshape(pair, model)
        low_d = dot_nt(grad, d_out_ref[...]).astype(BF)
        back_d[here, :] = low_d
        gb_d_ref[...] += SCALE_ADAPT * dot_tn(narrow_d[here, :], grad)

        def tile(t, carry):
            cols = pl.ds(pl.multiple_of(t * 256, 256), 256)
            grad = blocks[2 * k : 2 * k + 2].reshape(pair, model)
            dm = dot_nt(grad, down_w[cols, :]) + SCALE_ADAPT * dot(low_d, d_in_ref[:, cols])
            gate, up = acts[slot, 1, :, cols].astype(F32), acts[slot, 2, :, cols].astype(F32)
            sig = jax.nn.sigmoid(gate)
            silu = gate * sig
            dgu[k, 0, :, cols] = (dm * up * (sig + silu * (1.0 - sig))).astype(BF)
            dgu[k, 1, :, cols] = (dm * silu).astype(BF)
            return carry

        lax.fori_loop(0, hidden // 256, tile, 0)
        back_gu_ref[here, :rank] = dot_nt(dgu[k, 0], gu_out_ref[0]).astype(BF)
        back_gu_ref[here, rank:] = dot_nt(dgu[k, 1], gu_out_ref[1]).astype(BF)

        def body(n, carry):
            cols = columns(n)
            value = dot_nt(dgu[k, 0], gate_w[cols, :]) + dot_nt(dgu[k, 1], up_w[cols, :])
            store(k, cols, value + SCALE_ADAPT * dot(back_gu_ref[here, :], gu_in_ref[:, cols]))
            return carry

        lax.fori_loop(0, model // 512, body, 0)

    def adapter_maps():
        turns = [load_acts(k, 0, k) for k in range(2)]
        for k in range(4):
            here = slice(k * pair, (k + 1) * pair)
            turns[k].wait()
            maps_ref[0] += SCALE_ADAPT * dot_tn(back_d[here, :], acts[k % 2, 0])
            if k < 2:
                turns.append(load_acts(k + 2, 0, k + 2))
            for n in range(2):
                narrow = narrow_gu_ref[here, n * rank : (n + 1) * rank]
                maps_ref[1 + n] += SCALE_ADAPT * dot_tn(narrow, dgu[k, n])

    def to_core(k):
        return copies.remote(part(k).at[1], core_in.at[k], core)

    def by_tiles(size, work):
        def body(n, carry):
            work(pl.ds(pl.multiple_of(n * 64, 64), 64))
            return carry

        lax.fori_loop(0, size // 64, body, 0)

    def meet(k, copy):
        copy.wait_recv()

        def work(tile):
            blocks[2 * k, tile, :] = (blocks[2 * k, tile, :].astype(F32) + core_in[k, tile, :].astype(F32)).astype(BF)

        by_tiles(rows, work)

    top, low = pl.ds(0, half), pl.ds(half, half)

    def add(block, start, more):
        def work(tile):
            here = pl.ds(tile.start + start, tile.size)
            blocks[block, here, :] = (blocks[block, here, :].astype(F32) + more[tile, :].astype(F32)).astype(BF)

        by_tiles(half, work)

    def far_halves():
        return (
            copies.remote(blocks.at[6, top], by_x, across),
            copies.remote(blocks.at[6, low], by_y, over),
        )

    def send_top_across():
        return copies.remote(blocks.at[2, top], across_in.at[top], across)

    def finish_sum(far, own, parts):
        far_x, far_y = far
        parts.append(copies.remote(blocks.at[4, low], over_in.at[low], over))
        far_y.wait_recv()
        add(2, half, by_y)
        parts.append(copies.remote(blocks.at[2, low], across_in.at[low], across))
        far_x.wait_recv()
        add(4, 0, by_x)
        parts.append(copies.remote(blocks.at[4, top], over_in.at[top], over))
        own.wait_recv()
        for copy in parts:
            copy.wait_recv()

    def summed(tile):
        total = own_pair[0, tile, :].astype(F32) + core_in[0, tile, :].astype(F32)
        return total + across_in[tile, :].astype(F32) + over_in[tile, :].astype(F32)

    loaded.wait()
    gated_loads[0].wait()
    forward(3, 0)
    sent = to_core(3)
    gated_loads.append(load_acts(2, 0, first_order[2]))
    gated_loads[1].wait()
    forward(1, 1)
    sent1 = to_core(1)
    meet(3, sent)
    far = far_halves()
    gated_loads.append(load_acts(3, 0, first_order[3]))
    gated_loads[2].wait()
    forward(2, 0)
    sent2 = to_core(2)
    meet(1, sent1)
    parts = [send_top_across()]
    gated_loads[3].wait()
    forward(0, 1)
    own = to_core(0)
    meet(2, sent2)
    act_loads = [[load_acts(0, kind, 0) for kind in range(3)], [load_acts(1, kind, 1) for kind in range(3)]]
    finish_sum(far, own, parts)
    copies.finish()
    for device in (core, across, over):
        pl.semaphore_signal(free_sem, inc=1, device_id=device, device_id_type=pl.DeviceIdType.MESH)
    middle_load.wait()
    cot_load.wait()

    def close(tile):
        feed, gain = summed(tile), feed_gain_ref[...]
        result_ref[tile, :] = (tokens[tile, :] + feed * rms_inverse(feed) * gain).astype(BF)
        blocks[0, tile, :] = rms_backward(feed, gain, cot[tile, :].astype(F32)).astype(BF)

    by_tiles(rows, close)

    pl.semaphore_wait(free_sem, 3)
    copies.all = []
    to_x = copies.remote(blocks.at[0], blocks.at[2], across)
    to_y = copies.remote(blocks.at[0], blocks.at[4], over)
    to_c = copies.remote(blocks.at[0], blocks.at[1], core)
    attn_load = load(3, attn_any, tokens)
    for copy in feed_loads:
        copy.wait()
    to_c.wait_recv()
    for copy in act_loads[0]:
        copy.wait()
    backward(0, 0)
    own = to_core(0)
    act_loads.append([load_acts(2, kind, 3) for kind in range(3)])
    for t in range(1, reach):
        for copy in pulls:
            copy.wait_recv()
        pulls = pull(t)
    to_x.wait_recv()
    x_on = [copies.remote(blocks.at[2], blocks.at[3], core), copies.remote(blocks.at[2, top], blocks.at[6, top], over)]
    to_y.wait_recv()
    y_on = [copies.remote(blocks.at[4], blocks.at[5], core), copies.remote(blocks.at[4, low], blocks.at[6, low], across)]
    x_on[0].wait_recv()
    for copy in act_loads[1]:
        copy.wait()
    for copy in x_on:
        copy.wait_send()
    backward(1, 1)
    sent1 = to_core(1)
    act_loads.append([load_acts(3, kind, 2) for kind in range(3)])
    x_on[1].wait_recv()
    y_on[1].wait_recv()
    far_on = copies.remote(blocks.at[6], blocks.at[7], core)
    meet(1, sent1)
    parts = [send_top_across()]
    far_on.wait_recv()
    for copy in act_loads[2]:
        copy.wait()
    far_on.wait_send()
    backward(3, 0)
    sent = to_core(3)
    meet(3, sent)
    far = far_halves()
    y_on[0].wait_recv()
    for copy in act_loads[3]:
        copy.wait()
    for copy in y_on:
        copy.wait_send()
    backward(2, 1)
    sent2 = to_core(2)
    meet(2, sent2)
    finish_sum(far, own, parts)
    attn_load.wait()

    def open_attention(tile):
        mid = cot[tile, :].astype(F32) + summed(tile)
        mid_ref[tile, :] = mid
        grad_attn_ref[tile, :] = rms_backward(tokens[tile, :], attn_gain_ref[...], mid).astype(BF)

    by_tiles(rows, open_attention)

    def block(k):
        return grad_attn_ref.at[pl.ds(k * rows, rows)]

    to_x = copies.remote(block(0), block(2), across)
    to_c = copies.remote(block(0), block(1), core)
    to_x.wait_recv()
    on = copies.remote(block(2), block(3), core)
    adapter_maps()
    to_c.wait_recv()
    on.wait_recv()
    for copy in pulls:
        copy.wait_recv()
    done = (*x_on, far_on, *y_on)
    for copy in copies.all:
        if not any(copy is other for other in done):
            copy.wait_send()


def feed_layer(maps, narrow_gu, acts, weights, middle, cot, attn_out, query, log, reach):
    rows, model = cot.shape
    groups, hidden = weights[0].shape[0], weights[1].shape[0]
    rank = maps[0].shape[0]
    vm = pl.BlockSpec(memory_space=pltpu.VMEM)
    anywhere = pl.BlockSpec(memory_space=pl.ANY)
    block = lambda *shape: pltpu.VMEM(shape, BF)
    count = 48 + 2 * reach
    return pl.pallas_call(
        feed_kernel,
        in_specs=[vm] * 7 + [anywhere] * 10,
        out_specs=[vm] * 6 + [anywhere] * 2,
        out_shape=[
            jax.ShapeDtypeStruct((rows, model), BF),
            jax.ShapeDtypeStruct((rows, model), F32),
            jax.ShapeDtypeStruct((4 * rows, model), BF),
            jax.ShapeDtypeStruct((8 * rows, 2 * rank), BF),
            jax.ShapeDtypeStruct((3, rank, hidden), F32),
            jax.ShapeDtypeStruct((rank, model), F32),
            jax.ShapeDtypeStruct((reach,) + query.shape, BF),
            jax.ShapeDtypeStruct((reach,) + log.shape, F32),
        ],
        scratch_shapes=[
            block(hidden, model),
            block(model, hidden),
            block(model, hidden),
            block(2, 3, 2 * rows, hidden),
            block(8, rows, model),
            block(2, rows, model),
            block(4, rows, model),
            block(rows // 2, model),
            block(rows // 2, model),
            block(rows, model),
            block(rows, model),
            pltpu.VMEM((rows, model), F32),
            block(rows, model),
            block(4, 2, 2 * rows, hidden),
            block(8 * rows, rank),
            block(8 * rows, rank),
            pltpu.SemaphoreType.DMA((2 * groups + 4,)),
            pltpu.SemaphoreType.DMA((2, 3)),
            pltpu.SemaphoreType.REGULAR,
            pltpu.SemaphoreType.DMA((count,)),
            pltpu.SemaphoreType.DMA((count,)),
        ],
        compiler_params=pltpu.CompilerParams(
            collective_id=2, has_side_effects=True, vmem_limit_bytes=60 * 1024 * 1024
        ),
        name="feed_layer",
        cost_estimate=cost(170),
    )(*maps, narrow_gu, *acts, *weights, middle, cot, attn_out, query, log)


def by_rows(kernel, name, rows, width, args, dtypes, us):
    tile = 64 if rows % 64 == 0 else rows
    spec = lambda v: pl.BlockSpec((1, width), lambda r: (0, 0)) if v.shape[0] == 1 else pl.BlockSpec((tile, width), lambda r: (r, 0))
    row = pl.BlockSpec((tile, width), lambda r: (r, 0))
    return pl.pallas_call(
        kernel,
        grid=(rows // tile,),
        in_specs=[spec(v) for v in args],
        out_specs=[row] * len(dtypes),
        out_shape=[jax.ShapeDtypeStruct((rows, width), d) for d in dtypes],
        compiler_params=pltpu.CompilerParams(vmem_limit_bytes=VMEM_BYTES),
        name=name,
        cost_estimate=cost(us),
    )(*args)


def on_device(
    layer_input,
    cotangent,
    document_length,
    adapter_choice_index,
    query_weight,
    key_weight,
    value_weight,
    output_weight,
    gate_weight,
    up_weight,
    down_weight,
    query_norm_gain,
    key_norm_gain,
    attention_norm_gain,
    feedforward_norm_gain,
    adapter_model_input_maps,
    adapter_down_input_maps,
    adapter_model_output_maps,
    adapter_hidden_output_maps,
):
    at = Place()
    rows = layer_input.shape[1]
    width = layer_input.shape[2]
    heads = width // HD // 4
    local = heads * HD
    rank = adapter_model_input_maps.shape[2]
    depth = query_weight.shape[0]
    hidden_rows = down_weight.shape[0]
    hidden = hidden_rows * at.np
    reach = WINDOW // (2 * rows)
    count = reach + 1

    def head_cols(v, quarter):
        return pick(v.reshape(v.shape[:-1] + (heads, 4, HD)), v.ndim, quarter).reshape(v.shape[:-1] + (local,))

    def hidden_cols(v):
        lead = v.shape[:-1]
        n = len(lead)
        v = v.reshape(lead + (at.np, 2, 2, 2, hidden_rows))
        v = pick(v, n + 3, at.c)
        v = pick(v, n + 2, at.y)
        return pick(v, n + 1, at.x).reshape(lead + (-1,))

    own_inputs = layer_input[0]
    head_offsets = lambda x, y, c: [4 * k + 2 * x + c for k in range(heads)]
    feed_offsets = lambda x, y, c: [((2 * p + x) * 2 + y) * 2 + c for p in range(at.np)]
    w_qkv, feed_piece, inputs, o_own = start(
        at.np,
        reach,
        pack(at.spot, [query_weight, key_weight, value_weight], HD, head_offsets, TURNS4),
        pack(at.spot, [gate_weight], hidden_rows, feed_offsets, TURNS8),
        pack(at.spot, [up_weight], hidden_rows, feed_offsets, TURNS8),
        own_inputs,
        output_weight,
    )
    w_gu = lax.all_gather(feed_piece, "p", axis=0)
    if 2 * depth == HD:
        sent = lambda target: lax.ppermute(o_own, ("y", "c"), target)
        same = at.y == at.c
        mine_half = jnp.where(same, o_own, sent([(0, 2), (3, 1)]))
        other_half = jnp.where(same, sent([(1, 0), (2, 3)]), sent([(1, 2), (2, 1)]))
        halves = [jnp.where(at.c == 0, mine_half, other_half), jnp.where(at.c == 0, other_half, mine_half)]
        w_o = jnp.stack([v.reshape(at.np, depth, width) for v in halves], axis=1).reshape(local, width)
    else:
        o_full = lax.all_gather(output_weight, ("p", "x", "y", "c"), axis=0, tiled=True)
        w_o = pick(o_full.reshape(heads, 4, HD, width), 1, at.quarter).reshape(local, width)
    selected = adapter_choice_index[0]
    a_model = pick(adapter_model_input_maps, 0, selected)
    a_hidden = pick(adapter_down_input_maps, 0, selected)
    b_model = pick(adapter_model_output_maps, 0, selected)
    b_hidden = pick(adapter_hidden_output_maps, 0, selected)
    a_qkv = a_model[:3].reshape(3 * rank, width)
    a_gu = a_model[4:6].reshape(2 * rank, width)
    a_o = head_cols(a_model[3], at.quarter)
    a_d = hidden_cols(a_hidden)
    b_qkv = head_cols(b_model[:3], at.quarter)
    b_o, b_d = b_model[3], b_model[4]
    b_gu = hidden_cols(b_hidden)

    def diagonal(maps):
        k, r, n = maps.shape
        zero = jnp.zeros((r, n), BF)
        return jnp.concatenate(
            [jnp.concatenate([maps[a] if a == b else zero for b in range(k)], axis=1) for a in range(k)], axis=0
        )

    b_qkv_diag = diagonal(b_qkv)
    gain = jnp.concatenate(
        [head_cols(query_norm_gain[None], at.quarter), head_cols(key_norm_gain[None], at.quarter)], axis=1
    )

    step_rows = jnp.arange(rows, dtype=jnp.int32)
    spot = lambda xx: at.p * 2 * rows + xx * rows + step_rows
    pos = jnp.concatenate([spot(at.x), spot(1 - at.x)])
    lengths = lax.dynamic_slice_in_dim(document_length, 2 * at.y, 2, 0)
    bounds = jnp.cumsum(lengths, axis=1)
    bounds = jnp.where(at.c == 0, bounds, bounds[::-1])

    def lo_of(pos):
        begin = jnp.max(jnp.where(bounds[:, None, :] <= pos[None, :, None], bounds[:, None, :], 0), axis=2)
        return jnp.maximum(begin, pos[None] - (WINDOW - 1))

    lo = lo_of(pos)
    key = jnp.stack([pos - 2 * rows * t for t in range(count)])
    attention = Attention(rows, heads, count, lo[:, :, None], pos[:, None], key)

    half_dim = HD // 2
    inv_freq = ROPE_BASE ** (-(jnp.arange(half_dim, dtype=F32) * 2.0 / HD))
    spots = jnp.concatenate([spot(at.x), spot(at.x), spot(1 - at.x), spot(1 - at.x)])
    angles = jnp.concatenate([spots - 2 * rows * t for t in range(count)]).astype(F32)[:, None] * inv_freq
    cos, sin = jnp.cos(angles), jnp.sin(angles)
    cos = jnp.concatenate([cos, cos], axis=1)
    sin = jnp.concatenate([-sin, sin], axis=1)

    own = 4 * rows
    pre_q, pre_k, value_all, narrow_qkv, square_q, square_k = project(
        inputs, own, w_qkv, a_qkv, b_qkv, heads
    )
    w_d = lax.all_gather(after(down_weight, square_q), "p", axis=0, tiled=True)
    squares = jnp.concatenate([square_q[:1], square_k[:1]], axis=1)
    inv = lax.rsqrt(at.sum4(squares, 2 + reach) / width + EPS).reshape(-1, 1)
    inv_q, inv_k = inv[:own], inv[own:]
    query, key_all = post(pre_q, pre_k, inv_q, inv_k, gain, cos, sin, heads)
    o, log = attention.forward(query, key_all, value_all)
    narrow_o = dot_nt(o, a_o).astype(BF)
    def attn_part(part, mark=None):
        ins, narrow = o[part], narrow_o[part]
        if mark is not None:
            ins = after(ins, mark)
        return (dot(ins, w_o) + SCALE_ADAPT * dot(narrow, b_o)).astype(BF)

    near_rows, far_rows = slice(0, 2 * rows), slice(2 * rows, 4 * rows)
    attn_parts = at.scatter4(attn_part(far_rows), lambda mark: attn_part(near_rows, mark))
    attn_gain, feed_gain = attention_norm_gain[None], feedforward_norm_gain[None]
    attn_out, middle, low = by_rows(
        after_attention_kernel,
        "after_attention",
        rows,
        width,
        [*attn_parts, own_inputs, attn_gain],
        [F32, F32, BF],
        4,
    )
    middle_low = jnp.concatenate(at.gather8(low)[0])
    narrow_gu = dot_nt(middle_low, a_gu).astype(BF)
    gate, up, gated = gate_up(middle_low, w_gu, narrow_gu, b_gu)
    result, grad_mid, grad_attn, back_gu, wide, gb_d, later, later_logs = feed_layer(
        (a_d, b_d, b_gu, a_gu, feed_gain, attn_gain),
        narrow_gu,
        (gated, gate, up),
        (w_gu, w_d),
        middle,
        cotangent[0],
        attn_out,
        query,
        log[:, :, 0],
        reach,
    )
    lo_rows = jnp.stack([lo_of(pos + 2 * rows * t) for t in range(count)])
    query_rows = jnp.stack([pos + 2 * rows * t for t in range(count)])
    (dq, dk, dv), back_o = attend_back(
        at.np,
        reach,
        heads,
        rows,
        [
            grad_attn,
            w_o,
            a_o,
            b_o,
            *attention.tables,
            lo_rows,
            query_rows,
            log,
            later_logs,
            query,
            key_all,
            value_all,
            o,
        ],
        later,
    )
    def share_y(mine, other):
        return mine + at.swap_y(other)

    def share_p(v):
        total = pick(v, 1, at.p)
        for by in range(1, at.np):
            total = total + at.turn_p(pick(v, 1, (at.p + by) % at.np), by)
        return total

    def sum_model(v):
        v = v.reshape(-1, at.np, 2, 2, 2 * depth)
        v = pick(v, 2, at.x) + at.swap_x(pick(v, 2, 1 - at.x))
        return share_y(pick(v, 2, at.y), pick(v, 2, 1 - at.y))

    mine = (jnp.arange(4) == at.quarter).astype(F32)

    def spread(v):
        return (v.reshape(-1, heads, 1, HD) * mine[:, None]).reshape(-1, width)

    ga_gu = SCALE_ADAPT * dot_tn(back_gu, middle_low)
    ga_o = SCALE_ADAPT * dot_tn(back_o, o)
    gb_o = SCALE_ADAPT * dot_tn(narrow_o, grad_attn)
    early = jnp.concatenate([ga_gu, spread(ga_o), gb_o, gb_d])
    wide = wide.reshape(3 * rank, -1)
    if 2 * depth == HD and hidden_rows == 2 * HD:
        grad_input, sums, wide = finish(
            at.np,
            heads,
            [
                dq,
                dk,
                dv,
                pre_q,
                pre_k,
                inv_q,
                inv_k,
                gain,
                cos,
                sin,
                a_qkv,
                b_qkv,
                narrow_qkv,
                early,
                wide,
            ],
            w_qkv,
            inputs,
            grad_mid,
        )
        sums, wide = sums.reshape(-1, rank, depth), wide.reshape(-1, rank, hidden_rows)
        early, late = sums[:5], sums[5:]
    else:
        early = sum_model(after(early, dq))
        inputs, narrow_qkv, pre_k, inv_k, cos, sin = (v[:own] for v in (inputs, narrow_qkv, pre_k, inv_k, cos, sin))
        wide = wide.reshape(-1, at.np, hidden_rows)
        dk = after(dk, early)
        turn, inner = unpost(dq, dk, pre_q, pre_k, gain, cos, sin, heads)
        inner = at.sum4(inner.T, 1).T / width

        def unnorm(part, pre, scale):
            cols = slice(part * local, (part + 1) * local)
            return (scale * turn[:, cols] - pre * (scale * scale * scale * inner[:, part : part + 1])).astype(BF)

        grad_qkv = jnp.concatenate(
            [unnorm(0, pre_q, inv_q), unnorm(1, pre_k, inv_k), dv.astype(BF)], axis=1
        )
        back_qkv = dot_nt(grad_qkv, b_qkv_diag).astype(BF)

        def late_adapters(mark):
            back = after(back_qkv, mark)
            ga_qkv = SCALE_ADAPT * dot_tn(back, inputs)
            gb_qkv = [
                SCALE_ADAPT * dot_tn(narrow_qkv[:, k * rank : (k + 1) * rank], grad_qkv[:, k * local : (k + 1) * local])
                for k in range(3)
            ]
            return sum_model(jnp.concatenate([ga_qkv, spread(jnp.concatenate(gb_qkv))]))

        def end_part(part, mark=None):
            ins, back = grad_qkv[part], back_qkv[part]
            if mark is not None:
                ins = after(ins, mark)
            return (dot_nt(ins, w_qkv) + SCALE_ADAPT * dot(back, a_qkv)).astype(BF)

        marks = []

        def end_near(mark):
            marks.append(mark)
            return end_part(near_rows, mark)

        end_parts = at.scatter4(end_part(far_rows), end_near)
        (grad_input,) = by_rows(end_kernel, "end", rows, width, [*end_parts, grad_mid], [F32], 3)
        late = late_adapters(marks[0])
        narrow_sums = share_p(jnp.concatenate([late, early], axis=0))
        narrow_sums = narrow_sums.reshape(narrow_sums.shape[0], 2, depth)
        sums = pick(narrow_sums, 1, at.c) + at.swap_core(pick(narrow_sums, 1, 1 - at.c))
        sums = sums.reshape(-1, rank, depth)
        late, early = sums[:6], sums[6:]
        wide = share_p(after(wide, marks[0])).reshape(-1, rank, hidden_rows)
    choose = (jnp.arange(adapter_model_input_maps.shape[0], dtype=jnp.int32) == selected).astype(F32)
    sum_a_model = choose[:, None, None, None] * jnp.concatenate([late[:3], early[2:3], early[:2]])[None]
    sum_a_hidden = choose[:, None, None] * wide[0][None]
    sum_b_model = choose[:, None, None, None] * jnp.concatenate([late[3:], early[3:]])[None]
    sum_b_hidden = choose[:, None, None, None] * wide[1:][None]
    return (result[None], grad_input[None], sum_a_model, sum_a_hidden, sum_b_model, sum_b_hidden)


def solution(mesh):
    grid = mesh.devices.reshape(mesh.shape["ctx"] // 2, 2, mesh.shape["wt"] // 2, 2)
    split = Mesh(grid, ("p", "x", "y", "c"))
    everyone = ("p", "x", "y", "c")
    rows = P(everyone, None)
    tokens = P(("y", "c"), ("p", "x"), None)
    placed = (tokens, tokens, P(), P()) + (rows,) * 7 + (P(),) * 8
    return jax.shard_map(
        on_device,
        mesh=split,
        in_specs=placed,
        out_specs=(
            tokens,
            tokens,
            P(None, None, None, everyone),
            P(None, None, everyone),
            P(None, None, None, everyone),
            P(None, None, None, everyone),
        ),
        check_vma=False,
    )
```

```python
import functools

import jax
import jax.numpy as jnp
from jax import lax
from jax.experimental import pallas as pl
from jax.experimental.pallas import tpu as pltpu
from jax.sharding import Mesh
from jax.sharding import PartitionSpec as P

HD = 128
WINDOW = 1024
SCALE_ADAPT = 0.5
ROPE_BASE = 500000.0
EPS = 1e-06
BF = jnp.bfloat16
F32 = jnp.float32
VMEM_BYTES = 56 * 1024 * 1024


def cost(us):
    return pl.CostEstimate(flops=int(us * 1.1e9), bytes_accessed=int(us * 1e6), transcendentals=0)


def dot(a, b, dims=((1,), (0,))):
    return lax.dot_general(a, b, (dims, ((), ())), preferred_element_type=F32)


def dot_nt(a, b):
    return dot(a, b, ((1,), (1,)))


def dot_tn(a, b):
    return dot(a, b, ((0,), (0,)))


SWAP = [(0, 1), (1, 0)]


class Place:
    def __init__(self):
        self.np = lax.axis_size("p")
        self.p, self.x, self.y, self.c = (lax.axis_index(a) for a in ("p", "x", "y", "c"))
        self.quarter = 2 * self.x + self.c
        self.spot = jnp.stack([self.x, self.y, self.c]).astype(jnp.int32)

    def swap_core(self, value):
        return lax.ppermute(value, "c", SWAP)

    def swap_x(self, value):
        return lax.ppermute(value, "x", SWAP)

    def swap_both(self, value):
        return lax.ppermute(value, ("x", "c"), [(0, 3), (1, 2), (2, 1), (3, 0)])

    def swap_y(self, value):
        return lax.ppermute(value, "y", SWAP)

    def shift_p(self, value, by):
        return lax.ppermute(value, "p", [(p, p + by) for p in range(self.np) if 0 <= p + by < self.np])

    def turn_p(self, value, by):
        return lax.ppermute(value, "p", [(p, (p + by) % self.np) for p in range(self.np)])

    def gather4(self, own):
        across = self.swap_x(own)
        return self.paired(own), self.paired(across)

    def paired(self, block):
        return jnp.concatenate([block, self.swap_core(block)], axis=0)

    def gather8(self, own, work=None):
        half = own.shape[0] // 2
        across, over = self.swap_x(own), self.swap_y(own)
        first = self.paired(own)
        done = None
        if work is not None:
            done = work(first)
            across, over = after(across, done[0]), after(over, done[0])
        far = jnp.concatenate([self.swap_y(across[:half]), self.swap_x(over[half:])])
        return (first, self.paired(across), self.paired(over), self.paired(far)), done

    def met(self, pair):
        rows = pair.shape[0] // 2
        return (pair[:rows].astype(F32) + self.swap_core(pair[rows:]).astype(F32)).astype(BF)

    def scatter4(self, second, first):
        met = self.met(second)
        across = self.swap_x(met)
        first = first(met)
        return first, self.swap_core(first[first.shape[0] // 2 :]), across

    def scatter8(self, second, third, fourth, first):
        far = self.met(fourth)
        half = far.shape[0] // 2
        by_x, by_y = self.swap_x(far[:half]), self.swap_y(far[half:])
        second, third = self.met(second), self.met(third)
        add = lambda u, v: (u.astype(F32) + v.astype(F32)).astype(BF)
        across = [self.swap_x(second[:half]), self.swap_x(add(second[half:], by_y))]
        over = [self.swap_y(add(third[:half], by_x)), self.swap_y(third[half:])]
        first = first(far)
        core = self.swap_core(first[first.shape[0] // 2 :])
        return first, core, jnp.concatenate(across), jnp.concatenate(over)

    def sum4(self, value, parts):
        def reordered(v, x, c):
            v = v.reshape(v.shape[0], parts, 2, 2, -1)
            if x:
                v = jnp.concatenate([v[:, :, 1:], v[:, :, :1]], axis=2)
            if c:
                v = jnp.concatenate([v[:, :, :, 1:], v[:, :, :, :1]], axis=3)
            return v.reshape(value.shape)

        core, across, both = self.swap_core(value), self.swap_x(value), self.swap_both(value)
        return value + reordered(core, 0, 1) + reordered(across, 1, 0) + reordered(both, 1, 1)


def pick(v, axis, index):
    return lax.dynamic_index_in_dim(v, index, axis, keepdims=False)


def after(value, *others):
    return lax.optimization_barrier((value,) + others)[0]


class Copies:
    def __init__(self, send_sem, recv_sem):
        self.sems, self.used, self.all = (send_sem, recv_sem), 0, []

    def remote(self, src, dst, device):
        k = self.used
        self.used += 1
        copy = pltpu.make_async_remote_copy(
            src_ref=src,
            dst_ref=dst,
            send_sem=self.sems[0].at[k],
            recv_sem=self.sems[1].at[k],
            device_id=device,
            device_id_type=pl.DeviceIdType.MESH,
        )
        copy.start()
        self.all.append(copy)
        return copy

    def finish(self):
        for copy in self.all:
            copy.wait_send()


def pack_kernel(count, width, offsets, turns, spot_ref, *refs):
    spot = [spot_ref[k] for k in range(3)]
    for out, turn in zip(refs[count:], turns):
        places = offsets(*[(s + t) % 2 for s, t in zip(spot, turn)])
        for w, ref in enumerate(refs[:count]):
            for k, place in enumerate(places):
                at = (w * len(places) + k) * width
                out[:, at : at + width] = ref[:, pl.ds(pl.multiple_of(place * width, HD), width)]


def pack(spot, weights, width, offsets, turns):
    rows = weights[0].shape[0]
    size = len(weights) * len(offsets(0, 0, 0)) * width
    if width % HD:
        outs = []
        for turn in turns:
            places = offsets(*[(spot[k] + turn[k]) % 2 for k in range(3)])
            cuts = [lax.dynamic_slice_in_dim(w, place * width, width, 1) for w in weights for place in places]
            outs.append(jnp.concatenate(cuts, axis=1))
        return outs
    whole = pl.BlockSpec(memory_space=pltpu.VMEM)
    return pl.pallas_call(
        functools.partial(pack_kernel, len(weights), width, offsets, turns),
        in_specs=[pl.BlockSpec(memory_space=pltpu.SMEM)] + [whole] * len(weights),
        out_specs=[whole] * len(turns),
        out_shape=[jax.ShapeDtypeStruct((rows, size), BF)] * len(turns),
        compiler_params=pltpu.CompilerParams(vmem_limit_bytes=VMEM_BYTES),
        name="pack_columns",
        cost_estimate=cost(3),
    )(spot, *weights)


TURNS8 = [(dx, dy, dc) for dy in range(2) for dx in range(2) for dc in range(2)]
TURNS4 = TURNS8[:4]


def start_kernel(groups, reach, *refs):
    qkv_pack, feed_packs, x_ref, o_ref = refs[0:4], (refs[4:12], refs[12:20]), refs[20], refs[21]
    w_ref, feed_ref, all_ref, o_all_ref, local_sem, send_sem, recv_sem = refs[22:]
    p, x, y, c = (lax.axis_index(a) for a in ("p", "x", "y", "c"))
    turned = lambda u, t: 1 - u if t else u
    group = [(p, turned(x, dx), turned(y, dy), turned(c, dc)) for dx, dy, dc in TURNS8]
    core, across, over = group[1], group[2], group[4]
    right, left = (lax.rem(p + 1, groups), x, y, c), (lax.rem(p + groups - 1, groups), x, y, c)
    rows, depth, hidden = x_ref.shape[0], qkv_pack[0].shape[0], feed_packs[0][0].shape[1]
    used = [0]

    def remote(src, dst, device):
        k = used[0]
        used[0] += 1
        copy = pltpu.make_async_remote_copy(
            src_ref=src,
            dst_ref=dst,
            send_sem=send_sem.at[k],
            recv_sem=recv_sem.at[k],
            device_id=device,
            device_id_type=pl.DeviceIdType.MESH,
        )
        copy.start()
        return copy

    def local(k, src, dst):
        copy = pltpu.make_async_copy(src, dst, local_sem.at[k])
        copy.start()
        return copy

    barrier = pltpu.get_barrier_semaphore()
    for device in group[1:] + [right, left]:
        pl.semaphore_signal(barrier, inc=1, device_id=device, device_id_type=pl.DeviceIdType.MESH)
    pl.semaphore_wait(barrier, 9)

    def at(ref, start, size):
        return ref.at[pl.ds(pl.multiple_of(start, 16), size)]

    def tokens(t, block):
        return all_ref.at[pl.ds((4 * t + block) * rows, rows)]

    def owned(q):
        return w_ref.at[lax.rem(p + 2 * groups - q, groups), :, y]

    slot = (4 * x + 2 * y + c) * depth
    mine = [
        w_ref.at[p, x, y, pl.ds(pl.multiple_of(c * depth, 16), depth)],
        feed_ref.at[pl.ds(pl.multiple_of(slot, 16), depth), pl.ds(0, hidden)],
        feed_ref.at[pl.ds(pl.multiple_of(slot, 16), depth), pl.ds(hidden, hidden)],
    ]
    firsts = (qkv_pack[0], feed_packs[0][0], feed_packs[1][0])
    kept = [local(k, firsts[k], mine[k]) for k in range(3)] + [local(3, x_ref, tokens(0, 0))]
    kept.append(local(4, o_ref, o_all_ref.at[p]))
    o_of = lambda q: o_all_ref.at[lax.rem(p + 2 * groups - q, groups)]
    regrouped = [remote(qkv_pack[d], mine[0], group[d]) for d in (1, 2, 3)]
    moves = [remote(x_ref, tokens(1, 0), right)]
    sent = list(regrouped) + moves
    kept[0].wait()
    for copy in regrouped:
        copy.wait_recv()
    along = remote(owned(0), owned(0), right)
    o_along = remote(o_ref, o_of(0), right)
    sent.append(o_along)
    later = [remote(owned(0), owned(0), over)]
    spread = [(remote(x_ref, tokens(0, 1), core), remote(x_ref, tokens(0, 2), across))]
    for k in (1, 2):
        later += [remote(feed_packs[k - 1][d], mine[k], group[d]) for d in range(1, 8)]
    sent.append(along)
    step = 1
    ready = 0

    def pass_on(t):
        spread[t][1].wait_recv()
        later.append(remote(tokens(t, 2), tokens(t, 3), core))

    while step < groups or ready <= reach:
        if ready < reach:
            moves[ready].wait_recv()
            if ready + 1 < reach:
                moves.append(remote(tokens(ready + 1, 0), tokens(ready + 2, 0), right))
                sent.append(moves[-1])
            spread.append(
                (
                    remote(tokens(ready + 1, 0), tokens(ready + 1, 1), core),
                    remote(tokens(ready + 1, 0), tokens(ready + 1, 2), across),
                )
            )
        if step < groups:
            along.wait_recv()
            if step < groups - 1:
                along = remote(owned(step), owned(step), right)
                sent.append(along)
            later.append(remote(owned(step), owned(step), over))
            o_along.wait_recv()
            if step < groups - 1:
                o_along = remote(o_of(step), o_of(step), right)
                sent.append(o_along)
            step += 1
        if ready <= reach:
            pass_on(ready)
            ready += 1
    for near, far in spread:
        near.wait_recv()
        sent += [near, far]
    for copy in later:
        copy.wait_recv()
    for copy in sent + later:
        copy.wait_send()
    for copy in kept[1:]:
        copy.wait()


def start(groups, reach, qkv_pack, gate_pack, up_pack, own_inputs, own_o):
    depth, size = qkv_pack[0].shape
    rows, width = own_inputs.shape
    hidden = gate_pack[0].shape[1]
    copies = 3 + 1 + 1 + 1 + 14 + (groups - 1) + (groups - 2) + (groups - 1) + (reach - 1) + 2 * (reach + 1) + (reach + 1)
    anywhere = pl.BlockSpec(memory_space=pl.ANY)
    weight, feed, inputs, o_all = pl.pallas_call(
        functools.partial(start_kernel, groups, reach),
        in_specs=[anywhere] * 22,
        out_specs=[anywhere] * 4,
        out_shape=[
            jax.ShapeDtypeStruct((groups, 2, 2, 2 * depth, size), BF),
            jax.ShapeDtypeStruct((8 * depth, 2 * hidden), BF),
            jax.ShapeDtypeStruct((4 * (reach + 1) * rows, width), BF),
            jax.ShapeDtypeStruct((groups,) + own_o.shape, BF),
        ],
        scratch_shapes=[
            pltpu.SemaphoreType.DMA((5,)),
            pltpu.SemaphoreType.DMA((copies,)),
            pltpu.SemaphoreType.DMA((copies,)),
        ],
        compiler_params=pltpu.CompilerParams(collective_id=0, has_side_effects=True),
        name="start",
        cost_estimate=cost(120),
    )(*qkv_pack, *gate_pack, *up_pack, own_inputs, own_o)
    return weight.reshape(-1, size), feed, inputs, o_all.reshape(-1, width)


def gate_up_kernel(x_ref, gate_w_ref, up_w_ref, narrow_ref, maps_ref, gate_ref, up_ref, gated_ref):
    rank, tile = maps_ref.shape[1:]
    gate_w, up_w = gate_w_ref[...].reshape(-1, tile), up_w_ref[...].reshape(-1, tile)
    gate = dot(x_ref[...], gate_w) + SCALE_ADAPT * dot(narrow_ref[:, :rank], maps_ref[0])
    up = dot(x_ref[...], up_w) + SCALE_ADAPT * dot(narrow_ref[:, rank:], maps_ref[1])
    gate_ref[...] = gate.astype(BF)
    up_ref[...] = up.astype(BF)
    gated_ref[...] = (gate * jax.nn.sigmoid(gate) * up).astype(BF)


def gate_up(x, weight, narrow, maps):
    rows, width = x.shape
    groups = weight.shape[0]
    hidden = weight.shape[2] // 2
    tile = 256
    steps = hidden // tile
    out = pl.BlockSpec((rows, tile), lambda s: (0, s))
    return pl.pallas_call(
        gate_up_kernel,
        grid=(steps,),
        in_specs=[
            pl.BlockSpec((rows, width), lambda s: (0, 0)),
            pl.BlockSpec((groups, width // groups, tile), lambda s: (0, 0, s)),
            pl.BlockSpec((groups, width // groups, tile), lambda s: (0, 0, s + steps)),
            pl.BlockSpec(narrow.shape, lambda s: (0, 0)),
            pl.BlockSpec(maps.shape[:2] + (tile,), lambda s: (0, 0, s)),
        ],
        out_specs=[out] * 3,
        out_shape=[jax.ShapeDtypeStruct((rows, hidden), BF)] * 3,
        compiler_params=pltpu.CompilerParams(vmem_limit_bytes=VMEM_BYTES),
        name="gate_up",
        cost_estimate=cost(1),
    )(x, weight, weight, narrow, maps)


def project_kernel(heads, own_tiles, x_ref, w_ref, in_maps_ref, out_maps_ref, *out_refs):
    pre_q_ref, pre_k_ref, value_ref, narrow_ref, square_q_ref, square_k_ref = out_refs
    width = heads * HD
    rank = out_maps_ref.shape[1]
    narrow_ref[...] = dot_nt(x_ref[...], in_maps_ref[...]).astype(BF)

    def part(k):
        cols = slice(k * width, (k + 1) * width)
        return dot(x_ref[...], w_ref[:, cols]) + SCALE_ADAPT * dot(narrow_ref[:, k * rank : (k + 1) * rank], out_maps_ref[k])

    ones = jnp.ones((8, width), BF)
    key = part(1)
    pre_k_ref[...] = key
    square_k_ref[...] = dot_nt(ones, (key * key).astype(BF))
    value_ref[...] = part(2).astype(BF)

    @pl.when(pl.program_id(0) < own_tiles)
    def _():
        query = part(0)
        pre_q_ref[...] = query
        square_q_ref[...] = dot_nt(ones, (query * query).astype(BF))


def project(x, own_rows, weight, in_maps, out_maps, heads):
    rows, width = x.shape
    local = heads * HD
    tile = 512
    own_tiles = own_rows // tile
    fixed = lambda v: pl.BlockSpec(v.shape, lambda t: (0,) * v.ndim)
    row = lambda n: pl.BlockSpec((tile, n), lambda t: (t, 0))
    return pl.pallas_call(
        functools.partial(project_kernel, heads, own_tiles),
        grid=(rows // tile,),
        in_specs=[row(width), fixed(weight), fixed(in_maps), fixed(out_maps)],
        out_specs=[
            pl.BlockSpec((tile, local), lambda t: (jnp.minimum(t, own_tiles - 1), 0)),
            row(local),
            row(local),
            row(in_maps.shape[0]),
            pl.BlockSpec((8, tile), lambda t: (0, jnp.minimum(t, own_tiles - 1))),
            pl.BlockSpec((8, tile), lambda t: (0, t)),
        ],
        out_shape=[
            jax.ShapeDtypeStruct((own_rows, local), F32),
            jax.ShapeDtypeStruct((rows, local), F32),
            jax.ShapeDtypeStruct((rows, local), BF),
            jax.ShapeDtypeStruct((rows, in_maps.shape[0]), BF),
            jax.ShapeDtypeStruct((8, own_rows), F32),
            jax.ShapeDtypeStruct((8, rows), F32),
        ],
        compiler_params=pltpu.CompilerParams(vmem_limit_bytes=VMEM_BYTES),
        name="project",
        cost_estimate=cost(1),
    )(x, weight, in_maps, out_maps)


def post_kernel(heads, own_tiles, q_ref, k_ref, inv_q_ref, inv_k_ref, gain_ref, cos_ref, sin_ref, q_out, k_out):
    width = heads * HD
    cos, sin = cos_ref[...], sin_ref[...]

    def turn(pre_ref, inv, part, out_ref):
        for h in range(heads):
            cols = slice(h * HD, (h + 1) * HD)
            v = pre_ref[:, cols] * inv * gain_ref[:, part * width + h * HD : part * width + (h + 1) * HD]
            out_ref[:, cols] = (v * cos + pltpu.roll(v, HD // 2, 1) * sin).astype(BF)

    turn(k_ref, inv_k_ref[...], 1, k_out)

    @pl.when(pl.program_id(0) < own_tiles)
    def _():
        turn(q_ref, inv_q_ref[...], 0, q_out)


def post(pre_q, pre_k, inv_q, inv_k, gain, cos, sin, heads):
    rows, width = pre_k.shape
    tile = 256
    own_tiles = pre_q.shape[0] // tile
    row = lambda n: pl.BlockSpec((tile, n), lambda r: (r, 0))
    own = lambda n: pl.BlockSpec((tile, n), lambda r: (jnp.minimum(r, own_tiles - 1), 0))
    return pl.pallas_call(
        functools.partial(post_kernel, heads, own_tiles),
        grid=(rows // tile,),
        in_specs=[
            own(width),
            row(width),
            own(1),
            row(1),
            pl.BlockSpec((1, 2 * width), lambda r: (0, 0)),
            row(HD),
            row(HD),
        ],
        out_specs=[own(width), row(width)],
        out_shape=[jax.ShapeDtypeStruct(pre_q.shape, BF), jax.ShapeDtypeStruct(pre_k.shape, BF)],
        name="rope_forward",
        cost_estimate=cost(1),
    )(pre_q, pre_k, inv_q, inv_k, gain, cos, sin)


def unpost_kernel(heads, dq_ref, dk_ref, pre_q_ref, pre_k_ref, gain_ref, cos_ref, sin_ref, turn_ref, inner_ref):
    width = heads * HD
    cos, sin = cos_ref[...], sin_ref[...]
    for part, (d_ref, pre_ref) in enumerate(((dq_ref, pre_q_ref), (dk_ref, pre_k_ref))):
        total = None
        for h in range(heads):
            cols = slice(part * width + h * HD, part * width + (h + 1) * HD)
            v = d_ref[:, h * HD : (h + 1) * HD]
            turned = (v * cos - pltpu.roll(v, HD // 2, 1) * sin) * gain_ref[:, cols]
            turn_ref[:, cols] = turned
            inner = jnp.sum(turned * pre_ref[:, h * HD : (h + 1) * HD], axis=1, keepdims=True)
            total = inner if total is None else total + inner
        inner_ref[:, part : part + 1] = total


def unpost(dq, dk, pre_q, pre_k, gain, cos, sin, heads):
    rows, width = dq.shape
    tile = 256
    row = lambda n: pl.BlockSpec((tile, n), lambda r: (r, 0))
    return pl.pallas_call(
        functools.partial(unpost_kernel, heads),
        grid=(rows // tile,),
        in_specs=[row(width)] * 4 + [pl.BlockSpec((1, 2 * width), lambda r: (0, 0)), row(HD), row(HD)],
        out_specs=[row(2 * width), row(2)],
        out_shape=[jax.ShapeDtypeStruct((rows, 2 * width), F32), jax.ShapeDtypeStruct((rows, 2), F32)],
        name="rope_backward",
        cost_estimate=cost(8),
    )(dq, dk, pre_q, pre_k, gain, cos, sin)


def finish_kernel(groups, heads, early_rows, *refs):
    (
        dq_ref,
        dk_ref,
        dv_ref,
        pre_q_ref,
        pre_k_ref,
        inv_q_ref,
        inv_k_ref,
        gain_ref,
        cos_ref,
        sin_ref,
        in_maps_ref,
        out_maps_ref,
        narrow_ref,
        early_ref,
        wide_ref,
        weight_any,
        inputs_any,
        mid_any,
    ) = refs[:18]
    out_ref, sums_ref, wide_out_ref = refs[18:21]
    (
        weight,
        inputs,
        mid,
        turn,
        grad,
        back,
        stat,
        stat_in,
        far,
        near,
        core_in,
        met,
        across_in,
        near_in,
        maps,
        maps_in,
        by_x,
        by_y,
        by_y_in,
        by_p_in,
        own_sum,
        own_sum_in,
        wide_in,
        local_sem,
        send_sem,
        recv_sem,
    ) = refs[21:]
    p, x, y, c = (lax.axis_index(a) for a in ("p", "x", "y", "c"))
    core, across, both, over = (p, x, y, 1 - c), (p, 1 - x, y, c), (p, 1 - x, y, 1 - c), (p, x, 1 - y, c)
    others = [lax.rem(p + s, groups) for s in range(1, groups)]
    width = heads * HD
    rows = out_ref.shape[0]
    model = out_ref.shape[1]
    rank = out_maps_ref.shape[1]
    copies = Copies(send_sem, recv_sem)
    loads = []
    for k, (src, dst) in enumerate(((weight_any, weight), (inputs_any.at[pl.ds(0, 4 * mid.shape[0])], inputs), (mid_any, mid))):
        loads.append(pltpu.make_async_copy(src, dst, local_sem.at[k]))
        loads[-1].start()

    barrier = pltpu.get_barrier_semaphore()
    for device in [core, across, both, over] + [(q, x, y, c) for q in others]:
        pl.semaphore_signal(barrier, inc=1, device_id=device, device_id_type=pl.DeviceIdType.MESH)

    ones = jnp.ones((8, HD), BF)

    def unturn(b, carry):
        here = pl.ds(pl.multiple_of(b * rows, rows), rows)
        cos, sin = cos_ref[here, :], sin_ref[here, :]
        for part, pre_ref in enumerate((pre_q_ref, pre_k_ref)):
            product = None
            for h in range(heads):
                cols = slice(h * HD, (h + 1) * HD)
                wide_cols = slice(part * width + h * HD, part * width + (h + 1) * HD)
                v = dq_ref[here, cols] if part == 0 else dk_ref[here, cols]
                turned = (v * cos - pltpu.roll(v, HD // 2, 1) * sin) * gain_ref[:, wide_cols]
                turn[here, wide_cols] = turned
                term = turned * pre_ref[here, cols]
                product = term if product is None else product + term
            high = product.astype(BF)
            low = (product - high.astype(F32)).astype(BF)
            summed = dot_nt(ones, high) + dot_nt(ones, low)
            stat[part : part + 1, here] = summed[:1, :]
        grad[here, 2 * width :] = dv_ref[here, :].astype(BF)
        return carry

    stat[...] = jnp.zeros_like(stat)
    lax.fori_loop(0, 4, unturn, 0)
    for b in range(2 * groups):
        maps[b, :early_rows, :] = early_ref[:, b * 256 : (b + 1) * 256]
    pl.semaphore_wait(barrier, 3 + groups)
    stats = [copies.remote(stat, stat_in.at[k], device) for k, device in enumerate((core, across, both))]
    early = pl.ds(0, early_rows)
    exchanged = [copies.remote(maps.at[2 * q + 1 - x, early], maps_in.at[q, early], across) for q in range(groups)]
    wides = [
        copies.remote(wide_ref.at[:, pl.ds(pl.multiple_of(q * 256, 256), 256)], wide_in.at[k], (q, x, y, c))
        for k, q in enumerate(others)
    ]
    for copy in stats:
        copy.wait_recv()

    for b in range(4):
        here = slice(b * rows, (b + 1) * rows)
        total_row = stat[:, here]
        for k in range(3):
            d = b ^ (k + 1)
            total_row = total_row + stat_in[k, :, d * rows : (d + 1) * rows]
        inner = total_row.T / model
        for part, (pre_ref, inv_ref) in enumerate(((pre_q_ref, inv_q_ref), (pre_k_ref, inv_k_ref))):
            cols = slice(part * width, (part + 1) * width)
            inv = inv_ref[here, :]
            scale = inv * inv * inv * inner[:, part : part + 1]
            grad[here, cols] = (inv * turn[here, cols] - pre_ref[here, :] * scale).astype(BF)

    loads[0].wait()

    def into(start, dst):
        here = slice(start, start + 2 * rows)
        for k in range(3):
            part = dot_nt(grad[here, k * width : (k + 1) * width], out_maps_ref[k])
            back[here, k * rank : (k + 1) * rank] = part.astype(BF)

        def columns(n, carry):
            cols = pl.ds(pl.multiple_of(n * 512, 512), 512)
            full = dot_nt(grad[here, :], weight[cols, :]) + SCALE_ADAPT * dot(back[here, :], in_maps_ref[:, cols])
            dst[:, cols] = full.astype(BF)
            return carry

        lax.fori_loop(0, model // 512, columns, 0)

    into(2 * rows, far)
    far_copy = copies.remote(far.at[pl.ds(rows, rows)], core_in, core)
    far_copy.wait_recv()
    met[...] = (far[:rows, :].astype(F32) + core_in[...].astype(F32)).astype(BF)
    across_copy = copies.remote(met, across_in, across)
    into(0, near)
    near_copy = copies.remote(near.at[pl.ds(rows, rows)], near_in, core)

    loads[1].wait()
    late = early_rows + 3 * rank
    for b in range(2 * groups):
        cols = slice(b * 256, (b + 1) * 256)
        maps[b, early_rows:late, :] = SCALE_ADAPT * dot_tn(back[...], inputs[:, cols])
    send_late = pl.ds(early_rows, 3 * rank)
    exchanged += [
        copies.remote(maps.at[2 * q + 1 - x, send_late], maps_in.at[q, send_late], across) for q in range(groups)
    ]
    for q in range(groups):
        by_x[q, late:, :] = jnp.zeros_like(by_x[q, late:, :])
    for k in range(3):
        own = SCALE_ADAPT * dot_tn(narrow_ref[:, k * rank : (k + 1) * rank], grad[:, k * width : (k + 1) * width])
        here = slice(late + k * rank, late + (k + 1) * rank)
        for q in range(groups):
            by_x[q, here, pl.ds(pl.multiple_of(c * HD, HD), HD)] = own[:, q * HD : (q + 1) * HD]
    for copy in exchanged:
        copy.wait_recv()
    for q in range(groups):
        by_x[q, :late, :] = maps[2 * q + x, :late, :] + maps_in[q]
    halves = lambda ref, q, side: ref.at[q, :, pl.ds(pl.multiple_of(side * HD, HD), HD)]
    exchanged = [copies.remote(halves(by_x, q, 1 - y), by_y_in.at[q], over) for q in range(groups)]
    for q, copy in enumerate(exchanged):
        copy.wait_recv()
        by_y[q] = by_x[q, :, pl.ds(pl.multiple_of(y * HD, HD), HD)] + by_y_in[q]
    exchanged = [copies.remote(by_y.at[q], by_p_in.at[k], (q, x, y, c)) for k, q in enumerate(others)]
    summed = by_y[p]
    wide_sum = wide_ref[:, pl.ds(pl.multiple_of(p * 256, 256), 256)]
    for k, copy in enumerate(exchanged):
        copy.wait_recv()
        summed = summed + by_p_in[k]
    own_sum[...] = summed
    last = copies.remote(own_sum, own_sum_in, core)
    for k, copy in enumerate(wides):
        copy.wait_recv()
        wide_sum = wide_sum + wide_in[k]
    wide_out_ref[...] = wide_sum
    last.wait_recv()
    summed = summed + own_sum_in[...]
    sums_ref[...] = jnp.where(c == 0, summed[:, : HD // 2], summed[:, HD // 2 :])

    loads[2].wait()
    near_copy.wait_recv()
    across_copy.wait_recv()
    out_ref[...] = (
        mid[...]
        + near[:rows, :].astype(F32)
        + near_in[...].astype(F32)
        + across_in[...].astype(F32)
    )
    copies.finish()


def finish(groups, heads, args, weight, inputs, mid):
    own, width = args[0].shape
    rows, model = mid.shape
    rank = args[11].shape[1]
    early_rows, wide_rows = args[13].shape[0], args[14].shape[0]
    total_rows = early_rows + 6 * rank
    late = early_rows + 3 * rank
    vm = pl.BlockSpec(memory_space=pltpu.VMEM)
    anywhere = pl.BlockSpec(memory_space=pl.ANY)
    count = 3 + groups + (groups - 1) + 3 + 2 * groups + (groups - 1) + 1
    block = lambda *shape: pltpu.VMEM(shape, BF)
    full = lambda *shape: pltpu.VMEM(shape, F32)
    first_rows = lambda v: vm if v.shape[0] <= own else pl.BlockSpec(
        (own, v.shape[1]), lambda k: (0, 0), pipeline_mode=pl.Buffered(1)
    )
    return pl.pallas_call(
        functools.partial(finish_kernel, groups, heads, early_rows),
        grid=(1,),
        in_specs=[first_rows(v) for v in args] + [anywhere] * 3,
        out_specs=[vm] * 3,
        out_shape=[
            jax.ShapeDtypeStruct((rows, model), F32),
            jax.ShapeDtypeStruct((total_rows, HD // 2), F32),
            jax.ShapeDtypeStruct((wide_rows, 256), F32),
        ],
        scratch_shapes=[
            pltpu.VMEM(weight.shape, BF),
            pltpu.VMEM((own, model), BF),
            pltpu.VMEM(mid.shape, F32),
            full(own, 2 * width),
            block(own, 3 * width),
            block(own, 3 * rank),
            full(8, own),
            full(3, 8, own),
            block(2 * rows, model),
            block(2 * rows, model),
            block(rows, model),
            block(rows, model),
            block(rows, model),
            block(rows, model),
            full(2 * groups, late, 256),
            full(groups, late, 256),
            full(groups, total_rows, 256),
            full(groups, total_rows, HD),
            full(groups, total_rows, HD),
            full(groups - 1, total_rows, HD),
            full(total_rows, HD),
            full(total_rows, HD),
            full(groups - 1, wide_rows, 256),
            pltpu.SemaphoreType.DMA((3,)),
            pltpu.SemaphoreType.DMA((count,)),
            pltpu.SemaphoreType.DMA((count,)),
        ],
        compiler_params=pltpu.CompilerParams(
            collective_id=1, has_side_effects=True, vmem_limit_bytes=VMEM_BYTES
        ),
        name="finish",
        cost_estimate=cost(60),
    )(*args, weight, inputs, mid)


NEG_FILL = -1e30


def attend_kernel(count, scale, q_ref, *refs):
    ks, vs = refs[:count], refs[count : 2 * count]
    lo_ref, pos_ref, key_ref, o_ref, log_ref = refs[2 * count :]
    rows = q_ref.shape[0] * q_ref.shape[2]
    q = q_ref[...].reshape(rows, HD)
    lo, pos = lo_ref[0], pos_ref[...]
    scores = []
    for t in range(count):
        s = dot_nt(q, ks[t][...].reshape(rows, HD)) * scale
        key = key_ref[t : t + 1, :]
        scores.append(jnp.where((key >= lo) & (key <= pos), s, NEG_FILL))
    top = functools.reduce(jnp.maximum, [jnp.max(s, axis=1, keepdims=True) for s in scores])
    powers = [jnp.exp(s - top) for s in scores]
    total = sum(jnp.sum(e, axis=1, keepdims=True) for e in powers)
    share = 1.0 / total
    out = sum(dot((e * share).astype(BF), vs[t][...].reshape(rows, HD)) for t, e in enumerate(powers))
    o_ref[...] = out.astype(BF).reshape(o_ref.shape)
    log_ref[0] = top + jnp.log(total)


def attend_back_kernel(groups, reach, heads, scale, *refs):
    (
        grad_ref,
        weight_ref,
        in_maps_ref,
        out_maps_ref,
        lo_ref,
        pos_ref,
        key_ref,
        lo_rows_ref,
        query_rows_ref,
        log_ref,
        log_rows_ref,
        q_any,
        k_any,
        v_any,
        o_any,
    ) = refs[:15]
    later_any = refs[15]
    dq_ref, dk_ref, dv_ref, back_ref = refs[16:20]
    (
        q_buf,
        k_buf,
        v_buf,
        o_buf,
        later_buf,
        do_buf,
        do_in,
        inner,
        inner_in,
        load_sem,
        send_sem,
        recv_sem,
    ) = refs[20:]
    p, x, y, c = (lax.axis_index(a) for a in ("p", "x", "y", "c"))
    right, left = (lax.rem(p + 1, groups), x, y, c), (lax.rem(p + groups - 1, groups), x, y, c)
    rows = q_buf.shape[2]
    full = 2 * rows
    copies = Copies(send_sem, recv_sem)
    sources = [(q_any, q_buf), (k_any, k_buf), (v_any, v_buf), (o_any, o_buf)]
    sources.append((later_any, later_buf))
    loads = []
    for n, (src, dst) in enumerate(sources):
        loads.append(pltpu.make_async_copy(src, dst, load_sem.at[n]))
        loads[-1].start()
    barrier = pltpu.get_barrier_semaphore()
    for device in (left, right):
        pl.semaphore_signal(barrier, inc=1, device_id=device, device_id_type=pl.DeviceIdType.MESH)

    for b in range(2):
        here = slice(b * full, (b + 1) * full)
        low = dot_nt(grad_ref[here, :], out_maps_ref[...]).astype(BF)
        back_ref[here, :] = low
        value = dot_nt(grad_ref[here, :], weight_ref[...]) + SCALE_ADAPT * dot(low, in_maps_ref[...])
        do_buf[b] = value.astype(BF).reshape(2, rows, heads * HD)
    pl.semaphore_wait(barrier, 2)
    moves = [copies.remote(do_buf, do_in.at[0], left)]
    for load in loads:
        load.wait()

    def piece(ref, s, cols, first=0):
        return ref[first : first + 2, s, :, cols].reshape(full, HD)

    def put(ref, s, cols, value):
        ref[:, s, :, cols] = value.reshape(2, rows, HD)

    ones = jnp.ones((8, HD), BF)

    def sums(n, carry):
        s, cols = n // heads, pl.ds(pl.multiple_of(n % heads * HD, HD), HD)
        product = piece(do_buf, s, cols).astype(F32) * piece(o_buf, s, cols).astype(F32)
        high = product.astype(BF)
        low = (product - high.astype(F32)).astype(BF)
        inner[pl.ds(n, 1), :] = (dot_nt(ones, high) + dot_nt(ones, low))[:1, :]
        return carry

    lax.fori_loop(0, 2 * heads, sums, 0)
    inner_moves = [copies.remote(inner, inner_in.at[0], left)]

    def own(n, carry):
        s, cols = n // heads, pl.ds(pl.multiple_of(n % heads * HD, HD), HD)
        q, do = piece(q_buf, s, cols), piece(do_buf, s, cols)
        delta = jnp.sum(do.astype(F32) * piece(o_buf, s, cols).astype(F32), axis=1, keepdims=True)
        lo, pos, log_total = lo_ref[s], pos_ref[...], log_ref[n]
        dq = None
        for t in range(reach + 1):
            k, v = piece(k_buf, s, cols, 2 * t), piece(v_buf, s, cols, 2 * t)
            key = key_ref[t : t + 1, :]
            score = dot_nt(q, k) * scale
            probs = jnp.where((key >= lo) & (key <= pos), jnp.exp(score - log_total), 0.0)
            ds = (probs * (dot_nt(do, v) - delta)).astype(BF)
            part = dot(ds, k)
            dq = part if dq is None else dq + part
            if t == 0:
                put(dv_ref, s, cols, dot_tn(probs.astype(BF), do))
                put(dk_ref, s, cols, dot_tn(ds, q) * scale)
        put(dq_ref, s, cols, dq * scale)
        return carry

    lax.fori_loop(0, 2 * heads, own, 0)

    for t in range(1, reach + 1):
        moves[-1].wait_recv()
        inner_moves[-1].wait_recv()
        if t < reach:
            moves.append(copies.remote(do_in.at[t - 1], do_in.at[t], left))
            inner_moves.append(copies.remote(inner_in.at[t - 1], inner_in.at[t], left))

        def from_later(n, carry, t=t):
            s, cols = n // heads, pl.ds(pl.multiple_of(n % heads * HD, HD), HD)
            k, v = piece(k_buf, s, cols), piece(v_buf, s, cols)
            q, do = piece(later_buf.at[t - 1], s, cols), piece(do_in.at[t - 1], s, cols)
            score = dot_nt(k, q) * scale
            key = pos_ref[...]
            lo, pos = lo_rows_ref[t, pl.ds(s, 1), :], query_rows_ref[t : t + 1, :]
            probs = jnp.where((key >= lo) & (key <= pos), jnp.exp(score - log_rows_ref[t - 1, pl.ds(n, 1), :]), 0.0)
            ds = (probs * (dot_nt(v, do) - inner_in[t - 1, pl.ds(n, 1), :])).astype(BF)
            put(dv_ref, s, cols, piece(dv_ref, s, cols) + dot(probs.astype(BF), do))
            put(dk_ref, s, cols, piece(dk_ref, s, cols) + dot(ds, q) * scale)
            return carry

        lax.fori_loop(0, 2 * heads, from_later, 0)
    copies.finish()


def attend_back(groups, reach, heads, rows, args, later):
    own = 4 * rows
    local = heads * HD
    vm = pl.BlockSpec(memory_space=pltpu.VMEM)
    anywhere = pl.BlockSpec(memory_space=pl.ANY)
    block = lambda n: pltpu.VMEM((2 * n, 2, rows, local), BF)
    view = lambda v: v.reshape(-1, 2, rows, local)
    count = 2 * reach
    dq, dk, dv, back = pl.pallas_call(
        functools.partial(attend_back_kernel, groups, reach, heads, HD**-0.5),
        in_specs=[vm] * 11 + [anywhere] * 5,
        out_specs=[vm] * 4,
        out_shape=[jax.ShapeDtypeStruct((2, 2, rows, local), F32)] * 3
        + [jax.ShapeDtypeStruct((own, args[2].shape[0]), BF)],
        scratch_shapes=[
            block(1),
            block(reach + 1),
            block(reach + 1),
            block(1),
            pltpu.VMEM((reach, 2, 2, rows, local), BF),
            block(1),
            pltpu.VMEM((reach, 2, 2, rows, local), BF),
            pltpu.VMEM((2 * heads, 2 * rows), F32),
            pltpu.VMEM((reach, 2 * heads, 2 * rows), F32),
            pltpu.SemaphoreType.DMA((5,)),
            pltpu.SemaphoreType.DMA((count,)),
            pltpu.SemaphoreType.DMA((count,)),
        ],
        compiler_params=pltpu.CompilerParams(
            collective_id=3, has_side_effects=True, vmem_limit_bytes=VMEM_BYTES
        ),
        name="attend_backward",
        cost_estimate=cost(70),
    )(*args[:11], *[view(v) for v in args[11:]], later.reshape(reach, 2, 2, rows, local))
    return [v.reshape(own, local) for v in (dq, dk, dv)], back


class Attention:
    def __init__(self, rows, heads, count, lo, pos, key):
        self.rows, self.heads, self.count = rows, heads, count
        self.tables = (lo, pos, key)
        full = 2 * rows
        self.block = pl.BlockSpec((2, 1, rows, HD), lambda s, h: (0, s, 0, h))
        self.part = lambda t: pl.BlockSpec((2, 1, rows, HD), lambda s, h: (t, s, 0, h))
        self.table_specs = lambda n: [
            pl.BlockSpec((1, full, 1), lambda s, h: (s, 0, 0)),
            pl.BlockSpec((full, 1), lambda s, h: (0, 0)),
            pl.BlockSpec((n, full), lambda s, h: (0, 0)),
        ]
        self.log_spec = pl.BlockSpec((1, full, 1), lambda s, h: (s * heads + h, 0, 0))
        self.params = pltpu.CompilerParams(vmem_limit_bytes=VMEM_BYTES)

    def shape(self, dtype):
        return jax.ShapeDtypeStruct((2, 2, self.rows, self.heads * HD), dtype)

    def view(self, v):
        return v.reshape(-1, 2, self.rows, v.shape[-1])

    def forward(self, q, key, value):
        count = self.count
        parts = [self.part(t) for t in range(count)]
        out, log = pl.pallas_call(
            functools.partial(attend_kernel, count, HD**-0.5),
            grid=(2, self.heads),
            in_specs=[self.block] + parts * 2 + self.table_specs(count),
            out_specs=[self.block, self.log_spec],
            out_shape=[self.shape(BF), jax.ShapeDtypeStruct((2 * self.heads, 2 * self.rows, 1), F32)],
            compiler_params=self.params,
            name="attend_forward",
            cost_estimate=cost(1),
        )(self.view(q), *[self.view(key)] * count, *[self.view(value)] * count, *self.tables)
        return out.reshape(q.shape), log


def rms_inverse(v):
    return lax.rsqrt(jnp.mean(v * v, axis=-1, keepdims=True) + EPS)


def rms_backward(v, gain, grad):
    inv = rms_inverse(v)
    turn = grad * gain
    inner = jnp.mean(v * turn, axis=-1, keepdims=True)
    return inv * turn - v * (inv * inv * inv) * inner


def total(refs):
    return sum(ref[...].astype(F32) for ref in refs)


def after_attention_kernel(*refs):
    inputs_ref, gain_ref, attn_ref, middle_ref, low_ref = refs[3:]
    attn = total(refs[:3])
    attn_ref[...] = attn
    middle = inputs_ref[...].astype(F32) + attn * rms_inverse(attn) * gain_ref[...]
    middle_ref[...] = middle
    low_ref[...] = middle.astype(BF)


def end_kernel(*refs):
    mid_ref, out_ref = refs[3:]
    out_ref[...] = mid_ref[...] + total(refs[:3])


def feed_kernel(*refs):
    (
        d_in_ref,
        d_out_ref,
        gu_out_ref,
        gu_in_ref,
        feed_gain_ref,
        attn_gain_ref,
        narrow_gu_ref,
        gated_any,
        gate_any,
        up_any,
        feed_any,
        down_any,
        middle_any,
        cot_any,
        attn_any,
        query_any,
        log_any,
    ) = refs[:17]
    result_ref, mid_ref, grad_attn_ref, back_gu_ref, maps_ref, gb_d_ref, later_any, later_log_any = refs[17:25]
    (
        down_w,
        gate_w,
        up_w,
        acts,
        blocks,
        own_pair,
        core_in,
        by_x,
        by_y,
        across_in,
        over_in,
        tokens,
        cot,
        dgu,
        narrow_d,
        back_d,
        load_sem,
        act_sem,
        free_sem,
        send_sem,
        recv_sem,
    ) = refs[25:]
    p, x, y, c = (lax.axis_index(a) for a in ("p", "x", "y", "c"))
    core, across, over = (p, x, y, 1 - c), (p, 1 - x, y, c), (p, x, 1 - y, c)
    rows, model = result_ref.shape
    size = rows // 2
    quarter = rows // 4
    hidden = down_w.shape[0]
    rank = d_in_ref.shape[0]
    copies = Copies(send_sem, recv_sem)

    def load(k, src, dst):
        copy = pltpu.make_async_copy(src, dst, load_sem.at[k])
        copy.start()
        return copy

    halves = (pl.ds(0, size), pl.ds(size, size))
    top = (pl.ds(0, quarter), pl.ds(size, quarter))
    low = (pl.ds(quarter, quarter), pl.ds(size + quarter, quarter))

    class Stream:
        def __init__(self, order, kinds):
            self.order, self.kinds, self.flight = order, kinds, []
            for _ in range(min(4, len(order))):
                self.fetch()

        def fetch(self):
            n = len(self.flight)
            if n < len(self.order):
                k, h = self.order[n]
                group = []
                for kind in self.kinds:
                    src = (gated_any, gate_any, up_any)[kind].at[pl.ds(2 * k, 2), halves[h]]
                    group.append(pltpu.make_async_copy(src, acts.at[n % 4, kind], act_sem.at[n % 4, kind]))
                    group[-1].start()
                self.flight.append(group)

        def slot(self, k, h):
            n = self.order.index((k, h))
            for copy in self.flight[n]:
                copy.wait()
            return n % 4

    def act(slot, kind, cols=slice(None)):
        return acts[slot, kind, :, :, cols].reshape(2 * size, -1)

    both = lambda order: [(k, h) for h in range(2) for k in order]
    stream = Stream(both((3, 1, 2, 0)), (0,))
    loaded = load(0, down_any, down_w)
    groups = feed_any.shape[0]
    depth = model // groups
    reach = later_any.shape[0]
    middle_load, cot_load = load(1, middle_any, tokens), load(2, cot_any, cot)
    feed_loads = []
    for k in range(groups):
        for n, dst in enumerate((gate_w, up_w)):
            src = feed_any.at[k, :, pl.ds(n * hidden, hidden)]
            feed_loads.append(load(4 + 2 * k + n, src, dst.at[pl.ds(k * depth, depth)]))
    ring = lax.axis_size("p")
    right, left = (lax.rem(p + 1, ring), x, y, c), (lax.rem(p + ring - 1, ring), x, y, c)
    barrier = pltpu.get_barrier_semaphore()
    for device in (core, across, over, right, left):
        pl.semaphore_signal(barrier, inc=1, device_id=device, device_id_type=pl.DeviceIdType.MESH)
    pl.semaphore_wait(barrier, 5)

    def pull(t):
        src = (query_any, log_any) if t == 0 else (later_any.at[t - 1], later_log_any.at[t - 1])
        return [copies.remote(src[0], later_any.at[t], left), copies.remote(src[1], later_log_any.at[t], left)]

    maps_ref[...] = jnp.zeros_like(maps_ref)
    gb_d_ref[...] = jnp.zeros_like(gb_d_ref)

    def part(k):
        return own_pair if k == 0 else blocks.at[pl.ds(2 * k, 2)]

    def store(k, h, cols, value):
        dst = part(k)
        dst[0, halves[h], cols] = value[:size].astype(BF)
        dst[1, halves[h], cols] = value[size:].astype(BF)

    def columns(n):
        return pl.ds(pl.multiple_of(n * 512, 512), 512)

    def forward(k, h):
        slot = stream.slot(k, h)
        here = 2 * k + h
        narrow_d[here] = dot_nt(act(slot, 0), d_in_ref[...]).astype(BF)

        def body(n, carry):
            cols = columns(n)
            value = dot(act(slot, 0), down_w[:, cols])
            store(k, h, cols, value + SCALE_ADAPT * dot(narrow_d[here], d_out_ref[:, cols]))
            return carry

        lax.fori_loop(0, model // 512, body, 0)
        stream.fetch()

    def taken(k, h):
        return blocks[2 * k : 2 * k + 2, halves[h], :].reshape(2 * size, model)

    def backward(k, h):
        slot = stream.slot(k, h)
        here = 2 * k + h
        low_d = dot_nt(taken(k, h), d_out_ref[...]).astype(BF)
        back_d[here] = low_d
        gb_d_ref[...] += SCALE_ADAPT * dot_tn(narrow_d[here], taken(k, h))

        def tile(t, carry):
            cols = pl.ds(pl.multiple_of(t * 256, 256), 256)
            dm = dot_nt(taken(k, h), down_w[cols, :]) + SCALE_ADAPT * dot(low_d, d_in_ref[:, cols])
            gate, up = act(slot, 1, cols).astype(F32), act(slot, 2, cols).astype(F32)
            sig = jax.nn.sigmoid(gate)
            silu = gate * sig
            dgu[here, 0, :, cols] = (dm * up * (sig + silu * (1.0 - sig))).astype(BF)
            dgu[here, 1, :, cols] = (dm * silu).astype(BF)
            return carry

        lax.fori_loop(0, hidden // 256, tile, 0)
        back_g = dot_nt(dgu[here, 0], gu_out_ref[0]).astype(BF)
        back_u = dot_nt(dgu[here, 1], gu_out_ref[1]).astype(BF)
        back = jnp.concatenate([back_g, back_u], axis=1)
        back_gu_ref[2 * k : 2 * k + 2, halves[h], :] = back.reshape(2, size, 2 * rank)

        def body(n, carry):
            cols = columns(n)
            value = dot_nt(dgu[here, 0], gate_w[cols, :]) + dot_nt(dgu[here, 1], up_w[cols, :])
            store(k, h, cols, value + SCALE_ADAPT * dot(back, gu_in_ref[:, cols]))
            return carry

        lax.fori_loop(0, model // 512, body, 0)
        stream.fetch()

    def adapter_maps():
        for k, h in stream.order:
            slot = stream.slot(k, h)
            here = 2 * k + h
            maps_ref[0] += SCALE_ADAPT * dot_tn(back_d[here], act(slot, 0))
            narrow = narrow_gu_ref[2 * k : 2 * k + 2, halves[h], :].reshape(2 * size, 2 * rank)
            for n in range(2):
                maps_ref[1 + n] += SCALE_ADAPT * dot_tn(narrow[:, n * rank : (n + 1) * rank], dgu[here, n])
            stream.fetch()

    def by_tiles(start, count, work):
        def body(n, carry):
            work(pl.multiple_of(n * 32, 32))
            return carry

        lax.fori_loop(start // 32, (start + count) // 32, body, 0)

    class Half:
        def __init__(self, h):
            self.h, self.met, self.parts, self.gone = h, {}, [], []

        def to_core(self, k):
            here = halves[self.h]
            self.met[k] = copies.remote(part(k).at[1, here], core_in.at[k, here], core)

        def meet(self, k):
            self.met[k].wait_recv()

            def work(start):
                tile = pl.ds(start, 32)
                blocks[2 * k, tile, :] = (
                    blocks[2 * k, tile, :].astype(F32) + core_in[k, tile, :].astype(F32)
                ).astype(BF)

            by_tiles(self.h * size, size, work)
            h = self.h
            if k == 3:
                self.far_x = copies.remote(blocks.at[6, top[h]], by_x.at[h], across)
                self.far_y = copies.remote(blocks.at[6, low[h]], by_y.at[h], over)
            if k == 1:
                self.parts.append(copies.remote(blocks.at[2, top[h]], across_in.at[top[h]], across))
            if k == 2:
                self.parts.append(copies.remote(blocks.at[4, low[h]], over_in.at[low[h]], over))

        def pass_far(self):
            h = self.h

            def add(block, start, more):
                def work(n):
                    here = pl.ds(n + start, 32)
                    blocks[block, here, :] = (
                        blocks[block, here, :].astype(F32) + more[h, pl.ds(n, 32), :].astype(F32)
                    ).astype(BF)

                by_tiles(0, quarter, work)

            self.far_y.wait_recv()
            add(2, h * size + quarter, by_y)
            self.parts.append(copies.remote(blocks.at[2, low[h]], across_in.at[low[h]], across))
            self.far_x.wait_recv()
            add(4, h * size, by_x)
            self.parts.append(copies.remote(blocks.at[4, top[h]], over_in.at[top[h]], over))

        def close(self, work):
            self.met[0].wait_recv()
            for copy in self.parts:
                copy.wait_recv()

            def body(start):
                tile = pl.ds(start, 32)
                total = own_pair[0, tile, :].astype(F32) + core_in[0, tile, :].astype(F32)
                work(tile, total + across_in[tile, :].astype(F32) + over_in[tile, :].astype(F32))

            by_tiles(self.h * size, size, body)

        def share(self):
            here = halves[self.h]
            self.to_x = copies.remote(blocks.at[0, here], blocks.at[2, here], across)
            self.to_y = copies.remote(blocks.at[0, here], blocks.at[4, here], over)
            self.to_c = copies.remote(blocks.at[0, here], blocks.at[1, here], core)

        def pass_x(self):
            h, here = self.h, halves[self.h]
            self.to_x.wait_recv()
            self.x_on = copies.remote(blocks.at[2, here], blocks.at[3, here], core)
            self.x_far = copies.remote(blocks.at[2, top[h]], blocks.at[6, top[h]], over)

        def pass_y(self):
            h, here = self.h, halves[self.h]
            self.to_y.wait_recv()
            self.y_on = copies.remote(blocks.at[4, here], blocks.at[5, here], core)
            self.y_far = copies.remote(blocks.at[4, low[h]], blocks.at[6, low[h]], across)

        def pass_on(self):
            here = halves[self.h]
            self.x_far.wait_recv()
            self.y_far.wait_recv()
            self.far_on = copies.remote(blocks.at[6, here], blocks.at[7, here], core)

        def ready(self, k):
            here = (self.to_c, getattr(self, "x_on", None), getattr(self, "y_on", None), getattr(self, "far_on", None))[k]
            here.wait_recv()
            gone = [] if k == 0 else [here]
            if k in (1, 2):
                gone.append(self.x_far if k == 1 else self.y_far)
            for copy in gone:
                copy.wait_send()
            self.gone += gone

    first, second = Half(0), Half(1)
    loaded.wait()
    forward(3, 0)
    first.to_core(3)
    forward(1, 0)
    first.to_core(1)
    first.meet(3)
    forward(2, 0)
    first.to_core(2)
    first.meet(1)
    forward(0, 0)
    first.to_core(0)
    first.meet(2)
    forward(3, 1)
    second.to_core(3)
    first.pass_far()
    forward(1, 1)
    second.to_core(1)
    second.meet(3)
    forward(2, 1)
    second.to_core(2)
    second.meet(1)
    forward(0, 1)
    second.to_core(0)
    second.meet(2)
    stream = Stream([(0, 0), (0, 1), (1, 0), (3, 0), (1, 1), (2, 0), (3, 1), (2, 1)], (0, 1, 2))
    middle_load.wait()
    cot_load.wait()

    def end(tile, feed):
        gain = feed_gain_ref[...]
        result_ref[tile, :] = (tokens[tile, :] + feed * rms_inverse(feed) * gain).astype(BF)
        blocks[0, tile, :] = rms_backward(feed, gain, cot[tile, :].astype(F32)).astype(BF)

    def free(half):
        for copy in [*half.met.values(), *half.parts, half.far_x, half.far_y]:
            copy.wait_send()
        for device in (core, across, over):
            pl.semaphore_signal(free_sem.at[half.h], inc=1, device_id=device, device_id_type=pl.DeviceIdType.MESH)

    first.close(end)
    free(first)
    pl.semaphore_wait(free_sem.at[0], 3)
    first.share()
    second.pass_far()
    second.close(end)
    free(second)
    pl.semaphore_wait(free_sem.at[1], 3)
    second.share()
    copies.all = [first.to_x, first.to_y, first.to_c, second.to_x, second.to_y, second.to_c]
    attn_load = load(3, attn_any, tokens)
    pulls = pull(0)
    for copy in feed_loads:
        copy.wait()
    for half in (first, second):
        half.met, half.parts = {}, []

    first.ready(0)
    backward(0, 0)
    first.to_core(0)
    first.pass_x()
    first.pass_y()
    second.ready(0)
    backward(0, 1)
    second.to_core(0)
    first.pass_on()
    first.ready(1)
    backward(1, 0)
    first.to_core(1)
    second.pass_x()
    second.pass_y()
    first.meet(1)
    for t in range(1, reach):
        for copy in pulls:
            copy.wait_recv()
        pulls = pull(t)
    first.ready(3)
    backward(3, 0)
    first.to_core(3)
    second.ready(1)
    backward(1, 1)
    second.to_core(1)
    first.meet(3)
    second.pass_on()
    first.ready(2)
    backward(2, 0)
    first.to_core(2)
    second.meet(1)
    second.ready(3)
    first.meet(2)
    backward(3, 1)
    second.to_core(3)
    first.pass_far()
    second.ready(2)
    second.meet(3)
    backward(2, 1)
    second.to_core(2)
    stream = Stream([(k, h) for k in range(4) for h in range(2)], (0,))
    attn_load.wait()

    def open_attention(tile, total):
        mid = cot[tile, :].astype(F32) + total
        mid_ref[tile, :] = mid
        grad_attn_ref[0, tile, :] = rms_backward(tokens[tile, :], attn_gain_ref[...], mid).astype(BF)

    def share_attention(h):
        here = halves[h]
        block = lambda k: grad_attn_ref.at[k, here]
        return copies.remote(block(0), block(2), across), copies.remote(block(0), block(1), core)

    def pass_attention(h, to_x):
        to_x.wait_recv()
        return copies.remote(grad_attn_ref.at[2, halves[h]], grad_attn_ref.at[3, halves[h]], core)

    second.meet(2)
    first.close(open_attention)
    to_x, to_c = share_attention(0)
    last = [to_c]
    second.pass_far()
    last.append(pass_attention(0, to_x))
    second.close(open_attention)
    to_x, to_c = share_attention(1)
    last.append(to_c)
    adapter_maps()
    last.append(pass_attention(1, to_x))
    for copy in last + pulls:
        copy.wait_recv()
    gone = first.gone + second.gone
    for copy in copies.all:
        if not any(copy is other for other in gone):
            copy.wait_send()


def feed_layer(maps, narrow_gu, acts, weights, middle, cot, attn_out, query, log, reach):
    rows, model = cot.shape
    groups, hidden = weights[0].shape[0], weights[1].shape[0]
    rank = maps[0].shape[0]
    vm = pl.BlockSpec(memory_space=pltpu.VMEM)
    anywhere = pl.BlockSpec(memory_space=pl.ANY)
    block = lambda *shape: pltpu.VMEM(shape, BF)
    count = 96 + 2 * reach
    return pl.pallas_call(
        feed_kernel,
        in_specs=[vm] * 7 + [anywhere] * 10,
        out_specs=[vm] * 6 + [anywhere] * 2,
        out_shape=[
            jax.ShapeDtypeStruct((rows, model), BF),
            jax.ShapeDtypeStruct((rows, model), F32),
            jax.ShapeDtypeStruct((4, rows, model), BF),
            jax.ShapeDtypeStruct((8, rows, 2 * rank), BF),
            jax.ShapeDtypeStruct((3, rank, hidden), F32),
            jax.ShapeDtypeStruct((rank, model), F32),
            jax.ShapeDtypeStruct((reach,) + query.shape, BF),
            jax.ShapeDtypeStruct((reach,) + log.shape, F32),
        ],
        scratch_shapes=[
            block(hidden, model),
            block(model, hidden),
            block(model, hidden),
            block(4, 3, 2, rows // 2, hidden),
            block(8, rows, model),
            block(2, rows, model),
            block(4, rows, model),
            block(2, rows // 4, model),
            block(2, rows // 4, model),
            block(rows, model),
            block(rows, model),
            pltpu.VMEM((rows, model), F32),
            block(rows, model),
            block(8, 2, rows, hidden),
            block(8, rows, rank),
            block(8, rows, rank),
            pltpu.SemaphoreType.DMA((2 * groups + 4,)),
            pltpu.SemaphoreType.DMA((4, 3)),
            pltpu.SemaphoreType.REGULAR((2,)),
            pltpu.SemaphoreType.DMA((count,)),
            pltpu.SemaphoreType.DMA((count,)),
        ],
        compiler_params=pltpu.CompilerParams(
            collective_id=2, has_side_effects=True, vmem_limit_bytes=60 * 1024 * 1024
        ),
        name="feed_layer",
        cost_estimate=cost(170),
    )(
        *maps,
        narrow_gu.reshape(8, rows, -1),
        *[v.reshape(8, rows, hidden) for v in acts],
        *weights,
        middle,
        cot,
        attn_out,
        query,
        log,
    )


def by_rows(kernel, name, rows, width, args, dtypes, us):
    tile = 64 if rows % 64 == 0 else rows
    spec = lambda v: pl.BlockSpec((1, width), lambda r: (0, 0)) if v.shape[0] == 1 else pl.BlockSpec((tile, width), lambda r: (r, 0))
    row = pl.BlockSpec((tile, width), lambda r: (r, 0))
    return pl.pallas_call(
        kernel,
        grid=(rows // tile,),
        in_specs=[spec(v) for v in args],
        out_specs=[row] * len(dtypes),
        out_shape=[jax.ShapeDtypeStruct((rows, width), d) for d in dtypes],
        compiler_params=pltpu.CompilerParams(vmem_limit_bytes=VMEM_BYTES),
        name=name,
        cost_estimate=cost(us),
    )(*args)


def on_device(
    layer_input,
    cotangent,
    document_length,
    adapter_choice_index,
    query_weight,
    key_weight,
    value_weight,
    output_weight,
    gate_weight,
    up_weight,
    down_weight,
    query_norm_gain,
    key_norm_gain,
    attention_norm_gain,
    feedforward_norm_gain,
    adapter_model_input_maps,
    adapter_down_input_maps,
    adapter_model_output_maps,
    adapter_hidden_output_maps,
):
    at = Place()
    rows = layer_input.shape[1]
    width = layer_input.shape[2]
    heads = width // HD // 4
    local = heads * HD
    rank = adapter_model_input_maps.shape[2]
    depth = query_weight.shape[0]
    hidden_rows = down_weight.shape[0]
    hidden = hidden_rows * at.np
    reach = WINDOW // (2 * rows)
    count = reach + 1

    def head_cols(v, quarter):
        return pick(v.reshape(v.shape[:-1] + (heads, 4, HD)), v.ndim, quarter).reshape(v.shape[:-1] + (local,))

    def hidden_cols(v):
        lead = v.shape[:-1]
        n = len(lead)
        v = v.reshape(lead + (at.np, 2, 2, 2, hidden_rows))
        v = pick(v, n + 3, at.c)
        v = pick(v, n + 2, at.y)
        return pick(v, n + 1, at.x).reshape(lead + (-1,))

    own_inputs = layer_input[0]
    head_offsets = lambda x, y, c: [4 * k + 2 * x + c for k in range(heads)]
    feed_offsets = lambda x, y, c: [((2 * p + x) * 2 + y) * 2 + c for p in range(at.np)]
    w_qkv, feed_piece, inputs, o_own = start(
        at.np,
        reach,
        pack(at.spot, [query_weight, key_weight, value_weight], HD, head_offsets, TURNS4),
        pack(at.spot, [gate_weight], hidden_rows, feed_offsets, TURNS8),
        pack(at.spot, [up_weight], hidden_rows, feed_offsets, TURNS8),
        own_inputs,
        output_weight,
    )
    w_gu = lax.all_gather(feed_piece, "p", axis=0)
    if 2 * depth == HD:
        sent = lambda target: lax.ppermute(o_own, ("y", "c"), target)
        same = at.y == at.c
        mine_half = jnp.where(same, o_own, sent([(0, 2), (3, 1)]))
        other_half = jnp.where(same, sent([(1, 0), (2, 3)]), sent([(1, 2), (2, 1)]))
        halves = [jnp.where(at.c == 0, mine_half, other_half), jnp.where(at.c == 0, other_half, mine_half)]
        w_o = jnp.stack([v.reshape(at.np, depth, width) for v in halves], axis=1).reshape(local, width)
    else:
        o_full = lax.all_gather(output_weight, ("p", "x", "y", "c"), axis=0, tiled=True)
        w_o = pick(o_full.reshape(heads, 4, HD, width), 1, at.quarter).reshape(local, width)
    selected = adapter_choice_index[0]
    a_model = pick(adapter_model_input_maps, 0, selected)
    a_hidden = pick(adapter_down_input_maps, 0, selected)
    b_model = pick(adapter_model_output_maps, 0, selected)
    b_hidden = pick(adapter_hidden_output_maps, 0, selected)
    a_qkv = a_model[:3].reshape(3 * rank, width)
    a_gu = a_model[4:6].reshape(2 * rank, width)
    a_o = head_cols(a_model[3], at.quarter)
    a_d = hidden_cols(a_hidden)
    b_qkv = head_cols(b_model[:3], at.quarter)
    b_o, b_d = b_model[3], b_model[4]
    b_gu = hidden_cols(b_hidden)

    def diagonal(maps):
        k, r, n = maps.shape
        zero = jnp.zeros((r, n), BF)
        return jnp.concatenate(
            [jnp.concatenate([maps[a] if a == b else zero for b in range(k)], axis=1) for a in range(k)], axis=0
        )

    b_qkv_diag = diagonal(b_qkv)
    gain = jnp.concatenate(
        [head_cols(query_norm_gain[None], at.quarter), head_cols(key_norm_gain[None], at.quarter)], axis=1
    )

    step_rows = jnp.arange(rows, dtype=jnp.int32)
    spot = lambda xx: at.p * 2 * rows + xx * rows + step_rows
    pos = jnp.concatenate([spot(at.x), spot(1 - at.x)])
    lengths = lax.dynamic_slice_in_dim(document_length, 2 * at.y, 2, 0)
    bounds = jnp.cumsum(lengths, axis=1)
    bounds = jnp.where(at.c == 0, bounds, bounds[::-1])

    def lo_of(pos):
        begin = jnp.max(jnp.where(bounds[:, None, :] <= pos[None, :, None], bounds[:, None, :], 0), axis=2)
        return jnp.maximum(begin, pos[None] - (WINDOW - 1))

    lo = lo_of(pos)
    key = jnp.stack([pos - 2 * rows * t for t in range(count)])
    attention = Attention(rows, heads, count, lo[:, :, None], pos[:, None], key)

    half_dim = HD // 2
    inv_freq = ROPE_BASE ** (-(jnp.arange(half_dim, dtype=F32) * 2.0 / HD))
    spots = jnp.concatenate([spot(at.x), spot(at.x), spot(1 - at.x), spot(1 - at.x)])
    angles = jnp.concatenate([spots - 2 * rows * t for t in range(count)]).astype(F32)[:, None] * inv_freq
    cos, sin = jnp.cos(angles), jnp.sin(angles)
    cos = jnp.concatenate([cos, cos], axis=1)
    sin = jnp.concatenate([-sin, sin], axis=1)

    own = 4 * rows
    pre_q, pre_k, value_all, narrow_qkv, square_q, square_k = project(
        inputs, own, w_qkv, a_qkv, b_qkv, heads
    )
    w_d = lax.all_gather(after(down_weight, square_q), "p", axis=0, tiled=True)
    squares = jnp.concatenate([square_q[:1], square_k[:1]], axis=1)
    inv = lax.rsqrt(at.sum4(squares, 2 + reach) / width + EPS).reshape(-1, 1)
    inv_q, inv_k = inv[:own], inv[own:]
    query, key_all = post(pre_q, pre_k, inv_q, inv_k, gain, cos, sin, heads)
    o, log = attention.forward(query, key_all, value_all)
    narrow_o = dot_nt(o, a_o).astype(BF)
    def attn_part(part, mark=None):
        ins, narrow = o[part], narrow_o[part]
        if mark is not None:
            ins = after(ins, mark)
        return (dot(ins, w_o) + SCALE_ADAPT * dot(narrow, b_o)).astype(BF)

    near_rows, far_rows = slice(0, 2 * rows), slice(2 * rows, 4 * rows)
    attn_parts = at.scatter4(attn_part(far_rows), lambda mark: attn_part(near_rows, mark))
    attn_gain, feed_gain = attention_norm_gain[None], feedforward_norm_gain[None]
    attn_out, middle, low = by_rows(
        after_attention_kernel,
        "after_attention",
        rows,
        width,
        [*attn_parts, own_inputs, attn_gain],
        [F32, F32, BF],
        4,
    )
    middle_low = jnp.concatenate(at.gather8(low)[0])
    narrow_gu = dot_nt(middle_low, a_gu).astype(BF)
    gate, up, gated = gate_up(middle_low, w_gu, narrow_gu, b_gu)
    result, grad_mid, grad_attn, back_gu, wide, gb_d, later, later_logs = feed_layer(
        (a_d, b_d, b_gu, a_gu, feed_gain, attn_gain),
        narrow_gu,
        (gated, gate, up),
        (w_gu, w_d),
        middle,
        cotangent[0],
        attn_out,
        query,
        log[:, :, 0],
        reach,
    )
    lo_rows = jnp.stack([lo_of(pos + 2 * rows * t) for t in range(count)])
    query_rows = jnp.stack([pos + 2 * rows * t for t in range(count)])
    (dq, dk, dv), back_o = attend_back(
        at.np,
        reach,
        heads,
        rows,
        [
            grad_attn.reshape(4 * rows, width),
            w_o,
            a_o,
            b_o,
            *attention.tables,
            lo_rows,
            query_rows,
            log,
            later_logs,
            query,
            key_all,
            value_all,
            o,
        ],
        later,
    )
    def share_y(mine, other):
        return mine + at.swap_y(other)

    def share_p(v):
        total = pick(v, 1, at.p)
        for by in range(1, at.np):
            total = total + at.turn_p(pick(v, 1, (at.p + by) % at.np), by)
        return total

    def sum_model(v):
        v = v.reshape(-1, at.np, 2, 2, 2 * depth)
        v = pick(v, 2, at.x) + at.swap_x(pick(v, 2, 1 - at.x))
        return share_y(pick(v, 2, at.y), pick(v, 2, 1 - at.y))

    mine = (jnp.arange(4) == at.quarter).astype(F32)

    def spread(v):
        return (v.reshape(-1, heads, 1, HD) * mine[:, None]).reshape(-1, width)

    back_gu, grad_attn = back_gu.reshape(8 * rows, -1), grad_attn.reshape(4 * rows, -1)
    ga_gu = SCALE_ADAPT * dot_tn(back_gu, middle_low)
    ga_o = SCALE_ADAPT * dot_tn(back_o, o)
    gb_o = SCALE_ADAPT * dot_tn(narrow_o, grad_attn)
    early = jnp.concatenate([ga_gu, spread(ga_o), gb_o, gb_d])
    wide = wide.reshape(3 * rank, -1)
    if 2 * depth == HD and hidden_rows == 2 * HD:
        grad_input, sums, wide = finish(
            at.np,
            heads,
            [
                dq,
                dk,
                dv,
                pre_q,
                pre_k,
                inv_q,
                inv_k,
                gain,
                cos,
                sin,
                a_qkv,
                b_qkv,
                narrow_qkv,
                early,
                wide,
            ],
            w_qkv,
            inputs,
            grad_mid,
        )
        sums, wide = sums.reshape(-1, rank, depth), wide.reshape(-1, rank, hidden_rows)
        early, late = sums[:5], sums[5:]
    else:
        early = sum_model(after(early, dq))
        inputs, narrow_qkv, pre_k, inv_k, cos, sin = (v[:own] for v in (inputs, narrow_qkv, pre_k, inv_k, cos, sin))
        wide = wide.reshape(-1, at.np, hidden_rows)
        dk = after(dk, early)
        turn, inner = unpost(dq, dk, pre_q, pre_k, gain, cos, sin, heads)
        inner = at.sum4(inner.T, 1).T / width

        def unnorm(part, pre, scale):
            cols = slice(part * local, (part + 1) * local)
            return (scale * turn[:, cols] - pre * (scale * scale * scale * inner[:, part : part + 1])).astype(BF)

        grad_qkv = jnp.concatenate(
            [unnorm(0, pre_q, inv_q), unnorm(1, pre_k, inv_k), dv.astype(BF)], axis=1
        )
        back_qkv = dot_nt(grad_qkv, b_qkv_diag).astype(BF)

        def late_adapters(mark):
            back = after(back_qkv, mark)
            ga_qkv = SCALE_ADAPT * dot_tn(back, inputs)
            gb_qkv = [
                SCALE_ADAPT * dot_tn(narrow_qkv[:, k * rank : (k + 1) * rank], grad_qkv[:, k * local : (k + 1) * local])
                for k in range(3)
            ]
            return sum_model(jnp.concatenate([ga_qkv, spread(jnp.concatenate(gb_qkv))]))

        def end_part(part, mark=None):
            ins, back = grad_qkv[part], back_qkv[part]
            if mark is not None:
                ins = after(ins, mark)
            return (dot_nt(ins, w_qkv) + SCALE_ADAPT * dot(back, a_qkv)).astype(BF)

        marks = []

        def end_near(mark):
            marks.append(mark)
            return end_part(near_rows, mark)

        end_parts = at.scatter4(end_part(far_rows), end_near)
        (grad_input,) = by_rows(end_kernel, "end", rows, width, [*end_parts, grad_mid], [F32], 3)
        late = late_adapters(marks[0])
        narrow_sums = share_p(jnp.concatenate([late, early], axis=0))
        narrow_sums = narrow_sums.reshape(narrow_sums.shape[0], 2, depth)
        sums = pick(narrow_sums, 1, at.c) + at.swap_core(pick(narrow_sums, 1, 1 - at.c))
        sums = sums.reshape(-1, rank, depth)
        late, early = sums[:6], sums[6:]
        wide = share_p(after(wide, marks[0])).reshape(-1, rank, hidden_rows)
    choose = (jnp.arange(adapter_model_input_maps.shape[0], dtype=jnp.int32) == selected).astype(F32)
    sum_a_model = choose[:, None, None, None] * jnp.concatenate([late[:3], early[2:3], early[:2]])[None]
    sum_a_hidden = choose[:, None, None] * wide[0][None]
    sum_b_model = choose[:, None, None, None] * jnp.concatenate([late[3:], early[3:]])[None]
    sum_b_hidden = choose[:, None, None, None] * wide[1:][None]
    return (result[None], grad_input[None], sum_a_model, sum_a_hidden, sum_b_model, sum_b_hidden)


def solution(mesh):
    grid = mesh.devices.reshape(mesh.shape["ctx"] // 2, 2, mesh.shape["wt"] // 2, 2)
    split = Mesh(grid, ("p", "x", "y", "c"))
    everyone = ("p", "x", "y", "c")
    rows = P(everyone, None)
    tokens = P(("y", "c"), ("p", "x"), None)
    placed = (tokens, tokens, P(), P()) + (rows,) * 7 + (P(),) * 8
    return jax.shard_map(
        on_device,
        mesh=split,
        in_specs=placed,
        out_specs=(
            tokens,
            tokens,
            P(None, None, None, everyone),
            P(None, None, everyone),
            P(None, None, None, everyone),
            P(None, None, None, everyone),
        ),
        check_vma=False,
    )
```

```python
import functools

import jax
import jax.numpy as jnp
from jax import lax
from jax.experimental import pallas as pl
from jax.experimental.pallas import tpu as pltpu
from jax.sharding import Mesh
from jax.sharding import PartitionSpec as P

HD = 128
WINDOW = 1024
SCALE_ADAPT = 0.5
ROPE_BASE = 500000.0
EPS = 1e-06
BF = jnp.bfloat16
F32 = jnp.float32
VMEM_BYTES = 56 * 1024 * 1024


def cost(us):
    return pl.CostEstimate(flops=int(us * 1.1e9), bytes_accessed=int(us * 1e6), transcendentals=0)


def dot(a, b, dims=((1,), (0,))):
    return lax.dot_general(a, b, (dims, ((), ())), preferred_element_type=F32)


def dot_nt(a, b):
    return dot(a, b, ((1,), (1,)))


def dot_tn(a, b):
    return dot(a, b, ((0,), (0,)))


SWAP = [(0, 1), (1, 0)]


class Place:
    def __init__(self):
        self.np = lax.axis_size("p")
        self.p, self.x, self.y, self.c = (lax.axis_index(a) for a in ("p", "x", "y", "c"))
        self.quarter = 2 * self.x + self.c
        self.spot = jnp.stack([self.x, self.y, self.c]).astype(jnp.int32)

    def swap_core(self, value):
        return lax.ppermute(value, "c", SWAP)

    def swap_x(self, value):
        return lax.ppermute(value, "x", SWAP)

    def swap_both(self, value):
        return lax.ppermute(value, ("x", "c"), [(0, 3), (1, 2), (2, 1), (3, 0)])

    def swap_y(self, value):
        return lax.ppermute(value, "y", SWAP)

    def shift_p(self, value, by):
        return lax.ppermute(value, "p", [(p, p + by) for p in range(self.np) if 0 <= p + by < self.np])

    def turn_p(self, value, by):
        return lax.ppermute(value, "p", [(p, (p + by) % self.np) for p in range(self.np)])

    def gather4(self, own):
        across = self.swap_x(own)
        return self.paired(own), self.paired(across)

    def paired(self, block):
        return jnp.concatenate([block, self.swap_core(block)], axis=0)

    def gather8(self, own, work=None):
        half = own.shape[0] // 2
        across, over = self.swap_x(own), self.swap_y(own)
        first = self.paired(own)
        done = None
        if work is not None:
            done = work(first)
            across, over = after(across, done[0]), after(over, done[0])
        far = jnp.concatenate([self.swap_y(across[:half]), self.swap_x(over[half:])])
        return (first, self.paired(across), self.paired(over), self.paired(far)), done

    def met(self, pair):
        rows = pair.shape[0] // 2
        return (pair[:rows].astype(F32) + self.swap_core(pair[rows:]).astype(F32)).astype(BF)

    def scatter4(self, second, first):
        met = self.met(second)
        across = self.swap_x(met)
        first = first(met)
        return first, self.swap_core(first[first.shape[0] // 2 :]), across

    def scatter8(self, second, third, fourth, first):
        far = self.met(fourth)
        half = far.shape[0] // 2
        by_x, by_y = self.swap_x(far[:half]), self.swap_y(far[half:])
        second, third = self.met(second), self.met(third)
        add = lambda u, v: (u.astype(F32) + v.astype(F32)).astype(BF)
        across = [self.swap_x(second[:half]), self.swap_x(add(second[half:], by_y))]
        over = [self.swap_y(add(third[:half], by_x)), self.swap_y(third[half:])]
        first = first(far)
        core = self.swap_core(first[first.shape[0] // 2 :])
        return first, core, jnp.concatenate(across), jnp.concatenate(over)

    def sum4(self, value, parts):
        def reordered(v, x, c):
            v = v.reshape(v.shape[0], parts, 2, 2, -1)
            if x:
                v = jnp.concatenate([v[:, :, 1:], v[:, :, :1]], axis=2)
            if c:
                v = jnp.concatenate([v[:, :, :, 1:], v[:, :, :, :1]], axis=3)
            return v.reshape(value.shape)

        core, across, both = self.swap_core(value), self.swap_x(value), self.swap_both(value)
        return value + reordered(core, 0, 1) + reordered(across, 1, 0) + reordered(both, 1, 1)


def pick(v, axis, index):
    return lax.dynamic_index_in_dim(v, index, axis, keepdims=False)


def after(value, *others):
    return lax.optimization_barrier((value,) + others)[0]


class Copies:
    def __init__(self, send_sem, recv_sem):
        self.sems, self.used, self.all = (send_sem, recv_sem), 0, []

    def remote(self, src, dst, device):
        k = self.used
        self.used += 1
        copy = pltpu.make_async_remote_copy(
            src_ref=src,
            dst_ref=dst,
            send_sem=self.sems[0].at[k],
            recv_sem=self.sems[1].at[k],
            device_id=device,
            device_id_type=pl.DeviceIdType.MESH,
        )
        copy.start()
        self.all.append(copy)
        return copy

    def finish(self):
        for copy in self.all:
            copy.wait_send()


def pack_kernel(count, width, offsets, turns, spot_ref, *refs):
    spot = [spot_ref[k] for k in range(3)]
    for out, turn in zip(refs[count:], turns):
        places = offsets(*[(s + t) % 2 for s, t in zip(spot, turn)])
        for w, ref in enumerate(refs[:count]):
            for k, place in enumerate(places):
                at = (w * len(places) + k) * width
                out[:, at : at + width] = ref[:, pl.ds(pl.multiple_of(place * width, HD), width)]


def pack(spot, weights, width, offsets, turns):
    rows = weights[0].shape[0]
    size = len(weights) * len(offsets(0, 0, 0)) * width
    if width % HD:
        outs = []
        for turn in turns:
            places = offsets(*[(spot[k] + turn[k]) % 2 for k in range(3)])
            cuts = [lax.dynamic_slice_in_dim(w, place * width, width, 1) for w in weights for place in places]
            outs.append(jnp.concatenate(cuts, axis=1))
        return outs
    whole = pl.BlockSpec(memory_space=pltpu.VMEM)
    return pl.pallas_call(
        functools.partial(pack_kernel, len(weights), width, offsets, turns),
        in_specs=[pl.BlockSpec(memory_space=pltpu.SMEM)] + [whole] * len(weights),
        out_specs=[whole] * len(turns),
        out_shape=[jax.ShapeDtypeStruct((rows, size), BF)] * len(turns),
        compiler_params=pltpu.CompilerParams(vmem_limit_bytes=VMEM_BYTES),
        name="pack_columns",
        cost_estimate=cost(3),
    )(spot, *weights)


TURNS8 = [(dx, dy, dc) for dy in range(2) for dx in range(2) for dc in range(2)]
TURNS4 = TURNS8[:4]


def start_kernel(groups, reach, raw, *refs):
    p, x, y, c = (lax.axis_index(a) for a in ("p", "x", "y", "c"))
    if raw:
        sources, x_ref, o_ref = refs[0:5], refs[5], refs[6]
        w_ref, feed_ref, all_ref, o_all_ref, local_sem, send_sem, recv_sem = refs[7:14]
        whole, (qkv_packs, feed_all), load_sem = refs[14:19], refs[19:21], refs[21]
        loads = [pltpu.make_async_copy(sources[k], whole[k], load_sem.at[k]) for k in range(5)]
        for load in loads:
            load.start()
        qkv_pack = [qkv_packs.at[d] for d in range(4)]
        feed_packs = [[feed_all.at[k, d] for d in range(8)] for k in range(2)]

        def packed(kinds, offsets, turns, width, dst):
            for kind in kinds:
                loads[kind].wait()
            for d, turn in enumerate(turns):
                places = offsets(*[(u + t) % 2 for u, t in zip((x, y, c), turn)])
                for w, kind in enumerate(kinds):
                    for k, place in enumerate(places):
                        at = (w * len(places) + k) * width
                        cut = whole[kind][:, pl.ds(pl.multiple_of(place * width, HD), width)]
                        dst[d, :, at : at + width] = cut

    else:
        qkv_pack, feed_packs, x_ref, o_ref = refs[0:4], (refs[4:12], refs[12:20]), refs[20], refs[21]
        w_ref, feed_ref, all_ref, o_all_ref, local_sem, send_sem, recv_sem = refs[22:]
    turned = lambda u, t: 1 - u if t else u
    group = [(p, turned(x, dx), turned(y, dy), turned(c, dc)) for dx, dy, dc in TURNS8]
    core, across, over = group[1], group[2], group[4]
    right, left = (lax.rem(p + 1, groups), x, y, c), (lax.rem(p + groups - 1, groups), x, y, c)
    rows, depth, hidden = x_ref.shape[0], qkv_pack[0].shape[0], feed_packs[0][0].shape[1]
    used = [0]

    def remote(src, dst, device):
        k = used[0]
        used[0] += 1
        copy = pltpu.make_async_remote_copy(
            src_ref=src,
            dst_ref=dst,
            send_sem=send_sem.at[k],
            recv_sem=recv_sem.at[k],
            device_id=device,
            device_id_type=pl.DeviceIdType.MESH,
        )
        copy.start()
        return copy

    def local(k, src, dst):
        copy = pltpu.make_async_copy(src, dst, local_sem.at[k])
        copy.start()
        return copy

    barrier = pltpu.get_barrier_semaphore()
    for device in group[1:] + [right, left]:
        pl.semaphore_signal(barrier, inc=1, device_id=device, device_id_type=pl.DeviceIdType.MESH)
    pl.semaphore_wait(barrier, 9)

    def at(ref, start, size):
        return ref.at[pl.ds(pl.multiple_of(start, 16), size)]

    def tokens(t, block):
        return all_ref.at[pl.ds((4 * t + block) * rows, rows)]

    def owned(q):
        return w_ref.at[lax.rem(p + 2 * groups - q, groups), :, y]

    slot = (4 * x + 2 * y + c) * depth
    mine = [
        w_ref.at[p, x, y, pl.ds(pl.multiple_of(c * depth, 16), depth)],
        feed_ref.at[pl.ds(pl.multiple_of(slot, 16), depth), pl.ds(0, hidden)],
        feed_ref.at[pl.ds(pl.multiple_of(slot, 16), depth), pl.ds(hidden, hidden)],
    ]
    firsts = (qkv_pack[0], feed_packs[0][0], feed_packs[1][0])
    if raw:
        packed((0, 1, 2), raw[0], TURNS4, HD, qkv_packs)
    kept = [local(0, firsts[0], mine[0]), local(3, x_ref, tokens(0, 0))]
    kept.append(local(4, o_ref, o_all_ref.at[p]))
    o_of = lambda q: o_all_ref.at[lax.rem(p + 2 * groups - q, groups)]
    regrouped = [remote(qkv_pack[d], mine[0], group[d]) for d in (1, 2, 3)]
    moves = [remote(x_ref, tokens(1, 0), right)]
    sent = list(regrouped) + moves
    if raw:
        for k in range(2):
            packed((3 + k,), raw[1], TURNS8, feed_all.shape[3] // groups, feed_all.at[k])
    kept += [local(k, firsts[k], mine[k]) for k in (1, 2)]
    kept[0].wait()
    for copy in regrouped:
        copy.wait_recv()
    along = remote(owned(0), owned(0), right)
    o_along = remote(o_ref, o_of(0), right)
    sent.append(o_along)
    later = [remote(owned(0), owned(0), over)]
    spread = [(remote(x_ref, tokens(0, 1), core), remote(x_ref, tokens(0, 2), across))]
    for k in (1, 2):
        later += [remote(feed_packs[k - 1][d], mine[k], group[d]) for d in range(1, 8)]
    sent.append(along)
    step = 1
    ready = 0

    def pass_on(t):
        spread[t][1].wait_recv()
        later.append(remote(tokens(t, 2), tokens(t, 3), core))

    while step < groups or ready <= reach:
        if ready < reach:
            moves[ready].wait_recv()
            if ready + 1 < reach:
                moves.append(remote(tokens(ready + 1, 0), tokens(ready + 2, 0), right))
                sent.append(moves[-1])
            spread.append(
                (
                    remote(tokens(ready + 1, 0), tokens(ready + 1, 1), core),
                    remote(tokens(ready + 1, 0), tokens(ready + 1, 2), across),
                )
            )
        if step < groups:
            along.wait_recv()
            if step < groups - 1:
                along = remote(owned(step), owned(step), right)
                sent.append(along)
            later.append(remote(owned(step), owned(step), over))
            o_along.wait_recv()
            if step < groups - 1:
                o_along = remote(o_of(step), o_of(step), right)
                sent.append(o_along)
            step += 1
        if ready <= reach:
            pass_on(ready)
            ready += 1
    for near, far in spread:
        near.wait_recv()
        sent += [near, far]
    for copy in later:
        copy.wait_recv()
    for copy in sent + later:
        copy.wait_send()
    for copy in kept[1:]:
        copy.wait()


def start(groups, reach, spot, weights, offsets, width, own_inputs, own_o):
    depth = weights[0].shape[0]
    rows, model = own_inputs.shape
    size = 3 * len(offsets[0](0, 0, 0)) * HD
    hidden = len(offsets[1](0, 0, 0)) * width
    copies = 3 + 1 + 1 + 1 + 14 + (groups - 1) + (groups - 2) + (groups - 1) + (reach - 1) + 2 * (reach + 1) + (reach + 1)
    anywhere = pl.BlockSpec(memory_space=pl.ANY)
    scratch = [
        pltpu.SemaphoreType.DMA((5,)),
        pltpu.SemaphoreType.DMA((copies,)),
        pltpu.SemaphoreType.DMA((copies,)),
    ]
    raw = None
    if width % HD == 0:
        raw = offsets
        scratch += [pltpu.VMEM(w.shape, BF) for w in weights]
        scratch += [pltpu.VMEM((4, depth, size), BF), pltpu.VMEM((2, 8, depth, hidden), BF)]
        scratch.append(pltpu.SemaphoreType.DMA((5,)))
    else:
        weights = [
            *pack(spot, weights[:3], HD, offsets[0], TURNS4),
            *pack(spot, weights[3:4], width, offsets[1], TURNS8),
            *pack(spot, weights[4:5], width, offsets[1], TURNS8),
        ]
    weight, feed, inputs, o_all = pl.pallas_call(
        functools.partial(start_kernel, groups, reach, raw),
        in_specs=[anywhere] * (len(weights) + 2),
        out_specs=[anywhere] * 4,
        out_shape=[
            jax.ShapeDtypeStruct((groups, 2, 2, 2 * depth, size), BF),
            jax.ShapeDtypeStruct((8 * depth, 2 * hidden), BF),
            jax.ShapeDtypeStruct((4 * (reach + 1) * rows, model), BF),
            jax.ShapeDtypeStruct((groups,) + own_o.shape, BF),
        ],
        scratch_shapes=scratch,
        compiler_params=pltpu.CompilerParams(
            collective_id=0, has_side_effects=True, vmem_limit_bytes=VMEM_BYTES
        ),
        name="start",
        cost_estimate=cost(120),
    )(*weights, own_inputs, own_o)
    return weight.reshape(-1, size), feed, inputs, o_all.reshape(-1, model)


def gate_up_kernel(x_ref, gate_w_ref, up_w_ref, narrow_ref, maps_ref, gate_ref, up_ref, gated_ref):
    rank, tile = maps_ref.shape[1:]
    gate_w, up_w = gate_w_ref[...].reshape(-1, tile), up_w_ref[...].reshape(-1, tile)
    gate = dot(x_ref[...], gate_w) + SCALE_ADAPT * dot(narrow_ref[:, :rank], maps_ref[0])
    up = dot(x_ref[...], up_w) + SCALE_ADAPT * dot(narrow_ref[:, rank:], maps_ref[1])
    gate_ref[...] = gate.astype(BF)
    up_ref[...] = up.astype(BF)
    gated_ref[...] = (gate * jax.nn.sigmoid(gate) * up).astype(BF)


def gate_up(x, weight, narrow, maps):
    rows, width = x.shape
    groups = weight.shape[0]
    hidden = weight.shape[2] // 2
    tile = 256
    steps = hidden // tile
    out = pl.BlockSpec((rows, tile), lambda s: (0, s))
    return pl.pallas_call(
        gate_up_kernel,
        grid=(steps,),
        in_specs=[
            pl.BlockSpec((rows, width), lambda s: (0, 0)),
            pl.BlockSpec((groups, width // groups, tile), lambda s: (0, 0, s)),
            pl.BlockSpec((groups, width // groups, tile), lambda s: (0, 0, s + steps)),
            pl.BlockSpec(narrow.shape, lambda s: (0, 0)),
            pl.BlockSpec(maps.shape[:2] + (tile,), lambda s: (0, 0, s)),
        ],
        out_specs=[out] * 3,
        out_shape=[jax.ShapeDtypeStruct((rows, hidden), BF)] * 3,
        compiler_params=pltpu.CompilerParams(vmem_limit_bytes=VMEM_BYTES),
        name="gate_up",
        cost_estimate=cost(1),
    )(x, weight, weight, narrow, maps)


def project_kernel(heads, own_tiles, x_ref, w_ref, in_maps_ref, out_maps_ref, *out_refs):
    pre_q_ref, pre_k_ref, value_ref, narrow_ref, square_q_ref, square_k_ref = out_refs
    width = heads * HD
    rank = out_maps_ref.shape[1]
    narrow_ref[...] = dot_nt(x_ref[...], in_maps_ref[...]).astype(BF)

    def part(k):
        cols = slice(k * width, (k + 1) * width)
        return dot(x_ref[...], w_ref[:, cols]) + SCALE_ADAPT * dot(narrow_ref[:, k * rank : (k + 1) * rank], out_maps_ref[k])

    ones = jnp.ones((8, width), BF)
    key = part(1)
    pre_k_ref[...] = key
    square_k_ref[...] = dot_nt(ones, (key * key).astype(BF))
    value_ref[...] = part(2).astype(BF)

    @pl.when(pl.program_id(0) < own_tiles)
    def _():
        query = part(0)
        pre_q_ref[...] = query
        square_q_ref[...] = dot_nt(ones, (query * query).astype(BF))


def project(x, own_rows, weight, in_maps, out_maps, heads):
    rows, width = x.shape
    local = heads * HD
    tile = 512
    own_tiles = own_rows // tile
    fixed = lambda v: pl.BlockSpec(v.shape, lambda t: (0,) * v.ndim)
    row = lambda n: pl.BlockSpec((tile, n), lambda t: (t, 0))
    return pl.pallas_call(
        functools.partial(project_kernel, heads, own_tiles),
        grid=(rows // tile,),
        in_specs=[row(width), fixed(weight), fixed(in_maps), fixed(out_maps)],
        out_specs=[
            pl.BlockSpec((tile, local), lambda t: (jnp.minimum(t, own_tiles - 1), 0)),
            row(local),
            row(local),
            row(in_maps.shape[0]),
            pl.BlockSpec((8, tile), lambda t: (0, jnp.minimum(t, own_tiles - 1))),
            pl.BlockSpec((8, tile), lambda t: (0, t)),
        ],
        out_shape=[
            jax.ShapeDtypeStruct((own_rows, local), F32),
            jax.ShapeDtypeStruct((rows, local), F32),
            jax.ShapeDtypeStruct((rows, local), BF),
            jax.ShapeDtypeStruct((rows, in_maps.shape[0]), BF),
            jax.ShapeDtypeStruct((8, own_rows), F32),
            jax.ShapeDtypeStruct((8, rows), F32),
        ],
        compiler_params=pltpu.CompilerParams(vmem_limit_bytes=VMEM_BYTES),
        name="project",
        cost_estimate=cost(1),
    )(x, weight, in_maps, out_maps)


def scales_kernel(model, q_ref, k_ref, inv_q_ref, inv_k_ref, mine, others, send_sem, recv_sem):
    p, x, y, c = (lax.axis_index(a) for a in ("p", "x", "y", "c"))
    devices = ((p, x, y, 1 - c), (p, 1 - x, y, c), (p, 1 - x, y, 1 - c))
    lines, wide = mine.shape
    half = wide // 2
    q_lines = q_ref.shape[1] // wide
    copies = Copies(send_sem, recv_sem)
    barrier = pltpu.get_barrier_semaphore()
    for device in devices:
        pl.semaphore_signal(barrier, inc=1, device_id=device, device_id_type=pl.DeviceIdType.MESH)
    for n in range(lines):
        src, at = (q_ref, n) if n < q_lines else (k_ref, n - q_lines)
        mine[n : n + 1, :] = src[:1, at * wide : (at + 1) * wide]
    pl.semaphore_wait(barrier, 3)
    moves = [copies.remote(mine, others.at[k], device) for k, device in enumerate(devices)]
    swap_lanes = lambda v: jnp.concatenate([v[:, half:], v[:, :half]], axis=1)
    swap_lines = lambda v: jnp.concatenate([v[n ^ 1 : (n ^ 1) + 1] for n in range(lines)], axis=0)
    for move in moves:
        move.wait_recv()
    total = mine[...] + swap_lanes(others[0]) + swap_lines(others[1]) + swap_lines(swap_lanes(others[2]))
    inv = lax.rsqrt(total / model + EPS).T
    for n in range(lines):
        out, at = (inv_q_ref, n) if n < q_lines else (inv_k_ref, n - q_lines)
        out[at * wide : (at + 1) * wide, :] = inv[:, n : n + 1]
    copies.finish()


def scales(square_q, square_k, model, wide):
    lines = (square_q.shape[1] + square_k.shape[1]) // wide
    vm = pl.BlockSpec(memory_space=pltpu.VMEM)
    return pl.pallas_call(
        functools.partial(scales_kernel, model),
        in_specs=[vm] * 2,
        out_specs=[vm] * 2,
        out_shape=[jax.ShapeDtypeStruct((v.shape[1], 1), F32) for v in (square_q, square_k)],
        scratch_shapes=[
            pltpu.VMEM((lines, wide), F32),
            pltpu.VMEM((3, lines, wide), F32),
            pltpu.SemaphoreType.DMA((3,)),
            pltpu.SemaphoreType.DMA((3,)),
        ],
        compiler_params=pltpu.CompilerParams(collective_id=4, has_side_effects=True),
        name="scales",
        cost_estimate=cost(1),
    )(square_q, square_k)


def rotation(row_ref, block_ref, b):
    here = slice(b, b + 1) if isinstance(b, int) else pl.ds(b, 1)
    cos, sin = block_ref[0, here, :], block_ref[1, here, :]
    return cos * row_ref[0] - sin * row_ref[1], sin * row_ref[2] + cos * row_ref[3]


def post_kernel(heads, own_tiles, q_ref, k_ref, inv_q_ref, inv_k_ref, gain_ref, row_ref, block_ref, q_out, k_out):
    width = heads * HD
    cos, sin = rotation(row_ref, block_ref, pl.program_id(0))

    def turn(pre_ref, inv, part, out_ref):
        for h in range(heads):
            cols = slice(h * HD, (h + 1) * HD)
            v = pre_ref[:, cols] * inv * gain_ref[:, part * width + h * HD : part * width + (h + 1) * HD]
            out_ref[:, cols] = (v * cos + pltpu.roll(v, HD // 2, 1) * sin).astype(BF)

    turn(k_ref, inv_k_ref[...], 1, k_out)

    @pl.when(pl.program_id(0) < own_tiles)
    def _():
        turn(q_ref, inv_q_ref[...], 0, q_out)


def post(pre_q, pre_k, inv_q, inv_k, gain, row_tables, block_tables, heads):
    rows, width = pre_k.shape
    tile = row_tables.shape[1]
    own_tiles = pre_q.shape[0] // tile
    row = lambda n: pl.BlockSpec((tile, n), lambda r: (r, 0))
    own = lambda n: pl.BlockSpec((tile, n), lambda r: (jnp.minimum(r, own_tiles - 1), 0))
    return pl.pallas_call(
        functools.partial(post_kernel, heads, own_tiles),
        grid=(rows // tile,),
        in_specs=[
            own(width),
            row(width),
            own(1),
            row(1),
            pl.BlockSpec((1, 2 * width), lambda r: (0, 0)),
            pl.BlockSpec(row_tables.shape, lambda r: (0, 0, 0)),
            pl.BlockSpec(block_tables.shape, lambda r: (0, 0, 0)),
        ],
        out_specs=[own(width), row(width)],
        out_shape=[jax.ShapeDtypeStruct(pre_q.shape, BF), jax.ShapeDtypeStruct(pre_k.shape, BF)],
        name="rope_forward",
        cost_estimate=cost(1),
    )(pre_q, pre_k, inv_q, inv_k, gain, row_tables, block_tables)


def unpost_kernel(heads, dq_ref, dk_ref, pre_q_ref, pre_k_ref, gain_ref, cos_ref, sin_ref, turn_ref, inner_ref):
    width = heads * HD
    cos, sin = cos_ref[...], sin_ref[...]
    for part, (d_ref, pre_ref) in enumerate(((dq_ref, pre_q_ref), (dk_ref, pre_k_ref))):
        total = None
        for h in range(heads):
            cols = slice(part * width + h * HD, part * width + (h + 1) * HD)
            v = d_ref[:, h * HD : (h + 1) * HD]
            turned = (v * cos - pltpu.roll(v, HD // 2, 1) * sin) * gain_ref[:, cols]
            turn_ref[:, cols] = turned
            inner = jnp.sum(turned * pre_ref[:, h * HD : (h + 1) * HD], axis=1, keepdims=True)
            total = inner if total is None else total + inner
        inner_ref[:, part : part + 1] = total


def unpost(dq, dk, pre_q, pre_k, gain, cos, sin, heads):
    rows, width = dq.shape
    tile = 256
    row = lambda n: pl.BlockSpec((tile, n), lambda r: (r, 0))
    return pl.pallas_call(
        functools.partial(unpost_kernel, heads),
        grid=(rows // tile,),
        in_specs=[row(width)] * 4 + [pl.BlockSpec((1, 2 * width), lambda r: (0, 0)), row(HD), row(HD)],
        out_specs=[row(2 * width), row(2)],
        out_shape=[jax.ShapeDtypeStruct((rows, 2 * width), F32), jax.ShapeDtypeStruct((rows, 2), F32)],
        name="rope_backward",
        cost_estimate=cost(8),
    )(dq, dk, pre_q, pre_k, gain, cos, sin)


def finish_kernel(groups, heads, early_rows, *refs):
    (
        dq_ref,
        dk_ref,
        dv_ref,
        pre_q_ref,
        pre_k_ref,
        inv_q_ref,
        inv_k_ref,
        gain_ref,
        row_ref,
        block_ref,
        in_maps_ref,
        out_maps_ref,
        narrow_ref,
        early_ref,
        wide_ref,
        choose_ref,
        weight_any,
        inputs_any,
        mid_any,
    ) = refs[:19]
    out_ref, a_model_ref, a_hidden_ref, b_model_ref, b_hidden_ref = refs[19:24]
    (
        weight,
        inputs,
        mid,
        turn,
        grad,
        back,
        stat,
        stat_in,
        far,
        near,
        core_in,
        met,
        across_in,
        near_in,
        maps,
        maps_in,
        by_x,
        by_y,
        by_y_in,
        by_p_in,
        own_sum,
        own_sum_in,
        wide_in,
        local_sem,
        send_sem,
        recv_sem,
    ) = refs[24:]
    p, x, y, c = (lax.axis_index(a) for a in ("p", "x", "y", "c"))
    core, across, both, over = (p, x, y, 1 - c), (p, 1 - x, y, c), (p, 1 - x, y, 1 - c), (p, x, 1 - y, c)
    others = [lax.rem(p + s, groups) for s in range(1, groups)]
    width = heads * HD
    rows = out_ref.shape[0]
    model = out_ref.shape[1]
    rank = out_maps_ref.shape[1]
    copies = Copies(send_sem, recv_sem)
    loads = []
    for k, (src, dst) in enumerate(((weight_any, weight), (inputs_any.at[pl.ds(0, 4 * mid.shape[0])], inputs), (mid_any, mid))):
        loads.append(pltpu.make_async_copy(src, dst, local_sem.at[k]))
        loads[-1].start()

    barrier = pltpu.get_barrier_semaphore()
    for device in [core, across, both, over] + [(q, x, y, c) for q in others]:
        pl.semaphore_signal(barrier, inc=1, device_id=device, device_id_type=pl.DeviceIdType.MESH)

    ones = jnp.ones((8, HD), BF)

    def unturn(b, carry):
        here = pl.ds(pl.multiple_of(b * rows, rows), rows)
        cos, sin = rotation(row_ref, block_ref, b)
        for part, pre_ref in enumerate((pre_q_ref, pre_k_ref)):
            product = None
            for h in range(heads):
                cols = slice(h * HD, (h + 1) * HD)
                wide_cols = slice(part * width + h * HD, part * width + (h + 1) * HD)
                v = dq_ref[here, cols] if part == 0 else dk_ref[here, cols]
                turned = (v * cos - pltpu.roll(v, HD // 2, 1) * sin) * gain_ref[:, wide_cols]
                turn[here, wide_cols] = turned
                term = turned * pre_ref[here, cols]
                product = term if product is None else product + term
            high = product.astype(BF)
            low = (product - high.astype(F32)).astype(BF)
            summed = dot_nt(ones, high) + dot_nt(ones, low)
            stat[part : part + 1, here] = summed[:1, :]
        grad[here, 2 * width :] = dv_ref[here, :].astype(BF)
        return carry

    stat[...] = jnp.zeros_like(stat)
    lax.fori_loop(0, 4, unturn, 0)
    for b in range(2 * groups):
        maps[b, :early_rows, :] = early_ref[:, b * 256 : (b + 1) * 256]
    pl.semaphore_wait(barrier, 3 + groups)
    stats = [copies.remote(stat, stat_in.at[k], device) for k, device in enumerate((core, across, both))]
    early = pl.ds(0, early_rows)
    exchanged = [copies.remote(maps.at[2 * q + 1 - x, early], maps_in.at[q, early], across) for q in range(groups)]
    wides = [
        copies.remote(wide_ref.at[:, pl.ds(pl.multiple_of(q * 256, 256), 256)], wide_in.at[k], (q, x, y, c))
        for k, q in enumerate(others)
    ]
    for copy in stats:
        copy.wait_recv()

    for b in range(4):
        here = slice(b * rows, (b + 1) * rows)
        total_row = stat[:, here]
        for k in range(3):
            d = b ^ (k + 1)
            total_row = total_row + stat_in[k, :, d * rows : (d + 1) * rows]
        inner = total_row.T / model
        for part, (pre_ref, inv_ref) in enumerate(((pre_q_ref, inv_q_ref), (pre_k_ref, inv_k_ref))):
            cols = slice(part * width, (part + 1) * width)
            inv = inv_ref[here, :]
            scale = inv * inv * inv * inner[:, part : part + 1]
            grad[here, cols] = (inv * turn[here, cols] - pre_ref[here, :] * scale).astype(BF)

    loads[0].wait()

    def backed(start):
        here = slice(start, start + 2 * rows)
        for k in range(3):
            part = dot_nt(grad[here, k * width : (k + 1) * width], out_maps_ref[k])
            back[here, k * rank : (k + 1) * rank] = part.astype(BF)

    def into(start, dst, side):
        here = slice(start, start + 2 * rows)

        def columns(n, carry):
            cols = pl.ds(pl.multiple_of(n * 512, 512), 512)
            full = dot_nt(grad[here, :], weight[cols, :]) + SCALE_ADAPT * dot(back[here, :], in_maps_ref[:, cols])
            dst[:, cols] = full.astype(BF)
            return carry

        steps = model // 1024
        lax.fori_loop(side * steps, (side + 1) * steps, columns, 0)

    sides = [pl.ds(k * (model // 2), model // 2) for k in range(2)]
    backed(2 * rows)
    far_copies = []
    for k in range(2):
        into(2 * rows, far, k)
        far_copies.append(
            copies.remote(far.at[pl.ds(rows, rows), sides[k]], core_in.at[:, sides[k]], core)
        )
    across_copies = []
    for k in range(2):
        far_copies[k].wait_recv()
        met[:, sides[k]] = (far[:rows, sides[k]].astype(F32) + core_in[:, sides[k]].astype(F32)).astype(BF)
        across_copies.append(copies.remote(met.at[:, sides[k]], across_in.at[:, sides[k]], across))
    backed(0)
    for k in range(2):
        into(0, near, k)
    near_copy = copies.remote(near.at[pl.ds(rows, rows)], near_in, core)

    loads[1].wait()
    late = early_rows + 3 * rank
    for b in range(2 * groups):
        cols = slice(b * 256, (b + 1) * 256)
        maps[b, early_rows:late, :] = SCALE_ADAPT * dot_tn(back[...], inputs[:, cols])
    send_late = pl.ds(early_rows, 3 * rank)
    exchanged += [
        copies.remote(maps.at[2 * q + 1 - x, send_late], maps_in.at[q, send_late], across) for q in range(groups)
    ]
    for q in range(groups):
        by_x[q, late:, :] = jnp.zeros_like(by_x[q, late:, :])
    for k in range(3):
        own = SCALE_ADAPT * dot_tn(narrow_ref[:, k * rank : (k + 1) * rank], grad[:, k * width : (k + 1) * width])
        here = slice(late + k * rank, late + (k + 1) * rank)
        for q in range(groups):
            by_x[q, here, pl.ds(pl.multiple_of(c * HD, HD), HD)] = own[:, q * HD : (q + 1) * HD]
    for copy in exchanged:
        copy.wait_recv()
    for q in range(groups):
        by_x[q, :late, :] = maps[2 * q + x, :late, :] + maps_in[q]
    halves = lambda ref, q, side: ref.at[q, :, pl.ds(pl.multiple_of(side * HD, HD), HD)]
    exchanged = [copies.remote(halves(by_x, q, 1 - y), by_y_in.at[q], over) for q in range(groups)]
    for q, copy in enumerate(exchanged):
        copy.wait_recv()
        by_y[q] = by_x[q, :, pl.ds(pl.multiple_of(y * HD, HD), HD)] + by_y_in[q]
    exchanged = [copies.remote(by_y.at[q], by_p_in.at[k], (q, x, y, c)) for k, q in enumerate(others)]
    summed = by_y[p]
    wide_sum = wide_ref[:, pl.ds(pl.multiple_of(p * 256, 256), 256)]
    for k, copy in enumerate(exchanged):
        copy.wait_recv()
        summed = summed + by_p_in[k]
    own_sum[...] = summed
    last = copies.remote(own_sum, own_sum_in, core)
    for k, copy in enumerate(wides):
        copy.wait_recv()
        wide_sum = wide_sum + wide_in[k]
    last.wait_recv()
    summed = summed + own_sum_in[...]
    summed = jnp.where(c == 0, summed[:, : HD // 2], summed[:, HD // 2 :])
    for n in range(choose_ref.shape[0]):
        mask = choose_ref[n : n + 1, :]
        low = mask[:, : HD // 2]
        for at, k in enumerate((5, 6, 7, 2, 0, 1)):
            a_model_ref[n, at] = low * summed[k * rank : (k + 1) * rank, :]
        for at, k in enumerate((8, 9, 10, 3, 4)):
            b_model_ref[n, at] = low * summed[k * rank : (k + 1) * rank, :]
        a_hidden_ref[n] = mask * wide_sum[:rank, :]
        for at in range(2):
            b_hidden_ref[n, at] = mask * wide_sum[(1 + at) * rank : (2 + at) * rank, :]

    loads[2].wait()
    near_copy.wait_recv()
    for copy in across_copies:
        copy.wait_recv()
    out_ref[...] = (
        mid[...]
        + near[:rows, :].astype(F32)
        + near_in[...].astype(F32)
        + across_in[...].astype(F32)
    )
    copies.finish()


def finish(groups, heads, args, weight, inputs, mid):
    own, width = args[0].shape
    rows, model = mid.shape
    rank = args[11].shape[1]
    early_rows, wide_rows, adapters = args[13].shape[0], args[14].shape[0], args[15].shape[0]
    total_rows = early_rows + 6 * rank
    late = early_rows + 3 * rank
    vm = pl.BlockSpec(memory_space=pltpu.VMEM)
    anywhere = pl.BlockSpec(memory_space=pl.ANY)
    count = 3 + groups + (groups - 1) + 5 + 2 * groups + (groups - 1) + 1
    block = lambda *shape: pltpu.VMEM(shape, BF)
    full = lambda *shape: pltpu.VMEM(shape, F32)
    first_rows = lambda v: vm if v.ndim != 2 or v.shape[0] <= own else pl.BlockSpec(
        (own, v.shape[1]), lambda k: (0, 0), pipeline_mode=pl.Buffered(1)
    )
    return pl.pallas_call(
        functools.partial(finish_kernel, groups, heads, early_rows),
        grid=(1,),
        in_specs=[first_rows(v) for v in args] + [anywhere] * 3,
        out_specs=[vm] * 5,
        out_shape=[
            jax.ShapeDtypeStruct((rows, model), F32),
            jax.ShapeDtypeStruct((adapters, 6, rank, HD // 2), F32),
            jax.ShapeDtypeStruct((adapters, rank, 256), F32),
            jax.ShapeDtypeStruct((adapters, 5, rank, HD // 2), F32),
            jax.ShapeDtypeStruct((adapters, 2, rank, 256), F32),
        ],
        scratch_shapes=[
            pltpu.VMEM(weight.shape, BF),
            pltpu.VMEM((own, model), BF),
            pltpu.VMEM(mid.shape, F32),
            full(own, 2 * width),
            block(own, 3 * width),
            block(own, 3 * rank),
            full(8, own),
            full(3, 8, own),
            block(2 * rows, model),
            block(2 * rows, model),
            block(rows, model),
            block(rows, model),
            block(rows, model),
            block(rows, model),
            full(2 * groups, late, 256),
            full(groups, late, 256),
            full(groups, total_rows, 256),
            full(groups, total_rows, HD),
            full(groups, total_rows, HD),
            full(groups - 1, total_rows, HD),
            full(total_rows, HD),
            full(total_rows, HD),
            full(groups - 1, wide_rows, 256),
            pltpu.SemaphoreType.DMA((3,)),
            pltpu.SemaphoreType.DMA((count,)),
            pltpu.SemaphoreType.DMA((count,)),
        ],
        compiler_params=pltpu.CompilerParams(
            collective_id=1, has_side_effects=True, vmem_limit_bytes=VMEM_BYTES
        ),
        name="finish",
        cost_estimate=cost(60),
    )(*args, weight, inputs, mid)


NEG_FILL = -1e30


def attend_kernel(count, scale, q_ref, *refs):
    ks, vs = refs[:count], refs[count : 2 * count]
    lo_ref, pos_ref, key_ref, o_ref, log_ref = refs[2 * count :]
    rows = q_ref.shape[0] * q_ref.shape[2]
    q = q_ref[...].reshape(rows, HD)
    lo, pos = lo_ref[0], pos_ref[...]
    scores = []
    for t in range(count):
        s = dot_nt(q, ks[t][...].reshape(rows, HD)) * scale
        key = key_ref[t : t + 1, :]
        scores.append(jnp.where((key >= lo) & (key <= pos), s, NEG_FILL))
    top = functools.reduce(jnp.maximum, [jnp.max(s, axis=1, keepdims=True) for s in scores])
    powers = [jnp.exp(s - top) for s in scores]
    total = sum(jnp.sum(e, axis=1, keepdims=True) for e in powers)
    share = 1.0 / total
    out = sum(dot((e * share).astype(BF), vs[t][...].reshape(rows, HD)) for t, e in enumerate(powers))
    o_ref[...] = out.astype(BF).reshape(o_ref.shape)
    log_ref[0] = top + jnp.log(total)


def attend_back_kernel(groups, reach, heads, scale, *refs):
    (
        grad_ref,
        weight_ref,
        in_maps_ref,
        out_maps_ref,
        lo_ref,
        pos_ref,
        key_ref,
        lo_rows_ref,
        query_rows_ref,
        log_ref,
        log_rows_ref,
        back_gu_ref,
        q_any,
        k_any,
        v_any,
        o_any,
        later_any,
        middle_any,
    ) = refs[:18]
    dq_ref, dk_ref, dv_ref, back_ref, maps_ref = refs[18:23]
    (
        q_buf,
        k_buf,
        v_buf,
        o_buf,
        later_buf,
        do_buf,
        do_in,
        inner,
        inner_in,
        middle_buf,
        load_sem,
        send_sem,
        recv_sem,
    ) = refs[23:]
    p, x, y, c = (lax.axis_index(a) for a in ("p", "x", "y", "c"))
    right, left = (lax.rem(p + 1, groups), x, y, c), (lax.rem(p + groups - 1, groups), x, y, c)
    rows = q_buf.shape[2]
    full = 2 * rows
    copies = Copies(send_sem, recv_sem)
    sources = [(q_any, q_buf), (k_any, k_buf), (v_any, v_buf), (o_any, o_buf)]
    sources.append((later_any, later_buf))
    loads = []
    for n, (src, dst) in enumerate(sources):
        loads.append(pltpu.make_async_copy(src, dst, load_sem.at[n]))
        loads[-1].start()
    part = middle_buf.shape[1]

    def load_middle(n):
        src = middle_any.at[pl.ds(n * part, part)]
        copy = pltpu.make_async_copy(src, middle_buf.at[n % 2], load_sem.at[5 + n % 2])
        copy.start()
        return copy

    middles = [load_middle(n) for n in range(2)]
    barrier = pltpu.get_barrier_semaphore()
    for device in (left, right):
        pl.semaphore_signal(barrier, inc=1, device_id=device, device_id_type=pl.DeviceIdType.MESH)

    for b in range(2):
        here = slice(b * full, (b + 1) * full)
        low = dot_nt(grad_ref[here, :], out_maps_ref[...]).astype(BF)
        back_ref[here, :] = low
        value = dot_nt(grad_ref[here, :], weight_ref[...]) + SCALE_ADAPT * dot(low, in_maps_ref[...])
        do_buf[b] = value.astype(BF).reshape(2, rows, heads * HD)
        if b == 0:
            pl.semaphore_wait(barrier, 2)
            moves = []
        moves.append(copies.remote(do_buf.at[b], do_in.at[0, b], left))
    for load in loads:
        load.wait()

    def piece(ref, s, cols, first=0):
        return ref[first : first + 2, s, :, cols].reshape(full, HD)

    def put(ref, s, cols, value):
        ref[:, s, :, cols] = value.reshape(2, rows, HD)

    ones = jnp.ones((8, HD), BF)

    def sums(n, carry):
        s, cols = n // heads, pl.ds(pl.multiple_of(n % heads * HD, HD), HD)
        product = piece(do_buf, s, cols).astype(F32) * piece(o_buf, s, cols).astype(F32)
        high = product.astype(BF)
        low = (product - high.astype(F32)).astype(BF)
        inner[pl.ds(n, 1), :] = (dot_nt(ones, high) + dot_nt(ones, low))[:1, :]
        return carry

    lax.fori_loop(0, 2 * heads, sums, 0)
    inner_moves = [copies.remote(inner, inner_in.at[0], left)]

    def own(n, carry):
        s, cols = n // heads, pl.ds(pl.multiple_of(n % heads * HD, HD), HD)
        q, do = piece(q_buf, s, cols), piece(do_buf, s, cols)
        delta = jnp.sum(do.astype(F32) * piece(o_buf, s, cols).astype(F32), axis=1, keepdims=True)
        lo, pos, log_total = lo_ref[s], pos_ref[...], log_ref[n]
        dq = None
        for t in range(reach + 1):
            k, v = piece(k_buf, s, cols, 2 * t), piece(v_buf, s, cols, 2 * t)
            key = key_ref[t : t + 1, :]
            score = dot_nt(q, k) * scale
            probs = jnp.where((key >= lo) & (key <= pos), jnp.exp(score - log_total), 0.0)
            ds = (probs * (dot_nt(do, v) - delta)).astype(BF)
            part = dot(ds, k)
            dq = part if dq is None else dq + part
            if t == 0:
                put(dv_ref, s, cols, dot_tn(probs.astype(BF), do))
                put(dk_ref, s, cols, dot_tn(ds, q) * scale)
        put(dq_ref, s, cols, dq * scale)
        return carry

    lax.fori_loop(0, 2 * heads, own, 0)

    for t in range(1, reach + 1):
        arrived, moves = moves, []
        for b in range(2):
            arrived[b].wait_recv()
            if t < reach:
                moves.append(copies.remote(do_in.at[t - 1, b], do_in.at[t, b], left))
        inner_moves[-1].wait_recv()
        if t < reach:
            inner_moves.append(copies.remote(inner_in.at[t - 1], inner_in.at[t], left))

        def from_later(n, carry, t=t):
            s, cols = n // heads, pl.ds(pl.multiple_of(n % heads * HD, HD), HD)
            k, v = piece(k_buf, s, cols), piece(v_buf, s, cols)
            q, do = piece(later_buf.at[t - 1], s, cols), piece(do_in.at[t - 1], s, cols)
            score = dot_nt(k, q) * scale
            key = pos_ref[...]
            lo, pos = lo_rows_ref[t, pl.ds(s, 1), :], query_rows_ref[t : t + 1, :]
            probs = jnp.where((key >= lo) & (key <= pos), jnp.exp(score - log_rows_ref[t - 1, pl.ds(n, 1), :]), 0.0)
            ds = (probs * (dot_nt(v, do) - inner_in[t - 1, pl.ds(n, 1), :])).astype(BF)
            put(dv_ref, s, cols, piece(dv_ref, s, cols) + dot(probs.astype(BF), do))
            put(dk_ref, s, cols, piece(dk_ref, s, cols) + dot(ds, q) * scale)
            return carry

        lax.fori_loop(0, 2 * heads, from_later, 0)
        if t == 1:
            for n in range(middle_any.shape[0] // part):
                middles[n].wait()
                term = SCALE_ADAPT * dot_tn(back_gu_ref[n * part : (n + 1) * part, :], middle_buf[n % 2])
                maps_ref[...] = term if n == 0 else maps_ref[...] + term
                if (n + 3) * part <= middle_any.shape[0]:
                    middles.append(load_middle(n + 2))
    copies.finish()


def attend_back(groups, reach, heads, rows, args, later, middle_low):
    own = 4 * rows
    local = heads * HD
    vm = pl.BlockSpec(memory_space=pltpu.VMEM)
    anywhere = pl.BlockSpec(memory_space=pl.ANY)
    block = lambda n: pltpu.VMEM((2 * n, 2, rows, local), BF)
    view = lambda v: v.reshape(-1, 2, rows, local)
    count = 3 * reach
    rank2, model = args[11].shape[1], middle_low.shape[1]
    dq, dk, dv, back, maps = pl.pallas_call(
        functools.partial(attend_back_kernel, groups, reach, heads, HD**-0.5),
        in_specs=[vm] * 12 + [anywhere] * 6,
        out_specs=[vm] * 5,
        out_shape=[jax.ShapeDtypeStruct((2, 2, rows, local), F32)] * 3
        + [jax.ShapeDtypeStruct((own, args[2].shape[0]), BF), jax.ShapeDtypeStruct((rank2, model), F32)],
        scratch_shapes=[
            block(1),
            block(reach + 1),
            block(reach + 1),
            block(1),
            pltpu.VMEM((reach, 2, 2, rows, local), BF),
            block(1),
            pltpu.VMEM((reach, 2, 2, rows, local), BF),
            pltpu.VMEM((2 * heads, 2 * rows), F32),
            pltpu.VMEM((reach, 2 * heads, 2 * rows), F32),
            pltpu.VMEM((2, 2 * rows, model), BF),
            pltpu.SemaphoreType.DMA((7,)),
            pltpu.SemaphoreType.DMA((count,)),
            pltpu.SemaphoreType.DMA((count,)),
        ],
        compiler_params=pltpu.CompilerParams(
            collective_id=3, has_side_effects=True, vmem_limit_bytes=VMEM_BYTES
        ),
        name="attend_backward",
        cost_estimate=cost(70),
    )(*args[:12], *[view(v) for v in args[12:]], later.reshape(reach, 2, 2, rows, local), middle_low)
    return [v.reshape(own, local) for v in (dq, dk, dv)], back, maps


class Attention:
    def __init__(self, rows, heads, count, lo, pos, key):
        self.rows, self.heads, self.count = rows, heads, count
        self.tables = (lo, pos, key)
        full = 2 * rows
        self.block = pl.BlockSpec((2, 1, rows, HD), lambda s, h: (0, s, 0, h))
        self.part = lambda t: pl.BlockSpec((2, 1, rows, HD), lambda s, h: (t, s, 0, h))
        self.table_specs = lambda n: [
            pl.BlockSpec((1, full, 1), lambda s, h: (s, 0, 0)),
            pl.BlockSpec((full, 1), lambda s, h: (0, 0)),
            pl.BlockSpec((n, full), lambda s, h: (0, 0)),
        ]
        self.log_spec = pl.BlockSpec((1, full, 1), lambda s, h: (s * heads + h, 0, 0))
        self.params = pltpu.CompilerParams(vmem_limit_bytes=VMEM_BYTES)

    def shape(self, dtype):
        return jax.ShapeDtypeStruct((2, 2, self.rows, self.heads * HD), dtype)

    def view(self, v):
        return v.reshape(-1, 2, self.rows, v.shape[-1])

    def forward(self, q, key, value):
        count = self.count
        parts = [self.part(t) for t in range(count)]
        out, log = pl.pallas_call(
            functools.partial(attend_kernel, count, HD**-0.5),
            grid=(2, self.heads),
            in_specs=[self.block] + parts * 2 + self.table_specs(count),
            out_specs=[self.block, self.log_spec],
            out_shape=[self.shape(BF), jax.ShapeDtypeStruct((2 * self.heads, 2 * self.rows, 1), F32)],
            compiler_params=self.params,
            name="attend_forward",
            cost_estimate=cost(1),
        )(self.view(q), *[self.view(key)] * count, *[self.view(value)] * count, *self.tables)
        return out.reshape(q.shape), log


def rms_inverse(v):
    return lax.rsqrt(jnp.mean(v * v, axis=-1, keepdims=True) + EPS)


def rms_backward(v, gain, grad):
    inv = rms_inverse(v)
    turn = grad * gain
    inner = jnp.mean(v * turn, axis=-1, keepdims=True)
    return inv * turn - v * (inv * inv * inv) * inner


def total(refs):
    return sum(ref[...].astype(F32) for ref in refs)


def after_attention_kernel(*refs):
    inputs_ref, gain_ref, attn_ref, middle_ref, low_ref = refs[3:]
    attn = total(refs[:3])
    attn_ref[...] = attn
    middle = inputs_ref[...].astype(F32) + attn * rms_inverse(attn) * gain_ref[...]
    middle_ref[...] = middle
    low_ref[...] = middle.astype(BF)


def end_kernel(*refs):
    mid_ref, out_ref = refs[3:]
    out_ref[...] = mid_ref[...] + total(refs[:3])


def feed_kernel(*refs):
    (
        d_in_ref,
        d_out_ref,
        gu_out_ref,
        gu_in_ref,
        feed_gain_ref,
        attn_gain_ref,
        narrow_gu_ref,
        gated_any,
        gate_any,
        up_any,
        feed_any,
        down_any,
        middle_any,
        cot_any,
        attn_any,
        query_any,
        log_any,
    ) = refs[:17]
    result_ref, mid_ref, grad_attn_ref, back_gu_ref, maps_ref, gb_d_ref, later_any, later_log_any = refs[17:25]
    (
        down_w,
        gate_w,
        up_w,
        acts,
        blocks,
        own_pair,
        core_in,
        by_x,
        by_y,
        across_in,
        over_in,
        tokens,
        cot,
        dgu,
        narrow_d,
        back_d,
        load_sem,
        act_sem,
        free_sem,
        send_sem,
        recv_sem,
    ) = refs[25:]
    p, x, y, c = (lax.axis_index(a) for a in ("p", "x", "y", "c"))
    core, across, over = (p, x, y, 1 - c), (p, 1 - x, y, c), (p, x, 1 - y, c)
    rows, model = result_ref.shape
    size = rows // 2
    quarter = rows // 4
    hidden = down_w.shape[0]
    rank = d_in_ref.shape[0]
    copies = Copies(send_sem, recv_sem)

    def load(k, src, dst):
        copy = pltpu.make_async_copy(src, dst, load_sem.at[k])
        copy.start()
        return copy

    halves = (pl.ds(0, size), pl.ds(size, size))
    top = (pl.ds(0, quarter), pl.ds(size, quarter))
    low = (pl.ds(quarter, quarter), pl.ds(size + quarter, quarter))

    class Stream:
        def __init__(self, order, kinds):
            self.order, self.kinds, self.flight = order, kinds, []
            for _ in range(min(4, len(order))):
                self.fetch()

        def fetch(self):
            n = len(self.flight)
            if n < len(self.order):
                k, h = self.order[n]
                group = []
                for kind in self.kinds:
                    src = (gated_any, gate_any, up_any)[kind].at[pl.ds(2 * k, 2), halves[h]]
                    group.append(pltpu.make_async_copy(src, acts.at[n % 4, kind], act_sem.at[n % 4, kind]))
                    group[-1].start()
                self.flight.append(group)

        def slot(self, k, h):
            n = self.order.index((k, h))
            for copy in self.flight[n]:
                copy.wait()
            return n % 4

    def act(slot, kind, cols=slice(None)):
        return acts[slot, kind, :, :, cols].reshape(2 * size, -1)

    both = lambda order: [(k, h) for h in range(2) for k in order]
    stream = Stream(both((3, 1, 2, 0)), (0,))
    loaded = load(0, down_any, down_w)
    groups = feed_any.shape[0]
    depth = model // groups
    reach = later_any.shape[0]
    middle_load, cot_load = load(1, middle_any, tokens), load(2, cot_any, cot)
    feed_loads = []
    for k in range(groups):
        for n, dst in enumerate((gate_w, up_w)):
            src = feed_any.at[k, :, pl.ds(n * hidden, hidden)]
            feed_loads.append(load(4 + 2 * k + n, src, dst.at[pl.ds(k * depth, depth)]))
    ring = lax.axis_size("p")
    right, left = (lax.rem(p + 1, ring), x, y, c), (lax.rem(p + ring - 1, ring), x, y, c)
    barrier = pltpu.get_barrier_semaphore()
    for device in (core, across, over, right, left):
        pl.semaphore_signal(barrier, inc=1, device_id=device, device_id_type=pl.DeviceIdType.MESH)
    pl.semaphore_wait(barrier, 5)

    def pull(t):
        src = (query_any, log_any) if t == 0 else (later_any.at[t - 1], later_log_any.at[t - 1])
        return [copies.remote(src[0], later_any.at[t], left), copies.remote(src[1], later_log_any.at[t], left)]

    maps_ref[...] = jnp.zeros_like(maps_ref)
    gb_d_ref[...] = jnp.zeros_like(gb_d_ref)

    def part(k):
        return own_pair if k == 0 else blocks.at[pl.ds(2 * k, 2)]

    def store(k, h, cols, value):
        dst = part(k)
        dst[0, halves[h], cols] = value[:size].astype(BF)
        dst[1, halves[h], cols] = value[size:].astype(BF)

    def columns(n):
        return pl.ds(pl.multiple_of(n * 512, 512), 512)

    def forward(k, h):
        slot = stream.slot(k, h)
        here = 2 * k + h
        narrow_d[here] = dot_nt(act(slot, 0), d_in_ref[...]).astype(BF)

        def body(n, carry):
            cols = columns(n)
            value = dot(act(slot, 0), down_w[:, cols])
            store(k, h, cols, value + SCALE_ADAPT * dot(narrow_d[here], d_out_ref[:, cols]))
            return carry

        lax.fori_loop(0, model // 512, body, 0)
        stream.fetch()

    def taken(k, h):
        return blocks[2 * k : 2 * k + 2, halves[h], :].reshape(2 * size, model)

    def backward(k, h):
        slot = stream.slot(k, h)
        here = 2 * k + h
        low_d = dot_nt(taken(k, h), d_out_ref[...]).astype(BF)
        back_d[here] = low_d
        gb_d_ref[...] += SCALE_ADAPT * dot_tn(narrow_d[here], taken(k, h))

        def tile(t, carry):
            cols = pl.ds(pl.multiple_of(t * 256, 256), 256)
            dm = dot_nt(taken(k, h), down_w[cols, :]) + SCALE_ADAPT * dot(low_d, d_in_ref[:, cols])
            gate, up = act(slot, 1, cols).astype(F32), act(slot, 2, cols).astype(F32)
            sig = jax.nn.sigmoid(gate)
            silu = gate * sig
            dgu[here, 0, :, cols] = (dm * up * (sig + silu * (1.0 - sig))).astype(BF)
            dgu[here, 1, :, cols] = (dm * silu).astype(BF)
            return carry

        lax.fori_loop(0, hidden // 256, tile, 0)
        back_g = dot_nt(dgu[here, 0], gu_out_ref[0]).astype(BF)
        back_u = dot_nt(dgu[here, 1], gu_out_ref[1]).astype(BF)
        back = jnp.concatenate([back_g, back_u], axis=1)
        back_gu_ref[2 * k : 2 * k + 2, halves[h], :] = back.reshape(2, size, 2 * rank)

        def body(n, carry):
            cols = columns(n)
            value = dot_nt(dgu[here, 0], gate_w[cols, :]) + dot_nt(dgu[here, 1], up_w[cols, :])
            store(k, h, cols, value + SCALE_ADAPT * dot(back, gu_in_ref[:, cols]))
            return carry

        lax.fori_loop(0, model // 512, body, 0)
        stream.fetch()

    def adapter_maps():
        for k, h in stream.order:
            slot = stream.slot(k, h)
            here = 2 * k + h
            maps_ref[0] += SCALE_ADAPT * dot_tn(back_d[here], act(slot, 0))
            narrow = narrow_gu_ref[2 * k : 2 * k + 2, halves[h], :].reshape(2 * size, 2 * rank)
            for n in range(2):
                maps_ref[1 + n] += SCALE_ADAPT * dot_tn(narrow[:, n * rank : (n + 1) * rank], dgu[here, n])
            stream.fetch()

    def by_tiles(start, count, work):
        def body(n, carry):
            work(pl.multiple_of(n * 32, 32))
            return carry

        lax.fori_loop(start // 32, (start + count) // 32, body, 0)

    class Half:
        def __init__(self, h):
            self.h, self.met, self.parts, self.gone = h, {}, [], []

        def to_core(self, k):
            here = halves[self.h]
            self.met[k] = copies.remote(part(k).at[1, here], core_in.at[k, here], core)

        def meet(self, k):
            self.met[k].wait_recv()

            def work(start):
                tile = pl.ds(start, 32)
                blocks[2 * k, tile, :] = (
                    blocks[2 * k, tile, :].astype(F32) + core_in[k, tile, :].astype(F32)
                ).astype(BF)

            by_tiles(self.h * size, size, work)
            h = self.h
            if k == 3:
                self.far_x = copies.remote(blocks.at[6, top[h]], by_x.at[h], across)
                self.far_y = copies.remote(blocks.at[6, low[h]], by_y.at[h], over)
            if k == 1:
                self.parts.append(copies.remote(blocks.at[2, top[h]], across_in.at[top[h]], across))
            if k == 2:
                self.parts.append(copies.remote(blocks.at[4, low[h]], over_in.at[low[h]], over))

        def pass_far(self):
            h = self.h

            def add(block, start, more):
                def work(n):
                    here = pl.ds(n + start, 32)
                    blocks[block, here, :] = (
                        blocks[block, here, :].astype(F32) + more[h, pl.ds(n, 32), :].astype(F32)
                    ).astype(BF)

                by_tiles(0, quarter, work)

            self.far_y.wait_recv()
            add(2, h * size + quarter, by_y)
            self.parts.append(copies.remote(blocks.at[2, low[h]], across_in.at[low[h]], across))
            self.far_x.wait_recv()
            add(4, h * size, by_x)
            self.parts.append(copies.remote(blocks.at[4, top[h]], over_in.at[top[h]], over))

        def close(self, work):
            self.met[0].wait_recv()
            for copy in self.parts:
                copy.wait_recv()

            def body(start):
                tile = pl.ds(start, 32)
                total = own_pair[0, tile, :].astype(F32) + core_in[0, tile, :].astype(F32)
                work(tile, total + across_in[tile, :].astype(F32) + over_in[tile, :].astype(F32))

            by_tiles(self.h * size, size, body)

        def share(self):
            here = halves[self.h]
            self.to_x = copies.remote(blocks.at[0, here], blocks.at[2, here], across)
            self.to_y = copies.remote(blocks.at[0, here], blocks.at[4, here], over)
            self.to_c = copies.remote(blocks.at[0, here], blocks.at[1, here], core)

        def pass_x(self):
            h, here = self.h, halves[self.h]
            self.to_x.wait_recv()
            self.x_on = copies.remote(blocks.at[2, here], blocks.at[3, here], core)
            self.x_far = copies.remote(blocks.at[2, top[h]], blocks.at[6, top[h]], over)

        def pass_y(self):
            h, here = self.h, halves[self.h]
            self.to_y.wait_recv()
            self.y_on = copies.remote(blocks.at[4, here], blocks.at[5, here], core)
            self.y_far = copies.remote(blocks.at[4, low[h]], blocks.at[6, low[h]], across)

        def pass_on(self):
            here = halves[self.h]
            self.x_far.wait_recv()
            self.y_far.wait_recv()
            self.far_on = copies.remote(blocks.at[6, here], blocks.at[7, here], core)

        def ready(self, k):
            here = (self.to_c, getattr(self, "x_on", None), getattr(self, "y_on", None), getattr(self, "far_on", None))[k]
            here.wait_recv()
            gone = [] if k == 0 else [here]
            if k in (1, 2):
                gone.append(self.x_far if k == 1 else self.y_far)
            for copy in gone:
                copy.wait_send()
            self.gone += gone

    first, second = Half(0), Half(1)
    loaded.wait()
    forward(3, 0)
    first.to_core(3)
    forward(1, 0)
    first.to_core(1)
    first.meet(3)
    forward(2, 0)
    first.to_core(2)
    first.meet(1)
    forward(0, 0)
    first.to_core(0)
    first.meet(2)
    forward(3, 1)
    second.to_core(3)
    first.pass_far()
    forward(1, 1)
    second.to_core(1)
    second.meet(3)
    forward(2, 1)
    second.to_core(2)
    second.meet(1)
    forward(0, 1)
    second.to_core(0)
    second.meet(2)
    stream = Stream([(0, 0), (0, 1), (1, 0), (3, 0), (1, 1), (2, 0), (3, 1), (2, 1)], (0, 1, 2))
    middle_load.wait()
    cot_load.wait()

    def end(tile, feed):
        gain = feed_gain_ref[...]
        result_ref[tile, :] = (tokens[tile, :] + feed * rms_inverse(feed) * gain).astype(BF)
        blocks[0, tile, :] = rms_backward(feed, gain, cot[tile, :].astype(F32)).astype(BF)

    def free(half):
        for copy in [*half.met.values(), *half.parts, half.far_x, half.far_y]:
            copy.wait_send()
        for device in (core, across, over):
            pl.semaphore_signal(free_sem.at[half.h], inc=1, device_id=device, device_id_type=pl.DeviceIdType.MESH)

    first.close(end)
    free(first)
    pl.semaphore_wait(free_sem.at[0], 3)
    first.share()
    second.pass_far()
    second.close(end)
    free(second)
    pl.semaphore_wait(free_sem.at[1], 3)
    second.share()
    copies.all = [first.to_x, first.to_y, first.to_c, second.to_x, second.to_y, second.to_c]
    attn_load = load(3, attn_any, tokens)
    pulls = pull(0)
    for copy in feed_loads:
        copy.wait()
    for half in (first, second):
        half.met, half.parts = {}, []

    first.ready(0)
    backward(0, 0)
    first.to_core(0)
    first.pass_x()
    first.pass_y()
    second.ready(0)
    backward(0, 1)
    second.to_core(0)
    first.pass_on()
    first.ready(1)
    backward(1, 0)
    first.to_core(1)
    second.pass_x()
    second.pass_y()
    first.meet(1)
    for t in range(1, reach):
        for copy in pulls:
            copy.wait_recv()
        pulls = pull(t)
    first.ready(3)
    backward(3, 0)
    first.to_core(3)
    second.ready(1)
    backward(1, 1)
    second.to_core(1)
    first.meet(3)
    second.pass_on()
    first.ready(2)
    backward(2, 0)
    first.to_core(2)
    second.meet(1)
    second.ready(3)
    first.meet(2)
    backward(3, 1)
    second.to_core(3)
    first.pass_far()
    second.ready(2)
    second.meet(3)
    backward(2, 1)
    second.to_core(2)
    stream = Stream([(k, h) for k in range(4) for h in range(2)], (0,))
    attn_load.wait()

    def open_attention(tile, total):
        mid = cot[tile, :].astype(F32) + total
        mid_ref[tile, :] = mid
        grad_attn_ref[0, tile, :] = rms_backward(tokens[tile, :], attn_gain_ref[...], mid).astype(BF)

    def share_attention(h):
        here = halves[h]
        block = lambda k: grad_attn_ref.at[k, here]
        return copies.remote(block(0), block(2), across), copies.remote(block(0), block(1), core)

    def pass_attention(h, to_x):
        to_x.wait_recv()
        return copies.remote(grad_attn_ref.at[2, halves[h]], grad_attn_ref.at[3, halves[h]], core)

    second.meet(2)
    first.close(open_attention)
    to_x, to_c = share_attention(0)
    last = [to_c]
    second.pass_far()
    last.append(pass_attention(0, to_x))
    second.close(open_attention)
    to_x, to_c = share_attention(1)
    last.append(to_c)
    adapter_maps()
    last.append(pass_attention(1, to_x))
    for copy in last + pulls:
        copy.wait_recv()
    gone = first.gone + second.gone
    for copy in copies.all:
        if not any(copy is other for other in gone):
            copy.wait_send()


def feed_layer(maps, narrow_gu, acts, weights, middle, cot, attn_out, query, log, reach):
    rows, model = cot.shape
    groups, hidden = weights[0].shape[0], weights[1].shape[0]
    rank = maps[0].shape[0]
    vm = pl.BlockSpec(memory_space=pltpu.VMEM)
    anywhere = pl.BlockSpec(memory_space=pl.ANY)
    block = lambda *shape: pltpu.VMEM(shape, BF)
    count = 96 + 2 * reach
    return pl.pallas_call(
        feed_kernel,
        in_specs=[vm] * 7 + [anywhere] * 10,
        out_specs=[vm] * 6 + [anywhere] * 2,
        out_shape=[
            jax.ShapeDtypeStruct((rows, model), BF),
            jax.ShapeDtypeStruct((rows, model), F32),
            jax.ShapeDtypeStruct((4, rows, model), BF),
            jax.ShapeDtypeStruct((8, rows, 2 * rank), BF),
            jax.ShapeDtypeStruct((3, rank, hidden), F32),
            jax.ShapeDtypeStruct((rank, model), F32),
            jax.ShapeDtypeStruct((reach,) + query.shape, BF),
            jax.ShapeDtypeStruct((reach,) + log.shape, F32),
        ],
        scratch_shapes=[
            block(hidden, model),
            block(model, hidden),
            block(model, hidden),
            block(4, 3, 2, rows // 2, hidden),
            block(8, rows, model),
            block(2, rows, model),
            block(4, rows, model),
            block(2, rows // 4, model),
            block(2, rows // 4, model),
            block(rows, model),
            block(rows, model),
            pltpu.VMEM((rows, model), F32),
            block(rows, model),
            block(8, 2, rows, hidden),
            block(8, rows, rank),
            block(8, rows, rank),
            pltpu.SemaphoreType.DMA((2 * groups + 4,)),
            pltpu.SemaphoreType.DMA((4, 3)),
            pltpu.SemaphoreType.REGULAR((2,)),
            pltpu.SemaphoreType.DMA((count,)),
            pltpu.SemaphoreType.DMA((count,)),
        ],
        compiler_params=pltpu.CompilerParams(
            collective_id=2, has_side_effects=True, vmem_limit_bytes=60 * 1024 * 1024
        ),
        name="feed_layer",
        cost_estimate=cost(170),
    )(
        *maps,
        narrow_gu.reshape(8, rows, -1),
        *[v.reshape(8, rows, hidden) for v in acts],
        *weights,
        middle,
        cot,
        attn_out,
        query,
        log,
    )


def by_rows(kernel, name, rows, width, args, dtypes, us):
    tile = 64 if rows % 64 == 0 else rows
    spec = lambda v: pl.BlockSpec((1, width), lambda r: (0, 0)) if v.shape[0] == 1 else pl.BlockSpec((tile, width), lambda r: (r, 0))
    row = pl.BlockSpec((tile, width), lambda r: (r, 0))
    return pl.pallas_call(
        kernel,
        grid=(rows // tile,),
        in_specs=[spec(v) for v in args],
        out_specs=[row] * len(dtypes),
        out_shape=[jax.ShapeDtypeStruct((rows, width), d) for d in dtypes],
        compiler_params=pltpu.CompilerParams(vmem_limit_bytes=VMEM_BYTES),
        name=name,
        cost_estimate=cost(us),
    )(*args)


def on_device(
    layer_input,
    cotangent,
    document_length,
    adapter_choice_index,
    query_weight,
    key_weight,
    value_weight,
    output_weight,
    gate_weight,
    up_weight,
    down_weight,
    query_norm_gain,
    key_norm_gain,
    attention_norm_gain,
    feedforward_norm_gain,
    adapter_model_input_maps,
    adapter_down_input_maps,
    adapter_model_output_maps,
    adapter_hidden_output_maps,
):
    at = Place()
    rows = layer_input.shape[1]
    width = layer_input.shape[2]
    heads = width // HD // 4
    local = heads * HD
    rank = adapter_model_input_maps.shape[2]
    depth = query_weight.shape[0]
    hidden_rows = down_weight.shape[0]
    hidden = hidden_rows * at.np
    reach = WINDOW // (2 * rows)
    count = reach + 1

    def head_cols(v, quarter):
        return pick(v.reshape(v.shape[:-1] + (heads, 4, HD)), v.ndim, quarter).reshape(v.shape[:-1] + (local,))

    def hidden_cols(v):
        lead = v.shape[:-1]
        n = len(lead)
        v = v.reshape(lead + (at.np, 2, 2, 2, hidden_rows))
        v = pick(v, n + 3, at.c)
        v = pick(v, n + 2, at.y)
        return pick(v, n + 1, at.x).reshape(lead + (-1,))

    own_inputs = layer_input[0]
    head_offsets = lambda x, y, c: [4 * k + 2 * x + c for k in range(heads)]
    feed_offsets = lambda x, y, c: [((2 * p + x) * 2 + y) * 2 + c for p in range(at.np)]
    w_qkv, feed_piece, inputs, o_own = start(
        at.np,
        reach,
        at.spot,
        [query_weight, key_weight, value_weight, gate_weight, up_weight],
        (head_offsets, feed_offsets),
        hidden_rows,
        own_inputs,
        output_weight,
    )
    w_gu = lax.all_gather(feed_piece, "p", axis=0)
    if 2 * depth == HD:
        sent = lambda target: lax.ppermute(o_own, ("y", "c"), target)
        same = at.y == at.c
        mine_half = jnp.where(same, o_own, sent([(0, 2), (3, 1)]))
        other_half = jnp.where(same, sent([(1, 0), (2, 3)]), sent([(1, 2), (2, 1)]))
        halves = [jnp.where(at.c == 0, mine_half, other_half), jnp.where(at.c == 0, other_half, mine_half)]
        w_o = jnp.stack([v.reshape(at.np, depth, width) for v in halves], axis=1).reshape(local, width)
    else:
        o_full = lax.all_gather(output_weight, ("p", "x", "y", "c"), axis=0, tiled=True)
        w_o = pick(o_full.reshape(heads, 4, HD, width), 1, at.quarter).reshape(local, width)
    selected = adapter_choice_index[0]
    a_model = pick(adapter_model_input_maps, 0, selected)
    a_hidden = pick(adapter_down_input_maps, 0, selected)
    b_model = pick(adapter_model_output_maps, 0, selected)
    b_hidden = pick(adapter_hidden_output_maps, 0, selected)
    a_qkv = a_model[:3].reshape(3 * rank, width)
    a_gu = a_model[4:6].reshape(2 * rank, width)
    a_o = head_cols(a_model[3], at.quarter)
    a_d = hidden_cols(a_hidden)
    b_qkv = head_cols(b_model[:3], at.quarter)
    b_o, b_d = b_model[3], b_model[4]
    b_gu = hidden_cols(b_hidden)

    def diagonal(maps):
        k, r, n = maps.shape
        zero = jnp.zeros((r, n), BF)
        return jnp.concatenate(
            [jnp.concatenate([maps[a] if a == b else zero for b in range(k)], axis=1) for a in range(k)], axis=0
        )

    b_qkv_diag = diagonal(b_qkv)
    gain = jnp.concatenate(
        [head_cols(query_norm_gain[None], at.quarter), head_cols(key_norm_gain[None], at.quarter)], axis=1
    )

    step_rows = jnp.arange(rows, dtype=jnp.int32)
    spot = lambda xx: at.p * 2 * rows + xx * rows + step_rows
    pos = jnp.concatenate([spot(at.x), spot(1 - at.x)])
    lengths = lax.dynamic_slice_in_dim(document_length, 2 * at.y, 2, 0)
    bounds = jnp.cumsum(lengths, axis=1)
    bounds = jnp.where(at.c == 0, bounds, bounds[::-1])

    def lo_of(pos):
        begin = jnp.max(jnp.where(bounds[:, None, :] <= pos[None, :, None], bounds[:, None, :], 0), axis=2)
        return jnp.maximum(begin, pos[None] - (WINDOW - 1))

    lo = lo_of(pos)
    key = jnp.stack([pos - 2 * rows * t for t in range(count)])
    attention = Attention(rows, heads, count, lo[:, :, None], pos[:, None], key)

    half_dim = HD // 2
    inv_freq = ROPE_BASE ** (-(jnp.arange(half_dim, dtype=F32) * 2.0 / HD))
    first = at.p * 2 * rows
    starts = jnp.stack([first + xx * rows - 2 * rows * t for t in range(count) for xx in (at.x, at.x, 1 - at.x, 1 - at.x)])
    wide_freq = jnp.concatenate([inv_freq, inv_freq])[None]
    sign = jnp.where(jnp.arange(HD) < half_dim, -1.0, 1.0)[None]
    turn_angle = starts.astype(F32)[:, None] * wide_freq
    row_angle = step_rows.astype(F32)[:, None] * wide_freq
    row_cos, row_sin = jnp.cos(row_angle), jnp.sin(row_angle)
    row_tables = jnp.stack([row_cos, row_sin, sign * row_cos, sign * row_sin])
    block_tables = jnp.stack([jnp.cos(turn_angle), jnp.sin(turn_angle)])

    own = 4 * rows
    pre_q, pre_k, value_all, narrow_qkv, square_q, square_k = project(
        inputs, own, w_qkv, a_qkv, b_qkv, heads
    )
    w_d = lax.all_gather(after(down_weight, square_q), "p", axis=0, tiled=True)
    inv_q, inv_k = scales(square_q, square_k, width, 2 * rows)
    query, key_all = post(pre_q, pre_k, inv_q, inv_k, gain, row_tables, block_tables, heads)
    o, log = attention.forward(query, key_all, value_all)
    narrow_o = dot_nt(o, a_o).astype(BF)
    def attn_part(part, mark=None):
        ins, narrow = o[part], narrow_o[part]
        if mark is not None:
            ins = after(ins, mark)
        return (dot(ins, w_o) + SCALE_ADAPT * dot(narrow, b_o)).astype(BF)

    near_rows, far_rows = slice(0, 2 * rows), slice(2 * rows, 4 * rows)
    attn_parts = at.scatter4(attn_part(far_rows), lambda mark: attn_part(near_rows, mark))
    attn_gain, feed_gain = attention_norm_gain[None], feedforward_norm_gain[None]
    attn_out, middle, low = by_rows(
        after_attention_kernel,
        "after_attention",
        rows,
        width,
        [*attn_parts, own_inputs, attn_gain],
        [F32, F32, BF],
        4,
    )
    middle_low = jnp.concatenate(at.gather8(low)[0])
    narrow_gu = dot_nt(middle_low, a_gu).astype(BF)
    gate, up, gated = gate_up(middle_low, w_gu, narrow_gu, b_gu)
    result, grad_mid, grad_attn, back_gu, wide, gb_d, later, later_logs = feed_layer(
        (a_d, b_d, b_gu, a_gu, feed_gain, attn_gain),
        narrow_gu,
        (gated, gate, up),
        (w_gu, w_d),
        middle,
        cotangent[0],
        attn_out,
        query,
        log[:, :, 0],
        reach,
    )
    lo_rows = jnp.stack([lo_of(pos + 2 * rows * t) for t in range(count)])
    query_rows = jnp.stack([pos + 2 * rows * t for t in range(count)])
    (dq, dk, dv), back_o, ga_gu = attend_back(
        at.np,
        reach,
        heads,
        rows,
        [
            grad_attn.reshape(4 * rows, width),
            w_o,
            a_o,
            b_o,
            *attention.tables,
            lo_rows,
            query_rows,
            log,
            later_logs,
            back_gu.reshape(8 * rows, -1),
            query,
            key_all,
            value_all,
            o,
        ],
        later,
        middle_low,
    )
    def share_y(mine, other):
        return mine + at.swap_y(other)

    def share_p(v):
        total = pick(v, 1, at.p)
        for by in range(1, at.np):
            total = total + at.turn_p(pick(v, 1, (at.p + by) % at.np), by)
        return total

    def sum_model(v):
        v = v.reshape(-1, at.np, 2, 2, 2 * depth)
        v = pick(v, 2, at.x) + at.swap_x(pick(v, 2, 1 - at.x))
        return share_y(pick(v, 2, at.y), pick(v, 2, 1 - at.y))

    mine = (jnp.arange(4) == at.quarter).astype(F32)

    def spread(v):
        return (v.reshape(-1, heads, 1, HD) * mine[:, None]).reshape(-1, width)

    grad_attn = grad_attn.reshape(4 * rows, -1)
    ga_o = SCALE_ADAPT * dot_tn(back_o, o)
    gb_o = SCALE_ADAPT * dot_tn(narrow_o, grad_attn)
    choose = (jnp.arange(adapter_model_input_maps.shape[0], dtype=jnp.int32) == selected).astype(F32)
    early = jnp.concatenate([ga_gu, spread(ga_o), gb_o, gb_d])
    wide = wide.reshape(3 * rank, -1)
    if 2 * depth == HD and hidden_rows == 2 * HD:
        outs = finish(
            at.np,
            heads,
            [
                dq,
                dk,
                dv,
                pre_q,
                pre_k,
                inv_q,
                inv_k,
                gain,
                row_tables,
                block_tables,
                a_qkv,
                b_qkv,
                narrow_qkv,
                early,
                wide,
                jnp.broadcast_to(choose[:, None], (choose.shape[0], 256)),
            ],
            w_qkv,
            inputs,
            grad_mid,
        )
        return (result[None], outs[0][None], *outs[1:])
    else:
        early = sum_model(after(early, dq))
        inputs, narrow_qkv, pre_k, inv_k = (v[:own] for v in (inputs, narrow_qkv, pre_k, inv_k))
        tables = [jnp.concatenate([rotation(row_tables, block_tables, b)[k] for b in range(4)]) for k in range(2)]
        cos, sin = tables
        wide = wide.reshape(-1, at.np, hidden_rows)
        dk = after(dk, early)
        turn, inner = unpost(dq, dk, pre_q, pre_k, gain, cos, sin, heads)
        inner = at.sum4(inner.T, 1).T / width

        def unnorm(part, pre, scale):
            cols = slice(part * local, (part + 1) * local)
            return (scale * turn[:, cols] - pre * (scale * scale * scale * inner[:, part : part + 1])).astype(BF)

        grad_qkv = jnp.concatenate(
            [unnorm(0, pre_q, inv_q), unnorm(1, pre_k, inv_k), dv.astype(BF)], axis=1
        )
        back_qkv = dot_nt(grad_qkv, b_qkv_diag).astype(BF)

        def late_adapters(mark):
            back = after(back_qkv, mark)
            ga_qkv = SCALE_ADAPT * dot_tn(back, inputs)
            gb_qkv = [
                SCALE_ADAPT * dot_tn(narrow_qkv[:, k * rank : (k + 1) * rank], grad_qkv[:, k * local : (k + 1) * local])
                for k in range(3)
            ]
            return sum_model(jnp.concatenate([ga_qkv, spread(jnp.concatenate(gb_qkv))]))

        def end_part(part, mark=None):
            ins, back = grad_qkv[part], back_qkv[part]
            if mark is not None:
                ins = after(ins, mark)
            return (dot_nt(ins, w_qkv) + SCALE_ADAPT * dot(back, a_qkv)).astype(BF)

        marks = []

        def end_near(mark):
            marks.append(mark)
            return end_part(near_rows, mark)

        end_parts = at.scatter4(end_part(far_rows), end_near)
        (grad_input,) = by_rows(end_kernel, "end", rows, width, [*end_parts, grad_mid], [F32], 3)
        late = late_adapters(marks[0])
        narrow_sums = share_p(jnp.concatenate([late, early], axis=0))
        narrow_sums = narrow_sums.reshape(narrow_sums.shape[0], 2, depth)
        sums = pick(narrow_sums, 1, at.c) + at.swap_core(pick(narrow_sums, 1, 1 - at.c))
        sums = sums.reshape(-1, rank, depth)
        late, early = sums[:6], sums[6:]
        wide = share_p(after(wide, marks[0])).reshape(-1, rank, hidden_rows)
    sum_a_model = choose[:, None, None, None] * jnp.concatenate([late[:3], early[2:3], early[:2]])[None]
    sum_a_hidden = choose[:, None, None] * wide[0][None]
    sum_b_model = choose[:, None, None, None] * jnp.concatenate([late[3:], early[3:]])[None]
    sum_b_hidden = choose[:, None, None, None] * wide[1:][None]
    return (result[None], grad_input[None], sum_a_model, sum_a_hidden, sum_b_model, sum_b_hidden)


def solution(mesh):
    grid = mesh.devices.reshape(mesh.shape["ctx"] // 2, 2, mesh.shape["wt"] // 2, 2)
    split = Mesh(grid, ("p", "x", "y", "c"))
    everyone = ("p", "x", "y", "c")
    rows = P(everyone, None)
    tokens = P(("y", "c"), ("p", "x"), None)
    placed = (tokens, tokens, P(), P()) + (rows,) * 7 + (P(),) * 8
    return jax.shard_map(
        on_device,
        mesh=split,
        in_specs=placed,
        out_specs=(
            tokens,
            tokens,
            P(None, None, None, everyone),
            P(None, None, everyone),
            P(None, None, None, everyone),
            P(None, None, None, everyone),
        ),
        check_vma=False,
    )
```

```python
import functools

import jax
import jax.numpy as jnp
from jax import lax
from jax.experimental import pallas as pl
from jax.experimental.pallas import tpu as pltpu
from jax.sharding import Mesh
from jax.sharding import PartitionSpec as P

HD = 128
WINDOW = 1024
SCALE_ADAPT = 0.5
ROPE_BASE = 500000.0
EPS = 1e-06
BF = jnp.bfloat16
F32 = jnp.float32
VMEM_BYTES = 56 * 1024 * 1024


def cost(us):
    return pl.CostEstimate(flops=int(us * 1.1e9), bytes_accessed=int(us * 1e6), transcendentals=0)


def dot(a, b, dims=((1,), (0,))):
    return lax.dot_general(a, b, (dims, ((), ())), preferred_element_type=F32)


def dot_nt(a, b):
    return dot(a, b, ((1,), (1,)))


def dot_tn(a, b):
    return dot(a, b, ((0,), (0,)))


SWAP = [(0, 1), (1, 0)]


class Place:
    def __init__(self):
        self.np = lax.axis_size("p")
        self.p, self.x, self.y, self.c = (lax.axis_index(a) for a in ("p", "x", "y", "c"))
        self.quarter = 2 * self.x + self.c
        self.spot = jnp.stack([self.x, self.y, self.c]).astype(jnp.int32)

    def swap_core(self, value):
        return lax.ppermute(value, "c", SWAP)

    def swap_x(self, value):
        return lax.ppermute(value, "x", SWAP)

    def swap_both(self, value):
        return lax.ppermute(value, ("x", "c"), [(0, 3), (1, 2), (2, 1), (3, 0)])

    def swap_y(self, value):
        return lax.ppermute(value, "y", SWAP)

    def shift_p(self, value, by):
        return lax.ppermute(value, "p", [(p, p + by) for p in range(self.np) if 0 <= p + by < self.np])

    def turn_p(self, value, by):
        return lax.ppermute(value, "p", [(p, (p + by) % self.np) for p in range(self.np)])

    def gather4(self, own):
        across = self.swap_x(own)
        return self.paired(own), self.paired(across)

    def paired(self, block):
        return jnp.concatenate([block, self.swap_core(block)], axis=0)

    def gather8(self, own, work=None):
        half = own.shape[0] // 2
        across, over = self.swap_x(own), self.swap_y(own)
        first = self.paired(own)
        done = None
        if work is not None:
            done = work(first)
            across, over = after(across, done[0]), after(over, done[0])
        far = jnp.concatenate([self.swap_y(across[:half]), self.swap_x(over[half:])])
        return (first, self.paired(across), self.paired(over), self.paired(far)), done

    def met(self, pair):
        rows = pair.shape[0] // 2
        return (pair[:rows].astype(F32) + self.swap_core(pair[rows:]).astype(F32)).astype(BF)

    def scatter4(self, second, first):
        met = self.met(second)
        across = self.swap_x(met)
        first = first(met)
        return first, self.swap_core(first[first.shape[0] // 2 :]), across

    def scatter8(self, second, third, fourth, first):
        far = self.met(fourth)
        half = far.shape[0] // 2
        by_x, by_y = self.swap_x(far[:half]), self.swap_y(far[half:])
        second, third = self.met(second), self.met(third)
        add = lambda u, v: (u.astype(F32) + v.astype(F32)).astype(BF)
        across = [self.swap_x(second[:half]), self.swap_x(add(second[half:], by_y))]
        over = [self.swap_y(add(third[:half], by_x)), self.swap_y(third[half:])]
        first = first(far)
        core = self.swap_core(first[first.shape[0] // 2 :])
        return first, core, jnp.concatenate(across), jnp.concatenate(over)

    def sum4(self, value, parts):
        def reordered(v, x, c):
            v = v.reshape(v.shape[0], parts, 2, 2, -1)
            if x:
                v = jnp.concatenate([v[:, :, 1:], v[:, :, :1]], axis=2)
            if c:
                v = jnp.concatenate([v[:, :, :, 1:], v[:, :, :, :1]], axis=3)
            return v.reshape(value.shape)

        core, across, both = self.swap_core(value), self.swap_x(value), self.swap_both(value)
        return value + reordered(core, 0, 1) + reordered(across, 1, 0) + reordered(both, 1, 1)


def pick(v, axis, index):
    return lax.dynamic_index_in_dim(v, index, axis, keepdims=False)


def after(value, *others):
    return lax.optimization_barrier((value,) + others)[0]


class Copies:
    def __init__(self, send_sem, recv_sem):
        self.sems, self.used, self.all = (send_sem, recv_sem), 0, []

    def remote(self, src, dst, device):
        k = self.used
        self.used += 1
        copy = pltpu.make_async_remote_copy(
            src_ref=src,
            dst_ref=dst,
            send_sem=self.sems[0].at[k],
            recv_sem=self.sems[1].at[k],
            device_id=device,
            device_id_type=pl.DeviceIdType.MESH,
        )
        copy.start()
        self.all.append(copy)
        return copy

    def finish(self):
        for copy in self.all:
            copy.wait_send()


def pack_kernel(count, width, offsets, turns, spot_ref, *refs):
    spot = [spot_ref[k] for k in range(3)]
    for out, turn in zip(refs[count:], turns):
        places = offsets(*[(s + t) % 2 for s, t in zip(spot, turn)])
        for w, ref in enumerate(refs[:count]):
            for k, place in enumerate(places):
                at = (w * len(places) + k) * width
                out[:, at : at + width] = ref[:, pl.ds(pl.multiple_of(place * width, HD), width)]


def pack(spot, weights, width, offsets, turns):
    rows = weights[0].shape[0]
    size = len(weights) * len(offsets(0, 0, 0)) * width
    if width % HD:
        outs = []
        for turn in turns:
            places = offsets(*[(spot[k] + turn[k]) % 2 for k in range(3)])
            cuts = [lax.dynamic_slice_in_dim(w, place * width, width, 1) for w in weights for place in places]
            outs.append(jnp.concatenate(cuts, axis=1))
        return outs
    whole = pl.BlockSpec(memory_space=pltpu.VMEM)
    return pl.pallas_call(
        functools.partial(pack_kernel, len(weights), width, offsets, turns),
        in_specs=[pl.BlockSpec(memory_space=pltpu.SMEM)] + [whole] * len(weights),
        out_specs=[whole] * len(turns),
        out_shape=[jax.ShapeDtypeStruct((rows, size), BF)] * len(turns),
        compiler_params=pltpu.CompilerParams(vmem_limit_bytes=VMEM_BYTES),
        name="pack_columns",
        cost_estimate=cost(3),
    )(spot, *weights)


TURNS8 = [(dx, dy, dc) for dy in range(2) for dx in range(2) for dc in range(2)]
TURNS4 = TURNS8[:4]


def start_kernel(groups, reach, raw, *refs):
    p, x, y, c = (lax.axis_index(a) for a in ("p", "x", "y", "c"))
    if raw:
        sources, x_ref, o_ref = refs[0:5], refs[5], refs[6]
        w_ref, feed_ref, all_ref, o_all_ref, local_sem, send_sem, recv_sem = refs[7:14]
        whole, (qkv_packs, feed_all), load_sem = refs[14:19], refs[19:21], refs[21]
        loads = [pltpu.make_async_copy(sources[k], whole[k], load_sem.at[k]) for k in range(5)]
        for load in loads:
            load.start()
        qkv_pack = [qkv_packs.at[d] for d in range(4)]
        feed_packs = [[feed_all.at[k, d] for d in range(8)] for k in range(2)]

        def packed(kinds, offsets, turns, width, dst):
            for kind in kinds:
                loads[kind].wait()
            for d, turn in enumerate(turns):
                places = offsets(*[(u + t) % 2 for u, t in zip((x, y, c), turn)])
                for w, kind in enumerate(kinds):
                    for k, place in enumerate(places):
                        at = (w * len(places) + k) * width
                        cut = whole[kind][:, pl.ds(pl.multiple_of(place * width, HD), width)]
                        dst[d, :, at : at + width] = cut

    else:
        qkv_pack, feed_packs, x_ref, o_ref = refs[0:4], (refs[4:12], refs[12:20]), refs[20], refs[21]
        w_ref, feed_ref, all_ref, o_all_ref, local_sem, send_sem, recv_sem = refs[22:]
    turned = lambda u, t: 1 - u if t else u
    group = [(p, turned(x, dx), turned(y, dy), turned(c, dc)) for dx, dy, dc in TURNS8]
    core, across, over = group[1], group[2], group[4]
    right, left = (lax.rem(p + 1, groups), x, y, c), (lax.rem(p + groups - 1, groups), x, y, c)
    rows, depth, hidden = x_ref.shape[0], qkv_pack[0].shape[0], feed_packs[0][0].shape[1]
    used = [0]

    def remote(src, dst, device):
        k = used[0]
        used[0] += 1
        copy = pltpu.make_async_remote_copy(
            src_ref=src,
            dst_ref=dst,
            send_sem=send_sem.at[k],
            recv_sem=recv_sem.at[k],
            device_id=device,
            device_id_type=pl.DeviceIdType.MESH,
        )
        copy.start()
        return copy

    def local(k, src, dst):
        copy = pltpu.make_async_copy(src, dst, local_sem.at[k])
        copy.start()
        return copy

    barrier = pltpu.get_barrier_semaphore()
    for device in group[1:] + [right, left]:
        pl.semaphore_signal(barrier, inc=1, device_id=device, device_id_type=pl.DeviceIdType.MESH)
    pl.semaphore_wait(barrier, 9)

    def at(ref, start, size):
        return ref.at[pl.ds(pl.multiple_of(start, 16), size)]

    part = rows // 2

    def tokens(t, block, i):
        return all_ref.at[pl.ds((4 * t + block) * rows + i * part, part)]

    def own_tokens(i):
        return x_ref.at[pl.ds(i * part, part)]

    def owned(q, i):
        return w_ref.at[lax.rem(p + 2 * groups - q, groups), i, y]

    slot = (4 * x + 2 * y + c) * depth
    mine = [
        w_ref.at[p, x, y, pl.ds(pl.multiple_of(c * depth, 16), depth)],
        feed_ref.at[pl.ds(pl.multiple_of(slot, 16), depth), pl.ds(0, hidden)],
        feed_ref.at[pl.ds(pl.multiple_of(slot, 16), depth), pl.ds(hidden, hidden)],
    ]
    firsts = (qkv_pack[0], feed_packs[0][0], feed_packs[1][0])
    if raw:
        packed((0, 1, 2), raw[0], TURNS4, HD, qkv_packs)
    kept = [local(0, firsts[0], mine[0]), local(3, x_ref, all_ref.at[pl.ds(0, rows)])]
    kept.append(local(4, o_ref, o_all_ref.at[p]))
    o_of = lambda q: o_all_ref.at[lax.rem(p + 2 * groups - q, groups)]
    regrouped = [remote(qkv_pack[d], mine[0], group[d]) for d in (1, 2, 3)]
    moves = [[remote(own_tokens(i), tokens(1, 0, i), right) for i in range(2)]]
    sent = regrouped + moves[0]
    if raw:
        for k in range(2):
            packed((3 + k,), raw[1], TURNS8, feed_all.shape[3] // groups, feed_all.at[k])
    kept += [local(k, firsts[k], mine[k]) for k in (1, 2)]
    kept[0].wait()
    for copy in regrouped:
        copy.wait_recv()
    along = [remote(owned(0, i), owned(0, i), right) for i in range(2)]
    o_along = remote(o_ref, o_of(0), right)
    sent += [*along, o_along]
    later = [remote(owned(0, i), owned(0, i), over) for i in range(2)]
    spread = [[(remote(own_tokens(i), tokens(0, 1, i), core), remote(own_tokens(i), tokens(0, 2, i), across)) for i in range(2)]]
    for k in (1, 2):
        later += [remote(feed_packs[k - 1][d], mine[k], group[d]) for d in range(1, 8)]
    step = 1
    ready = 0
    while step < groups or ready <= reach:
        if ready < reach:
            moves.append([])
            spread.append([])
            for i in range(2):
                moves[ready][i].wait_recv()
                src = tokens(ready + 1, 0, i)
                if ready + 1 < reach:
                    moves[-1].append(remote(src, tokens(ready + 2, 0, i), right))
                spread[-1].append(
                    (remote(src, tokens(ready + 1, 1, i), core), remote(src, tokens(ready + 1, 2, i), across))
                )
            sent += moves[-1]
        if step < groups:
            arrived, along = along, []
            for i in range(2):
                arrived[i].wait_recv()
                if step < groups - 1:
                    along.append(remote(owned(step, i), owned(step, i), right))
                later.append(remote(owned(step, i), owned(step, i), over))
            sent += along
            o_along.wait_recv()
            if step < groups - 1:
                o_along = remote(o_of(step), o_of(step), right)
                sent.append(o_along)
            step += 1
        if ready <= reach:
            for i in range(2):
                spread[ready][i][1].wait_recv()
                later.append(remote(tokens(ready, 2, i), tokens(ready, 3, i), core))
            ready += 1
    for pairs in spread:
        for near, far in pairs:
            near.wait_recv()
            sent += [near, far]
    for copy in later:
        copy.wait_recv()
    for copy in sent + later:
        copy.wait_send()
    for copy in kept[1:]:
        copy.wait()


def start(groups, reach, spot, weights, offsets, width, own_inputs, own_o):
    depth = weights[0].shape[0]
    rows, model = own_inputs.shape
    size = 3 * len(offsets[0](0, 0, 0)) * HD
    hidden = len(offsets[1](0, 0, 0)) * width
    copies = 3 + 14 + 2 * reach + 2 * (groups - 1) + 2 * groups + (groups - 1) + 6 * (reach + 1)
    anywhere = pl.BlockSpec(memory_space=pl.ANY)
    scratch = [
        pltpu.SemaphoreType.DMA((5,)),
        pltpu.SemaphoreType.DMA((copies,)),
        pltpu.SemaphoreType.DMA((copies,)),
    ]
    raw = None
    if width % HD == 0:
        raw = offsets
        scratch += [pltpu.VMEM(w.shape, BF) for w in weights]
        scratch += [pltpu.VMEM((4, depth, size), BF), pltpu.VMEM((2, 8, depth, hidden), BF)]
        scratch.append(pltpu.SemaphoreType.DMA((5,)))
    else:
        weights = [
            *pack(spot, weights[:3], HD, offsets[0], TURNS4),
            *pack(spot, weights[3:4], width, offsets[1], TURNS8),
            *pack(spot, weights[4:5], width, offsets[1], TURNS8),
        ]
    weight, feed, inputs, o_all = pl.pallas_call(
        functools.partial(start_kernel, groups, reach, raw),
        in_specs=[anywhere] * (len(weights) + 2),
        out_specs=[anywhere] * 4,
        out_shape=[
            jax.ShapeDtypeStruct((groups, 2, 2, 2 * depth, size), BF),
            jax.ShapeDtypeStruct((8 * depth, 2 * hidden), BF),
            jax.ShapeDtypeStruct((4 * (reach + 1) * rows, model), BF),
            jax.ShapeDtypeStruct((groups,) + own_o.shape, BF),
        ],
        scratch_shapes=scratch,
        compiler_params=pltpu.CompilerParams(
            collective_id=0, has_side_effects=True, vmem_limit_bytes=VMEM_BYTES
        ),
        name="start",
        cost_estimate=cost(120),
    )(*weights, own_inputs, own_o)
    return weight.reshape(-1, size), feed, inputs, o_all.reshape(-1, model)


def gate_up_kernel(x_ref, gate_w_ref, up_w_ref, narrow_ref, maps_ref, gate_ref, up_ref, gated_ref):
    rank, tile = maps_ref.shape[1:]
    gate_w, up_w = gate_w_ref[...].reshape(-1, tile), up_w_ref[...].reshape(-1, tile)
    gate = dot(x_ref[...], gate_w) + SCALE_ADAPT * dot(narrow_ref[:, :rank], maps_ref[0])
    up = dot(x_ref[...], up_w) + SCALE_ADAPT * dot(narrow_ref[:, rank:], maps_ref[1])
    gate_ref[...] = gate.astype(BF)
    up_ref[...] = up.astype(BF)
    gated_ref[...] = (gate * jax.nn.sigmoid(gate) * up).astype(BF)


def gate_up(x, weight, narrow, maps):
    rows, width = x.shape
    groups = weight.shape[0]
    hidden = weight.shape[2] // 2
    tile = 256
    steps = hidden // tile
    out = pl.BlockSpec((rows, tile), lambda s: (0, s))
    return pl.pallas_call(
        gate_up_kernel,
        grid=(steps,),
        in_specs=[
            pl.BlockSpec((rows, width), lambda s: (0, 0)),
            pl.BlockSpec((groups, width // groups, tile), lambda s: (0, 0, s)),
            pl.BlockSpec((groups, width // groups, tile), lambda s: (0, 0, s + steps)),
            pl.BlockSpec(narrow.shape, lambda s: (0, 0)),
            pl.BlockSpec(maps.shape[:2] + (tile,), lambda s: (0, 0, s)),
        ],
        out_specs=[out] * 3,
        out_shape=[jax.ShapeDtypeStruct((rows, hidden), BF)] * 3,
        compiler_params=pltpu.CompilerParams(vmem_limit_bytes=VMEM_BYTES),
        name="gate_up",
        cost_estimate=cost(1),
    )(x, weight, weight, narrow, maps)


def project_kernel(heads, own_tiles, x_ref, w_ref, in_maps_ref, out_maps_ref, *out_refs):
    pre_q_ref, pre_k_ref, value_ref, narrow_ref, square_q_ref, square_k_ref = out_refs
    width = heads * HD
    rank = out_maps_ref.shape[1]
    narrow_ref[...] = dot_nt(x_ref[...], in_maps_ref[...]).astype(BF)

    def part(k):
        cols = slice(k * width, (k + 1) * width)
        return dot(x_ref[...], w_ref[:, cols]) + SCALE_ADAPT * dot(narrow_ref[:, k * rank : (k + 1) * rank], out_maps_ref[k])

    ones = jnp.ones((8, width), BF)
    key = part(1)
    pre_k_ref[...] = key
    square_k_ref[...] = dot_nt(ones, (key * key).astype(BF))
    value_ref[...] = part(2).astype(BF)

    @pl.when(pl.program_id(0) < own_tiles)
    def _():
        query = part(0)
        pre_q_ref[...] = query
        square_q_ref[...] = dot_nt(ones, (query * query).astype(BF))


def project(x, own_rows, weight, in_maps, out_maps, heads):
    rows, width = x.shape
    local = heads * HD
    tile = 512
    own_tiles = own_rows // tile
    fixed = lambda v: pl.BlockSpec(v.shape, lambda t: (0,) * v.ndim)
    row = lambda n: pl.BlockSpec((tile, n), lambda t: (t, 0))
    return pl.pallas_call(
        functools.partial(project_kernel, heads, own_tiles),
        grid=(rows // tile,),
        in_specs=[row(width), fixed(weight), fixed(in_maps), fixed(out_maps)],
        out_specs=[
            pl.BlockSpec((tile, local), lambda t: (jnp.minimum(t, own_tiles - 1), 0)),
            row(local),
            row(local),
            row(in_maps.shape[0]),
            pl.BlockSpec((8, tile), lambda t: (0, jnp.minimum(t, own_tiles - 1))),
            pl.BlockSpec((8, tile), lambda t: (0, t)),
        ],
        out_shape=[
            jax.ShapeDtypeStruct((own_rows, local), F32),
            jax.ShapeDtypeStruct((rows, local), F32),
            jax.ShapeDtypeStruct((rows, local), BF),
            jax.ShapeDtypeStruct((rows, in_maps.shape[0]), BF),
            jax.ShapeDtypeStruct((8, own_rows), F32),
            jax.ShapeDtypeStruct((8, rows), F32),
        ],
        compiler_params=pltpu.CompilerParams(vmem_limit_bytes=VMEM_BYTES),
        name="project",
        cost_estimate=cost(1),
    )(x, weight, in_maps, out_maps)


def scales_kernel(model, q_ref, k_ref, inv_q_ref, inv_k_ref, mine, others, send_sem, recv_sem):
    p, x, y, c = (lax.axis_index(a) for a in ("p", "x", "y", "c"))
    devices = ((p, x, y, 1 - c), (p, 1 - x, y, c), (p, 1 - x, y, 1 - c))
    lines, wide = mine.shape
    half = wide // 2
    q_lines = q_ref.shape[1] // wide
    copies = Copies(send_sem, recv_sem)
    barrier = pltpu.get_barrier_semaphore()
    for device in devices:
        pl.semaphore_signal(barrier, inc=1, device_id=device, device_id_type=pl.DeviceIdType.MESH)
    for n in range(lines):
        src, at = (q_ref, n) if n < q_lines else (k_ref, n - q_lines)
        mine[n : n + 1, :] = src[:1, at * wide : (at + 1) * wide]
    pl.semaphore_wait(barrier, 3)
    moves = [copies.remote(mine, others.at[k], device) for k, device in enumerate(devices)]
    swap_lanes = lambda v: jnp.concatenate([v[:, half:], v[:, :half]], axis=1)
    swap_lines = lambda v: jnp.concatenate([v[n ^ 1 : (n ^ 1) + 1] for n in range(lines)], axis=0)
    for move in moves:
        move.wait_recv()
    total = mine[...] + swap_lanes(others[0]) + swap_lines(others[1]) + swap_lines(swap_lanes(others[2]))
    inv = lax.rsqrt(total / model + EPS).T
    for n in range(lines):
        out, at = (inv_q_ref, n) if n < q_lines else (inv_k_ref, n - q_lines)
        out[at * wide : (at + 1) * wide, :] = inv[:, n : n + 1]
    copies.finish()


def scales(square_q, square_k, model, wide):
    lines = (square_q.shape[1] + square_k.shape[1]) // wide
    vm = pl.BlockSpec(memory_space=pltpu.VMEM)
    return pl.pallas_call(
        functools.partial(scales_kernel, model),
        in_specs=[vm] * 2,
        out_specs=[vm] * 2,
        out_shape=[jax.ShapeDtypeStruct((v.shape[1], 1), F32) for v in (square_q, square_k)],
        scratch_shapes=[
            pltpu.VMEM((lines, wide), F32),
            pltpu.VMEM((3, lines, wide), F32),
            pltpu.SemaphoreType.DMA((3,)),
            pltpu.SemaphoreType.DMA((3,)),
        ],
        compiler_params=pltpu.CompilerParams(collective_id=4, has_side_effects=True),
        name="scales",
        cost_estimate=cost(1),
    )(square_q, square_k)


def rotation(row_ref, block_ref, b):
    here = slice(b, b + 1) if isinstance(b, int) else pl.ds(b, 1)
    cos, sin = block_ref[0, here, :], block_ref[1, here, :]
    return cos * row_ref[0] - sin * row_ref[1], sin * row_ref[2] + cos * row_ref[3]


def post_kernel(heads, own_tiles, q_ref, k_ref, inv_q_ref, inv_k_ref, gain_ref, row_ref, block_ref, q_out, k_out):
    width = heads * HD
    cos, sin = rotation(row_ref, block_ref, pl.program_id(0))

    def turn(pre_ref, inv, part, out_ref):
        for h in range(heads):
            cols = slice(h * HD, (h + 1) * HD)
            v = pre_ref[:, cols] * inv * gain_ref[:, part * width + h * HD : part * width + (h + 1) * HD]
            out_ref[:, cols] = (v * cos + pltpu.roll(v, HD // 2, 1) * sin).astype(BF)

    turn(k_ref, inv_k_ref[...], 1, k_out)

    @pl.when(pl.program_id(0) < own_tiles)
    def _():
        turn(q_ref, inv_q_ref[...], 0, q_out)


def post(pre_q, pre_k, inv_q, inv_k, gain, row_tables, block_tables, heads):
    rows, width = pre_k.shape
    tile = row_tables.shape[1]
    own_tiles = pre_q.shape[0] // tile
    row = lambda n: pl.BlockSpec((tile, n), lambda r: (r, 0))
    own = lambda n: pl.BlockSpec((tile, n), lambda r: (jnp.minimum(r, own_tiles - 1), 0))
    return pl.pallas_call(
        functools.partial(post_kernel, heads, own_tiles),
        grid=(rows // tile,),
        in_specs=[
            own(width),
            row(width),
            own(1),
            row(1),
            pl.BlockSpec((1, 2 * width), lambda r: (0, 0)),
            pl.BlockSpec(row_tables.shape, lambda r: (0, 0, 0)),
            pl.BlockSpec(block_tables.shape, lambda r: (0, 0, 0)),
        ],
        out_specs=[own(width), row(width)],
        out_shape=[jax.ShapeDtypeStruct(pre_q.shape, BF), jax.ShapeDtypeStruct(pre_k.shape, BF)],
        name="rope_forward",
        cost_estimate=cost(1),
    )(pre_q, pre_k, inv_q, inv_k, gain, row_tables, block_tables)


def unpost_kernel(heads, dq_ref, dk_ref, pre_q_ref, pre_k_ref, gain_ref, cos_ref, sin_ref, turn_ref, inner_ref):
    width = heads * HD
    cos, sin = cos_ref[...], sin_ref[...]
    for part, (d_ref, pre_ref) in enumerate(((dq_ref, pre_q_ref), (dk_ref, pre_k_ref))):
        total = None
        for h in range(heads):
            cols = slice(part * width + h * HD, part * width + (h + 1) * HD)
            v = d_ref[:, h * HD : (h + 1) * HD]
            turned = (v * cos - pltpu.roll(v, HD // 2, 1) * sin) * gain_ref[:, cols]
            turn_ref[:, cols] = turned
            inner = jnp.sum(turned * pre_ref[:, h * HD : (h + 1) * HD], axis=1, keepdims=True)
            total = inner if total is None else total + inner
        inner_ref[:, part : part + 1] = total


def unpost(dq, dk, pre_q, pre_k, gain, cos, sin, heads):
    rows, width = dq.shape
    tile = 256
    row = lambda n: pl.BlockSpec((tile, n), lambda r: (r, 0))
    return pl.pallas_call(
        functools.partial(unpost_kernel, heads),
        grid=(rows // tile,),
        in_specs=[row(width)] * 4 + [pl.BlockSpec((1, 2 * width), lambda r: (0, 0)), row(HD), row(HD)],
        out_specs=[row(2 * width), row(2)],
        out_shape=[jax.ShapeDtypeStruct((rows, 2 * width), F32), jax.ShapeDtypeStruct((rows, 2), F32)],
        name="rope_backward",
        cost_estimate=cost(8),
    )(dq, dk, pre_q, pre_k, gain, cos, sin)


def finish_kernel(groups, heads, early_rows, *refs):
    (
        dq_ref,
        dk_ref,
        dv_ref,
        pre_q_ref,
        pre_k_ref,
        inv_q_ref,
        inv_k_ref,
        gain_ref,
        row_ref,
        block_ref,
        in_maps_ref,
        out_maps_ref,
        narrow_ref,
        early_ref,
        wide_ref,
        choose_ref,
        weight_any,
        inputs_any,
        mid_any,
    ) = refs[:19]
    out_ref, a_model_ref, a_hidden_ref, b_model_ref, b_hidden_ref = refs[19:24]
    (
        weight,
        inputs,
        mid,
        turn,
        grad,
        back,
        stat,
        stat_in,
        far,
        near,
        core_in,
        met,
        across_in,
        near_in,
        maps,
        maps_in,
        by_x,
        by_y,
        by_y_in,
        by_p_in,
        own_sum,
        own_sum_in,
        wide_in,
        local_sem,
        send_sem,
        recv_sem,
    ) = refs[24:]
    p, x, y, c = (lax.axis_index(a) for a in ("p", "x", "y", "c"))
    core, across, both, over = (p, x, y, 1 - c), (p, 1 - x, y, c), (p, 1 - x, y, 1 - c), (p, x, 1 - y, c)
    others = [lax.rem(p + s, groups) for s in range(1, groups)]
    width = heads * HD
    rows = out_ref.shape[0]
    model = out_ref.shape[1]
    rank = out_maps_ref.shape[1]
    copies = Copies(send_sem, recv_sem)
    loads = []
    for k, (src, dst) in enumerate(((weight_any, weight), (inputs_any.at[pl.ds(0, 4 * mid.shape[0])], inputs), (mid_any, mid))):
        loads.append(pltpu.make_async_copy(src, dst, local_sem.at[k]))
        loads[-1].start()

    barrier = pltpu.get_barrier_semaphore()
    for device in [core, across, both, over] + [(q, x, y, c) for q in others]:
        pl.semaphore_signal(barrier, inc=1, device_id=device, device_id_type=pl.DeviceIdType.MESH)

    ones = jnp.ones((8, HD), BF)

    def unturn(b, carry):
        here = pl.ds(pl.multiple_of(b * rows, rows), rows)
        cos, sin = rotation(row_ref, block_ref, b)
        for part, pre_ref in enumerate((pre_q_ref, pre_k_ref)):
            product = None
            for h in range(heads):
                cols = slice(h * HD, (h + 1) * HD)
                wide_cols = slice(part * width + h * HD, part * width + (h + 1) * HD)
                v = dq_ref[here, cols] if part == 0 else dk_ref[here, cols]
                turned = (v * cos - pltpu.roll(v, HD // 2, 1) * sin) * gain_ref[:, wide_cols]
                turn[here, wide_cols] = turned
                term = turned * pre_ref[here, cols]
                product = term if product is None else product + term
            high = product.astype(BF)
            low = (product - high.astype(F32)).astype(BF)
            summed = dot_nt(ones, high) + dot_nt(ones, low)
            stat[part : part + 1, here] = summed[:1, :]
        grad[here, 2 * width :] = dv_ref[here, :].astype(BF)
        return carry

    stat[...] = jnp.zeros_like(stat)
    lax.fori_loop(0, 4, unturn, 0)
    for b in range(2 * groups):
        maps[b, :early_rows, :] = early_ref[:, b * 256 : (b + 1) * 256]
    pl.semaphore_wait(barrier, 3 + groups)
    stats = [copies.remote(stat, stat_in.at[k], device) for k, device in enumerate((core, across, both))]
    early = pl.ds(0, early_rows)
    exchanged = [copies.remote(maps.at[2 * q + 1 - x, early], maps_in.at[q, early], across) for q in range(groups)]
    wides = [
        copies.remote(wide_ref.at[:, pl.ds(pl.multiple_of(q * 256, 256), 256)], wide_in.at[k], (q, x, y, c))
        for k, q in enumerate(others)
    ]
    for copy in stats:
        copy.wait_recv()

    for b in range(4):
        here = slice(b * rows, (b + 1) * rows)
        total_row = stat[:, here]
        for k in range(3):
            d = b ^ (k + 1)
            total_row = total_row + stat_in[k, :, d * rows : (d + 1) * rows]
        inner = total_row.T / model
        for part, (pre_ref, inv_ref) in enumerate(((pre_q_ref, inv_q_ref), (pre_k_ref, inv_k_ref))):
            cols = slice(part * width, (part + 1) * width)
            inv = inv_ref[here, :]
            scale = inv * inv * inv * inner[:, part : part + 1]
            grad[here, cols] = (inv * turn[here, cols] - pre_ref[here, :] * scale).astype(BF)

    lanes = lambda side: pl.ds(pl.multiple_of(side * HD, HD), HD)

    def over_y(start, count):
        return [
            copies.remote(
                by_x.at[q, pl.ds(start, count), lanes(1 - y)], by_y_in.at[q, pl.ds(start, count)], over
            )
            for q in range(groups)
        ]

    def over_p(start, count, arriving):
        here = slice(start, start + count)
        for q, copy in enumerate(arriving):
            copy.wait_recv()
            by_y[q, here, :] = by_x[q, here, lanes(y)] + by_y_in[q, here, :]
        return [
            copies.remote(by_y.at[q, pl.ds(start, count)], by_p_in.at[k, pl.ds(start, count)], (q, x, y, c))
            for k, q in enumerate(others)
        ]

    for copy in exchanged:
        copy.wait_recv()
    for q in range(groups):
        by_x[q, :early_rows, :] = maps[2 * q + x, :early_rows, :] + maps_in[q, :early_rows, :]
    early_moves = over_y(0, early_rows)
    loads[0].wait()

    def backed(start):
        here = slice(start, start + 2 * rows)
        for k in range(3):
            part = dot_nt(grad[here, k * width : (k + 1) * width], out_maps_ref[k])
            back[here, k * rank : (k + 1) * rank] = part.astype(BF)

    def into(start, dst, side):
        here = slice(start, start + 2 * rows)

        def columns(n, carry):
            cols = pl.ds(pl.multiple_of(n * 512, 512), 512)
            full = dot_nt(grad[here, :], weight[cols, :]) + SCALE_ADAPT * dot(back[here, :], in_maps_ref[:, cols])
            dst[:, cols] = full.astype(BF)
            return carry

        steps = model // 1024
        lax.fori_loop(side * steps, (side + 1) * steps, columns, 0)

    sides = [pl.ds(k * (model // 2), model // 2) for k in range(2)]
    backed(2 * rows)
    far_copies = []
    for k in range(2):
        into(2 * rows, far, k)
        far_copies.append(
            copies.remote(far.at[pl.ds(rows, rows), sides[k]], core_in.at[:, sides[k]], core)
        )
    backed(0)

    loads[1].wait()
    late = early_rows + 3 * rank
    full_maps = SCALE_ADAPT * dot_tn(back[...], inputs[...])
    for b in range(2 * groups):
        maps[b, early_rows:late, :] = full_maps[:, b * 256 : (b + 1) * 256]
    send_late = pl.ds(early_rows, 3 * rank)
    exchanged = [
        copies.remote(maps.at[2 * q + 1 - x, send_late], maps_in.at[q, send_late], across) for q in range(groups)
    ]
    across_copies = []
    for k in range(2):
        far_copies[k].wait_recv()
        met[:, sides[k]] = (far[:rows, sides[k]].astype(F32) + core_in[:, sides[k]].astype(F32)).astype(BF)
        across_copies.append(copies.remote(met.at[:, sides[k]], across_in.at[:, sides[k]], across))
    early_moves = over_p(0, early_rows, early_moves)
    for k in range(2):
        into(0, near, k)
    near_copy = copies.remote(near.at[pl.ds(rows, rows)], near_in, core)
    for q in range(groups):
        by_x[q, late:, :] = jnp.zeros_like(by_x[q, late:, :])
    outs = SCALE_ADAPT * dot_tn(narrow_ref[...], grad[...])
    for k in range(3):
        here = slice(late + k * rank, late + (k + 1) * rank)
        for q in range(groups):
            cols = slice(k * width + q * HD, k * width + (q + 1) * HD)
            by_x[q, here, pl.ds(pl.multiple_of(c * HD, HD), HD)] = outs[k * rank : (k + 1) * rank, cols]
    for q, copy in enumerate(exchanged):
        copy.wait_recv()
        by_x[q, early_rows:late, :] = maps[2 * q + x, early_rows:late, :] + maps_in[q, early_rows:late, :]
    late_moves = over_p(early_rows, 6 * rank, over_y(early_rows, 6 * rank))
    summed = by_y[p]
    wide_sum = wide_ref[:, pl.ds(pl.multiple_of(p * 256, 256), 256)]
    for k in range(groups - 1):
        early_moves[k].wait_recv()
        late_moves[k].wait_recv()
        summed = summed + by_p_in[k]
    own_sum[...] = summed
    last = copies.remote(own_sum, own_sum_in, core)
    for k, copy in enumerate(wides):
        copy.wait_recv()
        wide_sum = wide_sum + wide_in[k]
    last.wait_recv()
    summed = summed + own_sum_in[...]
    summed = jnp.where(c == 0, summed[:, : HD // 2], summed[:, HD // 2 :])
    for n in range(choose_ref.shape[0]):
        mask = choose_ref[n : n + 1, :]
        low = mask[:, : HD // 2]
        for at, k in enumerate((5, 6, 7, 2, 0, 1)):
            a_model_ref[n, at] = low * summed[k * rank : (k + 1) * rank, :]
        for at, k in enumerate((8, 9, 10, 3, 4)):
            b_model_ref[n, at] = low * summed[k * rank : (k + 1) * rank, :]
        a_hidden_ref[n] = mask * wide_sum[:rank, :]
        for at in range(2):
            b_hidden_ref[n, at] = mask * wide_sum[(1 + at) * rank : (2 + at) * rank, :]

    loads[2].wait()
    near_copy.wait_recv()
    for copy in across_copies:
        copy.wait_recv()
    out_ref[...] = (
        mid[...]
        + near[:rows, :].astype(F32)
        + near_in[...].astype(F32)
        + across_in[...].astype(F32)
    )
    copies.finish()


def finish(groups, heads, args, weight, inputs, mid):
    own, width = args[0].shape
    rows, model = mid.shape
    rank = args[11].shape[1]
    early_rows, wide_rows, adapters = args[13].shape[0], args[14].shape[0], args[15].shape[0]
    total_rows = early_rows + 6 * rank
    late = early_rows + 3 * rank
    vm = pl.BlockSpec(memory_space=pltpu.VMEM)
    anywhere = pl.BlockSpec(memory_space=pl.ANY)
    count = 3 + groups + (groups - 1) + 5 + groups + 2 * groups + 2 * (groups - 1) + 1
    block = lambda *shape: pltpu.VMEM(shape, BF)
    full = lambda *shape: pltpu.VMEM(shape, F32)
    first_rows = lambda v: vm if v.ndim != 2 or v.shape[0] <= own else pl.BlockSpec(
        (own, v.shape[1]), lambda k: (0, 0), pipeline_mode=pl.Buffered(1)
    )
    return pl.pallas_call(
        functools.partial(finish_kernel, groups, heads, early_rows),
        grid=(1,),
        in_specs=[first_rows(v) for v in args] + [anywhere] * 3,
        out_specs=[vm] * 5,
        out_shape=[
            jax.ShapeDtypeStruct((rows, model), F32),
            jax.ShapeDtypeStruct((adapters, 6, rank, HD // 2), F32),
            jax.ShapeDtypeStruct((adapters, rank, 256), F32),
            jax.ShapeDtypeStruct((adapters, 5, rank, HD // 2), F32),
            jax.ShapeDtypeStruct((adapters, 2, rank, 256), F32),
        ],
        scratch_shapes=[
            pltpu.VMEM(weight.shape, BF),
            pltpu.VMEM((own, model), BF),
            pltpu.VMEM(mid.shape, F32),
            full(own, 2 * width),
            block(own, 3 * width),
            block(own, 3 * rank),
            full(8, own),
            full(3, 8, own),
            block(2 * rows, model),
            block(2 * rows, model),
            block(rows, model),
            block(rows, model),
            block(rows, model),
            block(rows, model),
            full(2 * groups, late, 256),
            full(groups, late, 256),
            full(groups, total_rows, 256),
            full(groups, total_rows, HD),
            full(groups, total_rows, HD),
            full(groups - 1, total_rows, HD),
            full(total_rows, HD),
            full(total_rows, HD),
            full(groups - 1, wide_rows, 256),
            pltpu.SemaphoreType.DMA((3,)),
            pltpu.SemaphoreType.DMA((count,)),
            pltpu.SemaphoreType.DMA((count,)),
        ],
        compiler_params=pltpu.CompilerParams(
            collective_id=1, has_side_effects=True, vmem_limit_bytes=VMEM_BYTES
        ),
        name="finish",
        cost_estimate=cost(60),
    )(*args, weight, inputs, mid)


NEG_FILL = -1e30


def attend_kernel(count, scale, q_ref, *refs):
    ks, vs = refs[:count], refs[count : 2 * count]
    lo_ref, pos_ref, key_ref, o_ref, log_ref = refs[2 * count :]
    rows = q_ref.shape[0] * q_ref.shape[2]
    q = q_ref[...].reshape(rows, HD)
    lo, pos = lo_ref[0], pos_ref[...]
    scores = []
    for t in range(count):
        s = dot_nt(q, ks[t][...].reshape(rows, HD)) * scale
        key = key_ref[t : t + 1, :]
        scores.append(jnp.where((key >= lo) & (key <= pos), s, NEG_FILL))
    top = functools.reduce(jnp.maximum, [jnp.max(s, axis=1, keepdims=True) for s in scores])
    powers = [jnp.exp(s - top) for s in scores]
    total = sum(jnp.sum(e, axis=1, keepdims=True) for e in powers)
    share = 1.0 / total
    out = sum(dot((e * share).astype(BF), vs[t][...].reshape(rows, HD)) for t, e in enumerate(powers))
    o_ref[...] = out.astype(BF).reshape(o_ref.shape)
    log_ref[0] = top + jnp.log(total)


def attend_back_kernel(groups, reach, heads, scale, *refs):
    (
        grad_ref,
        weight_ref,
        in_maps_ref,
        out_maps_ref,
        lo_ref,
        pos_ref,
        key_ref,
        lo_rows_ref,
        query_rows_ref,
        log_ref,
        log_rows_ref,
        back_gu_ref,
        q_any,
        k_any,
        v_any,
        o_any,
        later_any,
        middle_any,
    ) = refs[:18]
    dq_ref, dk_ref, dv_ref, back_ref, maps_ref = refs[18:23]
    (
        q_buf,
        k_buf,
        v_buf,
        o_buf,
        later_buf,
        do_buf,
        do_in,
        inner,
        inner_in,
        middle_buf,
        load_sem,
        send_sem,
        recv_sem,
    ) = refs[23:]
    p, x, y, c = (lax.axis_index(a) for a in ("p", "x", "y", "c"))
    right, left = (lax.rem(p + 1, groups), x, y, c), (lax.rem(p + groups - 1, groups), x, y, c)
    rows = q_buf.shape[2]
    full = 2 * rows
    copies = Copies(send_sem, recv_sem)
    sources = [(q_any, q_buf), (k_any, k_buf), (v_any, v_buf), (o_any, o_buf)]
    sources.append((later_any, later_buf))
    loads = []
    for n, (src, dst) in enumerate(sources):
        loads.append(pltpu.make_async_copy(src, dst, load_sem.at[n]))
        loads[-1].start()
    part = middle_buf.shape[1]

    def load_middle(n):
        src = middle_any.at[pl.ds(n * part, part)]
        copy = pltpu.make_async_copy(src, middle_buf.at[n % 2], load_sem.at[5 + n % 2])
        copy.start()
        return copy

    middles = [load_middle(n) for n in range(2)]
    barrier = pltpu.get_barrier_semaphore()
    for device in (left, right):
        pl.semaphore_signal(barrier, inc=1, device_id=device, device_id_type=pl.DeviceIdType.MESH)

    for b in range(2):
        here = slice(b * full, (b + 1) * full)
        low = dot_nt(grad_ref[here, :], out_maps_ref[...]).astype(BF)
        back_ref[here, :] = low
        value = dot_nt(grad_ref[here, :], weight_ref[...]) + SCALE_ADAPT * dot(low, in_maps_ref[...])
        do_buf[b] = value.astype(BF).reshape(2, rows, heads * HD)
        if b == 0:
            pl.semaphore_wait(barrier, 2)
            moves = []
        moves.append(copies.remote(do_buf.at[b], do_in.at[0, b], left))
    for load in loads:
        load.wait()

    def piece(ref, s, cols, first=0):
        return ref[first : first + 2, s, :, cols].reshape(full, HD)

    def put(ref, s, cols, value):
        ref[:, s, :, cols] = value.reshape(2, rows, HD)

    ones = jnp.ones((8, HD), BF)

    def sums(n, carry):
        s, cols = n // heads, pl.ds(pl.multiple_of(n % heads * HD, HD), HD)
        product = piece(do_buf, s, cols).astype(F32) * piece(o_buf, s, cols).astype(F32)
        high = product.astype(BF)
        low = (product - high.astype(F32)).astype(BF)
        inner[pl.ds(n, 1), :] = (dot_nt(ones, high) + dot_nt(ones, low))[:1, :]
        return carry

    lax.fori_loop(0, 2 * heads, sums, 0)
    inner_moves = [copies.remote(inner, inner_in.at[0], left)]

    def own(n, carry):
        s, cols = n // heads, pl.ds(pl.multiple_of(n % heads * HD, HD), HD)
        q, do = piece(q_buf, s, cols), piece(do_buf, s, cols)
        delta = jnp.sum(do.astype(F32) * piece(o_buf, s, cols).astype(F32), axis=1, keepdims=True)
        lo, pos, log_total = lo_ref[s], pos_ref[...], log_ref[n]
        dq = None
        for t in range(reach + 1):
            k, v = piece(k_buf, s, cols, 2 * t), piece(v_buf, s, cols, 2 * t)
            key = key_ref[t : t + 1, :]
            score = dot_nt(q, k) * scale
            probs = jnp.where((key >= lo) & (key <= pos), jnp.exp(score - log_total), 0.0)
            ds = (probs * (dot_nt(do, v) - delta)).astype(BF)
            part = dot(ds, k)
            dq = part if dq is None else dq + part
            if t == 0:
                put(dv_ref, s, cols, dot_tn(probs.astype(BF), do))
                put(dk_ref, s, cols, dot_tn(ds, q) * scale)
        put(dq_ref, s, cols, dq * scale)
        return carry

    lax.fori_loop(0, 2 * heads, own, 0)

    for t in range(1, reach + 1):
        arrived, moves = moves, []
        for b in range(2):
            arrived[b].wait_recv()
            if t < reach:
                moves.append(copies.remote(do_in.at[t - 1, b], do_in.at[t, b], left))
            if b == 0:
                inner_moves[-1].wait_recv()
                if t < reach:
                    inner_moves.append(copies.remote(inner_in.at[t - 1], inner_in.at[t], left))

            def from_later(n, carry, t=t, b=b):
                s, cols = n // heads, pl.ds(pl.multiple_of(n % heads * HD, HD), HD)
                lanes = slice(b * rows, (b + 1) * rows)
                k, v = piece(k_buf, s, cols), piece(v_buf, s, cols)
                q, do = later_buf[t - 1, b, s, :, cols], do_in[t - 1, b, s, :, cols]
                score = dot_nt(k, q) * scale
                key = pos_ref[...]
                lo, pos = lo_rows_ref[t, pl.ds(s, 1), lanes], query_rows_ref[t : t + 1, lanes]
                log_row = log_rows_ref[t - 1, pl.ds(n, 1), lanes]
                probs = jnp.where((key >= lo) & (key <= pos), jnp.exp(score - log_row), 0.0)
                ds = (probs * (dot_nt(v, do) - inner_in[t - 1, pl.ds(n, 1), lanes])).astype(BF)
                put(dv_ref, s, cols, piece(dv_ref, s, cols) + dot(probs.astype(BF), do))
                put(dk_ref, s, cols, piece(dk_ref, s, cols) + dot(ds, q) * scale)
                return carry

            lax.fori_loop(0, 2 * heads, from_later, 0)
        if t == 1:
            for n in range(middle_any.shape[0] // part):
                middles[n].wait()
                term = SCALE_ADAPT * dot_tn(back_gu_ref[n * part : (n + 1) * part, :], middle_buf[n % 2])
                maps_ref[...] = term if n == 0 else maps_ref[...] + term
                if (n + 3) * part <= middle_any.shape[0]:
                    middles.append(load_middle(n + 2))
    copies.finish()


def attend_back(groups, reach, heads, rows, args, later, middle_low):
    own = 4 * rows
    local = heads * HD
    vm = pl.BlockSpec(memory_space=pltpu.VMEM)
    anywhere = pl.BlockSpec(memory_space=pl.ANY)
    block = lambda n: pltpu.VMEM((2 * n, 2, rows, local), BF)
    view = lambda v: v.reshape(-1, 2, rows, local)
    count = 3 * reach
    rank2, model = args[11].shape[1], middle_low.shape[1]
    dq, dk, dv, back, maps = pl.pallas_call(
        functools.partial(attend_back_kernel, groups, reach, heads, HD**-0.5),
        in_specs=[vm] * 12 + [anywhere] * 6,
        out_specs=[vm] * 5,
        out_shape=[jax.ShapeDtypeStruct((2, 2, rows, local), F32)] * 3
        + [jax.ShapeDtypeStruct((own, args[2].shape[0]), BF), jax.ShapeDtypeStruct((rank2, model), F32)],
        scratch_shapes=[
            block(1),
            block(reach + 1),
            block(reach + 1),
            block(1),
            pltpu.VMEM((reach, 2, 2, rows, local), BF),
            block(1),
            pltpu.VMEM((reach, 2, 2, rows, local), BF),
            pltpu.VMEM((2 * heads, 2 * rows), F32),
            pltpu.VMEM((reach, 2 * heads, 2 * rows), F32),
            pltpu.VMEM((2, 2 * rows, model), BF),
            pltpu.SemaphoreType.DMA((7,)),
            pltpu.SemaphoreType.DMA((count,)),
            pltpu.SemaphoreType.DMA((count,)),
        ],
        compiler_params=pltpu.CompilerParams(
            collective_id=3, has_side_effects=True, vmem_limit_bytes=VMEM_BYTES
        ),
        name="attend_backward",
        cost_estimate=cost(70),
    )(*args[:12], *[view(v) for v in args[12:]], later.reshape(reach, 2, 2, rows, local), middle_low)
    return [v.reshape(own, local) for v in (dq, dk, dv)], back, maps


class Attention:
    def __init__(self, rows, heads, count, lo, pos, key):
        self.rows, self.heads, self.count = rows, heads, count
        self.tables = (lo, pos, key)
        full = 2 * rows
        self.block = pl.BlockSpec((2, 1, rows, HD), lambda s, h: (0, s, 0, h))
        self.part = lambda t: pl.BlockSpec((2, 1, rows, HD), lambda s, h: (t, s, 0, h))
        self.table_specs = lambda n: [
            pl.BlockSpec((1, full, 1), lambda s, h: (s, 0, 0)),
            pl.BlockSpec((full, 1), lambda s, h: (0, 0)),
            pl.BlockSpec((n, full), lambda s, h: (0, 0)),
        ]
        self.log_spec = pl.BlockSpec((1, full, 1), lambda s, h: (s * heads + h, 0, 0))
        self.params = pltpu.CompilerParams(vmem_limit_bytes=VMEM_BYTES)

    def shape(self, dtype):
        return jax.ShapeDtypeStruct((2, 2, self.rows, self.heads * HD), dtype)

    def view(self, v):
        return v.reshape(-1, 2, self.rows, v.shape[-1])

    def forward(self, q, key, value):
        count = self.count
        parts = [self.part(t) for t in range(count)]
        out, log = pl.pallas_call(
            functools.partial(attend_kernel, count, HD**-0.5),
            grid=(2, self.heads),
            in_specs=[self.block] + parts * 2 + self.table_specs(count),
            out_specs=[self.block, self.log_spec],
            out_shape=[self.shape(BF), jax.ShapeDtypeStruct((2 * self.heads, 2 * self.rows, 1), F32)],
            compiler_params=self.params,
            name="attend_forward",
            cost_estimate=cost(1),
        )(self.view(q), *[self.view(key)] * count, *[self.view(value)] * count, *self.tables)
        return out.reshape(q.shape), log


def rms_inverse(v):
    return lax.rsqrt(jnp.mean(v * v, axis=-1, keepdims=True) + EPS)


def rms_backward(v, gain, grad):
    inv = rms_inverse(v)
    turn = grad * gain
    inner = jnp.mean(v * turn, axis=-1, keepdims=True)
    return inv * turn - v * (inv * inv * inv) * inner


def total(refs):
    return sum(ref[...].astype(F32) for ref in refs)


def after_attention_kernel(*refs):
    inputs_ref, gain_ref, attn_ref, middle_ref, low_ref = refs[3:]
    attn = total(refs[:3])
    attn_ref[...] = attn
    middle = inputs_ref[...].astype(F32) + attn * rms_inverse(attn) * gain_ref[...]
    middle_ref[...] = middle
    low_ref[...] = middle.astype(BF)


def end_kernel(*refs):
    mid_ref, out_ref = refs[3:]
    out_ref[...] = mid_ref[...] + total(refs[:3])


def feed_kernel(*refs):
    (
        d_in_ref,
        d_out_ref,
        gu_out_ref,
        gu_in_ref,
        feed_gain_ref,
        attn_gain_ref,
        narrow_gu_ref,
        gated_any,
        gate_any,
        up_any,
        feed_any,
        down_any,
        middle_any,
        cot_any,
        attn_any,
        query_any,
        log_any,
    ) = refs[:17]
    result_ref, mid_ref, grad_attn_ref, back_gu_ref, maps_ref, gb_d_ref, later_any, later_log_any = refs[17:25]
    (
        down_w,
        gate_w,
        up_w,
        acts,
        blocks,
        own_pair,
        core_in,
        by_x,
        by_y,
        across_in,
        over_in,
        tokens,
        cot,
        dgu,
        narrow_d,
        back_d,
        load_sem,
        act_sem,
        free_sem,
        send_sem,
        recv_sem,
    ) = refs[25:]
    p, x, y, c = (lax.axis_index(a) for a in ("p", "x", "y", "c"))
    core, across, over = (p, x, y, 1 - c), (p, 1 - x, y, c), (p, x, 1 - y, c)
    rows, model = result_ref.shape
    size = rows // 2
    quarter = rows // 4
    hidden = down_w.shape[0]
    rank = d_in_ref.shape[0]
    copies = Copies(send_sem, recv_sem)

    def load(k, src, dst):
        copy = pltpu.make_async_copy(src, dst, load_sem.at[k])
        copy.start()
        return copy

    halves = (pl.ds(0, size), pl.ds(size, size))
    top = (pl.ds(0, quarter), pl.ds(size, quarter))
    low = (pl.ds(quarter, quarter), pl.ds(size + quarter, quarter))

    class Stream:
        def __init__(self, order, kinds):
            self.order, self.kinds, self.flight = order, kinds, []
            for _ in range(min(4, len(order))):
                self.fetch()

        def fetch(self):
            n = len(self.flight)
            if n < len(self.order):
                k, h = self.order[n]
                group = []
                for kind in self.kinds:
                    src = (gated_any, gate_any, up_any)[kind].at[pl.ds(2 * k, 2), halves[h]]
                    group.append(pltpu.make_async_copy(src, acts.at[n % 4, kind], act_sem.at[n % 4, kind]))
                    group[-1].start()
                self.flight.append(group)

        def slot(self, k, h):
            n = self.order.index((k, h))
            for copy in self.flight[n]:
                copy.wait()
            return n % 4

    def act(slot, kind, cols=slice(None)):
        return acts[slot, kind, :, :, cols].reshape(2 * size, -1)

    both = lambda order: [(k, h) for h in range(2) for k in order]
    stream = Stream(both((3, 1, 2, 0)), (0,))
    loaded = load(0, down_any, down_w)
    groups = feed_any.shape[0]
    depth = model // groups
    reach = later_any.shape[0]
    middle_load, cot_load = load(1, middle_any, tokens), load(2, cot_any, cot)
    feed_loads = []
    for k in range(groups):
        for n, dst in enumerate((gate_w, up_w)):
            src = feed_any.at[k, :, pl.ds(n * hidden, hidden)]
            feed_loads.append(load(4 + 2 * k + n, src, dst.at[pl.ds(k * depth, depth)]))
    ring = lax.axis_size("p")
    right, left = (lax.rem(p + 1, ring), x, y, c), (lax.rem(p + ring - 1, ring), x, y, c)
    barrier = pltpu.get_barrier_semaphore()
    for device in (core, across, over, right, left):
        pl.semaphore_signal(barrier, inc=1, device_id=device, device_id_type=pl.DeviceIdType.MESH)
    pl.semaphore_wait(barrier, 5)

    def pull(t):
        src = (query_any, log_any) if t == 0 else (later_any.at[t - 1], later_log_any.at[t - 1])
        return [copies.remote(src[0], later_any.at[t], left), copies.remote(src[1], later_log_any.at[t], left)]

    maps_ref[...] = jnp.zeros_like(maps_ref)
    gb_d_ref[...] = jnp.zeros_like(gb_d_ref)

    def part(k):
        return own_pair if k == 0 else blocks.at[pl.ds(2 * k, 2)]

    def store(k, h, cols, value):
        dst = part(k)
        dst[0, halves[h], cols] = value[:size].astype(BF)
        dst[1, halves[h], cols] = value[size:].astype(BF)

    def columns(n):
        return pl.ds(pl.multiple_of(n * 512, 512), 512)

    def forward(k, h):
        slot = stream.slot(k, h)
        here = 2 * k + h
        narrow_d[here] = dot_nt(act(slot, 0), d_in_ref[...]).astype(BF)

        def body(n, carry):
            cols = columns(n)
            value = dot(act(slot, 0), down_w[:, cols])
            store(k, h, cols, value + SCALE_ADAPT * dot(narrow_d[here], d_out_ref[:, cols]))
            return carry

        lax.fori_loop(0, model // 512, body, 0)
        stream.fetch()

    def taken(k, h):
        return blocks[2 * k : 2 * k + 2, halves[h], :].reshape(2 * size, model)

    def backward(k, h):
        slot = stream.slot(k, h)
        here = 2 * k + h
        low_d = dot_nt(taken(k, h), d_out_ref[...]).astype(BF)
        back_d[here] = low_d
        gb_d_ref[...] += SCALE_ADAPT * dot_tn(narrow_d[here], taken(k, h))

        def tile(t, carry):
            cols = pl.ds(pl.multiple_of(t * 256, 256), 256)
            dm = dot_nt(taken(k, h), down_w[cols, :]) + SCALE_ADAPT * dot(low_d, d_in_ref[:, cols])
            gate, up = act(slot, 1, cols).astype(F32), act(slot, 2, cols).astype(F32)
            sig = jax.nn.sigmoid(gate)
            silu = gate * sig
            dgu[here, 0, :, cols] = (dm * up * (sig + silu * (1.0 - sig))).astype(BF)
            dgu[here, 1, :, cols] = (dm * silu).astype(BF)
            return carry

        lax.fori_loop(0, hidden // 256, tile, 0)
        back_g = dot_nt(dgu[here, 0], gu_out_ref[0]).astype(BF)
        back_u = dot_nt(dgu[here, 1], gu_out_ref[1]).astype(BF)
        back = jnp.concatenate([back_g, back_u], axis=1)
        back_gu_ref[2 * k : 2 * k + 2, halves[h], :] = back.reshape(2, size, 2 * rank)

        def body(n, carry):
            cols = columns(n)
            value = dot_nt(dgu[here, 0], gate_w[cols, :]) + dot_nt(dgu[here, 1], up_w[cols, :])
            store(k, h, cols, value + SCALE_ADAPT * dot(back, gu_in_ref[:, cols]))
            return carry

        lax.fori_loop(0, model // 512, body, 0)
        stream.fetch()

    def adapter_maps():
        for k, h in stream.order:
            slot = stream.slot(k, h)
            here = 2 * k + h
            maps_ref[0] += SCALE_ADAPT * dot_tn(back_d[here], act(slot, 0))
            narrow = narrow_gu_ref[2 * k : 2 * k + 2, halves[h], :].reshape(2 * size, 2 * rank)
            for n in range(2):
                maps_ref[1 + n] += SCALE_ADAPT * dot_tn(narrow[:, n * rank : (n + 1) * rank], dgu[here, n])
            stream.fetch()

    def by_tiles(start, count, work):
        def body(n, carry):
            work(pl.multiple_of(n * 32, 32))
            return carry

        lax.fori_loop(start // 32, (start + count) // 32, body, 0)

    class Half:
        def __init__(self, h):
            self.h, self.met, self.parts, self.gone = h, {}, [], []

        def to_core(self, k):
            here = halves[self.h]
            self.met[k] = copies.remote(part(k).at[1, here], core_in.at[k, here], core)

        def meet(self, k):
            self.met[k].wait_recv()

            def work(start):
                tile = pl.ds(start, 32)
                blocks[2 * k, tile, :] = (
                    blocks[2 * k, tile, :].astype(F32) + core_in[k, tile, :].astype(F32)
                ).astype(BF)

            by_tiles(self.h * size, size, work)
            h = self.h
            if k == 3:
                self.far_x = copies.remote(blocks.at[6, top[h]], by_x.at[h], across)
                self.far_y = copies.remote(blocks.at[6, low[h]], by_y.at[h], over)
            if k == 1:
                self.parts.append(copies.remote(blocks.at[2, top[h]], across_in.at[top[h]], across))
            if k == 2:
                self.parts.append(copies.remote(blocks.at[4, low[h]], over_in.at[low[h]], over))

        def pass_far(self):
            h = self.h

            def add(block, start, more):
                def work(n):
                    here = pl.ds(n + start, 32)
                    blocks[block, here, :] = (
                        blocks[block, here, :].astype(F32) + more[h, pl.ds(n, 32), :].astype(F32)
                    ).astype(BF)

                by_tiles(0, quarter, work)

            self.far_y.wait_recv()
            add(2, h * size + quarter, by_y)
            self.parts.append(copies.remote(blocks.at[2, low[h]], across_in.at[low[h]], across))
            self.far_x.wait_recv()
            add(4, h * size, by_x)
            self.parts.append(copies.remote(blocks.at[4, top[h]], over_in.at[top[h]], over))

        def close(self, work):
            self.met[0].wait_recv()
            for copy in self.parts:
                copy.wait_recv()

            def body(start):
                tile = pl.ds(start, 32)
                total = own_pair[0, tile, :].astype(F32) + core_in[0, tile, :].astype(F32)
                work(tile, total + across_in[tile, :].astype(F32) + over_in[tile, :].astype(F32))

            by_tiles(self.h * size, size, body)

        def share(self):
            here = halves[self.h]
            self.to_x = copies.remote(blocks.at[0, here], blocks.at[2, here], across)
            self.to_y = copies.remote(blocks.at[0, here], blocks.at[4, here], over)
            self.to_c = copies.remote(blocks.at[0, here], blocks.at[1, here], core)

        def pass_x(self):
            h, here = self.h, halves[self.h]
            self.to_x.wait_recv()
            self.x_on = copies.remote(blocks.at[2, here], blocks.at[3, here], core)
            self.x_far = copies.remote(blocks.at[2, top[h]], blocks.at[6, top[h]], over)

        def pass_y(self):
            h, here = self.h, halves[self.h]
            self.to_y.wait_recv()
            self.y_on = copies.remote(blocks.at[4, here], blocks.at[5, here], core)
            self.y_far = copies.remote(blocks.at[4, low[h]], blocks.at[6, low[h]], across)

        def pass_on(self):
            here = halves[self.h]
            self.x_far.wait_recv()
            self.y_far.wait_recv()
            self.far_on = copies.remote(blocks.at[6, here], blocks.at[7, here], core)

        def ready(self, k):
            here = (self.to_c, getattr(self, "x_on", None), getattr(self, "y_on", None), getattr(self, "far_on", None))[k]
            here.wait_recv()
            gone = [] if k == 0 else [here]
            if k in (1, 2):
                gone.append(self.x_far if k == 1 else self.y_far)
            for copy in gone:
                copy.wait_send()
            self.gone += gone

    first, second = Half(0), Half(1)
    loaded.wait()
    forward(3, 0)
    first.to_core(3)
    forward(1, 0)
    first.to_core(1)
    first.meet(3)
    forward(2, 0)
    first.to_core(2)
    first.meet(1)
    forward(0, 0)
    first.to_core(0)
    first.meet(2)
    forward(3, 1)
    second.to_core(3)
    first.pass_far()
    forward(1, 1)
    second.to_core(1)
    second.meet(3)
    forward(2, 1)
    second.to_core(2)
    second.meet(1)
    forward(0, 1)
    second.to_core(0)
    second.meet(2)
    stream = Stream([(0, 0), (0, 1), (1, 0), (3, 0), (1, 1), (2, 0), (3, 1), (2, 1)], (0, 1, 2))
    middle_load.wait()
    cot_load.wait()

    def end(tile, feed):
        gain = feed_gain_ref[...]
        result_ref[tile, :] = (tokens[tile, :] + feed * rms_inverse(feed) * gain).astype(BF)
        blocks[0, tile, :] = rms_backward(feed, gain, cot[tile, :].astype(F32)).astype(BF)

    def free(half):
        for copy in [*half.met.values(), *half.parts, half.far_x, half.far_y]:
            copy.wait_send()
        for device in (core, across, over):
            pl.semaphore_signal(free_sem.at[half.h], inc=1, device_id=device, device_id_type=pl.DeviceIdType.MESH)

    first.close(end)
    free(first)
    pl.semaphore_wait(free_sem.at[0], 3)
    first.share()
    second.pass_far()
    second.close(end)
    free(second)
    pl.semaphore_wait(free_sem.at[1], 3)
    second.share()
    copies.all = [first.to_x, first.to_y, first.to_c, second.to_x, second.to_y, second.to_c]
    attn_load = load(3, attn_any, tokens)
    pulls = pull(0)
    for copy in feed_loads:
        copy.wait()
    for half in (first, second):
        half.met, half.parts = {}, []

    first.ready(0)
    backward(0, 0)
    first.to_core(0)
    first.pass_x()
    first.pass_y()
    second.ready(0)
    backward(0, 1)
    second.to_core(0)
    first.pass_on()
    first.ready(1)
    backward(1, 0)
    first.to_core(1)
    second.pass_x()
    second.pass_y()
    first.meet(1)
    for t in range(1, reach):
        for copy in pulls:
            copy.wait_recv()
        pulls = pull(t)
    first.ready(3)
    backward(3, 0)
    first.to_core(3)
    second.ready(1)
    backward(1, 1)
    second.to_core(1)
    first.meet(3)
    second.pass_on()
    first.ready(2)
    backward(2, 0)
    first.to_core(2)
    second.meet(1)
    second.ready(3)
    first.meet(2)
    backward(3, 1)
    second.to_core(3)
    first.pass_far()
    second.ready(2)
    second.meet(3)
    backward(2, 1)
    second.to_core(2)
    stream = Stream([(k, h) for k in range(4) for h in range(2)], (0,))
    attn_load.wait()

    def open_attention(tile, total):
        mid = cot[tile, :].astype(F32) + total
        mid_ref[tile, :] = mid
        grad_attn_ref[0, tile, :] = rms_backward(tokens[tile, :], attn_gain_ref[...], mid).astype(BF)

    def share_attention(h):
        here = halves[h]
        block = lambda k: grad_attn_ref.at[k, here]
        return copies.remote(block(0), block(2), across), copies.remote(block(0), block(1), core)

    def pass_attention(h, to_x):
        to_x.wait_recv()
        return copies.remote(grad_attn_ref.at[2, halves[h]], grad_attn_ref.at[3, halves[h]], core)

    second.meet(2)
    first.close(open_attention)
    to_x, to_c = share_attention(0)
    last = [to_c]
    second.pass_far()
    last.append(pass_attention(0, to_x))
    second.close(open_attention)
    to_x, to_c = share_attention(1)
    last.append(to_c)
    adapter_maps()
    last.append(pass_attention(1, to_x))
    for copy in last + pulls:
        copy.wait_recv()
    gone = first.gone + second.gone
    for copy in copies.all:
        if not any(copy is other for other in gone):
            copy.wait_send()


def feed_layer(maps, narrow_gu, acts, weights, middle, cot, attn_out, query, log, reach):
    rows, model = cot.shape
    groups, hidden = weights[0].shape[0], weights[1].shape[0]
    rank = maps[0].shape[0]
    vm = pl.BlockSpec(memory_space=pltpu.VMEM)
    anywhere = pl.BlockSpec(memory_space=pl.ANY)
    block = lambda *shape: pltpu.VMEM(shape, BF)
    count = 96 + 2 * reach
    return pl.pallas_call(
        feed_kernel,
        in_specs=[vm] * 7 + [anywhere] * 10,
        out_specs=[vm] * 6 + [anywhere] * 2,
        out_shape=[
            jax.ShapeDtypeStruct((rows, model), BF),
            jax.ShapeDtypeStruct((rows, model), F32),
            jax.ShapeDtypeStruct((4, rows, model), BF),
            jax.ShapeDtypeStruct((8, rows, 2 * rank), BF),
            jax.ShapeDtypeStruct((3, rank, hidden), F32),
            jax.ShapeDtypeStruct((rank, model), F32),
            jax.ShapeDtypeStruct((reach,) + query.shape, BF),
            jax.ShapeDtypeStruct((reach,) + log.shape, F32),
        ],
        scratch_shapes=[
            block(hidden, model),
            block(model, hidden),
            block(model, hidden),
            block(4, 3, 2, rows // 2, hidden),
            block(8, rows, model),
            block(2, rows, model),
            block(4, rows, model),
            block(2, rows // 4, model),
            block(2, rows // 4, model),
            block(rows, model),
            block(rows, model),
            pltpu.VMEM((rows, model), F32),
            block(rows, model),
            block(8, 2, rows, hidden),
            block(8, rows, rank),
            block(8, rows, rank),
            pltpu.SemaphoreType.DMA((2 * groups + 4,)),
            pltpu.SemaphoreType.DMA((4, 3)),
            pltpu.SemaphoreType.REGULAR((2,)),
            pltpu.SemaphoreType.DMA((count,)),
            pltpu.SemaphoreType.DMA((count,)),
        ],
        compiler_params=pltpu.CompilerParams(
            collective_id=2, has_side_effects=True, vmem_limit_bytes=60 * 1024 * 1024
        ),
        name="feed_layer",
        cost_estimate=cost(170),
    )(
        *maps,
        narrow_gu.reshape(8, rows, -1),
        *[v.reshape(8, rows, hidden) for v in acts],
        *weights,
        middle,
        cot,
        attn_out,
        query,
        log,
    )


def by_rows(kernel, name, rows, width, args, dtypes, us):
    tile = 64 if rows % 64 == 0 else rows
    spec = lambda v: pl.BlockSpec((1, width), lambda r: (0, 0)) if v.shape[0] == 1 else pl.BlockSpec((tile, width), lambda r: (r, 0))
    row = pl.BlockSpec((tile, width), lambda r: (r, 0))
    return pl.pallas_call(
        kernel,
        grid=(rows // tile,),
        in_specs=[spec(v) for v in args],
        out_specs=[row] * len(dtypes),
        out_shape=[jax.ShapeDtypeStruct((rows, width), d) for d in dtypes],
        compiler_params=pltpu.CompilerParams(vmem_limit_bytes=VMEM_BYTES),
        name=name,
        cost_estimate=cost(us),
    )(*args)


def on_device(
    layer_input,
    cotangent,
    document_length,
    adapter_choice_index,
    query_weight,
    key_weight,
    value_weight,
    output_weight,
    gate_weight,
    up_weight,
    down_weight,
    query_norm_gain,
    key_norm_gain,
    attention_norm_gain,
    feedforward_norm_gain,
    adapter_model_input_maps,
    adapter_down_input_maps,
    adapter_model_output_maps,
    adapter_hidden_output_maps,
):
    at = Place()
    rows = layer_input.shape[1]
    width = layer_input.shape[2]
    heads = width // HD // 4
    local = heads * HD
    rank = adapter_model_input_maps.shape[2]
    depth = query_weight.shape[0]
    hidden_rows = down_weight.shape[0]
    hidden = hidden_rows * at.np
    reach = WINDOW // (2 * rows)
    count = reach + 1

    def head_cols(v, quarter):
        return pick(v.reshape(v.shape[:-1] + (heads, 4, HD)), v.ndim, quarter).reshape(v.shape[:-1] + (local,))

    def hidden_cols(v):
        lead = v.shape[:-1]
        n = len(lead)
        v = v.reshape(lead + (at.np, 2, 2, 2, hidden_rows))
        v = pick(v, n + 3, at.c)
        v = pick(v, n + 2, at.y)
        return pick(v, n + 1, at.x).reshape(lead + (-1,))

    own_inputs = layer_input[0]
    head_offsets = lambda x, y, c: [4 * k + 2 * x + c for k in range(heads)]
    feed_offsets = lambda x, y, c: [((2 * p + x) * 2 + y) * 2 + c for p in range(at.np)]
    w_qkv, feed_piece, inputs, o_own = start(
        at.np,
        reach,
        at.spot,
        [query_weight, key_weight, value_weight, gate_weight, up_weight],
        (head_offsets, feed_offsets),
        hidden_rows,
        own_inputs,
        output_weight,
    )
    w_gu = lax.all_gather(feed_piece, "p", axis=0)
    if 2 * depth == HD:
        sent = lambda target: lax.ppermute(o_own, ("y", "c"), target)
        same = at.y == at.c
        mine_half = jnp.where(same, o_own, sent([(0, 2), (3, 1)]))
        other_half = jnp.where(same, sent([(1, 0), (2, 3)]), sent([(1, 2), (2, 1)]))
        halves = [jnp.where(at.c == 0, mine_half, other_half), jnp.where(at.c == 0, other_half, mine_half)]
        w_o = jnp.stack([v.reshape(at.np, depth, width) for v in halves], axis=1).reshape(local, width)
    else:
        o_full = lax.all_gather(output_weight, ("p", "x", "y", "c"), axis=0, tiled=True)
        w_o = pick(o_full.reshape(heads, 4, HD, width), 1, at.quarter).reshape(local, width)
    selected = adapter_choice_index[0]
    a_model = pick(adapter_model_input_maps, 0, selected)
    a_hidden = pick(adapter_down_input_maps, 0, selected)
    b_model = pick(adapter_model_output_maps, 0, selected)
    b_hidden = pick(adapter_hidden_output_maps, 0, selected)
    a_qkv = a_model[:3].reshape(3 * rank, width)
    a_gu = a_model[4:6].reshape(2 * rank, width)
    a_o = head_cols(a_model[3], at.quarter)
    a_d = hidden_cols(a_hidden)
    b_qkv = head_cols(b_model[:3], at.quarter)
    b_o, b_d = b_model[3], b_model[4]
    b_gu = hidden_cols(b_hidden)

    def diagonal(maps):
        k, r, n = maps.shape
        zero = jnp.zeros((r, n), BF)
        return jnp.concatenate(
            [jnp.concatenate([maps[a] if a == b else zero for b in range(k)], axis=1) for a in range(k)], axis=0
        )

    b_qkv_diag = diagonal(b_qkv)
    gain = jnp.concatenate(
        [head_cols(query_norm_gain[None], at.quarter), head_cols(key_norm_gain[None], at.quarter)], axis=1
    )

    step_rows = jnp.arange(rows, dtype=jnp.int32)
    spot = lambda xx: at.p * 2 * rows + xx * rows + step_rows
    pos = jnp.concatenate([spot(at.x), spot(1 - at.x)])
    lengths = lax.dynamic_slice_in_dim(document_length, 2 * at.y, 2, 0)
    bounds = jnp.cumsum(lengths, axis=1)
    bounds = jnp.where(at.c == 0, bounds, bounds[::-1])

    def lo_of(pos):
        begin = jnp.max(jnp.where(bounds[:, None, :] <= pos[None, :, None], bounds[:, None, :], 0), axis=2)
        return jnp.maximum(begin, pos[None] - (WINDOW - 1))

    lo = lo_of(pos)
    key = jnp.stack([pos - 2 * rows * t for t in range(count)])
    attention = Attention(rows, heads, count, lo[:, :, None], pos[:, None], key)

    half_dim = HD // 2
    inv_freq = ROPE_BASE ** (-(jnp.arange(half_dim, dtype=F32) * 2.0 / HD))
    first = at.p * 2 * rows
    starts = jnp.stack([first + xx * rows - 2 * rows * t for t in range(count) for xx in (at.x, at.x, 1 - at.x, 1 - at.x)])
    wide_freq = jnp.concatenate([inv_freq, inv_freq])[None]
    sign = jnp.where(jnp.arange(HD) < half_dim, -1.0, 1.0)[None]
    turn_angle = starts.astype(F32)[:, None] * wide_freq
    row_angle = step_rows.astype(F32)[:, None] * wide_freq
    row_cos, row_sin = jnp.cos(row_angle), jnp.sin(row_angle)
    row_tables = jnp.stack([row_cos, row_sin, sign * row_cos, sign * row_sin])
    block_tables = jnp.stack([jnp.cos(turn_angle), jnp.sin(turn_angle)])

    own = 4 * rows
    pre_q, pre_k, value_all, narrow_qkv, square_q, square_k = project(
        inputs, own, w_qkv, a_qkv, b_qkv, heads
    )
    w_d = lax.all_gather(after(down_weight, square_q), "p", axis=0, tiled=True)
    inv_q, inv_k = scales(square_q, square_k, width, 2 * rows)
    query, key_all = post(pre_q, pre_k, inv_q, inv_k, gain, row_tables, block_tables, heads)
    o, log = attention.forward(query, key_all, value_all)
    narrow_o = dot_nt(o, a_o).astype(BF)
    def attn_part(part, mark=None):
        ins, narrow = o[part], narrow_o[part]
        if mark is not None:
            ins = after(ins, mark)
        return (dot(ins, w_o) + SCALE_ADAPT * dot(narrow, b_o)).astype(BF)

    near_rows, far_rows = slice(0, 2 * rows), slice(2 * rows, 4 * rows)
    attn_parts = at.scatter4(attn_part(far_rows), lambda mark: attn_part(near_rows, mark))
    attn_gain, feed_gain = attention_norm_gain[None], feedforward_norm_gain[None]
    attn_out, middle, low = by_rows(
        after_attention_kernel,
        "after_attention",
        rows,
        width,
        [*attn_parts, own_inputs, attn_gain],
        [F32, F32, BF],
        4,
    )
    middle_low = jnp.concatenate(at.gather8(low)[0])
    narrow_gu = dot_nt(middle_low, a_gu).astype(BF)
    gate, up, gated = gate_up(middle_low, w_gu, narrow_gu, b_gu)
    result, grad_mid, grad_attn, back_gu, wide, gb_d, later, later_logs = feed_layer(
        (a_d, b_d, b_gu, a_gu, feed_gain, attn_gain),
        narrow_gu,
        (gated, gate, up),
        (w_gu, w_d),
        middle,
        cotangent[0],
        attn_out,
        query,
        log[:, :, 0],
        reach,
    )
    lo_rows = jnp.stack([lo_of(pos + 2 * rows * t) for t in range(count)])
    query_rows = jnp.stack([pos + 2 * rows * t for t in range(count)])
    (dq, dk, dv), back_o, ga_gu = attend_back(
        at.np,
        reach,
        heads,
        rows,
        [
            grad_attn.reshape(4 * rows, width),
            w_o,
            a_o,
            b_o,
            *attention.tables,
            lo_rows,
            query_rows,
            log,
            later_logs,
            back_gu.reshape(8 * rows, -1),
            query,
            key_all,
            value_all,
            o,
        ],
        later,
        middle_low,
    )
    def share_y(mine, other):
        return mine + at.swap_y(other)

    def share_p(v):
        total = pick(v, 1, at.p)
        for by in range(1, at.np):
            total = total + at.turn_p(pick(v, 1, (at.p + by) % at.np), by)
        return total

    def sum_model(v):
        v = v.reshape(-1, at.np, 2, 2, 2 * depth)
        v = pick(v, 2, at.x) + at.swap_x(pick(v, 2, 1 - at.x))
        return share_y(pick(v, 2, at.y), pick(v, 2, 1 - at.y))

    mine = (jnp.arange(4) == at.quarter).astype(F32)

    def spread(v):
        return (v.reshape(-1, heads, 1, HD) * mine[:, None]).reshape(-1, width)

    grad_attn = grad_attn.reshape(4 * rows, -1)
    ga_o = SCALE_ADAPT * dot_tn(back_o, o)
    gb_o = SCALE_ADAPT * dot_tn(narrow_o, grad_attn)
    choose = (jnp.arange(adapter_model_input_maps.shape[0], dtype=jnp.int32) == selected).astype(F32)
    early = jnp.concatenate([ga_gu, spread(ga_o), gb_o, gb_d])
    wide = wide.reshape(3 * rank, -1)
    if 2 * depth == HD and hidden_rows == 2 * HD:
        outs = finish(
            at.np,
            heads,
            [
                dq,
                dk,
                dv,
                pre_q,
                pre_k,
                inv_q,
                inv_k,
                gain,
                row_tables,
                block_tables,
                a_qkv,
                b_qkv,
                narrow_qkv,
                early,
                wide,
                jnp.broadcast_to(choose[:, None], (choose.shape[0], 256)),
            ],
            w_qkv,
            inputs,
            grad_mid,
        )
        return (result[None], outs[0][None], *outs[1:])
    else:
        early = sum_model(after(early, dq))
        inputs, narrow_qkv, pre_k, inv_k = (v[:own] for v in (inputs, narrow_qkv, pre_k, inv_k))
        tables = [jnp.concatenate([rotation(row_tables, block_tables, b)[k] for b in range(4)]) for k in range(2)]
        cos, sin = tables
        wide = wide.reshape(-1, at.np, hidden_rows)
        dk = after(dk, early)
        turn, inner = unpost(dq, dk, pre_q, pre_k, gain, cos, sin, heads)
        inner = at.sum4(inner.T, 1).T / width

        def unnorm(part, pre, scale):
            cols = slice(part * local, (part + 1) * local)
            return (scale * turn[:, cols] - pre * (scale * scale * scale * inner[:, part : part + 1])).astype(BF)

        grad_qkv = jnp.concatenate(
            [unnorm(0, pre_q, inv_q), unnorm(1, pre_k, inv_k), dv.astype(BF)], axis=1
        )
        back_qkv = dot_nt(grad_qkv, b_qkv_diag).astype(BF)

        def late_adapters(mark):
            back = after(back_qkv, mark)
            ga_qkv = SCALE_ADAPT * dot_tn(back, inputs)
            gb_qkv = [
                SCALE_ADAPT * dot_tn(narrow_qkv[:, k * rank : (k + 1) * rank], grad_qkv[:, k * local : (k + 1) * local])
                for k in range(3)
            ]
            return sum_model(jnp.concatenate([ga_qkv, spread(jnp.concatenate(gb_qkv))]))

        def end_part(part, mark=None):
            ins, back = grad_qkv[part], back_qkv[part]
            if mark is not None:
                ins = after(ins, mark)
            return (dot_nt(ins, w_qkv) + SCALE_ADAPT * dot(back, a_qkv)).astype(BF)

        marks = []

        def end_near(mark):
            marks.append(mark)
            return end_part(near_rows, mark)

        end_parts = at.scatter4(end_part(far_rows), end_near)
        (grad_input,) = by_rows(end_kernel, "end", rows, width, [*end_parts, grad_mid], [F32], 3)
        late = late_adapters(marks[0])
        narrow_sums = share_p(jnp.concatenate([late, early], axis=0))
        narrow_sums = narrow_sums.reshape(narrow_sums.shape[0], 2, depth)
        sums = pick(narrow_sums, 1, at.c) + at.swap_core(pick(narrow_sums, 1, 1 - at.c))
        sums = sums.reshape(-1, rank, depth)
        late, early = sums[:6], sums[6:]
        wide = share_p(after(wide, marks[0])).reshape(-1, rank, hidden_rows)
    sum_a_model = choose[:, None, None, None] * jnp.concatenate([late[:3], early[2:3], early[:2]])[None]
    sum_a_hidden = choose[:, None, None] * wide[0][None]
    sum_b_model = choose[:, None, None, None] * jnp.concatenate([late[3:], early[3:]])[None]
    sum_b_hidden = choose[:, None, None, None] * wide[1:][None]
    return (result[None], grad_input[None], sum_a_model, sum_a_hidden, sum_b_model, sum_b_hidden)


def solution(mesh):
    grid = mesh.devices.reshape(mesh.shape["ctx"] // 2, 2, mesh.shape["wt"] // 2, 2)
    split = Mesh(grid, ("p", "x", "y", "c"))
    everyone = ("p", "x", "y", "c")
    rows = P(everyone, None)
    tokens = P(("y", "c"), ("p", "x"), None)
    placed = (tokens, tokens, P(), P()) + (rows,) * 7 + (P(),) * 8
    return jax.shard_map(
        on_device,
        mesh=split,
        in_specs=placed,
        out_specs=(
            tokens,
            tokens,
            P(None, None, None, everyone),
            P(None, None, everyone),
            P(None, None, None, everyone),
            P(None, None, None, everyone),
        ),
        check_vma=False,
    )
```

```python
import functools

import jax
import jax.numpy as jnp
from jax import lax
from jax.experimental import pallas as pl
from jax.experimental.pallas import tpu as pltpu
from jax.sharding import Mesh
from jax.sharding import PartitionSpec as P

HD = 128
WINDOW = 1024
SCALE_ADAPT = 0.5
ROPE_BASE = 500000.0
EPS = 1e-06
BF = jnp.bfloat16
F32 = jnp.float32
VMEM_BYTES = 56 * 1024 * 1024


def cost(us):
    return pl.CostEstimate(flops=int(us * 1.1e9), bytes_accessed=int(us * 1e6), transcendentals=0)


def dot(a, b, dims=((1,), (0,))):
    return lax.dot_general(a, b, (dims, ((), ())), preferred_element_type=F32)


def dot_nt(a, b):
    return dot(a, b, ((1,), (1,)))


def dot_tn(a, b):
    return dot(a, b, ((0,), (0,)))


SWAP = [(0, 1), (1, 0)]


class Place:
    def __init__(self):
        self.np = lax.axis_size("p")
        self.p, self.x, self.y, self.c = (lax.axis_index(a) for a in ("p", "x", "y", "c"))
        self.quarter = 2 * self.x + self.c
        self.spot = jnp.stack([self.x, self.y, self.c]).astype(jnp.int32)

    def swap_core(self, value):
        return lax.ppermute(value, "c", SWAP)

    def swap_x(self, value):
        return lax.ppermute(value, "x", SWAP)

    def swap_both(self, value):
        return lax.ppermute(value, ("x", "c"), [(0, 3), (1, 2), (2, 1), (3, 0)])

    def swap_y(self, value):
        return lax.ppermute(value, "y", SWAP)

    def shift_p(self, value, by):
        return lax.ppermute(value, "p", [(p, p + by) for p in range(self.np) if 0 <= p + by < self.np])

    def turn_p(self, value, by):
        return lax.ppermute(value, "p", [(p, (p + by) % self.np) for p in range(self.np)])

    def gather4(self, own):
        across = self.swap_x(own)
        return self.paired(own), self.paired(across)

    def paired(self, block):
        return jnp.concatenate([block, self.swap_core(block)], axis=0)

    def gather8(self, own, work=None):
        half = own.shape[0] // 2
        across, over = self.swap_x(own), self.swap_y(own)
        first = self.paired(own)
        done = None
        if work is not None:
            done = work(first)
            across, over = after(across, done[0]), after(over, done[0])
        far = jnp.concatenate([self.swap_y(across[:half]), self.swap_x(over[half:])])
        return (first, self.paired(across), self.paired(over), self.paired(far)), done

    def met(self, pair):
        rows = pair.shape[0] // 2
        return (pair[:rows].astype(F32) + self.swap_core(pair[rows:]).astype(F32)).astype(BF)

    def scatter4(self, second, first):
        met = self.met(second)
        across = self.swap_x(met)
        first = first(met)
        return first, self.swap_core(first[first.shape[0] // 2 :]), across

    def scatter8(self, second, third, fourth, first):
        far = self.met(fourth)
        half = far.shape[0] // 2
        by_x, by_y = self.swap_x(far[:half]), self.swap_y(far[half:])
        second, third = self.met(second), self.met(third)
        add = lambda u, v: (u.astype(F32) + v.astype(F32)).astype(BF)
        across = [self.swap_x(second[:half]), self.swap_x(add(second[half:], by_y))]
        over = [self.swap_y(add(third[:half], by_x)), self.swap_y(third[half:])]
        first = first(far)
        core = self.swap_core(first[first.shape[0] // 2 :])
        return first, core, jnp.concatenate(across), jnp.concatenate(over)

    def sum4(self, value, parts):
        def reordered(v, x, c):
            v = v.reshape(v.shape[0], parts, 2, 2, -1)
            if x:
                v = jnp.concatenate([v[:, :, 1:], v[:, :, :1]], axis=2)
            if c:
                v = jnp.concatenate([v[:, :, :, 1:], v[:, :, :, :1]], axis=3)
            return v.reshape(value.shape)

        core, across, both = self.swap_core(value), self.swap_x(value), self.swap_both(value)
        return value + reordered(core, 0, 1) + reordered(across, 1, 0) + reordered(both, 1, 1)


def pick(v, axis, index):
    return lax.dynamic_index_in_dim(v, index, axis, keepdims=False)


def after(value, *others):
    return lax.optimization_barrier((value,) + others)[0]


class Copies:
    def __init__(self, send_sem, recv_sem):
        self.sems, self.used, self.all = (send_sem, recv_sem), 0, []

    def remote(self, src, dst, device):
        k = self.used
        self.used += 1
        copy = pltpu.make_async_remote_copy(
            src_ref=src,
            dst_ref=dst,
            send_sem=self.sems[0].at[k],
            recv_sem=self.sems[1].at[k],
            device_id=device,
            device_id_type=pl.DeviceIdType.MESH,
        )
        copy.start()
        self.all.append(copy)
        return copy

    def finish(self):
        for copy in self.all:
            copy.wait_send()


def pack_kernel(count, width, offsets, turns, spot_ref, *refs):
    spot = [spot_ref[k] for k in range(3)]
    for out, turn in zip(refs[count:], turns):
        places = offsets(*[(s + t) % 2 for s, t in zip(spot, turn)])
        for w, ref in enumerate(refs[:count]):
            for k, place in enumerate(places):
                at = (w * len(places) + k) * width
                out[:, at : at + width] = ref[:, pl.ds(pl.multiple_of(place * width, HD), width)]


def pack(spot, weights, width, offsets, turns):
    rows = weights[0].shape[0]
    size = len(weights) * len(offsets(0, 0, 0)) * width
    if width % HD:
        outs = []
        for turn in turns:
            places = offsets(*[(spot[k] + turn[k]) % 2 for k in range(3)])
            cuts = [lax.dynamic_slice_in_dim(w, place * width, width, 1) for w in weights for place in places]
            outs.append(jnp.concatenate(cuts, axis=1))
        return outs
    whole = pl.BlockSpec(memory_space=pltpu.VMEM)
    return pl.pallas_call(
        functools.partial(pack_kernel, len(weights), width, offsets, turns),
        in_specs=[pl.BlockSpec(memory_space=pltpu.SMEM)] + [whole] * len(weights),
        out_specs=[whole] * len(turns),
        out_shape=[jax.ShapeDtypeStruct((rows, size), BF)] * len(turns),
        compiler_params=pltpu.CompilerParams(vmem_limit_bytes=VMEM_BYTES),
        name="pack_columns",
        cost_estimate=cost(3),
    )(spot, *weights)


TURNS8 = [(dx, dy, dc) for dy in range(2) for dx in range(2) for dc in range(2)]
TURNS4 = TURNS8[:4]


def start_kernel(groups, reach, raw, *refs):
    p, x, y, c = (lax.axis_index(a) for a in ("p", "x", "y", "c"))
    if raw:
        sources, x_ref, o_ref = refs[0:5], refs[5], refs[6]
        w_ref, feed_ref, all_ref, o_all_ref, local_sem, send_sem, recv_sem = refs[7:14]
        whole, (qkv_packs, feed_all), load_sem = refs[14:19], refs[19:21], refs[21]
        loads = [pltpu.make_async_copy(sources[k], whole[k], load_sem.at[k]) for k in range(5)]
        for load in loads:
            load.start()
        qkv_pack = [qkv_packs.at[d] for d in range(4)]
        feed_packs = [[feed_all.at[k, d] for d in range(8)] for k in range(2)]

        def packed(kinds, offsets, turns, width, dst):
            for kind in kinds:
                loads[kind].wait()
            for d, turn in enumerate(turns):
                places = offsets(*[(u + t) % 2 for u, t in zip((x, y, c), turn)])
                for w, kind in enumerate(kinds):
                    for k, place in enumerate(places):
                        at = (w * len(places) + k) * width
                        cut = whole[kind][:, pl.ds(pl.multiple_of(place * width, HD), width)]
                        dst[d, :, at : at + width] = cut

    else:
        qkv_pack, feed_packs, x_ref, o_ref = refs[0:4], (refs[4:12], refs[12:20]), refs[20], refs[21]
        w_ref, feed_ref, all_ref, o_all_ref, local_sem, send_sem, recv_sem = refs[22:]
    turned = lambda u, t: 1 - u if t else u
    group = [(p, turned(x, dx), turned(y, dy), turned(c, dc)) for dx, dy, dc in TURNS8]
    core, across, over = group[1], group[2], group[4]
    right, left = (lax.rem(p + 1, groups), x, y, c), (lax.rem(p + groups - 1, groups), x, y, c)
    rows, depth, hidden = x_ref.shape[0], qkv_pack[0].shape[0], feed_packs[0][0].shape[1]
    used = [0]

    def remote(src, dst, device):
        k = used[0]
        used[0] += 1
        copy = pltpu.make_async_remote_copy(
            src_ref=src,
            dst_ref=dst,
            send_sem=send_sem.at[k],
            recv_sem=recv_sem.at[k],
            device_id=device,
            device_id_type=pl.DeviceIdType.MESH,
        )
        copy.start()
        return copy

    def local(k, src, dst):
        copy = pltpu.make_async_copy(src, dst, local_sem.at[k])
        copy.start()
        return copy

    barrier = pltpu.get_barrier_semaphore()
    for device in group[1:] + [right, left]:
        pl.semaphore_signal(barrier, inc=1, device_id=device, device_id_type=pl.DeviceIdType.MESH)
    pl.semaphore_wait(barrier, 9)

    def at(ref, start, size):
        return ref.at[pl.ds(pl.multiple_of(start, 16), size)]

    part = rows // 2

    def tokens(t, block, i):
        return all_ref.at[pl.ds((4 * t + block) * rows + i * part, part)]

    def own_tokens(i):
        return x_ref.at[pl.ds(i * part, part)]

    def owned(q, i):
        return w_ref.at[lax.rem(p + 2 * groups - q, groups), i, y]

    slot = (4 * x + 2 * y + c) * depth
    mine = [
        w_ref.at[p, x, y, pl.ds(pl.multiple_of(c * depth, 16), depth)],
        feed_ref.at[pl.ds(pl.multiple_of(slot, 16), depth), pl.ds(0, hidden)],
        feed_ref.at[pl.ds(pl.multiple_of(slot, 16), depth), pl.ds(hidden, hidden)],
    ]
    firsts = (qkv_pack[0], feed_packs[0][0], feed_packs[1][0])
    if raw:
        packed((0, 1, 2), raw[0], TURNS4, HD, qkv_packs)
    kept = [local(0, firsts[0], mine[0]), local(3, x_ref, all_ref.at[pl.ds(0, rows)])]
    kept.append(local(4, o_ref, o_all_ref.at[p]))
    o_of = lambda q: o_all_ref.at[lax.rem(p + 2 * groups - q, groups)]
    regrouped = [remote(qkv_pack[d], mine[0], group[d]) for d in (1, 2, 3)]
    moves = [[remote(own_tokens(i), tokens(1, 0, i), right) for i in range(2)]]
    sent = regrouped + moves[0]
    if raw:
        for k in range(2):
            packed((3 + k,), raw[1], TURNS8, feed_all.shape[3] // groups, feed_all.at[k])
    kept += [local(k, firsts[k], mine[k]) for k in (1, 2)]
    kept[0].wait()
    for copy in regrouped:
        copy.wait_recv()
    along = [remote(owned(0, i), owned(0, i), right) for i in range(2)]
    o_along = remote(o_ref, o_of(0), right)
    sent += [*along, o_along]
    later = [remote(owned(0, i), owned(0, i), over) for i in range(2)]
    spread = [[(remote(own_tokens(i), tokens(0, 1, i), core), remote(own_tokens(i), tokens(0, 2, i), across)) for i in range(2)]]
    for k in (1, 2):
        later += [remote(feed_packs[k - 1][d], mine[k], group[d]) for d in range(1, 8)]
    step = 1
    ready = 0
    while step < groups or ready <= reach:
        if ready < reach:
            moves.append([])
            spread.append([])
            for i in range(2):
                moves[ready][i].wait_recv()
                src = tokens(ready + 1, 0, i)
                if ready + 1 < reach:
                    moves[-1].append(remote(src, tokens(ready + 2, 0, i), right))
                spread[-1].append(
                    (remote(src, tokens(ready + 1, 1, i), core), remote(src, tokens(ready + 1, 2, i), across))
                )
            sent += moves[-1]
        if step < groups:
            arrived, along = along, []
            for i in range(2):
                arrived[i].wait_recv()
                if step < groups - 1:
                    along.append(remote(owned(step, i), owned(step, i), right))
                later.append(remote(owned(step, i), owned(step, i), over))
            sent += along
            o_along.wait_recv()
            if step < groups - 1:
                o_along = remote(o_of(step), o_of(step), right)
                sent.append(o_along)
            step += 1
        if ready <= reach:
            for i in range(2):
                spread[ready][i][1].wait_recv()
                later.append(remote(tokens(ready, 2, i), tokens(ready, 3, i), core))
            ready += 1
    for pairs in spread:
        for near, far in pairs:
            near.wait_recv()
            sent += [near, far]
    for copy in later:
        copy.wait_recv()
    for copy in sent + later:
        copy.wait_send()
    for copy in kept[1:]:
        copy.wait()


def start(groups, reach, spot, weights, offsets, width, own_inputs, own_o):
    depth = weights[0].shape[0]
    rows, model = own_inputs.shape
    size = 3 * len(offsets[0](0, 0, 0)) * HD
    hidden = len(offsets[1](0, 0, 0)) * width
    copies = 3 + 14 + 2 * reach + 2 * (groups - 1) + 2 * groups + (groups - 1) + 6 * (reach + 1)
    anywhere = pl.BlockSpec(memory_space=pl.ANY)
    scratch = [
        pltpu.SemaphoreType.DMA((5,)),
        pltpu.SemaphoreType.DMA((copies,)),
        pltpu.SemaphoreType.DMA((copies,)),
    ]
    raw = None
    if width % HD == 0:
        raw = offsets
        scratch += [pltpu.VMEM(w.shape, BF) for w in weights]
        scratch += [pltpu.VMEM((4, depth, size), BF), pltpu.VMEM((2, 8, depth, hidden), BF)]
        scratch.append(pltpu.SemaphoreType.DMA((5,)))
    else:
        weights = [
            *pack(spot, weights[:3], HD, offsets[0], TURNS4),
            *pack(spot, weights[3:4], width, offsets[1], TURNS8),
            *pack(spot, weights[4:5], width, offsets[1], TURNS8),
        ]
    weight, feed, inputs, o_all = pl.pallas_call(
        functools.partial(start_kernel, groups, reach, raw),
        in_specs=[anywhere] * (len(weights) + 2),
        out_specs=[anywhere] * 4,
        out_shape=[
            jax.ShapeDtypeStruct((groups, 2, 2, 2 * depth, size), BF),
            jax.ShapeDtypeStruct((8 * depth, 2 * hidden), BF),
            jax.ShapeDtypeStruct((4 * (reach + 1) * rows, model), BF),
            jax.ShapeDtypeStruct((groups,) + own_o.shape, BF),
        ],
        scratch_shapes=scratch,
        compiler_params=pltpu.CompilerParams(
            collective_id=0, has_side_effects=True, vmem_limit_bytes=VMEM_BYTES
        ),
        name="start",
        cost_estimate=cost(120),
    )(*weights, own_inputs, own_o)
    return weight.reshape(-1, size), feed, inputs, o_all.reshape(-1, model)


def gate_up_kernel(x_ref, gate_w_ref, up_w_ref, narrow_ref, maps_ref, gate_ref, up_ref, gated_ref):
    rank, tile = maps_ref.shape[1:]
    gate_w, up_w = gate_w_ref[...].reshape(-1, tile), up_w_ref[...].reshape(-1, tile)
    gate = dot(x_ref[...], gate_w) + SCALE_ADAPT * dot(narrow_ref[:, :rank], maps_ref[0])
    up = dot(x_ref[...], up_w) + SCALE_ADAPT * dot(narrow_ref[:, rank:], maps_ref[1])
    gate_ref[...] = gate.astype(BF)
    up_ref[...] = up.astype(BF)
    gated_ref[...] = (gate * jax.nn.sigmoid(gate) * up).astype(BF)


def gate_up(x, weight, narrow, maps):
    rows, width = x.shape
    groups = weight.shape[0]
    hidden = weight.shape[2] // 2
    tile = 256
    steps = hidden // tile
    out = pl.BlockSpec((rows, tile), lambda s: (0, s))
    return pl.pallas_call(
        gate_up_kernel,
        grid=(steps,),
        in_specs=[
            pl.BlockSpec((rows, width), lambda s: (0, 0)),
            pl.BlockSpec((groups, width // groups, tile), lambda s: (0, 0, s)),
            pl.BlockSpec((groups, width // groups, tile), lambda s: (0, 0, s + steps)),
            pl.BlockSpec(narrow.shape, lambda s: (0, 0)),
            pl.BlockSpec(maps.shape[:2] + (tile,), lambda s: (0, 0, s)),
        ],
        out_specs=[out] * 3,
        out_shape=[jax.ShapeDtypeStruct((rows, hidden), BF)] * 3,
        compiler_params=pltpu.CompilerParams(vmem_limit_bytes=VMEM_BYTES),
        name="gate_up",
        cost_estimate=cost(1),
    )(x, weight, weight, narrow, maps)


def project_kernel(heads, own_tiles, x_ref, w_ref, in_maps_ref, out_maps_ref, *out_refs):
    pre_q_ref, pre_k_ref, value_ref, narrow_ref, square_q_ref, square_k_ref = out_refs
    width = heads * HD
    rank = out_maps_ref.shape[1]
    narrow_ref[...] = dot_nt(x_ref[...], in_maps_ref[...]).astype(BF)

    def part(k):
        cols = slice(k * width, (k + 1) * width)
        return dot(x_ref[...], w_ref[:, cols]) + SCALE_ADAPT * dot(narrow_ref[:, k * rank : (k + 1) * rank], out_maps_ref[k])

    ones = jnp.ones((8, width), BF)
    key = part(1)
    pre_k_ref[...] = key
    square_k_ref[...] = dot_nt(ones, (key * key).astype(BF))
    value_ref[...] = part(2).astype(BF)

    @pl.when(pl.program_id(0) < own_tiles)
    def _():
        query = part(0)
        pre_q_ref[...] = query
        square_q_ref[...] = dot_nt(ones, (query * query).astype(BF))


def project(x, own_rows, weight, in_maps, out_maps, heads):
    rows, width = x.shape
    local = heads * HD
    tile = 512
    own_tiles = own_rows // tile
    fixed = lambda v: pl.BlockSpec(v.shape, lambda t: (0,) * v.ndim)
    row = lambda n: pl.BlockSpec((tile, n), lambda t: (t, 0))
    return pl.pallas_call(
        functools.partial(project_kernel, heads, own_tiles),
        grid=(rows // tile,),
        in_specs=[row(width), fixed(weight), fixed(in_maps), fixed(out_maps)],
        out_specs=[
            pl.BlockSpec((tile, local), lambda t: (jnp.minimum(t, own_tiles - 1), 0)),
            row(local),
            row(local),
            row(in_maps.shape[0]),
            pl.BlockSpec((8, tile), lambda t: (0, jnp.minimum(t, own_tiles - 1))),
            pl.BlockSpec((8, tile), lambda t: (0, t)),
        ],
        out_shape=[
            jax.ShapeDtypeStruct((own_rows, local), F32),
            jax.ShapeDtypeStruct((rows, local), F32),
            jax.ShapeDtypeStruct((rows, local), BF),
            jax.ShapeDtypeStruct((rows, in_maps.shape[0]), BF),
            jax.ShapeDtypeStruct((8, own_rows), F32),
            jax.ShapeDtypeStruct((8, rows), F32),
        ],
        compiler_params=pltpu.CompilerParams(vmem_limit_bytes=VMEM_BYTES),
        name="project",
        cost_estimate=cost(1),
    )(x, weight, in_maps, out_maps)


def scales_kernel(model, q_ref, k_ref, inv_q_ref, inv_k_ref, mine, others, send_sem, recv_sem):
    p, x, y, c = (lax.axis_index(a) for a in ("p", "x", "y", "c"))
    devices = ((p, x, y, 1 - c), (p, 1 - x, y, c), (p, 1 - x, y, 1 - c))
    lines, wide = mine.shape
    half = wide // 2
    q_lines = q_ref.shape[1] // wide
    copies = Copies(send_sem, recv_sem)
    barrier = pltpu.get_barrier_semaphore()
    for device in devices:
        pl.semaphore_signal(barrier, inc=1, device_id=device, device_id_type=pl.DeviceIdType.MESH)
    for n in range(lines):
        src, at = (q_ref, n) if n < q_lines else (k_ref, n - q_lines)
        mine[n : n + 1, :] = src[:1, at * wide : (at + 1) * wide]
    pl.semaphore_wait(barrier, 3)
    moves = [copies.remote(mine, others.at[k], device) for k, device in enumerate(devices)]
    swap_lanes = lambda v: jnp.concatenate([v[:, half:], v[:, :half]], axis=1)
    swap_lines = lambda v: jnp.concatenate([v[n ^ 1 : (n ^ 1) + 1] for n in range(lines)], axis=0)
    for move in moves:
        move.wait_recv()
    total = mine[...] + swap_lanes(others[0]) + swap_lines(others[1]) + swap_lines(swap_lanes(others[2]))
    inv = lax.rsqrt(total / model + EPS).T
    for n in range(lines):
        out, at = (inv_q_ref, n) if n < q_lines else (inv_k_ref, n - q_lines)
        out[at * wide : (at + 1) * wide, :] = inv[:, n : n + 1]
    copies.finish()


def scales(square_q, square_k, model, wide):
    lines = (square_q.shape[1] + square_k.shape[1]) // wide
    vm = pl.BlockSpec(memory_space=pltpu.VMEM)
    return pl.pallas_call(
        functools.partial(scales_kernel, model),
        in_specs=[vm] * 2,
        out_specs=[vm] * 2,
        out_shape=[jax.ShapeDtypeStruct((v.shape[1], 1), F32) for v in (square_q, square_k)],
        scratch_shapes=[
            pltpu.VMEM((lines, wide), F32),
            pltpu.VMEM((3, lines, wide), F32),
            pltpu.SemaphoreType.DMA((3,)),
            pltpu.SemaphoreType.DMA((3,)),
        ],
        compiler_params=pltpu.CompilerParams(collective_id=4, has_side_effects=True),
        name="scales",
        cost_estimate=cost(1),
    )(square_q, square_k)


def rotation(row_ref, block_ref, b):
    here = slice(b, b + 1) if isinstance(b, int) else pl.ds(b, 1)
    cos, sin = block_ref[0, here, :], block_ref[1, here, :]
    return cos * row_ref[0] - sin * row_ref[1], sin * row_ref[2] + cos * row_ref[3]


def post_kernel(heads, own_tiles, q_ref, k_ref, inv_q_ref, inv_k_ref, gain_ref, row_ref, block_ref, q_out, k_out):
    width = heads * HD
    cos, sin = rotation(row_ref, block_ref, pl.program_id(0))

    def turn(pre_ref, inv, part, out_ref):
        for h in range(heads):
            cols = slice(h * HD, (h + 1) * HD)
            v = pre_ref[:, cols] * inv * gain_ref[:, part * width + h * HD : part * width + (h + 1) * HD]
            out_ref[:, cols] = (v * cos + pltpu.roll(v, HD // 2, 1) * sin).astype(BF)

    turn(k_ref, inv_k_ref[...], 1, k_out)

    @pl.when(pl.program_id(0) < own_tiles)
    def _():
        turn(q_ref, inv_q_ref[...], 0, q_out)


def post(pre_q, pre_k, inv_q, inv_k, gain, row_tables, block_tables, heads):
    rows, width = pre_k.shape
    tile = row_tables.shape[1]
    own_tiles = pre_q.shape[0] // tile
    row = lambda n: pl.BlockSpec((tile, n), lambda r: (r, 0))
    own = lambda n: pl.BlockSpec((tile, n), lambda r: (jnp.minimum(r, own_tiles - 1), 0))
    return pl.pallas_call(
        functools.partial(post_kernel, heads, own_tiles),
        grid=(rows // tile,),
        in_specs=[
            own(width),
            row(width),
            own(1),
            row(1),
            pl.BlockSpec((1, 2 * width), lambda r: (0, 0)),
            pl.BlockSpec(row_tables.shape, lambda r: (0, 0, 0)),
            pl.BlockSpec(block_tables.shape, lambda r: (0, 0, 0)),
        ],
        out_specs=[own(width), row(width)],
        out_shape=[jax.ShapeDtypeStruct(pre_q.shape, BF), jax.ShapeDtypeStruct(pre_k.shape, BF)],
        name="rope_forward",
        cost_estimate=cost(1),
    )(pre_q, pre_k, inv_q, inv_k, gain, row_tables, block_tables)


def unpost_kernel(heads, dq_ref, dk_ref, pre_q_ref, pre_k_ref, gain_ref, cos_ref, sin_ref, turn_ref, inner_ref):
    width = heads * HD
    cos, sin = cos_ref[...], sin_ref[...]
    for part, (d_ref, pre_ref) in enumerate(((dq_ref, pre_q_ref), (dk_ref, pre_k_ref))):
        total = None
        for h in range(heads):
            cols = slice(part * width + h * HD, part * width + (h + 1) * HD)
            v = d_ref[:, h * HD : (h + 1) * HD]
            turned = (v * cos - pltpu.roll(v, HD // 2, 1) * sin) * gain_ref[:, cols]
            turn_ref[:, cols] = turned
            inner = jnp.sum(turned * pre_ref[:, h * HD : (h + 1) * HD], axis=1, keepdims=True)
            total = inner if total is None else total + inner
        inner_ref[:, part : part + 1] = total


def unpost(dq, dk, pre_q, pre_k, gain, cos, sin, heads):
    rows, width = dq.shape
    tile = 256
    row = lambda n: pl.BlockSpec((tile, n), lambda r: (r, 0))
    return pl.pallas_call(
        functools.partial(unpost_kernel, heads),
        grid=(rows // tile,),
        in_specs=[row(width)] * 4 + [pl.BlockSpec((1, 2 * width), lambda r: (0, 0)), row(HD), row(HD)],
        out_specs=[row(2 * width), row(2)],
        out_shape=[jax.ShapeDtypeStruct((rows, 2 * width), F32), jax.ShapeDtypeStruct((rows, 2), F32)],
        name="rope_backward",
        cost_estimate=cost(8),
    )(dq, dk, pre_q, pre_k, gain, cos, sin)


def finish_kernel(groups, heads, early_rows, *refs):
    (
        dq_ref,
        dk_ref,
        dv_ref,
        pre_q_ref,
        pre_k_ref,
        inv_q_ref,
        inv_k_ref,
        gain_ref,
        row_ref,
        block_ref,
        in_maps_ref,
        out_maps_ref,
        narrow_ref,
        early_ref,
        wide_ref,
        choose_ref,
        weight_any,
        inputs_any,
        mid_any,
    ) = refs[:19]
    out_ref, a_model_ref, a_hidden_ref, b_model_ref, b_hidden_ref = refs[19:24]
    (
        weight,
        inputs,
        mid,
        turn,
        grad,
        back,
        stat,
        stat_in,
        far,
        near,
        core_in,
        met,
        across_in,
        near_in,
        maps,
        maps_in,
        by_x,
        by_y,
        by_y_in,
        by_p_in,
        own_sum,
        own_sum_in,
        wide_in,
        local_sem,
        send_sem,
        recv_sem,
    ) = refs[24:]
    p, x, y, c = (lax.axis_index(a) for a in ("p", "x", "y", "c"))
    core, across, both, over = (p, x, y, 1 - c), (p, 1 - x, y, c), (p, 1 - x, y, 1 - c), (p, x, 1 - y, c)
    others = [lax.rem(p + s, groups) for s in range(1, groups)]
    width = heads * HD
    rows = out_ref.shape[0]
    model = out_ref.shape[1]
    rank = out_maps_ref.shape[1]
    copies = Copies(send_sem, recv_sem)
    loads = []
    for k, (src, dst) in enumerate(((weight_any, weight), (inputs_any.at[pl.ds(0, 4 * mid.shape[0])], inputs), (mid_any, mid))):
        loads.append(pltpu.make_async_copy(src, dst, local_sem.at[k]))
        loads[-1].start()

    barrier = pltpu.get_barrier_semaphore()
    for device in [core, across, both, over] + [(q, x, y, c) for q in others]:
        pl.semaphore_signal(barrier, inc=1, device_id=device, device_id_type=pl.DeviceIdType.MESH)

    ones = jnp.ones((8, HD), BF)

    def unturn(b, carry):
        here = pl.ds(pl.multiple_of(b * rows, rows), rows)
        cos, sin = rotation(row_ref, block_ref, b)
        for part, pre_ref in enumerate((pre_q_ref, pre_k_ref)):
            product = None
            for h in range(heads):
                cols = slice(h * HD, (h + 1) * HD)
                wide_cols = slice(part * width + h * HD, part * width + (h + 1) * HD)
                v = dq_ref[here, cols] if part == 0 else dk_ref[here, cols]
                turned = (v * cos - pltpu.roll(v, HD // 2, 1) * sin) * gain_ref[:, wide_cols]
                turn[here, wide_cols] = turned
                term = turned * pre_ref[here, cols]
                product = term if product is None else product + term
            high = product.astype(BF)
            low = (product - high.astype(F32)).astype(BF)
            summed = dot_nt(ones, high) + dot_nt(ones, low)
            stat[part : part + 1, here] = summed[:1, :]
        grad[here, 2 * width :] = dv_ref[here, :].astype(BF)
        return carry

    stat[...] = jnp.zeros_like(stat)
    lax.fori_loop(0, 4, unturn, 0)
    for b in range(2 * groups):
        maps[b, :early_rows, :] = early_ref[:, b * 256 : (b + 1) * 256]
    pl.semaphore_wait(barrier, 3 + groups)
    stats = [copies.remote(stat, stat_in.at[k], device) for k, device in enumerate((core, across, both))]
    early = pl.ds(0, early_rows)
    exchanged = [copies.remote(maps.at[2 * q + 1 - x, early], maps_in.at[q, early], across) for q in range(groups)]
    wides = [
        copies.remote(wide_ref.at[:, pl.ds(pl.multiple_of(q * 256, 256), 256)], wide_in.at[k], (q, x, y, c))
        for k, q in enumerate(others)
    ]
    for copy in stats:
        copy.wait_recv()

    for b in range(4):
        here = slice(b * rows, (b + 1) * rows)
        total_row = stat[:, here]
        for k in range(3):
            d = b ^ (k + 1)
            total_row = total_row + stat_in[k, :, d * rows : (d + 1) * rows]
        inner = total_row.T / model
        for part, (pre_ref, inv_ref) in enumerate(((pre_q_ref, inv_q_ref), (pre_k_ref, inv_k_ref))):
            cols = slice(part * width, (part + 1) * width)
            inv = inv_ref[here, :]
            scale = inv * inv * inv * inner[:, part : part + 1]
            grad[here, cols] = (inv * turn[here, cols] - pre_ref[here, :] * scale).astype(BF)

    lanes = lambda side: pl.ds(pl.multiple_of(side * HD, HD), HD)

    def over_y(start, count):
        return [
            copies.remote(
                by_x.at[q, pl.ds(start, count), lanes(1 - y)], by_y_in.at[q, pl.ds(start, count)], over
            )
            for q in range(groups)
        ]

    def over_p(start, count, arriving):
        here = slice(start, start + count)
        for q, copy in enumerate(arriving):
            copy.wait_recv()
            by_y[q, here, :] = by_x[q, here, lanes(y)] + by_y_in[q, here, :]
        return [
            copies.remote(by_y.at[q, pl.ds(start, count)], by_p_in.at[k, pl.ds(start, count)], (q, x, y, c))
            for k, q in enumerate(others)
        ]

    for copy in exchanged:
        copy.wait_recv()
    for q in range(groups):
        by_x[q, :early_rows, :] = maps[2 * q + x, :early_rows, :] + maps_in[q, :early_rows, :]
    early_moves = over_y(0, early_rows)
    loads[0].wait()

    def backed(start):
        here = slice(start, start + 2 * rows)
        for k in range(3):
            part = dot_nt(grad[here, k * width : (k + 1) * width], out_maps_ref[k])
            back[here, k * rank : (k + 1) * rank] = part.astype(BF)

    def into(start, dst, side):
        here = slice(start, start + 2 * rows)

        def columns(n, carry):
            cols = pl.ds(pl.multiple_of(n * 512, 512), 512)
            full = dot_nt(grad[here, :], weight[cols, :]) + SCALE_ADAPT * dot(back[here, :], in_maps_ref[:, cols])
            dst[:, cols] = full.astype(BF)
            return carry

        steps = model // 1024
        lax.fori_loop(side * steps, (side + 1) * steps, columns, 0)

    sides = [pl.ds(k * (model // 2), model // 2) for k in range(2)]
    backed(2 * rows)
    far_copies = []
    for k in range(2):
        into(2 * rows, far, k)
        far_copies.append(
            copies.remote(far.at[pl.ds(rows, rows), sides[k]], core_in.at[:, sides[k]], core)
        )
    backed(0)

    loads[1].wait()
    late = early_rows + 3 * rank
    full_maps = SCALE_ADAPT * dot_tn(back[...], inputs[...])
    for b in range(2 * groups):
        maps[b, early_rows:late, :] = full_maps[:, b * 256 : (b + 1) * 256]
    send_late = pl.ds(early_rows, 3 * rank)
    exchanged = [
        copies.remote(maps.at[2 * q + 1 - x, send_late], maps_in.at[q, send_late], across) for q in range(groups)
    ]
    across_copies = []
    for k in range(2):
        far_copies[k].wait_recv()
        met[:, sides[k]] = (far[:rows, sides[k]].astype(F32) + core_in[:, sides[k]].astype(F32)).astype(BF)
        across_copies.append(copies.remote(met.at[:, sides[k]], across_in.at[:, sides[k]], across))
    early_moves = over_p(0, early_rows, early_moves)
    for k in range(2):
        into(0, near, k)
    near_copy = copies.remote(near.at[pl.ds(rows, rows)], near_in, core)
    for q in range(groups):
        by_x[q, late:, :] = jnp.zeros_like(by_x[q, late:, :])
    outs = SCALE_ADAPT * dot_tn(narrow_ref[...], grad[...])
    for k in range(3):
        here = slice(late + k * rank, late + (k + 1) * rank)
        for q in range(groups):
            cols = slice(k * width + q * HD, k * width + (q + 1) * HD)
            by_x[q, here, pl.ds(pl.multiple_of(c * HD, HD), HD)] = outs[k * rank : (k + 1) * rank, cols]
    for q, copy in enumerate(exchanged):
        copy.wait_recv()
        by_x[q, early_rows:late, :] = maps[2 * q + x, early_rows:late, :] + maps_in[q, early_rows:late, :]
    late_moves = over_p(early_rows, 6 * rank, over_y(early_rows, 6 * rank))
    summed = by_y[p]
    wide_sum = wide_ref[:, pl.ds(pl.multiple_of(p * 256, 256), 256)]
    for k in range(groups - 1):
        early_moves[k].wait_recv()
        late_moves[k].wait_recv()
        summed = summed + by_p_in[k]
    own_sum[...] = summed
    last = copies.remote(own_sum, own_sum_in, core)
    for k, copy in enumerate(wides):
        copy.wait_recv()
        wide_sum = wide_sum + wide_in[k]
    last.wait_recv()
    summed = summed + own_sum_in[...]
    summed = jnp.where(c == 0, summed[:, : HD // 2], summed[:, HD // 2 :])
    for n in range(choose_ref.shape[0]):
        mask = choose_ref[n : n + 1, :]
        low = mask[:, : HD // 2]
        for at, k in enumerate((5, 6, 7, 2, 0, 1)):
            a_model_ref[n, at] = low * summed[k * rank : (k + 1) * rank, :]
        for at, k in enumerate((8, 9, 10, 3, 4)):
            b_model_ref[n, at] = low * summed[k * rank : (k + 1) * rank, :]
        a_hidden_ref[n] = mask * wide_sum[:rank, :]
        for at in range(2):
            b_hidden_ref[n, at] = mask * wide_sum[(1 + at) * rank : (2 + at) * rank, :]

    loads[2].wait()
    near_copy.wait_recv()
    for copy in across_copies:
        copy.wait_recv()
    out_ref[...] = (
        mid[...]
        + near[:rows, :].astype(F32)
        + near_in[...].astype(F32)
        + across_in[...].astype(F32)
    )
    copies.finish()


def finish(groups, heads, args, weight, inputs, mid):
    own, width = args[0].shape
    rows, model = mid.shape
    rank = args[11].shape[1]
    early_rows, wide_rows, adapters = args[13].shape[0], args[14].shape[0], args[15].shape[0]
    total_rows = early_rows + 6 * rank
    late = early_rows + 3 * rank
    vm = pl.BlockSpec(memory_space=pltpu.VMEM)
    anywhere = pl.BlockSpec(memory_space=pl.ANY)
    count = 3 + groups + (groups - 1) + 5 + groups + 2 * groups + 2 * (groups - 1) + 1
    block = lambda *shape: pltpu.VMEM(shape, BF)
    full = lambda *shape: pltpu.VMEM(shape, F32)
    first_rows = lambda v: vm if v.ndim != 2 or v.shape[0] <= own else pl.BlockSpec(
        (own, v.shape[1]), lambda k: (0, 0), pipeline_mode=pl.Buffered(1)
    )
    return pl.pallas_call(
        functools.partial(finish_kernel, groups, heads, early_rows),
        grid=(1,),
        in_specs=[first_rows(v) for v in args] + [anywhere] * 3,
        out_specs=[vm] * 5,
        out_shape=[
            jax.ShapeDtypeStruct((rows, model), F32),
            jax.ShapeDtypeStruct((adapters, 6, rank, HD // 2), F32),
            jax.ShapeDtypeStruct((adapters, rank, 256), F32),
            jax.ShapeDtypeStruct((adapters, 5, rank, HD // 2), F32),
            jax.ShapeDtypeStruct((adapters, 2, rank, 256), F32),
        ],
        scratch_shapes=[
            pltpu.VMEM(weight.shape, BF),
            pltpu.VMEM((own, model), BF),
            pltpu.VMEM(mid.shape, F32),
            full(own, 2 * width),
            block(own, 3 * width),
            block(own, 3 * rank),
            full(8, own),
            full(3, 8, own),
            block(2 * rows, model),
            block(2 * rows, model),
            block(rows, model),
            block(rows, model),
            block(rows, model),
            block(rows, model),
            full(2 * groups, late, 256),
            full(groups, late, 256),
            full(groups, total_rows, 256),
            full(groups, total_rows, HD),
            full(groups, total_rows, HD),
            full(groups - 1, total_rows, HD),
            full(total_rows, HD),
            full(total_rows, HD),
            full(groups - 1, wide_rows, 256),
            pltpu.SemaphoreType.DMA((3,)),
            pltpu.SemaphoreType.DMA((count,)),
            pltpu.SemaphoreType.DMA((count,)),
        ],
        compiler_params=pltpu.CompilerParams(
            collective_id=1, has_side_effects=True, vmem_limit_bytes=VMEM_BYTES
        ),
        name="finish",
        cost_estimate=cost(60),
    )(*args, weight, inputs, mid)


NEG_FILL = -1e30


def attend_kernel(count, scale, q_ref, *refs):
    ks, vs = refs[:count], refs[count : 2 * count]
    lo_ref, pos_ref, key_ref, o_ref, log_ref = refs[2 * count :]
    rows = q_ref.shape[0] * q_ref.shape[2]
    q = q_ref[...].reshape(rows, HD)
    lo, pos = lo_ref[0], pos_ref[...]
    scores = []
    for t in range(count):
        s = dot_nt(q, ks[t][...].reshape(rows, HD)) * scale
        key = key_ref[t : t + 1, :]
        scores.append(jnp.where((key >= lo) & (key <= pos), s, NEG_FILL))
    top = functools.reduce(jnp.maximum, [jnp.max(s, axis=1, keepdims=True) for s in scores])
    powers = [jnp.exp(s - top) for s in scores]
    total = sum(jnp.sum(e, axis=1, keepdims=True) for e in powers)
    share = 1.0 / total
    out = sum(dot((e * share).astype(BF), vs[t][...].reshape(rows, HD)) for t, e in enumerate(powers))
    o_ref[...] = out.astype(BF).reshape(o_ref.shape)
    log_ref[0] = top + jnp.log(total)


def attend_back_kernel(groups, reach, heads, scale, *refs):
    (
        grad_ref,
        weight_ref,
        in_maps_ref,
        out_maps_ref,
        lo_ref,
        pos_ref,
        key_ref,
        lo_rows_ref,
        query_rows_ref,
        log_ref,
        log_rows_ref,
        back_gu_ref,
        q_any,
        k_any,
        v_any,
        o_any,
        later_any,
        middle_any,
    ) = refs[:18]
    dq_ref, dk_ref, dv_ref, back_ref, maps_ref = refs[18:23]
    (
        q_buf,
        k_buf,
        v_buf,
        o_buf,
        later_buf,
        do_buf,
        do_in,
        inner,
        inner_in,
        middle_buf,
        load_sem,
        send_sem,
        recv_sem,
    ) = refs[23:]
    p, x, y, c = (lax.axis_index(a) for a in ("p", "x", "y", "c"))
    right, left = (lax.rem(p + 1, groups), x, y, c), (lax.rem(p + groups - 1, groups), x, y, c)
    rows = q_buf.shape[2]
    full = 2 * rows
    copies = Copies(send_sem, recv_sem)
    sources = [(q_any, q_buf), (k_any, k_buf), (v_any, v_buf), (o_any, o_buf)]
    sources.append((later_any, later_buf))
    loads = []
    for n, (src, dst) in enumerate(sources):
        loads.append(pltpu.make_async_copy(src, dst, load_sem.at[n]))
        loads[-1].start()
    part = middle_buf.shape[1]

    def load_middle(n):
        src = middle_any.at[pl.ds(n * part, part)]
        copy = pltpu.make_async_copy(src, middle_buf.at[n % 2], load_sem.at[5 + n % 2])
        copy.start()
        return copy

    middles = [load_middle(n) for n in range(2)]
    barrier = pltpu.get_barrier_semaphore()
    for device in (left, right):
        pl.semaphore_signal(barrier, inc=1, device_id=device, device_id_type=pl.DeviceIdType.MESH)

    for b in range(2):
        here = slice(b * full, (b + 1) * full)
        low = dot_nt(grad_ref[here, :], out_maps_ref[...]).astype(BF)
        back_ref[here, :] = low
        value = dot_nt(grad_ref[here, :], weight_ref[...]) + SCALE_ADAPT * dot(low, in_maps_ref[...])
        do_buf[b] = value.astype(BF).reshape(2, rows, heads * HD)
        if b == 0:
            pl.semaphore_wait(barrier, 2)
            moves = []
        moves.append(copies.remote(do_buf.at[b], do_in.at[0, b], left))
    for load in loads:
        load.wait()

    def piece(ref, s, cols, first=0):
        return ref[first : first + 2, s, :, cols].reshape(full, HD)

    def put(ref, s, cols, value):
        ref[:, s, :, cols] = value.reshape(2, rows, HD)

    ones = jnp.ones((8, HD), BF)

    def sums(n, carry):
        s, cols = n // heads, pl.ds(pl.multiple_of(n % heads * HD, HD), HD)
        product = piece(do_buf, s, cols).astype(F32) * piece(o_buf, s, cols).astype(F32)
        high = product.astype(BF)
        low = (product - high.astype(F32)).astype(BF)
        inner[pl.ds(n, 1), :] = (dot_nt(ones, high) + dot_nt(ones, low))[:1, :]
        return carry

    lax.fori_loop(0, 2 * heads, sums, 0)
    inner_moves = [copies.remote(inner, inner_in.at[0], left)]

    def own(n, carry):
        s, cols = n // heads, pl.ds(pl.multiple_of(n % heads * HD, HD), HD)
        q, do = piece(q_buf, s, cols), piece(do_buf, s, cols)
        delta = jnp.sum(do.astype(F32) * piece(o_buf, s, cols).astype(F32), axis=1, keepdims=True)
        lo, pos, log_total = lo_ref[s], pos_ref[...], log_ref[n]
        dq = None
        for t in range(reach + 1):
            k, v = piece(k_buf, s, cols, 2 * t), piece(v_buf, s, cols, 2 * t)
            key = key_ref[t : t + 1, :]
            score = dot_nt(q, k) * scale
            probs = jnp.where((key >= lo) & (key <= pos), jnp.exp(score - log_total), 0.0)
            ds = (probs * (dot_nt(do, v) - delta)).astype(BF)
            part = dot(ds, k)
            dq = part if dq is None else dq + part
            if t == 0:
                put(dv_ref, s, cols, dot_tn(probs.astype(BF), do))
                put(dk_ref, s, cols, dot_tn(ds, q) * scale)
        put(dq_ref, s, cols, dq * scale)
        return carry

    def pass_on(t, b):
        moves[t - 1][b].wait_recv()
        if b == 0:
            moves.append([])
        if t < reach:
            moves[t].append(copies.remote(do_in.at[t - 1, b], do_in.at[t, b], left))
        if b == 0:
            inner_moves[-1].wait_recv()
            if t < reach:
                inner_moves.append(copies.remote(inner_in.at[t - 1], inner_in.at[t], left))

    moves = [moves]
    lax.fori_loop(0, heads, own, 0)
    pass_on(1, 0)
    lax.fori_loop(heads, 2 * heads, own, 0)
    pass_on(1, 1)

    for t in range(1, reach + 1):
        for b in range(2):
            if t > 1:
                pass_on(t, b)

            def from_later(n, carry, t=t, b=b):
                s, cols = n // heads, pl.ds(pl.multiple_of(n % heads * HD, HD), HD)
                lanes = slice(b * rows, (b + 1) * rows)
                k, v = piece(k_buf, s, cols), piece(v_buf, s, cols)
                q, do = later_buf[t - 1, b, s, :, cols], do_in[t - 1, b, s, :, cols]
                score = dot_nt(k, q) * scale
                key = pos_ref[...]
                lo, pos = lo_rows_ref[t, pl.ds(s, 1), lanes], query_rows_ref[t : t + 1, lanes]
                log_row = log_rows_ref[t - 1, pl.ds(n, 1), lanes]
                probs = jnp.where((key >= lo) & (key <= pos), jnp.exp(score - log_row), 0.0)
                ds = (probs * (dot_nt(v, do) - inner_in[t - 1, pl.ds(n, 1), lanes])).astype(BF)
                put(dv_ref, s, cols, piece(dv_ref, s, cols) + dot(probs.astype(BF), do))
                put(dk_ref, s, cols, piece(dk_ref, s, cols) + dot(ds, q) * scale)
                return carry

            lax.fori_loop(0, 2 * heads, from_later, 0)
        if t == 1:
            for n in range(middle_any.shape[0] // part):
                middles[n].wait()
                term = SCALE_ADAPT * dot_tn(back_gu_ref[n * part : (n + 1) * part, :], middle_buf[n % 2])
                maps_ref[...] = term if n == 0 else maps_ref[...] + term
                if (n + 3) * part <= middle_any.shape[0]:
                    middles.append(load_middle(n + 2))
    copies.finish()


def attend_back(groups, reach, heads, rows, args, later, middle_low):
    own = 4 * rows
    local = heads * HD
    vm = pl.BlockSpec(memory_space=pltpu.VMEM)
    anywhere = pl.BlockSpec(memory_space=pl.ANY)
    block = lambda n: pltpu.VMEM((2 * n, 2, rows, local), BF)
    view = lambda v: v.reshape(-1, 2, rows, local)
    count = 3 * reach
    rank2, model = args[11].shape[1], middle_low.shape[1]
    dq, dk, dv, back, maps = pl.pallas_call(
        functools.partial(attend_back_kernel, groups, reach, heads, HD**-0.5),
        in_specs=[vm] * 12 + [anywhere] * 6,
        out_specs=[vm] * 5,
        out_shape=[jax.ShapeDtypeStruct((2, 2, rows, local), F32)] * 3
        + [jax.ShapeDtypeStruct((own, args[2].shape[0]), BF), jax.ShapeDtypeStruct((rank2, model), F32)],
        scratch_shapes=[
            block(1),
            block(reach + 1),
            block(reach + 1),
            block(1),
            pltpu.VMEM((reach, 2, 2, rows, local), BF),
            block(1),
            pltpu.VMEM((reach, 2, 2, rows, local), BF),
            pltpu.VMEM((2 * heads, 2 * rows), F32),
            pltpu.VMEM((reach, 2 * heads, 2 * rows), F32),
            pltpu.VMEM((2, 2 * rows, model), BF),
            pltpu.SemaphoreType.DMA((7,)),
            pltpu.SemaphoreType.DMA((count,)),
            pltpu.SemaphoreType.DMA((count,)),
        ],
        compiler_params=pltpu.CompilerParams(
            collective_id=3, has_side_effects=True, vmem_limit_bytes=VMEM_BYTES
        ),
        name="attend_backward",
        cost_estimate=cost(70),
    )(*args[:12], *[view(v) for v in args[12:]], later.reshape(reach, 2, 2, rows, local), middle_low)
    return [v.reshape(own, local) for v in (dq, dk, dv)], back, maps


class Attention:
    def __init__(self, rows, heads, count, lo, pos, key):
        self.rows, self.heads, self.count = rows, heads, count
        self.tables = (lo, pos, key)
        full = 2 * rows
        self.block = pl.BlockSpec((2, 1, rows, HD), lambda s, h: (0, s, 0, h))
        self.part = lambda t: pl.BlockSpec((2, 1, rows, HD), lambda s, h: (t, s, 0, h))
        self.table_specs = lambda n: [
            pl.BlockSpec((1, full, 1), lambda s, h: (s, 0, 0)),
            pl.BlockSpec((full, 1), lambda s, h: (0, 0)),
            pl.BlockSpec((n, full), lambda s, h: (0, 0)),
        ]
        self.log_spec = pl.BlockSpec((1, full, 1), lambda s, h: (s * heads + h, 0, 0))
        self.params = pltpu.CompilerParams(vmem_limit_bytes=VMEM_BYTES)

    def shape(self, dtype):
        return jax.ShapeDtypeStruct((2, 2, self.rows, self.heads * HD), dtype)

    def view(self, v):
        return v.reshape(-1, 2, self.rows, v.shape[-1])

    def forward(self, q, key, value):
        count = self.count
        parts = [self.part(t) for t in range(count)]
        out, log = pl.pallas_call(
            functools.partial(attend_kernel, count, HD**-0.5),
            grid=(2, self.heads),
            in_specs=[self.block] + parts * 2 + self.table_specs(count),
            out_specs=[self.block, self.log_spec],
            out_shape=[self.shape(BF), jax.ShapeDtypeStruct((2 * self.heads, 2 * self.rows, 1), F32)],
            compiler_params=self.params,
            name="attend_forward",
            cost_estimate=cost(1),
        )(self.view(q), *[self.view(key)] * count, *[self.view(value)] * count, *self.tables)
        return out.reshape(q.shape), log


def rms_inverse(v):
    return lax.rsqrt(jnp.mean(v * v, axis=-1, keepdims=True) + EPS)


def rms_backward(v, gain, grad):
    inv = rms_inverse(v)
    turn = grad * gain
    inner = jnp.mean(v * turn, axis=-1, keepdims=True)
    return inv * turn - v * (inv * inv * inv) * inner


def total(refs):
    return sum(ref[...].astype(F32) for ref in refs)


def after_attention_kernel(*refs):
    inputs_ref, gain_ref, attn_ref, middle_ref, low_ref = refs[3:]
    attn = total(refs[:3])
    attn_ref[...] = attn
    middle = inputs_ref[...].astype(F32) + attn * rms_inverse(attn) * gain_ref[...]
    middle_ref[...] = middle
    low_ref[...] = middle.astype(BF)


def end_kernel(*refs):
    mid_ref, out_ref = refs[3:]
    out_ref[...] = mid_ref[...] + total(refs[:3])


def feed_kernel(*refs):
    (
        d_in_ref,
        d_out_ref,
        gu_out_ref,
        gu_in_ref,
        feed_gain_ref,
        attn_gain_ref,
        narrow_gu_ref,
        gated_any,
        gate_any,
        up_any,
        feed_any,
        down_any,
        middle_any,
        cot_any,
        attn_any,
        query_any,
        log_any,
    ) = refs[:17]
    result_ref, mid_ref, grad_attn_ref, back_gu_ref, maps_ref, gb_d_ref, later_any, later_log_any = refs[17:25]
    (
        down_w,
        gate_w,
        up_w,
        acts,
        blocks,
        own_pair,
        core_in,
        by_x,
        by_y,
        across_in,
        over_in,
        tokens,
        cot,
        dgu,
        narrow_d,
        back_d,
        load_sem,
        act_sem,
        free_sem,
        send_sem,
        recv_sem,
    ) = refs[25:]
    p, x, y, c = (lax.axis_index(a) for a in ("p", "x", "y", "c"))
    core, across, over = (p, x, y, 1 - c), (p, 1 - x, y, c), (p, x, 1 - y, c)
    rows, model = result_ref.shape
    size = rows // 2
    quarter = rows // 4
    hidden = down_w.shape[0]
    rank = d_in_ref.shape[0]
    copies = Copies(send_sem, recv_sem)

    def load(k, src, dst):
        copy = pltpu.make_async_copy(src, dst, load_sem.at[k])
        copy.start()
        return copy

    halves = (pl.ds(0, size), pl.ds(size, size))
    top = (pl.ds(0, quarter), pl.ds(size, quarter))
    low = (pl.ds(quarter, quarter), pl.ds(size + quarter, quarter))

    class Stream:
        def __init__(self, order, kinds):
            self.order, self.kinds, self.flight = order, kinds, []
            for _ in range(min(4, len(order))):
                self.fetch()

        def fetch(self):
            n = len(self.flight)
            if n < len(self.order):
                k, h = self.order[n]
                group = []
                for kind in self.kinds:
                    src = (gated_any, gate_any, up_any)[kind].at[pl.ds(2 * k, 2), halves[h]]
                    group.append(pltpu.make_async_copy(src, acts.at[n % 4, kind], act_sem.at[n % 4, kind]))
                    group[-1].start()
                self.flight.append(group)

        def slot(self, k, h):
            n = self.order.index((k, h))
            for copy in self.flight[n]:
                copy.wait()
            return n % 4

    def act(slot, kind, cols=slice(None)):
        return acts[slot, kind, :, :, cols].reshape(2 * size, -1)

    both = lambda order: [(k, h) for h in range(2) for k in order]
    stream = Stream(both((3, 1, 2, 0)), (0,))
    loaded = load(0, down_any, down_w)
    groups = feed_any.shape[0]
    depth = model // groups
    reach = later_any.shape[0]
    middle_load, cot_load = load(1, middle_any, tokens), load(2, cot_any, cot)
    feed_loads = []
    for k in range(groups):
        for n, dst in enumerate((gate_w, up_w)):
            src = feed_any.at[k, :, pl.ds(n * hidden, hidden)]
            feed_loads.append(load(4 + 2 * k + n, src, dst.at[pl.ds(k * depth, depth)]))
    ring = lax.axis_size("p")
    right, left = (lax.rem(p + 1, ring), x, y, c), (lax.rem(p + ring - 1, ring), x, y, c)
    barrier = pltpu.get_barrier_semaphore()
    for device in (core, across, over, right, left):
        pl.semaphore_signal(barrier, inc=1, device_id=device, device_id_type=pl.DeviceIdType.MESH)
    pl.semaphore_wait(barrier, 5)

    def pull(t):
        src = (query_any, log_any) if t == 0 else (later_any.at[t - 1], later_log_any.at[t - 1])
        return [copies.remote(src[0], later_any.at[t], left), copies.remote(src[1], later_log_any.at[t], left)]

    maps_ref[...] = jnp.zeros_like(maps_ref)
    gb_d_ref[...] = jnp.zeros_like(gb_d_ref)

    def part(k):
        return own_pair if k == 0 else blocks.at[pl.ds(2 * k, 2)]

    def store(k, h, cols, value):
        dst = part(k)
        dst[0, halves[h], cols] = value[:size].astype(BF)
        dst[1, halves[h], cols] = value[size:].astype(BF)

    def columns(n):
        return pl.ds(pl.multiple_of(n * 512, 512), 512)

    def forward(k, h):
        slot = stream.slot(k, h)
        here = 2 * k + h
        narrow_d[here] = dot_nt(act(slot, 0), d_in_ref[...]).astype(BF)

        def body(n, carry):
            cols = columns(n)
            value = dot(act(slot, 0), down_w[:, cols])
            store(k, h, cols, value + SCALE_ADAPT * dot(narrow_d[here], d_out_ref[:, cols]))
            return carry

        lax.fori_loop(0, model // 512, body, 0)
        stream.fetch()

    def taken(k, h):
        return blocks[2 * k : 2 * k + 2, halves[h], :].reshape(2 * size, model)

    def backward(k, h):
        slot = stream.slot(k, h)
        here = 2 * k + h
        low_d = dot_nt(taken(k, h), d_out_ref[...]).astype(BF)
        back_d[here] = low_d
        gb_d_ref[...] += SCALE_ADAPT * dot_tn(narrow_d[here], taken(k, h))

        def tile(t, carry):
            cols = pl.ds(pl.multiple_of(t * 256, 256), 256)
            dm = dot_nt(taken(k, h), down_w[cols, :]) + SCALE_ADAPT * dot(low_d, d_in_ref[:, cols])
            gate, up = act(slot, 1, cols).astype(F32), act(slot, 2, cols).astype(F32)
            sig = jax.nn.sigmoid(gate)
            silu = gate * sig
            dgu[here, 0, :, cols] = (dm * up * (sig + silu * (1.0 - sig))).astype(BF)
            dgu[here, 1, :, cols] = (dm * silu).astype(BF)
            return carry

        lax.fori_loop(0, hidden // 256, tile, 0)
        back_g = dot_nt(dgu[here, 0], gu_out_ref[0]).astype(BF)
        back_u = dot_nt(dgu[here, 1], gu_out_ref[1]).astype(BF)
        back = jnp.concatenate([back_g, back_u], axis=1)
        back_gu_ref[2 * k : 2 * k + 2, halves[h], :] = back.reshape(2, size, 2 * rank)

        def body(n, carry):
            cols = columns(n)
            value = dot_nt(dgu[here, 0], gate_w[cols, :]) + dot_nt(dgu[here, 1], up_w[cols, :])
            store(k, h, cols, value + SCALE_ADAPT * dot(back, gu_in_ref[:, cols]))
            return carry

        lax.fori_loop(0, model // 512, body, 0)
        stream.fetch()

    def adapter_maps():
        for k, h in stream.order:
            slot = stream.slot(k, h)
            here = 2 * k + h
            maps_ref[0] += SCALE_ADAPT * dot_tn(back_d[here], act(slot, 0))
            narrow = narrow_gu_ref[2 * k : 2 * k + 2, halves[h], :].reshape(2 * size, 2 * rank)
            for n in range(2):
                maps_ref[1 + n] += SCALE_ADAPT * dot_tn(narrow[:, n * rank : (n + 1) * rank], dgu[here, n])
            stream.fetch()

    def by_tiles(start, count, work):
        def body(n, carry):
            work(pl.multiple_of(n * 32, 32))
            return carry

        lax.fori_loop(start // 32, (start + count) // 32, body, 0)

    class Half:
        def __init__(self, h):
            self.h, self.met, self.parts, self.gone = h, {}, [], []

        def to_core(self, k):
            here = halves[self.h]
            self.met[k] = copies.remote(part(k).at[1, here], core_in.at[k, here], core)

        def meet(self, k):
            self.met[k].wait_recv()

            def work(start):
                tile = pl.ds(start, 32)
                blocks[2 * k, tile, :] = (
                    blocks[2 * k, tile, :].astype(F32) + core_in[k, tile, :].astype(F32)
                ).astype(BF)

            by_tiles(self.h * size, size, work)
            h = self.h
            if k == 3:
                self.far_x = copies.remote(blocks.at[6, top[h]], by_x.at[h], across)
                self.far_y = copies.remote(blocks.at[6, low[h]], by_y.at[h], over)
            if k == 1:
                self.parts.append(copies.remote(blocks.at[2, top[h]], across_in.at[top[h]], across))
            if k == 2:
                self.parts.append(copies.remote(blocks.at[4, low[h]], over_in.at[low[h]], over))

        def pass_far(self):
            h = self.h

            def add(block, start, more):
                def work(n):
                    here = pl.ds(n + start, 32)
                    blocks[block, here, :] = (
                        blocks[block, here, :].astype(F32) + more[h, pl.ds(n, 32), :].astype(F32)
                    ).astype(BF)

                by_tiles(0, quarter, work)

            self.far_y.wait_recv()
            add(2, h * size + quarter, by_y)
            self.parts.append(copies.remote(blocks.at[2, low[h]], across_in.at[low[h]], across))
            self.far_x.wait_recv()
            add(4, h * size, by_x)
            self.parts.append(copies.remote(blocks.at[4, top[h]], over_in.at[top[h]], over))

        def close(self, work):
            self.met[0].wait_recv()
            for copy in self.parts:
                copy.wait_recv()

            def body(start):
                tile = pl.ds(start, 32)
                total = own_pair[0, tile, :].astype(F32) + core_in[0, tile, :].astype(F32)
                work(tile, total + across_in[tile, :].astype(F32) + over_in[tile, :].astype(F32))

            by_tiles(self.h * size, size, body)

        def share(self):
            here = halves[self.h]
            self.to_x = copies.remote(blocks.at[0, here], blocks.at[2, here], across)
            self.to_y = copies.remote(blocks.at[0, here], blocks.at[4, here], over)
            self.to_c = copies.remote(blocks.at[0, here], blocks.at[1, here], core)

        def pass_x(self):
            h, here = self.h, halves[self.h]
            self.to_x.wait_recv()
            self.x_on = copies.remote(blocks.at[2, here], blocks.at[3, here], core)
            self.x_far = copies.remote(blocks.at[2, top[h]], blocks.at[6, top[h]], over)

        def pass_y(self):
            h, here = self.h, halves[self.h]
            self.to_y.wait_recv()
            self.y_on = copies.remote(blocks.at[4, here], blocks.at[5, here], core)
            self.y_far = copies.remote(blocks.at[4, low[h]], blocks.at[6, low[h]], across)

        def pass_on(self):
            here = halves[self.h]
            self.x_far.wait_recv()
            self.y_far.wait_recv()
            self.far_on = copies.remote(blocks.at[6, here], blocks.at[7, here], core)

        def ready(self, k):
            here = (self.to_c, getattr(self, "x_on", None), getattr(self, "y_on", None), getattr(self, "far_on", None))[k]
            here.wait_recv()
            gone = [] if k == 0 else [here]
            if k in (1, 2):
                gone.append(self.x_far if k == 1 else self.y_far)
            for copy in gone:
                copy.wait_send()
            self.gone += gone

    first, second = Half(0), Half(1)
    loaded.wait()
    forward(3, 0)
    first.to_core(3)
    forward(1, 0)
    first.to_core(1)
    first.meet(3)
    forward(2, 0)
    first.to_core(2)
    first.meet(1)
    forward(0, 0)
    first.to_core(0)
    first.meet(2)
    forward(3, 1)
    second.to_core(3)
    first.pass_far()
    forward(1, 1)
    second.to_core(1)
    second.meet(3)
    forward(2, 1)
    second.to_core(2)
    second.meet(1)
    forward(0, 1)
    second.to_core(0)
    second.meet(2)
    stream = Stream([(0, 0), (0, 1), (1, 0), (3, 0), (1, 1), (2, 0), (3, 1), (2, 1)], (0, 1, 2))
    middle_load.wait()
    cot_load.wait()

    def end(tile, feed):
        gain = feed_gain_ref[...]
        result_ref[tile, :] = (tokens[tile, :] + feed * rms_inverse(feed) * gain).astype(BF)
        blocks[0, tile, :] = rms_backward(feed, gain, cot[tile, :].astype(F32)).astype(BF)

    def free(half):
        for copy in [*half.met.values(), *half.parts, half.far_x, half.far_y]:
            copy.wait_send()
        for device in (core, across, over):
            pl.semaphore_signal(free_sem.at[half.h], inc=1, device_id=device, device_id_type=pl.DeviceIdType.MESH)

    first.close(end)
    free(first)
    pl.semaphore_wait(free_sem.at[0], 3)
    first.share()
    second.pass_far()
    second.close(end)
    free(second)
    pl.semaphore_wait(free_sem.at[1], 3)
    second.share()
    copies.all = [first.to_x, first.to_y, first.to_c, second.to_x, second.to_y, second.to_c]
    attn_load = load(3, attn_any, tokens)
    pulls = pull(0)
    for copy in feed_loads:
        copy.wait()
    for half in (first, second):
        half.met, half.parts = {}, []

    first.ready(0)
    backward(0, 0)
    first.to_core(0)
    first.pass_x()
    first.pass_y()
    second.ready(0)
    backward(0, 1)
    second.to_core(0)
    first.pass_on()
    first.ready(1)
    backward(1, 0)
    first.to_core(1)
    second.pass_x()
    second.pass_y()
    first.meet(1)
    for t in range(1, reach):
        for copy in pulls:
            copy.wait_recv()
        pulls = pull(t)
    first.ready(3)
    backward(3, 0)
    first.to_core(3)
    second.ready(1)
    backward(1, 1)
    second.to_core(1)
    first.meet(3)
    second.pass_on()
    first.ready(2)
    backward(2, 0)
    first.to_core(2)
    second.meet(1)
    second.ready(3)
    first.meet(2)
    backward(3, 1)
    second.to_core(3)
    first.pass_far()
    second.ready(2)
    second.meet(3)
    backward(2, 1)
    second.to_core(2)
    stream = Stream([(k, h) for k in range(4) for h in range(2)], (0,))
    attn_load.wait()

    def open_attention(tile, total):
        mid = cot[tile, :].astype(F32) + total
        mid_ref[tile, :] = mid
        grad_attn_ref[0, tile, :] = rms_backward(tokens[tile, :], attn_gain_ref[...], mid).astype(BF)

    def share_attention(h):
        here = halves[h]
        block = lambda k: grad_attn_ref.at[k, here]
        return copies.remote(block(0), block(2), across), copies.remote(block(0), block(1), core)

    def pass_attention(h, to_x):
        to_x.wait_recv()
        return copies.remote(grad_attn_ref.at[2, halves[h]], grad_attn_ref.at[3, halves[h]], core)

    second.meet(2)
    first.close(open_attention)
    to_x, to_c = share_attention(0)
    last = [to_c]
    second.pass_far()
    last.append(pass_attention(0, to_x))
    second.close(open_attention)
    to_x, to_c = share_attention(1)
    last.append(to_c)
    adapter_maps()
    last.append(pass_attention(1, to_x))
    for copy in last + pulls:
        copy.wait_recv()
    gone = first.gone + second.gone
    for copy in copies.all:
        if not any(copy is other for other in gone):
            copy.wait_send()


def feed_layer(maps, narrow_gu, acts, weights, middle, cot, attn_out, query, log, reach):
    rows, model = cot.shape
    groups, hidden = weights[0].shape[0], weights[1].shape[0]
    rank = maps[0].shape[0]
    vm = pl.BlockSpec(memory_space=pltpu.VMEM)
    anywhere = pl.BlockSpec(memory_space=pl.ANY)
    block = lambda *shape: pltpu.VMEM(shape, BF)
    count = 96 + 2 * reach
    return pl.pallas_call(
        feed_kernel,
        in_specs=[vm] * 7 + [anywhere] * 10,
        out_specs=[vm] * 6 + [anywhere] * 2,
        out_shape=[
            jax.ShapeDtypeStruct((rows, model), BF),
            jax.ShapeDtypeStruct((rows, model), F32),
            jax.ShapeDtypeStruct((4, rows, model), BF),
            jax.ShapeDtypeStruct((8, rows, 2 * rank), BF),
            jax.ShapeDtypeStruct((3, rank, hidden), F32),
            jax.ShapeDtypeStruct((rank, model), F32),
            jax.ShapeDtypeStruct((reach,) + query.shape, BF),
            jax.ShapeDtypeStruct((reach,) + log.shape, F32),
        ],
        scratch_shapes=[
            block(hidden, model),
            block(model, hidden),
            block(model, hidden),
            block(4, 3, 2, rows // 2, hidden),
            block(8, rows, model),
            block(2, rows, model),
            block(4, rows, model),
            block(2, rows // 4, model),
            block(2, rows // 4, model),
            block(rows, model),
            block(rows, model),
            pltpu.VMEM((rows, model), F32),
            block(rows, model),
            block(8, 2, rows, hidden),
            block(8, rows, rank),
            block(8, rows, rank),
            pltpu.SemaphoreType.DMA((2 * groups + 4,)),
            pltpu.SemaphoreType.DMA((4, 3)),
            pltpu.SemaphoreType.REGULAR((2,)),
            pltpu.SemaphoreType.DMA((count,)),
            pltpu.SemaphoreType.DMA((count,)),
        ],
        compiler_params=pltpu.CompilerParams(
            collective_id=2, has_side_effects=True, vmem_limit_bytes=60 * 1024 * 1024
        ),
        name="feed_layer",
        cost_estimate=cost(170),
    )(
        *maps,
        narrow_gu.reshape(8, rows, -1),
        *[v.reshape(8, rows, hidden) for v in acts],
        *weights,
        middle,
        cot,
        attn_out,
        query,
        log,
    )


def by_rows(kernel, name, rows, width, args, dtypes, us):
    tile = 64 if rows % 64 == 0 else rows
    spec = lambda v: pl.BlockSpec((1, width), lambda r: (0, 0)) if v.shape[0] == 1 else pl.BlockSpec((tile, width), lambda r: (r, 0))
    row = pl.BlockSpec((tile, width), lambda r: (r, 0))
    return pl.pallas_call(
        kernel,
        grid=(rows // tile,),
        in_specs=[spec(v) for v in args],
        out_specs=[row] * len(dtypes),
        out_shape=[jax.ShapeDtypeStruct((rows, width), d) for d in dtypes],
        compiler_params=pltpu.CompilerParams(vmem_limit_bytes=VMEM_BYTES),
        name=name,
        cost_estimate=cost(us),
    )(*args)


def on_device(
    layer_input,
    cotangent,
    document_length,
    adapter_choice_index,
    query_weight,
    key_weight,
    value_weight,
    output_weight,
    gate_weight,
    up_weight,
    down_weight,
    query_norm_gain,
    key_norm_gain,
    attention_norm_gain,
    feedforward_norm_gain,
    adapter_model_input_maps,
    adapter_down_input_maps,
    adapter_model_output_maps,
    adapter_hidden_output_maps,
):
    at = Place()
    rows = layer_input.shape[1]
    width = layer_input.shape[2]
    heads = width // HD // 4
    local = heads * HD
    rank = adapter_model_input_maps.shape[2]
    depth = query_weight.shape[0]
    hidden_rows = down_weight.shape[0]
    hidden = hidden_rows * at.np
    reach = WINDOW // (2 * rows)
    count = reach + 1

    def head_cols(v, quarter):
        return pick(v.reshape(v.shape[:-1] + (heads, 4, HD)), v.ndim, quarter).reshape(v.shape[:-1] + (local,))

    def hidden_cols(v):
        lead = v.shape[:-1]
        n = len(lead)
        v = v.reshape(lead + (at.np, 2, 2, 2, hidden_rows))
        v = pick(v, n + 3, at.c)
        v = pick(v, n + 2, at.y)
        return pick(v, n + 1, at.x).reshape(lead + (-1,))

    own_inputs = layer_input[0]
    head_offsets = lambda x, y, c: [4 * k + 2 * x + c for k in range(heads)]
    feed_offsets = lambda x, y, c: [((2 * p + x) * 2 + y) * 2 + c for p in range(at.np)]
    w_qkv, feed_piece, inputs, o_own = start(
        at.np,
        reach,
        at.spot,
        [query_weight, key_weight, value_weight, gate_weight, up_weight],
        (head_offsets, feed_offsets),
        hidden_rows,
        own_inputs,
        output_weight,
    )
    w_gu = lax.all_gather(feed_piece, "p", axis=0)
    if 2 * depth == HD:
        sent = lambda target: lax.ppermute(o_own, ("y", "c"), target)
        same = at.y == at.c
        mine_half = jnp.where(same, o_own, sent([(0, 2), (3, 1)]))
        other_half = jnp.where(same, sent([(1, 0), (2, 3)]), sent([(1, 2), (2, 1)]))
        halves = [jnp.where(at.c == 0, mine_half, other_half), jnp.where(at.c == 0, other_half, mine_half)]
        w_o = jnp.stack([v.reshape(at.np, depth, width) for v in halves], axis=1).reshape(local, width)
    else:
        o_full = lax.all_gather(output_weight, ("p", "x", "y", "c"), axis=0, tiled=True)
        w_o = pick(o_full.reshape(heads, 4, HD, width), 1, at.quarter).reshape(local, width)
    selected = adapter_choice_index[0]
    a_model = pick(adapter_model_input_maps, 0, selected)
    a_hidden = pick(adapter_down_input_maps, 0, selected)
    b_model = pick(adapter_model_output_maps, 0, selected)
    b_hidden = pick(adapter_hidden_output_maps, 0, selected)
    a_qkv = a_model[:3].reshape(3 * rank, width)
    a_gu = a_model[4:6].reshape(2 * rank, width)
    a_o = head_cols(a_model[3], at.quarter)
    a_d = hidden_cols(a_hidden)
    b_qkv = head_cols(b_model[:3], at.quarter)
    b_o, b_d = b_model[3], b_model[4]
    b_gu = hidden_cols(b_hidden)

    def diagonal(maps):
        k, r, n = maps.shape
        zero = jnp.zeros((r, n), BF)
        return jnp.concatenate(
            [jnp.concatenate([maps[a] if a == b else zero for b in range(k)], axis=1) for a in range(k)], axis=0
        )

    b_qkv_diag = diagonal(b_qkv)
    gain = jnp.concatenate(
        [head_cols(query_norm_gain[None], at.quarter), head_cols(key_norm_gain[None], at.quarter)], axis=1
    )

    step_rows = jnp.arange(rows, dtype=jnp.int32)
    spot = lambda xx: at.p * 2 * rows + xx * rows + step_rows
    pos = jnp.concatenate([spot(at.x), spot(1 - at.x)])
    lengths = lax.dynamic_slice_in_dim(document_length, 2 * at.y, 2, 0)
    bounds = jnp.cumsum(lengths, axis=1)
    bounds = jnp.where(at.c == 0, bounds, bounds[::-1])

    def lo_of(pos):
        begin = jnp.max(jnp.where(bounds[:, None, :] <= pos[None, :, None], bounds[:, None, :], 0), axis=2)
        return jnp.maximum(begin, pos[None] - (WINDOW - 1))

    lo = lo_of(pos)
    key = jnp.stack([pos - 2 * rows * t for t in range(count)])
    attention = Attention(rows, heads, count, lo[:, :, None], pos[:, None], key)

    half_dim = HD // 2
    inv_freq = ROPE_BASE ** (-(jnp.arange(half_dim, dtype=F32) * 2.0 / HD))
    first = at.p * 2 * rows
    starts = jnp.stack([first + xx * rows - 2 * rows * t for t in range(count) for xx in (at.x, at.x, 1 - at.x, 1 - at.x)])
    wide_freq = jnp.concatenate([inv_freq, inv_freq])[None]
    sign = jnp.where(jnp.arange(HD) < half_dim, -1.0, 1.0)[None]
    turn_angle = starts.astype(F32)[:, None] * wide_freq
    row_angle = step_rows.astype(F32)[:, None] * wide_freq
    row_cos, row_sin = jnp.cos(row_angle), jnp.sin(row_angle)
    row_tables = jnp.stack([row_cos, row_sin, sign * row_cos, sign * row_sin])
    block_tables = jnp.stack([jnp.cos(turn_angle), jnp.sin(turn_angle)])

    own = 4 * rows
    pre_q, pre_k, value_all, narrow_qkv, square_q, square_k = project(
        inputs, own, w_qkv, a_qkv, b_qkv, heads
    )
    w_d = lax.all_gather(after(down_weight, square_q), "p", axis=0, tiled=True)
    inv_q, inv_k = scales(square_q, square_k, width, 2 * rows)
    query, key_all = post(pre_q, pre_k, inv_q, inv_k, gain, row_tables, block_tables, heads)
    o, log = attention.forward(query, key_all, value_all)
    narrow_o = dot_nt(o, a_o).astype(BF)
    def attn_part(part, mark=None):
        ins, narrow = o[part], narrow_o[part]
        if mark is not None:
            ins = after(ins, mark)
        return (dot(ins, w_o) + SCALE_ADAPT * dot(narrow, b_o)).astype(BF)

    near_rows, far_rows = slice(0, 2 * rows), slice(2 * rows, 4 * rows)
    attn_parts = at.scatter4(attn_part(far_rows), lambda mark: attn_part(near_rows, mark))
    attn_gain, feed_gain = attention_norm_gain[None], feedforward_norm_gain[None]
    attn_out, middle, low = by_rows(
        after_attention_kernel,
        "after_attention",
        rows,
        width,
        [*attn_parts, own_inputs, attn_gain],
        [F32, F32, BF],
        4,
    )
    middle_low = jnp.concatenate(at.gather8(low)[0])
    narrow_gu = dot_nt(middle_low, a_gu).astype(BF)
    gate, up, gated = gate_up(middle_low, w_gu, narrow_gu, b_gu)
    result, grad_mid, grad_attn, back_gu, wide, gb_d, later, later_logs = feed_layer(
        (a_d, b_d, b_gu, a_gu, feed_gain, attn_gain),
        narrow_gu,
        (gated, gate, up),
        (w_gu, w_d),
        middle,
        cotangent[0],
        attn_out,
        query,
        log[:, :, 0],
        reach,
    )
    lo_rows = jnp.stack([lo_of(pos + 2 * rows * t) for t in range(count)])
    query_rows = jnp.stack([pos + 2 * rows * t for t in range(count)])
    (dq, dk, dv), back_o, ga_gu = attend_back(
        at.np,
        reach,
        heads,
        rows,
        [
            grad_attn.reshape(4 * rows, width),
            w_o,
            a_o,
            b_o,
            *attention.tables,
            lo_rows,
            query_rows,
            log,
            later_logs,
            back_gu.reshape(8 * rows, -1),
            query,
            key_all,
            value_all,
            o,
        ],
        later,
        middle_low,
    )
    def share_y(mine, other):
        return mine + at.swap_y(other)

    def share_p(v):
        total = pick(v, 1, at.p)
        for by in range(1, at.np):
            total = total + at.turn_p(pick(v, 1, (at.p + by) % at.np), by)
        return total

    def sum_model(v):
        v = v.reshape(-1, at.np, 2, 2, 2 * depth)
        v = pick(v, 2, at.x) + at.swap_x(pick(v, 2, 1 - at.x))
        return share_y(pick(v, 2, at.y), pick(v, 2, 1 - at.y))

    mine = (jnp.arange(4) == at.quarter).astype(F32)

    def spread(v):
        return (v.reshape(-1, heads, 1, HD) * mine[:, None]).reshape(-1, width)

    grad_attn = grad_attn.reshape(4 * rows, -1)
    ga_o = SCALE_ADAPT * dot_tn(back_o, o)
    gb_o = SCALE_ADAPT * dot_tn(narrow_o, grad_attn)
    choose = (jnp.arange(adapter_model_input_maps.shape[0], dtype=jnp.int32) == selected).astype(F32)
    early = jnp.concatenate([ga_gu, spread(ga_o), gb_o, gb_d])
    wide = wide.reshape(3 * rank, -1)
    if 2 * depth == HD and hidden_rows == 2 * HD:
        outs = finish(
            at.np,
            heads,
            [
                dq,
                dk,
                dv,
                pre_q,
                pre_k,
                inv_q,
                inv_k,
                gain,
                row_tables,
                block_tables,
                a_qkv,
                b_qkv,
                narrow_qkv,
                early,
                wide,
                jnp.broadcast_to(choose[:, None], (choose.shape[0], 256)),
            ],
            w_qkv,
            inputs,
            grad_mid,
        )
        return (result[None], outs[0][None], *outs[1:])
    else:
        early = sum_model(after(early, dq))
        inputs, narrow_qkv, pre_k, inv_k = (v[:own] for v in (inputs, narrow_qkv, pre_k, inv_k))
        tables = [jnp.concatenate([rotation(row_tables, block_tables, b)[k] for b in range(4)]) for k in range(2)]
        cos, sin = tables
        wide = wide.reshape(-1, at.np, hidden_rows)
        dk = after(dk, early)
        turn, inner = unpost(dq, dk, pre_q, pre_k, gain, cos, sin, heads)
        inner = at.sum4(inner.T, 1).T / width

        def unnorm(part, pre, scale):
            cols = slice(part * local, (part + 1) * local)
            return (scale * turn[:, cols] - pre * (scale * scale * scale * inner[:, part : part + 1])).astype(BF)

        grad_qkv = jnp.concatenate(
            [unnorm(0, pre_q, inv_q), unnorm(1, pre_k, inv_k), dv.astype(BF)], axis=1
        )
        back_qkv = dot_nt(grad_qkv, b_qkv_diag).astype(BF)

        def late_adapters(mark):
            back = after(back_qkv, mark)
            ga_qkv = SCALE_ADAPT * dot_tn(back, inputs)
            gb_qkv = [
                SCALE_ADAPT * dot_tn(narrow_qkv[:, k * rank : (k + 1) * rank], grad_qkv[:, k * local : (k + 1) * local])
                for k in range(3)
            ]
            return sum_model(jnp.concatenate([ga_qkv, spread(jnp.concatenate(gb_qkv))]))

        def end_part(part, mark=None):
            ins, back = grad_qkv[part], back_qkv[part]
            if mark is not None:
                ins = after(ins, mark)
            return (dot_nt(ins, w_qkv) + SCALE_ADAPT * dot(back, a_qkv)).astype(BF)

        marks = []

        def end_near(mark):
            marks.append(mark)
            return end_part(near_rows, mark)

        end_parts = at.scatter4(end_part(far_rows), end_near)
        (grad_input,) = by_rows(end_kernel, "end", rows, width, [*end_parts, grad_mid], [F32], 3)
        late = late_adapters(marks[0])
        narrow_sums = share_p(jnp.concatenate([late, early], axis=0))
        narrow_sums = narrow_sums.reshape(narrow_sums.shape[0], 2, depth)
        sums = pick(narrow_sums, 1, at.c) + at.swap_core(pick(narrow_sums, 1, 1 - at.c))
        sums = sums.reshape(-1, rank, depth)
        late, early = sums[:6], sums[6:]
        wide = share_p(after(wide, marks[0])).reshape(-1, rank, hidden_rows)
    sum_a_model = choose[:, None, None, None] * jnp.concatenate([late[:3], early[2:3], early[:2]])[None]
    sum_a_hidden = choose[:, None, None] * wide[0][None]
    sum_b_model = choose[:, None, None, None] * jnp.concatenate([late[3:], early[3:]])[None]
    sum_b_hidden = choose[:, None, None, None] * wide[1:][None]
    return (result[None], grad_input[None], sum_a_model, sum_a_hidden, sum_b_model, sum_b_hidden)


def solution(mesh):
    grid = mesh.devices.reshape(mesh.shape["ctx"] // 2, 2, mesh.shape["wt"] // 2, 2)
    split = Mesh(grid, ("p", "x", "y", "c"))
    everyone = ("p", "x", "y", "c")
    rows = P(everyone, None)
    tokens = P(("y", "c"), ("p", "x"), None)
    placed = (tokens, tokens, P(), P()) + (rows,) * 7 + (P(),) * 8
    return jax.shard_map(
        on_device,
        mesh=split,
        in_specs=placed,
        out_specs=(
            tokens,
            tokens,
            P(None, None, None, everyone),
            P(None, None, everyone),
            P(None, None, None, everyone),
            P(None, None, None, everyone),
        ),
        check_vma=False,
    )
```
